32 devices in a mesh: pre: 4 (over x, core), seq: 8 (over z, y).
Axes of the slice: x: 2, y: 2, z: 4, core: 2. Of those that a mesh axis runs over, the one named last changes fastest.
Arguments:
- prefix_in: bfloat16 [8, 512, 2048], P('seq', 'pre'), may hold values from -13 to 13
- later_in: bfloat16 [8, 768, 2048], P('seq', 'pre'), may hold values from -13 to 13
- doc_lengths: int32 [8, 4], P('seq'), may hold values from 1 to 384, 768 in all within a row
- doc_exit: int32 [8, 4], P('seq'), may hold values from 1 to 24
- token_skip: int32 [8, 768], P('seq'), may hold values 0 or 1
- first_gain: bfloat16 [2048], P('seq'), may hold values from 0.5 to 1.5
- first_bias: bfloat16 [2048], P('seq'), may hold values from -1.25 to 1.25
- qkv_weight: bfloat16 [2048, 6144], P('seq'), may hold values from -0.125 to 0.125
- query_bias: bfloat16 [2048], P('seq'), may hold values from -3 to 3
- value_bias: bfloat16 [2048], P('seq'), may hold values from -1.75 to 1.75
- out_weight: bfloat16 [2048, 2048], P('seq'), may hold values from -1 to 1
- out_bias: bfloat16 [2048], P('seq'), may hold values from -1.25 to 1.25
- second_gain: bfloat16 [2048], P('seq'), may hold values from 0.5 to 1.5
- second_bias: bfloat16 [2048], P('seq'), may hold values from -1.25 to 1.25
- up_weight: bfloat16 [2048, 8192], P('seq'), may hold values from -0.125 to 0.125
- up_bias: bfloat16 [8192], P('seq'), may hold values from -1.75 to 1.75
- down_weight: bfloat16 [2048, 8192], P('seq'), may hold values from -0.0625 to 0.0625
- down_bias: bfloat16 [2048], P('seq'), may hold values from -1.25 to 1.25
- prefix_cot: bfloat16 [8, 512, 2048], P('seq', 'pre'), may hold values from -6 to 6
- later_cot: bfloat16 [8, 768, 2048], P('seq', 'pre'), may hold values from -6 to 6
Outputs:
- prefix_out: bfloat16 [8, 512, 2048], P('seq', 'pre')
- later_out: bfloat16 [8, 768, 2048], P('seq', 'pre')
- prefix_grad: bfloat16 [8, 512, 2048], P('seq', 'pre')
- later_grad: bfloat16 [8, 768, 2048], P('seq', 'pre')
- first_gain_grad: float32 [2048], P('seq')
- first_bias_grad: float32 [2048], P('seq')
- qkv_weight_grad: float32 [2048, 6144], P('seq')
- query_bias_grad: float32 [2048], P('seq')
- value_bias_grad: float32 [2048], P('seq')
- out_weight_grad: float32 [2048, 2048], P('seq')
- out_bias_grad: float32 [2048], P('seq')
- second_gain_grad: float32 [2048], P('seq')
- second_bias_grad: float32 [2048], P('seq')
- up_weight_grad: float32 [2048, 8192], P('seq')
- up_bias_grad: float32 [8192], P('seq')
- down_weight_grad: float32 [2048, 8192], P('seq')
- down_bias_grad: float32 [2048], P('seq')
- residual_rms: float32 [3], replicated
The draws below stay inside these ranges and needn't reach their ends.
Inputs may be any that keep to these rules, and one draw needn't show every extreme that they name: `doc_lengths`: each row's 4 lengths sum to 768; the longest in each row is exactly 384.
All inputs are finite; a program needn't handle non-finite values. No bound on the sum of `token_skip` on one device may be relied on, other than what follows from the above.
Results may differ from the reference program's by a relative error of at most 0.018.
Values may be sent and summed in bfloat16 or wider, within the bound.
A program may use at most 768 MiB of HBM per device.

```python
import math
import jax
import jax.numpy as jnp
import numpy as np
from jax import lax

D = 2048
HEADS = 32
HEAD_DIM = 64
FF = 8192
LAYERS = 24
LAYER = 12
PRE = 512
NDOC = 4
SUF = 768
ROWS = 8


def input_draw(key, places, shape):
    scaling = 0.6 + 0.8 * places.astype(jnp.float32) / (PRE + SUF)
    row_place = jnp.arange(ROWS).astype(jnp.float32) / max(ROWS - 1, 1)
    row_scaling = 0.5 * jnp.exp(row_place * 1.0986123)
    base = jnp.clip(jax.random.normal(key, shape, jnp.float32), -6.0, 6.0)
    return (base * scaling[None, :, None] * row_scaling[:, None, None]).astype(jnp.bfloat16)


def draw_prefix_in(key, part):
    return input_draw(jax.random.fold_in(key, 17), jnp.arange(PRE), (ROWS, PRE, D))


def draw_later_in(key, part):
    return input_draw(jax.random.fold_in(key, 29), PRE + jnp.arange(SUF), (ROWS, SUF, D))


def set_ends(values, stream_key, least, high):
    shape = values.shape
    place = [jax.random.randint(jax.random.fold_in(stream_key, axis), (), 0, shape[axis]) for axis in range(len(shape))]
    values = values.at[tuple(place)].set(least)
    longest = shape.index(max(shape))
    place[longest] = (place[longest] + 1) % shape[longest]
    return values.at[tuple(place)].set(high)


def block_levels(stream_key, shape, pieces, smallest, high):
    def one(position, shards_of):
        draws = jax.random.uniform(jax.random.fold_in(jax.random.fold_in(stream_key, 6), position), (shards_of,), jnp.float32, smallest / len(pieces), high / len(pieces))
        return jnp.repeat(jnp.exp(draws), shape[position] // shards_of).reshape((-1,) + (1,) * (len(shape) - position - 1))

    level = one(*pieces[0])
    for cut in pieces[1:]:
        level = level * one(*cut)
    return level


def length_profile(count, total, reach, lean):
    portions = [(1 << 20) // math.isqrt(standing ** lean) + 1 for standing in range(2, count + 1)]
    spare, counts = total - reach - (count - 1), [1] * (count - 1)
    while spare > 0:
        movable = [i for i in range(count - 1) if counts[i] < reach]
        pool, remaining = sum([portions[i] for i in movable]), spare
        for i in movable:
            extra = min(reach - counts[i], max(1, remaining * portions[i] // pool), spare)
            counts[i] = counts[i] + extra
            spare = spare - extra
    return np.array([reach] + counts)


def uneven(own_key, amount, total, bound, lean):
    if amount == 2:
        one = jax.random.randint(own_key, (), max(1, total - bound), min(bound, total - 1) + 1)
        return jnp.stack([one, total - one])
    sizes = jnp.asarray(length_profile(amount, total, bound, lean), jnp.int32)
    couples = (amount - 1) // 2
    donor, taker = sizes[1:1 + 2 * couples:2], sizes[2:2 + 2 * couples:2]
    room = jnp.minimum(donor - 1, bound - taker)
    shifted = jax.random.randint(jax.random.fold_in(own_key, 1), (couples,), 0, 1 << 20) % (room + 1)
    sizes = sizes.at[1:1 + 2 * couples:2].set(donor - shifted).at[2:2 + 2 * couples:2].set(taker + shifted)
    return sizes[jax.random.permutation(jax.random.fold_in(own_key, 2), amount)]


def gaussian(key, dims, spread, limit, shards=(), kind=jnp.bfloat16):
    loudness = block_levels(key, dims, shards, -0.22, 0.18) if shards else 1.0
    entries = jax.random.normal(key, dims, jnp.float32) * spread * loudness
    return jnp.minimum(jnp.maximum(entries, -limit), limit).astype(kind)


def setup_inputs(seed: int = 0) -> dict:
    splits = jax.random.split(jax.random.key(seed), 21)
    prefix_in = draw_prefix_in(jax.random.fold_in(splits[20], 71), 0)
    later_in = draw_later_in(jax.random.fold_in(splits[20], 71), 0)
    doc_lengths = jax.vmap(lambda own: uneven(own, NDOC, SUF, SUF // 2, 2))(jax.random.split(splits[2], ROWS)).reshape((ROWS, NDOC)).astype(jnp.int32)
    doc_exit = set_ends(jax.random.randint(splits[3], (ROWS, NDOC), 1, LAYERS + 1), jax.random.fold_in(splits[3], 1), 1, LAYERS).astype(jnp.int32)
    token_skip = set_ends((jax.random.randint(splits[4], (ROWS, SUF), 0, 4) < 1).astype(jnp.int32), jax.random.fold_in(splits[4], 1), 0, 1)
    first_gain = jnp.clip(1.0 + 0.1 * jax.random.normal(splits[5], (D,), jnp.float32), 0.5, 1.5).astype(jnp.bfloat16)
    first_bias = gaussian(splits[6], (D,), 0.2, 1.25, ((0, 8),))
    qkv_weight = gaussian(splits[7], (D, 3 * D), D ** -0.5, 0.125, ((0, 8),))
    query_bias = gaussian(splits[8], (D,), 0.5, 3.0, ((0, 8),))
    value_bias = gaussian(splits[9], (D,), 0.3, 1.75, ((0, 8),))
    out_weight = gaussian(splits[10], (D, D), (D // 64) ** -0.5, 1.0, ((0, 8),))
    out_bias = gaussian(splits[11], (D,), 0.2, 1.25, ((0, 8),))
    second_gain = jnp.clip(1.0 + 0.1 * jax.random.normal(splits[12], (D,), jnp.float32), 0.5, 1.5).astype(jnp.bfloat16)
    second_bias = gaussian(splits[13], (D,), 0.2, 1.25, ((0, 8),))
    up_weight = gaussian(splits[14], (D, FF), D ** -0.5, 0.125, ((0, 8),))
    up_bias = gaussian(splits[15], (FF,), 0.3, 1.75, ((0, 8),))
    down_weight = gaussian(splits[16], (D, FF), FF ** -0.5, 0.0625, ((0, 8),))
    down_bias = gaussian(splits[17], (D,), 0.2, 1.25, ((0, 8),))
    prefix_cot = gaussian(splits[18], (ROWS, PRE, D), 1.0, 6.0, ((0, 8), (1, 4)))
    later_cot = gaussian(splits[19], (ROWS, SUF, D), 1.0, 6.0, ((0, 8), (1, 4)))
    return {"prefix_in": prefix_in, "later_in": later_in, "doc_lengths": doc_lengths, "doc_exit": doc_exit, "token_skip": token_skip, "first_gain": first_gain, "first_bias": first_bias, "qkv_weight": qkv_weight, "query_bias": query_bias, "value_bias": value_bias, "out_weight": out_weight, "out_bias": out_bias, "second_gain": second_gain, "second_bias": second_bias, "up_weight": up_weight, "up_bias": up_bias, "down_weight": down_weight, "down_bias": down_bias, "prefix_cot": prefix_cot, "later_cot": later_cot}


EPS = 1e-05
NEG = -1e+30
HIGH = lax.Precision.HIGHEST

@jax.custom_vjp
def low(v):
    return lax.optimization_barrier(v.astype(jnp.bfloat16)).astype(jnp.float32)

@jax.custom_vjp
def low_back(v):
    return v

def low_keep(v):
    return (low(v), None)

def low_pass(kept, grad):
    return (grad,)

def back_keep(v):
    return (v, None)

def back_low(kept, grad):
    return (low(grad),)
low.defvjp(low_keep, low_pass)
low_back.defvjp(back_keep, back_low)

def layer_norm(values, gain, bias):
    mean = lax.optimization_barrier(jnp.mean(values, axis=-1, keepdims=True))
    centred = values - mean
    variance = lax.optimization_barrier(jnp.mean(centred * centred, axis=-1, keepdims=True))
    return centred * lax.rsqrt(variance + EPS) * gain + bias

def token_tables(doc_lengths, doc_exit, token_skip):
    ends = jnp.cumsum(doc_lengths, axis=-1, dtype=jnp.int32)
    starts = ends - doc_lengths
    places = jnp.arange(token_skip.shape[-1], dtype=jnp.int32)
    doc_id = lax.optimization_barrier(jnp.sum((places[:, None] >= starts[..., None, :]).astype(jnp.int32), axis=-1, dtype=jnp.int32)) - 1
    kinds = jnp.arange(doc_lengths.shape[-1], dtype=jnp.int32)
    live_doc = doc_exit > LAYER
    live = jnp.any((doc_id[..., None] == kinds) & live_doc[..., None, :], axis=-1) & (token_skip == 0)
    return (doc_id, live)

def row_forward(params, row_in, lengths, exits, skips):
    first_gain, first_bias, qkv_weight, query_bias, value_bias, out_weight, out_bias, second_gain, second_bias, up_weight, up_bias, down_weight, down_bias = params
    length = row_in.shape[0]
    scale = 1.0 / math.sqrt(HEAD_DIM)
    doc_id, live = token_tables(lengths, exits, skips)
    doc_all = jnp.concatenate([jnp.full((PRE,), -1, jnp.int32), doc_id.astype(jnp.int32)])
    live_all = jnp.concatenate([jnp.ones((PRE,), jnp.int32), live.astype(jnp.int32)]) > 0
    places = jnp.arange(length, dtype=jnp.int32)
    allowed = (places[None, :] <= places[:, None]) & ((places[None, :] < PRE) | (doc_all[:, None] == doc_all[None, :]) & live_all[None, :])
    active = live_all.astype(jnp.float32)
    first_h = low(layer_norm(row_in, first_gain, first_bias))
    projected = jnp.dot(first_h, qkv_weight, precision=HIGH)
    queries = low(low_back((projected[:, :D] + query_bias) * scale))
    keys = low(low_back(projected[:, D:2 * D]))
    values = low(low_back(projected[:, 2 * D:] + value_bias))
    heads_q = queries.reshape(length, HEADS, HEAD_DIM)
    heads_k = keys.reshape(length, HEADS, HEAD_DIM)
    heads_v = values.reshape(length, HEADS, HEAD_DIM)
    scores = low_back(jnp.einsum('qhd,khd->hqk', heads_q, heads_k, precision=HIGH))
    scores = jnp.where(allowed[None], scores, NEG)
    probs = low(jax.nn.softmax(scores, axis=-1))
    mixed = jnp.einsum('hqk,khd->qhd', probs, heads_v, precision=HIGH).reshape(length, D)
    mixed = low(low_back(mixed))
    attn = low_back(jnp.dot(mixed, out_weight, precision=HIGH) + out_bias)
    middle = row_in + attn
    second_h = low(layer_norm(middle, second_gain, second_bias))
    upper = low_back(jnp.dot(second_h, up_weight, precision=HIGH) + up_bias)
    acted = low(jax.nn.gelu(upper, approximate=False))
    ffn = jnp.dot(acted, down_weight.T, precision=HIGH) + down_bias
    result = row_in + active[:, None] * (attn + ffn)
    sums = jnp.stack([jnp.sum(active * lax.optimization_barrier(jnp.sum(result * result, axis=-1))), jnp.sum(active * lax.optimization_barrier(jnp.sum(attn * attn, axis=-1))), jnp.sum(active * lax.optimization_barrier(jnp.sum(ffn * ffn, axis=-1))), jnp.sum(active)])
    return (result, sums)

def reference(prefix_in, later_in, doc_lengths, doc_exit, token_skip, first_gain, first_bias, qkv_weight, query_bias, value_bias, out_weight, out_bias, second_gain, second_bias, up_weight, up_bias, down_weight, down_bias, prefix_cot, later_cot):
    params = tuple((w.astype(jnp.float32) for w in (first_gain, first_bias, qkv_weight, query_bias, value_bias, out_weight, out_bias, second_gain, second_bias, up_weight, up_bias, down_weight, down_bias)))
    joined = jnp.concatenate([prefix_in, later_in], axis=1).astype(jnp.float32)

    def run(weights, inputs):

        def step(totals, row):
            row_in, lengths, exits, skips = row
            result, sums = jax.checkpoint(row_forward)(weights, row_in, lengths, exits, skips)
            return (totals + sums, result)
        totals, results = lax.scan(step, jnp.zeros((4,), jnp.float32), (inputs, doc_lengths, doc_exit, token_skip))
        return (results, totals)
    results, pullback, totals = jax.vjp(run, params, joined, has_aux=True)
    cotangent = jnp.concatenate([prefix_cot, later_cot], axis=1).astype(jnp.float32)
    grads, input_grad = pullback(cotangent)
    residual_rms = jnp.sqrt(totals[:3] / (totals[3] * D))
    return (results[:, :PRE].astype(jnp.bfloat16), results[:, PRE:].astype(jnp.bfloat16), input_grad[:, :PRE].astype(jnp.bfloat16), input_grad[:, PRE:].astype(jnp.bfloat16), grads[0], grads[1], grads[2], grads[3], grads[4], grads[5], grads[6], grads[7], grads[8], grads[9], grads[10], grads[11], grads[12], residual_rms)
```

```python
import functools
import math

import jax
import jax.numpy as jnp
from jax import lax
from jax.experimental import pallas as pl
from jax.experimental.pallas import tpu as pltpu
from jax.sharding import PartitionSpec as P

D = 2048
HEADS = 32
HEAD_DIM = 64
FF = 8192
LAYER = 12
PRE = 512

EPS = 1e-05
NEG = -1e30
BF = jnp.bfloat16
F32 = jnp.float32
TILE = 256


def layer_norm_parts(values, gain, bias):
    mean = jnp.mean(values, axis=-1, keepdims=True)
    centred = values - mean
    variance = jnp.mean(centred * centred, axis=-1, keepdims=True)
    scaling = lax.rsqrt(variance + EPS)
    normed = centred * scaling
    return (normed * gain + bias, normed, scaling)


def norm_back(grad, normed, scaling, gain):
    scaled = grad * gain
    inner = jnp.mean(scaled, axis=-1, keepdims=True)
    cross = jnp.mean(scaled * normed, axis=-1, keepdims=True)
    return scaling * (scaled - inner - normed * cross)


def gelu_slope(upper):
    cumulative = 0.5 * (1.0 + lax.erf(upper * (1.0 / math.sqrt(2.0))))
    density = jnp.exp(-0.5 * upper * upper) * (1.0 / math.sqrt(2.0 * math.pi))
    return cumulative + upper * density


def token_tables(doc_lengths, doc_exit, token_skip):
    order = jnp.arange(doc_lengths.shape[-1], dtype=jnp.int32)
    earlier = order[None, :] < order[:, None]
    starts = jnp.sum(
        jnp.where(earlier, doc_lengths[..., None, :], 0), axis=-1, dtype=jnp.int32
    )
    places = jnp.arange(token_skip.shape[-1], dtype=jnp.int32)
    doc_id = (
        jnp.sum(
            (places[:, None] >= starts[..., None, :]).astype(jnp.int32), axis=-1, dtype=jnp.int32
        )
        - 1
    )
    live_doc = doc_exit > LAYER
    live = jnp.any((doc_id[..., None] == order) & live_doc[..., None, :], axis=-1) & (
        token_skip == 0
    )
    return (doc_id, live)


def dot_nt(a, b):
    return lax.dot_general(a, b, (((1,), (1,)), ((), ())), preferred_element_type=F32)


def dot_nn(a, b):
    return lax.dot_general(a, b, (((1,), (0,)), ((), ())), preferred_element_type=F32)


def dot_tn(a, b):
    return lax.dot_general(a, b, (((0,), (0,)), ((), ())), preferred_element_type=F32)


def gather_positions(place, ref, whole, pre_part, later_part):
    parts = ref.shape[0]
    for member in range(parts):
        source = jnp.bitwise_xor(place, member)
        whole[member * pre_part : (member + 1) * pre_part, :] = ref[source, :pre_part, :]
        start = parts * pre_part + member * later_part
        whole[start : start + later_part, :] = ref[source, pre_part:, :]


def scatter_positions(place, whole, ref, pre_part, later_part, lanes):
    parts = ref.shape[0]
    for member in range(parts):
        target = jnp.bitwise_xor(place, member)
        ref[target, :pre_part, lanes] = whole[
            member * pre_part : (member + 1) * pre_part, :
        ].astype(ref.dtype)
        start = parts * pre_part + member * later_part
        ref[target, pre_part:, lanes] = whole[start : start + later_part, :].astype(ref.dtype)


def masked_scores(block, scores, tile, codes_q, codes_k):
    rows = lax.broadcasted_iota(jnp.int32, (TILE, TILE), 0)
    cols = lax.broadcasted_iota(jnp.int32, (TILE, TILE), 1)
    allowed = None
    if tile == block:
        allowed = cols <= rows
    if tile * TILE >= PRE:
        same = (
            codes_q[block * TILE : (block + 1) * TILE, :]
            == codes_k[:, tile * TILE : (tile + 1) * TILE]
        )
        allowed = same if allowed is None else allowed & same
    if allowed is None:
        return scores
    return jnp.where(allowed, scores, NEG)


def attend_kernel(
    pre_part, later_part, place_ref, q_ref, k_ref, v_ref, cq_ref, ck_ref, o_ref, stat_ref, q_all, k_all, v_all, o_all
):
    place = place_ref[0]
    gather_positions(place, q_ref, q_all, pre_part, later_part)
    gather_positions(place, k_ref, k_all, pre_part, later_part)
    gather_positions(place, v_ref, v_all, pre_part, later_part)
    codes_q = cq_ref[...]
    codes_k = ck_ref[...]
    blocks = q_all.shape[0] // TILE
    for head in range(2):
        lanes = slice(head * HEAD_DIM, (head + 1) * HEAD_DIM)
        for block in range(blocks):
            rows = slice(block * TILE, (block + 1) * TILE)
            queries = q_all[rows, lanes]
            scores = [
                masked_scores(
                    block,
                    dot_nt(queries, k_all[tile * TILE : (tile + 1) * TILE, lanes]),
                    tile,
                    codes_q,
                    codes_k,
                )
                for tile in range(block + 1)
            ]
            top = functools.reduce(jnp.maximum, [jnp.max(s, axis=1, keepdims=True) for s in scores])
            powers = [jnp.exp(s - top) for s in scores]
            total = functools.reduce(jnp.add, [jnp.sum(e, axis=1, keepdims=True) for e in powers])
            share = 1.0 / total
            mixed = functools.reduce(
                jnp.add,
                [
                    dot_nn((e * share).astype(BF), v_all[tile * TILE : (tile + 1) * TILE, lanes])
                    for tile, e in enumerate(powers)
                ],
            )
            o_all[rows, lanes] = mixed
            stat_ref[0, rows, lanes] = jnp.broadcast_to(top + jnp.log(total), (TILE, HEAD_DIM))
    scatter_positions(place, o_all, o_ref, pre_part, later_part, slice(None))


def attend(place, qkv, codes_q, codes_k, pre_part, later_part):
    parts, part, width = qkv.shape
    pairs = width // 3 // 128
    length = parts * part
    block = (parts, part, 128)
    return pl.pallas_call(
        functools.partial(attend_kernel, pre_part, later_part),
        out_shape=(
            jax.ShapeDtypeStruct((parts, part, width // 3), BF),
            jax.ShapeDtypeStruct((pairs, length, 128), F32),
        ),
        grid_spec=pltpu.PrefetchScalarGridSpec(
            num_scalar_prefetch=1,
            grid=(pairs,),
            in_specs=[
                pl.BlockSpec(block, lambda i, _: (0, 0, i)),
                pl.BlockSpec(block, lambda i, _: (0, 0, pairs + i)),
                pl.BlockSpec(block, lambda i, _: (0, 0, 2 * pairs + i)),
                pl.BlockSpec((length, 1), lambda i, _: (0, 0)),
                pl.BlockSpec((1, length), lambda i, _: (0, 0)),
            ],
            out_specs=[
                pl.BlockSpec(block, lambda i, _: (0, 0, i)),
                pl.BlockSpec((1, length, 128), lambda i, _: (i, 0, 0)),
            ],
            scratch_shapes=[
                pltpu.VMEM((length, 128), BF),
                pltpu.VMEM((length, 128), BF),
                pltpu.VMEM((length, 128), BF),
                pltpu.VMEM((length, 128), F32),
            ],
        ),
        compiler_params=pltpu.CompilerParams(vmem_limit_bytes=48 * 2**20),
        cost_estimate=pl.CostEstimate(
            flops=pairs * 2 * 15 * 4 * 2 * TILE * TILE * 256,
            bytes_accessed=length * width * 3,
            transcendentals=pairs * 2 * 15 * TILE * TILE,
        ),
        name="attend",
    )(place, qkv, qkv, qkv, codes_q, codes_k)


def attend_back_kernel(
    pre_part,
    later_part,
    pairs,
    place_ref,
    q_ref,
    k_ref,
    v_ref,
    do_ref,
    stat_ref,
    cq_ref,
    ck_ref,
    grad_ref,
    q_all,
    k_all,
    v_all,
    do_all,
    dq_all,
    dk_all,
    dv_all,
):
    place = place_ref[0]
    step = pl.program_id(0)
    gather_positions(place, q_ref, q_all, pre_part, later_part)
    gather_positions(place, k_ref, k_all, pre_part, later_part)
    gather_positions(place, v_ref, v_all, pre_part, later_part)
    gather_positions(place, do_ref, do_all, pre_part, later_part)
    codes_q = cq_ref[...]
    codes_k = ck_ref[...]
    dk_all[...] = jnp.zeros_like(dk_all)
    dv_all[...] = jnp.zeros_like(dv_all)
    blocks = q_all.shape[0] // TILE
    for head in range(2):
        lanes = slice(head * HEAD_DIM, (head + 1) * HEAD_DIM)
        for block in range(blocks):
            rows = slice(block * TILE, (block + 1) * TILE)
            queries = q_all[rows, lanes]
            grads = do_all[rows, lanes]
            level = stat_ref[0, rows, head * HEAD_DIM : head * HEAD_DIM + 1]
            probs = []
            dprobs = []
            for tile in range(block + 1):
                cols = slice(tile * TILE, (tile + 1) * TILE)
                scores = masked_scores(
                    block, dot_nt(queries, k_all[cols, lanes]), tile, codes_q, codes_k
                )
                probs.append(jnp.exp(scores - level))
                dprobs.append(dot_nt(grads, v_all[cols, lanes]))
            delta = functools.reduce(
                jnp.add, [jnp.sum(a * b, axis=1, keepdims=True) for a, b in zip(probs, dprobs)]
            )
            dq = None
            for tile in range(block + 1):
                cols = slice(tile * TILE, (tile + 1) * TILE)
                ds = (probs[tile] * (dprobs[tile] - delta)).astype(BF)
                part = dot_nn(ds, k_all[cols, lanes])
                dq = part if dq is None else dq + part
                dk_all[cols, lanes] += dot_tn(ds, queries)
                dv_all[cols, lanes] += dot_tn(probs[tile].astype(BF), grads)
            dq_all[rows, lanes] = dq * (1.0 / math.sqrt(HEAD_DIM))
    for third, source in enumerate((dq_all, dk_all, dv_all)):
        start = pl.multiple_of((third * pairs + step) * 128, 128)
        scatter_positions(place, source, grad_ref, pre_part, later_part, pl.ds(start, 128))


def attend_back(place, qkv, grad_out, stats, codes_q, codes_k, pre_part, later_part):
    parts, part, width = qkv.shape
    pairs = width // 3 // 128
    length = parts * part
    block = (parts, part, 128)
    return pl.pallas_call(
        functools.partial(attend_back_kernel, pre_part, later_part, pairs),
        out_shape=jax.ShapeDtypeStruct((parts, part, width), BF),
        grid_spec=pltpu.PrefetchScalarGridSpec(
            num_scalar_prefetch=1,
            grid=(pairs,),
            in_specs=[
                pl.BlockSpec(block, lambda i, _: (0, 0, i)),
                pl.BlockSpec(block, lambda i, _: (0, 0, pairs + i)),
                pl.BlockSpec(block, lambda i, _: (0, 0, 2 * pairs + i)),
                pl.BlockSpec(block, lambda i, _: (0, 0, i)),
                pl.BlockSpec((1, length, 128), lambda i, _: (i, 0, 0)),
                pl.BlockSpec((length, 1), lambda i, _: (0, 0)),
                pl.BlockSpec((1, length), lambda i, _: (0, 0)),
            ],
            out_specs=pl.BlockSpec((parts, part, width), lambda i, _: (0, 0, 0)),
            scratch_shapes=[pltpu.VMEM((length, 128), BF)] * 4 + [pltpu.VMEM((length, 128), F32)] * 3,
        ),
        compiler_params=pltpu.CompilerParams(vmem_limit_bytes=56 * 2**20),
        cost_estimate=pl.CostEstimate(
            flops=pairs * 2 * 15 * 10 * TILE * TILE * 256,
            bytes_accessed=length * width * 6,
            transcendentals=pairs * 2 * 15 * TILE * TILE,
        ),
        name="attend_back",
    )(place, qkv, qkv, qkv, grad_out, stats, codes_q, codes_k)


class Seq:
    def __init__(self):
        self.size = lax.axis_size("seq")
        self.lines = self.size // 2
        place = lax.axis_index("seq")
        self.line = place // 2
        self.twin = place % 2

    def send(self, value, shift, valid):
        pairs = [
            (i, i + 2 * shift)
            for i in range(self.size)
            if valid(i // 2) and 0 <= i // 2 + shift < self.lines
        ]
        return lax.ppermute(value, "seq", pairs)

    def swap(self, value, valid=lambda line: True):
        return lax.ppermute(value, "seq", [(i, i ^ 1) for i in range(self.size) if valid(i // 2)])

    def gather(self, own):
        lines = self.lines
        below, above = {0: own}, {0: own}
        twin_below, twin_above = {}, {}
        twin_own = self.swap(own)
        for k in range(1, lines):
            below[k] = self.send(below[k - 1], 1, lambda line, k=k: line >= k - 1)
            above[k] = self.send(above[k - 1], -1, lambda line, k=k: line + k - 1 < lines)
            twin_below[k] = self.swap(below[k], lambda line, k=k: line >= k)
            twin_above[k] = self.swap(above[k], lambda line, k=k: line + k < lines)
        blocks = [own, twin_own]
        for m in range(1, lines):
            up = self.line + m < lines
            blocks.append(jnp.where(up, above[m], below[lines - m]))
            blocks.append(jnp.where(up, twin_above[m], twin_below[lines - m]))
        return blocks

    def reduce(self, blocks):
        lines = self.lines
        held = {}
        order = sorted(range(lines), key=lambda m: -min(m, lines - m) if m else 1)
        for m in order:
            other = self.swap(blocks[2 * m + 1])
            held[m] = blocks[2 * m].astype(F32) + other.astype(F32)
        up = down = None
        for k in range(lines - 1, 0, -1):
            going_up = held[k] if up is None else held[k] + up.astype(F32)
            up = self.send(going_up.astype(BF), 1, lambda line, k=k: line + k < lines)
            going_down = held[lines - k] if down is None else held[lines - k] + down.astype(F32)
            down = self.send(going_down.astype(BF), -1, lambda line, k=k: line - k >= 0)
        return held[0] + up.astype(F32) + down.astype(F32)

    def to_relative(self, value, axis):
        size = value.shape[axis]
        block = size // self.size
        twice = jnp.concatenate([value, value], axis=axis)
        rolled = lax.dynamic_slice_in_dim(twice, self.line * 2 * block, size, axis)
        return self.flip(rolled, axis)

    def flip(self, value, axis):
        shape = value.shape
        block = shape[axis] // self.size
        split = shape[:axis] + (self.lines, 2, block) + shape[axis + 1 :]
        swapped = lax.rev(value.reshape(split), (axis + 1,)).reshape(shape)
        return jnp.where(self.twin == 1, swapped, value)

    def to_absolute(self, value, axis):
        size = value.shape[axis]
        block = size // self.size
        flipped = self.flip(value, axis)
        twice = jnp.concatenate([flipped, flipped], axis=axis)
        start = lax.rem(self.lines - self.line, self.lines) * 2 * block
        return lax.dynamic_slice_in_dim(twice, start, size, axis)


def over_pre(value, mask):
    return lax.ppermute(value, "pre", [(i, i ^ mask) for i in range(lax.axis_size("pre"))])


def gather_pre(own):
    far = over_pre(own, 2)
    near = over_pre(own, 1)
    return [own, near, far, over_pre(far, 1)]


def scatter_pre(blocks):
    a = blocks[0] + over_pre(blocks[1].astype(BF), 1).astype(F32)
    b = blocks[2] + over_pre(blocks[3].astype(BF), 1).astype(F32)
    return a + over_pre(b.astype(BF), 2).astype(F32)


def sum_all(value):
    for mask in (1, 2):
        value = value + over_pre(value, mask)
    size = lax.axis_size("seq")
    mask = 1
    while mask < size:
        value = value + lax.ppermute(value, "seq", [(i, i ^ mask) for i in range(size)])
        mask *= 2
    return value


def absolute_pre(blocks, place):
    first = place % 2 == 0
    low = place < 2
    a = [jnp.where(first, blocks[0], blocks[1]), jnp.where(first, blocks[1], blocks[0])]
    b = [jnp.where(first, blocks[2], blocks[3]), jnp.where(first, blocks[3], blocks[2])]
    return [jnp.where(low, u, w) for u, w in zip(a, b)] + [jnp.where(low, w, u) for u, w in zip(a, b)]


def on_device(
    prefix_in,
    later_in,
    doc_lengths,
    doc_exit,
    token_skip,
    first_gain,
    first_bias,
    qkv_weight,
    query_bias,
    value_bias,
    out_weight,
    out_bias,
    second_gain,
    second_bias,
    up_weight,
    up_bias,
    down_weight,
    down_bias,
    prefix_cot,
    later_cot,
):
    scale = 1.0 / math.sqrt(HEAD_DIM)
    pre_part = prefix_in.shape[1]
    later_part = later_in.shape[1]
    part = pre_part + later_part
    parts = lax.axis_size("pre")
    place = lax.axis_index("pre")
    seq = Seq()
    seq_count = seq.size
    seq_place = lax.axis_index("seq")
    own_d = D // seq_count
    cols = D // parts
    ff_cols = FF // parts
    length = parts * part

    packed = jnp.concatenate(
        [
            first_gain,
            first_bias,
            query_bias,
            value_bias,
            out_bias,
            second_gain,
            second_bias,
            down_bias,
            up_bias,
        ]
    ).reshape(-1, 128)
    small = jnp.stack(seq.gather(packed)).reshape(seq_count, -1)
    small = seq.to_absolute(small, 0).astype(F32)
    vectors = [small[:, i * own_d : (i + 1) * own_d].reshape(D) for i in range(8)]
    full_up_bias = small[:, 8 * own_d :].reshape(FF)
    (gain1, bias1, qb, vb, ob, gain2, bias2, db) = vectors

    def section(weight, start, width):
        return lax.dynamic_slice_in_dim(weight, start + place * width, width, 1)

    own_qkv = jnp.concatenate([section(qkv_weight, i * D, cols) for i in range(3)], axis=1)
    block_rows = own_d // parts
    out_block = lax.dynamic_slice_in_dim(out_weight, place * block_rows, block_rows, 0)
    out_block = out_weight.reshape(parts, block_rows, D)
    out_block = lax.dynamic_index_in_dim(out_block, place, 0, keepdims=False)
    shuffle = [
        ((b % parts) * seq_count + b // parts, (b // seq_count) * seq_count + b % seq_count)
        for b in range(parts * seq_count)
    ]
    own_out = lax.ppermute(out_block, ("pre", "seq"), shuffle)
    w_qkv = jnp.concatenate(seq.gather(own_qkv), axis=0)
    w_out = seq.to_absolute(jnp.concatenate(seq.gather(own_out), axis=0), 0)
    w_up = jnp.concatenate(seq.gather(section(up_weight, 0, ff_cols)), axis=0)
    w_down = jnp.concatenate(seq.gather(section(down_weight, 0, ff_cols)), axis=0)

    doc_id, live = token_tables(doc_lengths, doc_exit, token_skip)
    live_here = lax.dynamic_slice_in_dim(live[0], place * later_part, later_part, 0)
    active = jnp.concatenate([jnp.ones((pre_part,), F32), live_here.astype(F32)])[:, None]
    codes_q = jnp.concatenate([jnp.full((PRE,), -1, jnp.int32), doc_id[0]])[:, None]
    codes_k = jnp.concatenate(
        [jnp.full((PRE,), -1, jnp.int32), jnp.where(live[0], doc_id[0], -2)]
    )[None, :]
    place_vec = place.reshape(1).astype(jnp.int32)

    tokens = jnp.concatenate([prefix_in[0], later_in[0]], axis=0).astype(F32)
    cotangent = jnp.concatenate([prefix_cot[0], later_cot[0]], axis=0).astype(F32)
    ffn_grad = (active * cotangent).astype(BF)

    first_out, first_normed, first_scaling = layer_norm_parts(tokens, gain1, bias1)
    h1 = jnp.concatenate(gather_pre(seq.to_relative(first_out.astype(BF), 1)), axis=0)
    df = jnp.concatenate(gather_pre(seq.to_relative(ffn_grad, 1)), axis=0)
    projected = jnp.dot(h1, w_qkv, preferred_element_type=F32)
    own_qb = lax.dynamic_slice_in_dim(qb, place * cols, cols, 0)
    own_vb = lax.dynamic_slice_in_dim(vb, place * cols, cols, 0)
    shift = jnp.concatenate([own_qb, jnp.zeros((cols,), F32), own_vb])
    factor = jnp.concatenate([jnp.full((cols,), scale, F32), jnp.ones((2 * cols,), F32)])
    qkv = ((projected + shift) * factor).astype(BF).reshape(parts, part, 3 * cols)
    mixed, stats = attend(place_vec, qkv, codes_q, codes_k, pre_part, later_part)
    mixed = mixed.reshape(length, cols)
    attn_terms = jnp.dot(mixed, w_out, preferred_element_type=F32)
    attn = scatter_pre([attn_terms[i * part : (i + 1) * part] for i in range(parts)]) + ob

    middle = tokens + attn
    second_out, second_normed, second_scaling = layer_norm_parts(middle, gain2, bias2)
    h2 = jnp.concatenate(gather_pre(seq.to_relative(second_out.astype(BF), 1)), axis=0)
    own_ub = lax.dynamic_slice_in_dim(full_up_bias, place * ff_cols, ff_cols, 0)
    upper = jnp.dot(h2, w_up, preferred_element_type=F32) + own_ub
    acted = jax.nn.gelu(upper, approximate=False).astype(BF)
    down_grad = lax.dot_general(df, acted, (((0,), (0,)), ((), ())), preferred_element_type=F32)
    down_grad = down_grad.astype(BF)
    ffn_terms = lax.dot_general(
        acted, w_down, (((1,), (1,)), ((), ())), preferred_element_type=F32
    )
    ffn = scatter_pre([ffn_terms[i * part : (i + 1) * part] for i in range(parts)])
    ffn = seq.to_absolute(ffn, 1) + db
    result = tokens + active * (attn + ffn)
    square_sums = jnp.stack(
        [
            jnp.sum(active * result * result),
            jnp.sum(active * attn * attn),
            jnp.sum(active * ffn * ffn),
            jnp.sum(active),
        ]
    )

    acted_grad = jnp.dot(df, w_down, preferred_element_type=F32)
    upper_grad = (acted_grad * gelu_slope(upper)).astype(BF)
    second_terms = lax.dot_general(
        upper_grad, w_up, (((1,), (1,)), ((), ())), preferred_element_type=F32
    )
    up_grad = lax.dot_general(h2, upper_grad, (((0,), (0,)), ((), ())), preferred_element_type=F32)
    up_grad = up_grad.astype(BF)
    second_grad = scatter_pre([second_terms[i * part : (i + 1) * part] for i in range(parts)])
    second_grad = seq.to_absolute(second_grad, 1)
    middle_grad = norm_back(second_grad, second_normed, second_scaling, gain2)
    attn_grad = (active * cotangent + middle_grad).astype(BF)

    dattn = jnp.concatenate(gather_pre(attn_grad), axis=0)
    mixed_grad = lax.dot_general(
        dattn, w_out, (((1,), (1,)), ((), ())), preferred_element_type=F32
    ).astype(BF)
    out_grad = lax.dot_general(mixed, dattn, (((0,), (0,)), ((), ())), preferred_element_type=F32)
    out_grad = seq.to_relative(out_grad.astype(BF), 0)
    project_grad = attend_back(
        place_vec,
        qkv,
        mixed_grad.reshape(parts, part, cols),
        stats,
        codes_q,
        codes_k,
        pre_part,
        later_part,
    ).reshape(length, 3 * cols)
    qkv_grad = lax.dot_general(
        h1, project_grad, (((0,), (0,)), ((), ())), preferred_element_type=F32
    ).astype(BF)
    first_terms = lax.dot_general(
        project_grad, w_qkv, (((1,), (1,)), ((), ())), preferred_element_type=F32
    )
    first_grad = scatter_pre([first_terms[i * part : (i + 1) * part] for i in range(parts)])
    first_grad = seq.to_absolute(first_grad, 1)
    input_grad = cotangent + middle_grad + norm_back(first_grad, first_normed, first_scaling, gain1)

    def spread(grad):
        rows = grad.shape[0] // seq_count
        return seq.reduce([grad[i * rows : (i + 1) * rows] for i in range(seq_count)]).astype(BF)

    def shared(block):
        return absolute_pre(gather_pre(block), place)

    down_full = jnp.concatenate(shared(spread(down_grad)), axis=1).astype(F32)
    up_full = jnp.concatenate(shared(spread(up_grad)), axis=1).astype(F32)
    out_own = lax.ppermute(spread(out_grad), ("pre", "seq"), [(b, a) for a, b in shuffle])
    out_full = jnp.concatenate(shared(out_own), axis=0).astype(F32)
    qkv_blocks = shared(spread(qkv_grad))
    qkv_full = jnp.concatenate(
        [block[:, i * cols : (i + 1) * cols] for i in range(3) for block in qkv_blocks], axis=1
    ).astype(F32)

    def placed(vector, width):
        zeros = jnp.zeros((width * parts,), F32)
        return lax.dynamic_update_slice_in_dim(zeros, vector, place * width, 0)

    column_sums = jnp.sum(project_grad.astype(F32), axis=0)
    sums = [
        jnp.sum(first_grad * first_normed, axis=0),
        jnp.sum(first_grad, axis=0),
        placed(column_sums[:cols], cols),
        placed(column_sums[2 * cols :], cols),
        jnp.sum(attn_grad.astype(F32), axis=0),
        jnp.sum(second_grad * second_normed, axis=0),
        jnp.sum(second_grad, axis=0),
        jnp.sum(ffn_grad.astype(F32), axis=0),
        placed(jnp.sum(upper_grad.astype(F32), axis=0), ff_cols),
        jnp.concatenate([square_sums, jnp.zeros((124,), F32)]),
    ]
    flat = sum_all(jnp.concatenate(sums).reshape(-1, 128)).reshape(-1)
    totals = [flat[i * D : (i + 1) * D] for i in range(8)]
    total_ub = flat[8 * D : 8 * D + FF]
    total_squares = flat[8 * D + FF : 8 * D + FF + 4]

    def own_share(vector):
        width = vector.shape[0] // seq_count
        return lax.dynamic_slice_in_dim(vector, seq_place * width, width, 0)

    residual_rms = jnp.sqrt(total_squares[:3] / (total_squares[3] * D))
    return (
        result[:pre_part][None].astype(BF),
        result[pre_part:][None].astype(BF),
        input_grad[:pre_part][None].astype(BF),
        input_grad[pre_part:][None].astype(BF),
        own_share(totals[0]),
        own_share(totals[1]),
        qkv_full,
        own_share(totals[2]),
        own_share(totals[3]),
        out_full,
        own_share(totals[4]),
        own_share(totals[5]),
        own_share(totals[6]),
        up_full,
        own_share(total_ub),
        down_full,
        own_share(totals[7]),
        residual_rms,
    )


def solution(mesh):
    placed = (
        P("seq", "pre", None),
        P("seq", "pre", None),
        P("seq", None),
        P("seq", None),
        P("seq", None),
        P("seq"),
        P("seq"),
        P("seq", None),
        P("seq"),
        P("seq"),
        P("seq", None),
        P("seq"),
        P("seq"),
        P("seq"),
        P("seq", None),
        P("seq"),
        P("seq", None),
        P("seq"),
        P("seq", "pre", None),
        P("seq", "pre", None),
    )
    return jax.shard_map(
        on_device,
        mesh=mesh,
        in_specs=placed,
        out_specs=(
            P("seq", "pre", None),
            P("seq", "pre", None),
            P("seq", "pre", None),
            P("seq", "pre", None),
            P("seq"),
            P("seq"),
            P("seq", None),
            P("seq"),
            P("seq"),
            P("seq", None),
            P("seq"),
            P("seq"),
            P("seq"),
            P("seq", None),
            P("seq"),
            P("seq", None),
            P("seq"),
            P(),
        ),
        check_vma=False,
    )
```

```python
import functools
import math

import jax
import jax.numpy as jnp
from jax import lax
from jax.experimental import pallas as pl
from jax.experimental.pallas import tpu as pltpu
from jax.sharding import PartitionSpec as P

D = 2048
HEADS = 32
HEAD_DIM = 64
FF = 8192
LAYER = 12
PRE = 512

EPS = 1e-05
NEG = -1e30
BF = jnp.bfloat16
F32 = jnp.float32
TILE = 256


def layer_norm_parts(values, gain, bias):
    mean = jnp.mean(values, axis=-1, keepdims=True)
    centred = values - mean
    variance = jnp.mean(centred * centred, axis=-1, keepdims=True)
    scaling = lax.rsqrt(variance + EPS)
    normed = centred * scaling
    return (normed * gain + bias, normed, scaling)


def norm_back(grad, normed, scaling, gain):
    scaled = grad * gain
    inner = jnp.mean(scaled, axis=-1, keepdims=True)
    cross = jnp.mean(scaled * normed, axis=-1, keepdims=True)
    return scaling * (scaled - inner - normed * cross)


def token_tables(doc_lengths, doc_exit, token_skip):
    order = jnp.arange(doc_lengths.shape[-1], dtype=jnp.int32)
    earlier = order[None, :] < order[:, None]
    starts = jnp.sum(
        jnp.where(earlier, doc_lengths[..., None, :], 0), axis=-1, dtype=jnp.int32
    )
    places = jnp.arange(token_skip.shape[-1], dtype=jnp.int32)
    doc_id = (
        jnp.sum(
            (places[:, None] >= starts[..., None, :]).astype(jnp.int32), axis=-1, dtype=jnp.int32
        )
        - 1
    )
    live_doc = doc_exit > LAYER
    live = jnp.any((doc_id[..., None] == order) & live_doc[..., None, :], axis=-1) & (
        token_skip == 0
    )
    return (doc_id, live)


def dot_nt(a, b):
    return lax.dot_general(a, b, (((1,), (1,)), ((), ())), preferred_element_type=F32)


def dot_nn(a, b):
    return lax.dot_general(a, b, (((1,), (0,)), ((), ())), preferred_element_type=F32)


def dot_tn(a, b):
    return lax.dot_general(a, b, (((0,), (0,)), ((), ())), preferred_element_type=F32)


def masked_scores(block, scores, tile, codes_q, codes_k):
    rows = lax.broadcasted_iota(jnp.int32, (TILE, TILE), 0)
    cols = lax.broadcasted_iota(jnp.int32, (TILE, TILE), 1)
    allowed = None
    if tile == block:
        allowed = cols <= rows
    if tile * TILE >= PRE:
        same = (
            codes_q[block * TILE : (block + 1) * TILE, :]
            == codes_k[:, tile * TILE : (tile + 1) * TILE]
        )
        allowed = same if allowed is None else allowed & same
    if allowed is None:
        return scores
    return jnp.where(allowed, scores, NEG)


def attend_back_pair(qkv_lanes, do, level_of, codes_q, codes_k, dq_all, dk_all, dv_all, qkv):
    dk_all[...] = jnp.zeros_like(dk_all)
    dv_all[...] = jnp.zeros_like(dv_all)
    blocks = do.shape[0] // TILE
    for block in range(blocks):
        rows = slice(block * TILE, (block + 1) * TILE)
        both_q = qkv[0][rows, qkv_lanes[0]]
        both_do = do[rows, qkv_lanes[3]]
        parts = []
        for head in range(2):
            queries = head_lanes(both_q, head)
            grads = head_lanes(both_do, head)
            level = level_of(rows, head)
            probs = []
            dprobs = []
            for tile in range(block + 1):
                cols = slice(tile * TILE, (tile + 1) * TILE)
                scores = masked_scores(
                    block, dot_nt(queries, qkv[1][cols, qkv_lanes[1]]), tile, codes_q, codes_k
                )
                probs.append(jnp.exp(scores - level))
                dprobs.append(dot_nt(grads, qkv[2][cols, qkv_lanes[2]]))
            delta = functools.reduce(
                jnp.add, [jnp.sum(a * b, axis=1, keepdims=True) for a, b in zip(probs, dprobs)]
            )
            dq = None
            for tile in range(block + 1):
                cols = slice(tile * TILE, (tile + 1) * TILE)
                ds = (probs[tile] * (dprobs[tile] - delta)).astype(BF)
                part = dot_nn(ds, qkv[1][cols, qkv_lanes[1]])
                dq = part if dq is None else dq + part
                dk_all[cols, :] += dot_tn(ds, queries)
                dv_all[cols, :] += dot_tn(probs[tile].astype(BF), grads)
            parts.append(dq)
        dq_all[rows, :] = join_heads(*parts) * (1.0 / math.sqrt(HEAD_DIM))


def attend_back_kernel(q_ref, k_ref, v_ref, do_ref, stat_ref, cq_ref, ck_ref, dq_ref, dk_ref, dv_ref, dq, dk, dv):
    every = slice(None)
    attend_back_pair(
        [every] * 4,
        do_ref,
        lambda rows, head: stat_ref[rows, head * HEAD_DIM : head * HEAD_DIM + 1],
        cq_ref[...],
        ck_ref[...],
        dq,
        dk,
        dv,
        (q_ref, k_ref, v_ref),
    )
    dq_ref[...] = dq[...].astype(BF)
    dk_ref[...] = dk[...].astype(BF)
    dv_ref[...] = dv[...].astype(BF)


def attend_back(qkv, grad_out, stats, codes_q, codes_k):
    length, width = qkv.shape
    pairs = width // 3 // 128
    block = (length, 128)
    return pl.pallas_call(
        attend_back_kernel,
        out_shape=[jax.ShapeDtypeStruct((length, width // 3), BF)] * 3,
        grid=(pairs,),
        in_specs=[
            pl.BlockSpec(block, lambda i: (0, i)),
            pl.BlockSpec(block, lambda i: (0, pairs + i)),
            pl.BlockSpec(block, lambda i: (0, 2 * pairs + i)),
            pl.BlockSpec(block, lambda i: (0, i)),
            pl.BlockSpec(block, lambda i: (0, i)),
            pl.BlockSpec((length, 1), lambda i: (0, 0)),
            pl.BlockSpec((1, length), lambda i: (0, 0)),
        ],
        out_specs=[pl.BlockSpec(block, lambda i: (0, i))] * 3,
        scratch_shapes=[pltpu.VMEM((length, 128), F32)] * 3,
        compiler_params=pltpu.CompilerParams(vmem_limit_bytes=56 * 2**20),
        cost_estimate=pl.CostEstimate(
            flops=pairs * 2 * 15 * 10 * TILE * TILE * 256,
            bytes_accessed=length * width * 6,
            transcendentals=pairs * 2 * 15 * TILE * TILE,
        ),
        name="attend_back",
    )(qkv, qkv, qkv, grad_out, stats, codes_q, codes_k)


def xor(value, mask):
    bit = 1
    while bit <= mask:
        if mask & bit:
            value = value + bit * (1 - 2 * lax.rem(lax.div(value, jnp.int32(bit)), jnp.int32(2)))
        bit *= 2
    return value


def remote(src, dst, send_sem, recv_sem, **target):
    return pltpu.make_async_remote_copy(
        src_ref=src,
        dst_ref=dst,
        send_sem=send_sem,
        recv_sem=recv_sem,
        device_id=target,
        device_id_type=pl.DeviceIdType.MESH,
    )


def greet(wide):
    barrier = pltpu.get_barrier_semaphore()
    seq = lax.axis_index("seq")
    pre = lax.axis_index("pre")
    for mask in (1, *wide):
        pl.semaphore_signal(
            barrier, inc=1, device_id={"seq": xor(seq, mask)}, device_id_type=pl.DeviceIdType.MESH
        )
    for mask in (1, 2):
        pl.semaphore_signal(
            barrier, inc=1, device_id={"pre": xor(pre, mask)}, device_id_type=pl.DeviceIdType.MESH
        )
    pl.semaphore_wait(barrier, len(wide) + 3)


def rows_of(index, count):
    return pl.ds(pl.multiple_of(index * count, count), count)


class Gather:
    def __init__(self, own, land, rows, send_sem, recv_sem, local_sem):
        self.own, self.land, self.rows = own, land, rows
        self.send_sem, self.recv_sem, self.local_sem = send_sem, recv_sem, local_sem
        self.seq = lax.axis_index("seq")
        self.sent = []
        self.local = None

    def slot(self, place):
        return self.land.at[rows_of(place, self.rows), :]

    def begin(self, *masks):
        for mask in masks:
            copy = remote(
                self.own,
                self.slot(self.seq),
                self.send_sem.at[mask],
                self.recv_sem.at[mask],
                seq=xor(self.seq, mask),
            )
            copy.start()
            self.sent.append(copy)

    def keep(self):
        self.local = pltpu.make_async_copy(self.own, self.slot(self.seq), self.local_sem)
        self.local.start()

    def arrived(self, mask):
        here = self.slot(xor(self.seq, mask))
        remote(
            here, here, self.send_sem.at[mask], self.recv_sem.at[mask], seq=xor(self.seq, mask)
        ).wait_recv()

    def forward(self, mask):
        self.arrived(mask)
        here = self.slot(xor(self.seq, mask))
        copy = remote(
            here,
            here,
            self.send_sem.at[mask + 1],
            self.recv_sem.at[mask + 1],
            seq=xor(self.seq, 1),
        )
        copy.start()
        self.sent.append(copy)

    def finish(self, wide):
        self.local.wait()
        self.arrived(1)
        for mask in wide:
            self.arrived(mask + 1)

    def drain(self):
        for copy in self.sent:
            copy.wait_send()


class Spread:
    def __init__(self, own, land, rows, send_sem, recv_sem, local_sem):
        self.own, self.land, self.rows = own, land, rows
        self.send_sem, self.recv_sem, self.local_sem = send_sem, recv_sem, local_sem
        self.pre = lax.axis_index("pre")
        self.sent = []

    def slot(self, index):
        return self.land.at[index * self.rows : (index + 1) * self.rows, :]

    def copy(self, src, slot, mask):
        return remote(
            src, self.slot(slot), self.send_sem.at[slot], self.recv_sem.at[slot], pre=xor(self.pre, mask)
        )

    def begin(self):
        for mask in (2, 1):
            copy = self.copy(self.own, mask, mask)
            copy.start()
            self.sent.append(copy)
        self.local = pltpu.make_async_copy(self.own, self.slot(0), self.local_sem)
        self.local.start()

    def forward(self):
        self.copy(self.own, 2, 2).wait_recv()
        copy = self.copy(self.slot(2), 3, 1)
        copy.start()
        self.sent.append(copy)

    def finish(self):
        self.local.wait()
        self.copy(self.own, 1, 1).wait_recv()
        self.copy(self.own, 3, 1).wait_recv()

    def drain(self):
        for copy in self.sent:
            copy.wait_send()


def local_copies(pairs, sem):
    copies = [pltpu.make_async_copy(src, dst, sem.at[i]) for i, (src, dst) in enumerate(pairs)]
    for copy in copies:
        copy.start()
    for copy in copies:
        copy.wait()


def wide_masks(size):
    masks = list(range(2, size, 2))
    return sorted(masks, key=lambda m: (m != 2, -m))


def head_lanes(value, head):
    lane = lax.broadcasted_iota(jnp.int32, value.shape, 1)
    inside = (lane < HEAD_DIM) if head == 0 else (lane >= HEAD_DIM)
    return jnp.where(inside, value, jnp.zeros_like(value))


def join_heads(first, second):
    lane = lax.broadcasted_iota(jnp.int32, (first.shape[0], 2 * HEAD_DIM), 1)
    return jnp.where(lane < HEAD_DIM, first, second)


def attend_pair(pair, cols, qkv, codes_q, codes_k, mixed, stats):
    lanes = [pl.ds(pl.multiple_of(third * cols + pair * 128, 128), 128) for third in range(3)]
    blocks = qkv.shape[0] // TILE
    for block in range(blocks):
        rows = slice(block * TILE, (block + 1) * TILE)
        both = qkv[rows, lanes[0]]
        outs, levels = [], []
        for head in range(2):
            queries = head_lanes(both, head)
            scores = [
                masked_scores(
                    block,
                    dot_nt(queries, qkv[tile * TILE : (tile + 1) * TILE, lanes[1]]),
                    tile,
                    codes_q,
                    codes_k,
                )
                for tile in range(block + 1)
            ]
            top = functools.reduce(jnp.maximum, [jnp.max(x, axis=1, keepdims=True) for x in scores])
            powers = [jnp.exp(x - top) for x in scores]
            total = functools.reduce(jnp.add, [jnp.sum(e, axis=1, keepdims=True) for e in powers])
            share = 1.0 / total
            outs.append(
                functools.reduce(
                    jnp.add,
                    [
                        dot_nn((e * share).astype(BF), qkv[tile * TILE : (tile + 1) * TILE, lanes[2]])
                        for tile, e in enumerate(powers)
                    ],
                )
            )
            levels.append(top + jnp.log(total))
        mixed[rows, lanes_of(pair)] = join_heads(outs[0], outs[1]).astype(BF)
        stats[rows, lanes_of(pair)] = join_heads(levels[0], levels[1])


def lanes_of(pair):
    return pl.ds(pl.multiple_of(pair * 128, 128), 128)


def forward_kernel(
    sizes,
    own_qkv,
    own_out,
    own_up,
    own_down,
    prefix_in,
    later_in,
    prefix_cot,
    later_cot,
    active_ref,
    gain1,
    bias1,
    out_bias,
    gain2,
    bias2,
    shift,
    factor,
    up_bias,
    codes_q,
    codes_k,
    w_qkv,
    w_out,
    w_up,
    w_down,
    h1,
    df,
    h2,
    qkv,
    mixed,
    stats,
    attn,
    acted,
    slope,
    down_grad,
    wbuf,
    lhs,
    qkv_v,
    mixed_v,
    stats_v,
    x_v,
    cot_v,
    h1_v,
    df_v,
    h2_v,
    terms_v,
    near_v,
    pass_v,
    far_v,
    attn_v,
    acted_v,
    slope_v,
    grad_v,
    gather_send,
    gather_recv,
    spread_send,
    spread_recv,
    sum_send,
    sum_recv,
    local_sem,
):
    seq_size, pre_part, later_part = sizes
    part = pre_part + later_part
    cols = own_qkv.shape[1] // 3
    ff_cols = own_up.shape[1]
    wide = wide_masks(seq_size)
    pre = lax.axis_index("pre")
    near_id = {"pre": xor(pre, 1)}
    far_id = {"pre": xor(pre, 2)}

    def gather(i, own, land):
        return Gather(own, land, own.shape[0], gather_send.at[i], gather_recv.at[i], local_sem.at[i])

    get_qkv = gather(0, own_qkv, w_qkv)
    get_out = gather(1, own_out, w_out)
    get_up = gather(2, own_up, w_up)
    get_down = gather(3, own_down, w_down)
    get_h1 = Spread(h1_v, h1, part, spread_send.at[0], spread_recv.at[0], local_sem.at[4])
    get_df = Spread(df_v, df, part, spread_send.at[1], spread_recv.at[1], local_sem.at[5])
    get_h2 = Spread(h2_v, h2, part, spread_send.at[2], spread_recv.at[2], local_sem.at[6])

    greet(wide)
    get_qkv.begin(1, *wide)
    get_qkv.keep()
    get_out.begin(1, *wide)
    get_out.keep()
    local_copies(
        [
            (prefix_in, x_v.at[:pre_part, :]),
            (later_in, x_v.at[pre_part:, :]),
            (prefix_cot, cot_v.at[:pre_part, :]),
            (later_cot, cot_v.at[pre_part:, :]),
        ],
        local_sem.at[8:12],
    )
    chunk = 32

    @pl.loop(0, part // chunk)
    def _(i):
        rows = rows_of(i, chunk)
        value, _, _ = layer_norm_parts(x_v[rows, :].astype(F32), gain1[...], bias1[...])
        h1_v[rows, :] = value.astype(BF)

    get_h1.begin()

    @pl.loop(0, part // chunk)
    def _(i):
        rows = rows_of(i, chunk)
        df_v[rows, :] = (active_ref[rows, :] * cot_v[rows, :].astype(F32)).astype(BF)

    get_df.begin()
    get_qkv.forward(wide[0])
    get_h1.forward()
    for mask in wide[1:-1]:
        get_qkv.forward(mask)
    get_up.begin(1, *wide)
    get_up.keep()
    get_qkv.forward(wide[-1])
    get_h1.finish()
    get_df.forward()
    load = pltpu.make_async_copy(h1, lhs, local_sem.at[12])
    load.start()
    get_qkv.finish(wide)
    local_copies([(w_qkv, wbuf.at[:, : 3 * cols])], local_sem.at[8:9])
    load.wait()
    for mask in wide:
        get_out.forward(mask)

    @pl.loop(0, 4)
    def _(r):
        member = lax.rem(r, 2) * (xor(pre, 1) - pre) + lax.div(r, 2) * (xor(pre, 2) - pre) + pre
        head_rows = rows_of(member, pre_part)
        tail_rows = pl.ds(pl.multiple_of(4 * pre_part + member * later_part, 64), later_part)

        @pl.loop(0, 3)
        def _(j):
            lanes = pl.ds(pl.multiple_of(j * cols, cols), cols)
            value = dot_nn(lhs[rows_of(r, part), :], wbuf[:, lanes])
            value = ((value + shift[:, lanes]) * factor[:, lanes]).astype(BF)
            qkv_v[head_rows, lanes] = value[:pre_part]
            qkv_v[tail_rows, lanes] = value[pre_part:]

    save_qkv = pltpu.make_async_copy(qkv_v, qkv, local_sem.at[13])
    save_qkv.start()
    get_up.forward(wide[0])
    get_df.finish()
    pairs = cols // 128

    @pl.loop(0, pairs)
    def _(pair):
        attend_pair(pair, cols, qkv_v, codes_q[...], codes_k[...], mixed_v, stats_v)

    save_stats = pltpu.make_async_copy(stats_v, stats, local_sem.at[14])
    save_stats.start()
    for mask in wide[1:-1]:
        get_up.forward(mask)
    get_down.begin(1, *wide)
    get_down.keep()
    get_out.finish(wide)
    local_copies([(w_out, wbuf.at[:cols, :])], local_sem.at[8:9])

    def position_rows(r):
        member = xor(pre, r) if r else pre
        return (
            rows_of(member, pre_part),
            pl.ds(pl.multiple_of(4 * pre_part + member * later_part, 64), later_part),
        )

    def out_term(r, store):
        head_rows, tail_rows = position_rows(r)

        @pl.loop(0, D // 512)
        def _(j):
            lanes = rows_of(j, 512)
            store(
                lanes,
                dot_nn(mixed_v[head_rows, :], wbuf[:cols, lanes]),
                dot_nn(mixed_v[tail_rows, :], wbuf[:cols, lanes]),
            )

    def keep_term(slot):
        def store(lanes, head, tail):
            terms_v[slot, :pre_part, lanes] = head.astype(BF)
            terms_v[slot, pre_part:, lanes] = tail.astype(BF)

        return store

    near = [
        remote(terms_v.at[i], near_v.at[i], sum_send.at[i], sum_recv.at[i], **near_id)
        for i in range(2)
    ]
    far = remote(pass_v, far_v, sum_send.at[2], sum_recv.at[2], **far_id)
    out_term(3, keep_term(0))
    near[0].start()
    out_term(1, keep_term(1))
    near[1].start()
    near[0].wait_recv()

    def pass_term(lanes, head, tail):
        pass_v[:pre_part, lanes] = (head + near_v[0, :pre_part, lanes].astype(F32)).astype(BF)
        pass_v[pre_part:, lanes] = (tail + near_v[0, pre_part:, lanes].astype(F32)).astype(BF)

    out_term(2, pass_term)
    far.start()
    near[1].wait_recv()

    def own_term(lanes, head, tail):
        bias = out_bias[:, lanes]
        attn_v[:pre_part, lanes] = head + near_v[1, :pre_part, lanes].astype(F32) + bias
        attn_v[pre_part:, lanes] = tail + near_v[1, pre_part:, lanes].astype(F32) + bias

    out_term(0, own_term)
    moves = []
    for r in range(4):
        head_rows, tail_rows = position_rows(r)
        moves.append((mixed_v.at[head_rows, :], mixed.at[r * part : r * part + pre_part, :]))
        moves.append((mixed_v.at[tail_rows, :], mixed.at[r * part + pre_part : (r + 1) * part, :]))
    local_copies(moves, local_sem.at[16:24])
    get_up.forward(wide[-1])
    far.wait_recv()

    @pl.loop(0, part // chunk)
    def _(i):
        rows = rows_of(i, chunk)
        branch = attn_v[rows, :] + far_v[rows, :].astype(F32)
        attn_v[rows, :] = branch
        value, _, _ = layer_norm_parts(x_v[rows, :].astype(F32) + branch, gain2[...], bias2[...])
        h2_v[rows, :] = value.astype(BF)

    get_h2.begin()
    save_attn = pltpu.make_async_copy(attn_v, attn, local_sem.at[15])
    save_attn.start()
    get_down.forward(wide[0])
    get_up.finish(wide)
    load = pltpu.make_async_copy(w_up, wbuf, local_sem.at[12])
    load.start()
    get_h2.forward()
    get_h2.finish()
    local_copies([(h2, lhs)], local_sem.at[8:9])
    load.wait()

    @pl.loop(0, 4)
    def _(r):
        rows = rows_of(r, part)

        @pl.loop(0, ff_cols // 512)
        def _(j):
            lanes = rows_of(j, 512)
            upper = dot_nn(lhs[rows, :], wbuf[:, lanes]) + up_bias[:, lanes]
            cumulative = 0.5 * (1.0 + lax.erf(upper * (1.0 / math.sqrt(2.0))))
            density = jnp.exp(-0.5 * upper * upper) * (1.0 / math.sqrt(2.0 * math.pi))
            acted_v[rows, lanes] = (upper * cumulative).astype(BF)
            slope_v[rows, lanes] = (cumulative + upper * density).astype(BF)

    saves = [
        pltpu.make_async_copy(acted_v, acted, local_sem.at[12]),
        pltpu.make_async_copy(slope_v, slope, local_sem.at[8]),
    ]
    for save in saves:
        save.start()
    for mask in wide[1:-1]:
        get_down.forward(mask)
    local_copies([(df, lhs)], local_sem.at[9:10])

    @pl.loop(0, D // 256)
    def _(i):
        lanes = rows_of(i, 256)
        turned = lhs[:, lanes].T

        @pl.loop(0, ff_cols // 512)
        def _(j):
            grad_v[:, rows_of(j, 512)] = dot_nn(turned, acted_v[:, rows_of(j, 512)]).astype(BF)

        save = pltpu.make_async_copy(grad_v, down_grad.at[lanes, :], local_sem.at[9])
        save.start()
        save.wait()

    get_down.forward(wide[-1])
    get_down.finish(wide)
    for save in (*saves, save_qkv, save_stats, save_attn):
        save.wait()
    for item in (get_qkv, get_out, get_up, get_down, get_h1, get_df, get_h2):
        item.drain()
    for copy in (*near, far):
        copy.wait_send()


def forward_pass(seq_size, pre_part, later_part, *operands):
    own_qkv, own_out, own_up = operands[:3]
    part = pre_part + later_part
    length = 4 * part
    width = own_qkv.shape[1]
    cols = width // 3
    ff_cols = own_up.shape[1]
    hbm = pl.BlockSpec(memory_space=pl.ANY)
    vmem = pl.BlockSpec(memory_space=pltpu.VMEM)

    def out(shape, kind=BF):
        return jax.ShapeDtypeStruct(shape, kind)

    outs = (
        out((D, width)),
        out((cols, D)),
        out((D, ff_cols)),
        out((D, ff_cols)),
        out((length, D)),
        out((length, D)),
        out((length, D)),
        out((length, width)),
        out((length, cols)),
        out((length, cols), F32),
        out((part, D), F32),
        out((length, ff_cols)),
        out((length, ff_cols)),
        out((D, ff_cols)),
    )
    dma = pltpu.SemaphoreType.DMA
    return pl.pallas_call(
        functools.partial(forward_kernel, (seq_size, pre_part, later_part)),
        out_shape=outs,
        in_specs=[hbm] * 8 + [vmem] * (len(operands) - 8),
        out_specs=[hbm] * len(outs),
        scratch_shapes=[
            pltpu.VMEM((D, max(ff_cols, width)), BF),
            pltpu.VMEM((length, D), BF),
            pltpu.VMEM((length, width), BF),
            pltpu.VMEM((length, cols), BF),
            pltpu.VMEM((length, cols), F32),
            pltpu.VMEM((part, D), BF),
            pltpu.VMEM((part, D), BF),
            pltpu.VMEM((part, D), BF),
            pltpu.VMEM((part, D), BF),
            pltpu.VMEM((part, D), BF),
            pltpu.VMEM((2, part, D), BF),
            pltpu.VMEM((2, part, D), BF),
            pltpu.VMEM((part, D), BF),
            pltpu.VMEM((part, D), BF),
            pltpu.VMEM((part, D), F32),
            pltpu.VMEM((length, ff_cols), BF),
            pltpu.VMEM((length, ff_cols), BF),
            pltpu.VMEM((256, ff_cols), BF),
            dma((4, seq_size)),
            dma((4, seq_size)),
            dma((3, 4)),
            dma((3, 4)),
            dma((3,)),
            dma((3,)),
            dma((24,)),
        ],
        compiler_params=pltpu.CompilerParams(
            collective_id=0, has_side_effects=True, vmem_limit_bytes=62 * 2**20
        ),
        cost_estimate=pl.CostEstimate(
            flops=2 * length * D * (width + cols + 2 * ff_cols),
            bytes_accessed=8 * D * ff_cols,
            transcendentals=length * ff_cols,
        ),
        name="forward_pass",
    )(*operands)


class Seq:
    def __init__(self):
        self.size = lax.axis_size("seq")
        self.place = lax.axis_index("seq")

    def swap(self, value, mask):
        return lax.ppermute(value, "seq", [(i, i ^ mask) for i in range(self.size)])

    def gather(self, own):
        blocks = [own, self.swap(own, 1)]
        for mask in range(2, self.size, 2):
            blocks.append(self.swap(own, mask))
            blocks.append(self.swap(blocks[-1], 1))
        return blocks

    def reduce(self, blocks):
        total = None
        masks = [mask for mask in range(2, self.size, 2)][::-1] + [0]
        for mask in masks:
            other = self.swap(blocks[mask + 1], 1)
            part = blocks[mask].astype(F32) + other.astype(F32)
            if mask:
                part = self.swap(part.astype(BF), mask).astype(F32)
            total = part if total is None else total + part
        return total

    def reorder(self, value, axis):
        block = value.shape[axis] // self.size
        return jnp.concatenate(
            [
                lax.dynamic_slice_in_dim(value, jnp.bitwise_xor(self.place, i) * block, block, axis)
                for i in range(self.size)
            ],
            axis=axis,
        )


def over_pre(value, mask):
    return lax.ppermute(value, "pre", [(i, i ^ mask) for i in range(lax.axis_size("pre"))])


def gather_pre(own):
    far = over_pre(own, 2)
    near = over_pre(own, 1)
    return [own, near, far, over_pre(far, 1)]


def scatter_pre(blocks):
    a = blocks[0] + over_pre(blocks[1].astype(BF), 1).astype(F32)
    b = blocks[2] + over_pre(blocks[3].astype(BF), 1).astype(F32)
    return a + over_pre(b.astype(BF), 2).astype(F32)


def sum_all(value):
    for mask in (1, 2):
        value = value + over_pre(value, mask)
    size = lax.axis_size("seq")
    mask = 1
    while mask < size:
        value = value + lax.ppermute(value, "seq", [(i, i ^ mask) for i in range(size)])
        mask *= 2
    return value


def absolute_pre(blocks, place):
    first = place % 2 == 0
    low = place < 2
    a = [jnp.where(first, blocks[0], blocks[1]), jnp.where(first, blocks[1], blocks[0])]
    b = [jnp.where(first, blocks[2], blocks[3]), jnp.where(first, blocks[3], blocks[2])]
    return [jnp.where(low, u, w) for u, w in zip(a, b)] + [jnp.where(low, w, u) for u, w in zip(a, b)]


def on_device(
    prefix_in,
    later_in,
    doc_lengths,
    doc_exit,
    token_skip,
    first_gain,
    first_bias,
    qkv_weight,
    query_bias,
    value_bias,
    out_weight,
    out_bias,
    second_gain,
    second_bias,
    up_weight,
    up_bias,
    down_weight,
    down_bias,
    prefix_cot,
    later_cot,
):
    scale = 1.0 / math.sqrt(HEAD_DIM)
    pre_part = prefix_in.shape[1]
    later_part = later_in.shape[1]
    part = pre_part + later_part
    parts = lax.axis_size("pre")
    place = lax.axis_index("pre")
    seq = Seq()
    seq_count = seq.size
    seq_place = seq.place
    own_d = D // seq_count
    cols = D // parts
    ff_cols = FF // parts
    length = parts * part

    packed = jnp.concatenate(
        [
            first_gain,
            first_bias,
            query_bias,
            value_bias,
            out_bias,
            second_gain,
            second_bias,
            down_bias,
            up_bias,
        ]
    ).reshape(-1, 128)
    small = seq.reorder(jnp.stack(seq.gather(packed)).reshape(seq_count, -1), 0).astype(F32)
    vectors = [small[:, i * own_d : (i + 1) * own_d].reshape(1, D) for i in range(8)]
    full_up_bias = small[:, 8 * own_d :].reshape(1, FF)
    (gain1, bias1, qb, vb, ob, gain2, bias2, db) = vectors

    def section(weight, start, width):
        return lax.dynamic_slice_in_dim(weight, start + place * width, width, 1)

    own_qkv = jnp.concatenate([section(qkv_weight, i * D, cols) for i in range(3)], axis=1)
    block_rows = own_d // parts
    out_block = lax.dynamic_slice_in_dim(out_weight, place * block_rows, block_rows, 0)
    shuffle = [
        ((b % parts) * seq_count + b // parts, (b // seq_count) * seq_count + b % seq_count)
        for b in range(parts * seq_count)
    ]
    own_out = lax.ppermute(out_block, ("pre", "seq"), shuffle)
    doc_id, live = token_tables(doc_lengths, doc_exit, token_skip)
    live_here = lax.dynamic_slice_in_dim(live[0], place * later_part, later_part, 0)
    active = jnp.concatenate([jnp.ones((pre_part,), F32), live_here.astype(F32)])[:, None]
    codes_q = jnp.concatenate([jnp.full((PRE,), -1, jnp.int32), doc_id[0]])[:, None]
    codes_k = jnp.concatenate(
        [jnp.full((PRE,), -1, jnp.int32), jnp.where(live[0], doc_id[0], -2)]
    )[None, :]

    def own_columns(vector, width):
        return lax.dynamic_slice_in_dim(vector, place * width, width, 1)

    shift = jnp.concatenate(
        [own_columns(qb, cols), jnp.zeros((1, cols), F32), own_columns(vb, cols)], axis=1
    )
    factor = jnp.concatenate([jnp.full((1, cols), scale, F32), jnp.ones((1, 2 * cols), F32)], axis=1)
    (w_qkv, w_out, w_up, w_down, h1, df, h2, qkv, mixed, stats, attn, acted, slope, down_grad) = forward_pass(
        seq_count,
        pre_part,
        later_part,
        own_qkv,
        own_out,
        section(up_weight, 0, ff_cols),
        section(down_weight, 0, ff_cols),
        prefix_in[0],
        later_in[0],
        prefix_cot[0],
        later_cot[0],
        active,
        gain1,
        bias1,
        ob,
        gain2,
        bias2,
        shift,
        factor,
        own_columns(full_up_bias, ff_cols),
        codes_q,
        codes_k,
    )

    tokens = jnp.concatenate([prefix_in[0], later_in[0]], axis=0).astype(F32)
    cotangent = jnp.concatenate([prefix_cot[0], later_cot[0]], axis=0).astype(F32)
    ffn_grad = (active * cotangent).astype(BF)
    _, first_normed, first_scaling = layer_norm_parts(tokens, gain1, bias1)
    _, second_normed, second_scaling = layer_norm_parts(tokens + attn, gain2, bias2)
    ffn_terms = lax.dot_general(
        acted, w_down, (((1,), (1,)), ((), ())), preferred_element_type=F32
    )
    ffn = scatter_pre([ffn_terms[i * part : (i + 1) * part] for i in range(parts)]) + db
    result = tokens + active * (attn + ffn)
    square_sums = jnp.stack(
        [
            jnp.sum(active * result * result),
            jnp.sum(active * attn * attn),
            jnp.sum(active * ffn * ffn),
            jnp.sum(active),
        ]
    )

    acted_grad = jnp.dot(df, w_down, preferred_element_type=F32)
    upper_grad = (acted_grad * slope.astype(F32)).astype(BF)
    second_terms = lax.dot_general(
        upper_grad, w_up, (((1,), (1,)), ((), ())), preferred_element_type=F32
    )
    up_grad = lax.dot_general(h2, upper_grad, (((0,), (0,)), ((), ())), preferred_element_type=F32)
    up_grad = up_grad.astype(BF)
    second_grad = scatter_pre([second_terms[i * part : (i + 1) * part] for i in range(parts)])
    middle_grad = norm_back(second_grad, second_normed, second_scaling, gain2)
    attn_grad = (active * cotangent + middle_grad).astype(BF)

    dattn = jnp.concatenate(gather_pre(attn_grad), axis=0)
    mixed_grad = lax.dot_general(
        dattn, w_out, (((1,), (1,)), ((), ())), preferred_element_type=F32
    ).astype(BF)
    out_grad = lax.dot_general(mixed, dattn, (((0,), (0,)), ((), ())), preferred_element_type=F32)
    out_grad = out_grad.astype(BF)

    def by_member(blocks):
        return absolute_pre(blocks, place)

    do_blocks = by_member([mixed_grad[i * part : (i + 1) * part] for i in range(parts)])
    do = jnp.concatenate([b[:pre_part] for b in do_blocks] + [b[pre_part:] for b in do_blocks], axis=0)
    grads = jnp.concatenate(attend_back(qkv, do, stats, codes_q, codes_k), axis=1)
    blocks = [
        jnp.concatenate(
            [
                grads[i * pre_part : (i + 1) * pre_part],
                grads[PRE + i * later_part : PRE + (i + 1) * later_part],
            ],
            axis=0,
        )
        for i in range(parts)
    ]
    project_grad = jnp.concatenate(by_member(blocks), axis=0)
    qkv_grad = lax.dot_general(
        h1, project_grad, (((0,), (0,)), ((), ())), preferred_element_type=F32
    ).astype(BF)
    first_terms = lax.dot_general(
        project_grad, w_qkv, (((1,), (1,)), ((), ())), preferred_element_type=F32
    )
    first_grad = scatter_pre([first_terms[i * part : (i + 1) * part] for i in range(parts)])
    input_grad = cotangent + middle_grad + norm_back(first_grad, first_normed, first_scaling, gain1)

    def spread(grad):
        rows = grad.shape[0] // seq_count
        return seq.reduce(
            [
                lax.dynamic_slice_in_dim(grad, jnp.bitwise_xor(seq_place, i) * rows, rows, 0)
                for i in range(seq_count)
            ]
        ).astype(BF)

    def shared(block):
        return absolute_pre(gather_pre(block), place)

    down_full = jnp.concatenate(shared(spread(down_grad)), axis=1).astype(F32)
    up_full = jnp.concatenate(shared(spread(up_grad)), axis=1).astype(F32)
    out_own = lax.ppermute(spread(out_grad), ("pre", "seq"), [(b, a) for a, b in shuffle])
    out_full = jnp.concatenate(shared(out_own), axis=0).astype(F32)
    qkv_blocks = shared(spread(qkv_grad))
    qkv_full = jnp.concatenate(
        [block[:, i * cols : (i + 1) * cols] for i in range(3) for block in qkv_blocks], axis=1
    ).astype(F32)

    def placed(vector, width):
        zeros = jnp.zeros((width * parts,), F32)
        return lax.dynamic_update_slice_in_dim(zeros, vector, place * width, 0)

    column_sums = jnp.sum(project_grad.astype(F32), axis=0)
    feature_sums = jnp.stack(
        [
            jnp.sum(first_grad * first_normed, axis=0),
            jnp.sum(first_grad, axis=0),
            jnp.sum(attn_grad.astype(F32), axis=0),
            jnp.sum(second_grad * second_normed, axis=0),
            jnp.sum(second_grad, axis=0),
            jnp.sum(ffn_grad.astype(F32), axis=0),
        ]
    )
    sums = [
        feature_sums[0],
        feature_sums[1],
        placed(column_sums[:cols], cols),
        placed(column_sums[2 * cols :], cols),
        feature_sums[2],
        feature_sums[3],
        feature_sums[4],
        feature_sums[5],
        placed(jnp.sum(upper_grad.astype(F32), axis=0), ff_cols),
        jnp.concatenate([square_sums, jnp.zeros((124,), F32)]),
    ]
    flat = sum_all(jnp.concatenate(sums).reshape(-1, 128)).reshape(-1)
    totals = [flat[i * D : (i + 1) * D] for i in range(8)]
    total_ub = flat[8 * D : 8 * D + FF]
    total_squares = flat[8 * D + FF : 8 * D + FF + 4]

    def own_share(vector):
        width = vector.shape[0] // seq_count
        return lax.dynamic_slice_in_dim(vector, seq_place * width, width, 0)

    residual_rms = jnp.sqrt(total_squares[:3] / (total_squares[3] * D))
    result = result.astype(BF)
    input_grad = input_grad.astype(BF)
    return (
        result[:pre_part][None],
        result[pre_part:][None],
        input_grad[:pre_part][None],
        input_grad[pre_part:][None],
        own_share(totals[0]),
        own_share(totals[1]),
        qkv_full,
        own_share(totals[2]),
        own_share(totals[3]),
        out_full,
        own_share(totals[4]),
        own_share(totals[5]),
        own_share(totals[6]),
        up_full,
        own_share(total_ub),
        down_full,
        own_share(totals[7]),
        residual_rms,
    )


def solution(mesh):
    placed = (
        P("seq", "pre", None),
        P("seq", "pre", None),
        P("seq", None),
        P("seq", None),
        P("seq", None),
        P("seq"),
        P("seq"),
        P("seq", None),
        P("seq"),
        P("seq"),
        P("seq", None),
        P("seq"),
        P("seq"),
        P("seq"),
        P("seq", None),
        P("seq"),
        P("seq", None),
        P("seq"),
        P("seq", "pre", None),
        P("seq", "pre", None),
    )
    return jax.shard_map(
        on_device,
        mesh=mesh,
        in_specs=placed,
        out_specs=(
            P("seq", "pre", None),
            P("seq", "pre", None),
            P("seq", "pre", None),
            P("seq", "pre", None),
            P("seq"),
            P("seq"),
            P("seq", None),
            P("seq"),
            P("seq"),
            P("seq", None),
            P("seq"),
            P("seq"),
            P("seq"),
            P("seq", None),
            P("seq"),
            P("seq", None),
            P("seq"),
            P(),
        ),
        check_vma=False,
    )
```

```python
import functools
import math

import jax
import jax.numpy as jnp
from jax import lax
from jax.experimental import pallas as pl
from jax.experimental.pallas import tpu as pltpu
from jax.sharding import PartitionSpec as P

D = 2048
HEADS = 32
HEAD_DIM = 64
FF = 8192
LAYER = 12
PRE = 512

EPS = 1e-05
NEG = -1e30
BF = jnp.bfloat16
F32 = jnp.float32
TILE = 256


def layer_norm_parts(values, gain, bias):
    mean = jnp.mean(values, axis=-1, keepdims=True)
    centred = values - mean
    variance = jnp.mean(centred * centred, axis=-1, keepdims=True)
    scaling = lax.rsqrt(variance + EPS)
    normed = centred * scaling
    return (normed * gain + bias, normed, scaling)


def norm_back(grad, normed, scaling, gain):
    scaled = grad * gain
    inner = jnp.mean(scaled, axis=-1, keepdims=True)
    cross = jnp.mean(scaled * normed, axis=-1, keepdims=True)
    return scaling * (scaled - inner - normed * cross)


def token_tables(doc_lengths, doc_exit, token_skip):
    order = jnp.arange(doc_lengths.shape[-1], dtype=jnp.int32)
    earlier = order[None, :] < order[:, None]
    starts = jnp.sum(
        jnp.where(earlier, doc_lengths[..., None, :], 0), axis=-1, dtype=jnp.int32
    )
    places = jnp.arange(token_skip.shape[-1], dtype=jnp.int32)
    doc_id = (
        jnp.sum(
            (places[:, None] >= starts[..., None, :]).astype(jnp.int32), axis=-1, dtype=jnp.int32
        )
        - 1
    )
    live_doc = doc_exit > LAYER
    live = jnp.any((doc_id[..., None] == order) & live_doc[..., None, :], axis=-1) & (
        token_skip == 0
    )
    return (doc_id, live)


def dot_nt(a, b):
    return lax.dot_general(a, b, (((1,), (1,)), ((), ())), preferred_element_type=F32)


def dot_nn(a, b):
    return lax.dot_general(a, b, (((1,), (0,)), ((), ())), preferred_element_type=F32)


def dot_tn(a, b):
    return lax.dot_general(a, b, (((0,), (0,)), ((), ())), preferred_element_type=F32)


def masked_scores(block, scores, tile, codes_q, codes_k):
    rows = lax.broadcasted_iota(jnp.int32, (TILE, TILE), 0)
    cols = lax.broadcasted_iota(jnp.int32, (TILE, TILE), 1)
    allowed = None
    if tile == block:
        allowed = cols <= rows
    if tile * TILE >= PRE:
        same = (
            codes_q[block * TILE : (block + 1) * TILE, :]
            == codes_k[:, tile * TILE : (tile + 1) * TILE]
        )
        allowed = same if allowed is None else allowed & same
    if allowed is None:
        return scores
    return jnp.where(allowed, scores, NEG)


def xor(value, mask):
    bit = 1
    while bit <= mask:
        if mask & bit:
            value = value + bit * (1 - 2 * lax.rem(lax.div(value, jnp.int32(bit)), jnp.int32(2)))
        bit *= 2
    return value


def remote(src, dst, send_sem, recv_sem, **target):
    return pltpu.make_async_remote_copy(
        src_ref=src,
        dst_ref=dst,
        send_sem=send_sem,
        recv_sem=recv_sem,
        device_id=target,
        device_id_type=pl.DeviceIdType.MESH,
    )


def greet(wide):
    barrier = pltpu.get_barrier_semaphore()
    seq = lax.axis_index("seq")
    pre = lax.axis_index("pre")
    for mask in (1, *wide):
        pl.semaphore_signal(
            barrier, inc=1, device_id={"seq": xor(seq, mask)}, device_id_type=pl.DeviceIdType.MESH
        )
    for mask in (1, 2):
        pl.semaphore_signal(
            barrier, inc=1, device_id={"pre": xor(pre, mask)}, device_id_type=pl.DeviceIdType.MESH
        )
    pl.semaphore_wait(barrier, len(wide) + 3)


def rows_of(index, count):
    return pl.ds(pl.multiple_of(index * count, count), count)


class Gather:
    def __init__(self, own, land, rows, send_sem, recv_sem, local_sem):
        self.own, self.land, self.rows = own, land, rows
        self.send_sem, self.recv_sem, self.local_sem = send_sem, recv_sem, local_sem
        self.seq = lax.axis_index("seq")
        self.sent = []
        self.local = None

    def slot(self, place):
        return self.land.at[rows_of(place, self.rows), :]

    def begin(self, *masks):
        for mask in masks:
            copy = remote(
                self.own,
                self.slot(self.seq),
                self.send_sem.at[mask],
                self.recv_sem.at[mask],
                seq=xor(self.seq, mask),
            )
            copy.start()
            self.sent.append(copy)

    def keep(self):
        self.local = pltpu.make_async_copy(self.own, self.slot(self.seq), self.local_sem)
        self.local.start()

    def arrived(self, mask):
        here = self.slot(xor(self.seq, mask))
        remote(
            here, here, self.send_sem.at[mask], self.recv_sem.at[mask], seq=xor(self.seq, mask)
        ).wait_recv()

    def forward(self, mask):
        self.arrived(mask)
        here = self.slot(xor(self.seq, mask))
        copy = remote(
            here,
            here,
            self.send_sem.at[mask + 1],
            self.recv_sem.at[mask + 1],
            seq=xor(self.seq, 1),
        )
        copy.start()
        self.sent.append(copy)

    def finish(self, wide):
        self.local.wait()
        self.arrived(1)
        for mask in wide:
            self.arrived(mask + 1)

    def drain(self):
        for copy in self.sent:
            copy.wait_send()


class Spread:
    def __init__(self, own, land, rows, send_sem, recv_sem, local_sem):
        self.own, self.land, self.rows = own, land, rows
        self.send_sem, self.recv_sem, self.local_sem = send_sem, recv_sem, local_sem
        self.pre = lax.axis_index("pre")
        self.sent = []

    def slot(self, index):
        return self.land.at[index * self.rows : (index + 1) * self.rows, :]

    def copy(self, src, slot, mask):
        return remote(
            src, self.slot(slot), self.send_sem.at[slot], self.recv_sem.at[slot], pre=xor(self.pre, mask)
        )

    def begin(self):
        for mask in (2, 1):
            copy = self.copy(self.own, mask, mask)
            copy.start()
            self.sent.append(copy)
        self.local = pltpu.make_async_copy(self.own, self.slot(0), self.local_sem)
        self.local.start()

    def forward(self):
        self.copy(self.own, 2, 2).wait_recv()
        copy = self.copy(self.slot(2), 3, 1)
        copy.start()
        self.sent.append(copy)

    def finish(self):
        self.local.wait()
        self.copy(self.own, 1, 1).wait_recv()
        self.copy(self.own, 3, 1).wait_recv()

    def drain(self):
        for copy in self.sent:
            copy.wait_send()


def local_copies(pairs, sem):
    copies = [pltpu.make_async_copy(src, dst, sem.at[i]) for i, (src, dst) in enumerate(pairs)]
    for copy in copies:
        copy.start()
    for copy in copies:
        copy.wait()


def wide_masks(size):
    masks = list(range(2, size, 2))
    return sorted(masks, key=lambda m: (m != 2, -m))


def head_lanes(value, head):
    lane = lax.broadcasted_iota(jnp.int32, value.shape, 1)
    inside = (lane < HEAD_DIM) if head == 0 else (lane >= HEAD_DIM)
    return jnp.where(inside, value, jnp.zeros_like(value))


def join_heads(first, second):
    lane = lax.broadcasted_iota(jnp.int32, (first.shape[0], 2 * HEAD_DIM), 1)
    return jnp.where(lane < HEAD_DIM, first, second)


def attend_pair(pair, cols, qkv, codes_q, codes_k, mixed, stats):
    lanes = [pl.ds(pl.multiple_of(third * cols + pair * 128, 128), 128) for third in range(3)]
    blocks = qkv.shape[0] // TILE
    for block in range(blocks):
        rows = slice(block * TILE, (block + 1) * TILE)
        both = qkv[rows, lanes[0]]
        outs, levels = [], []
        for head in range(2):
            queries = head_lanes(both, head)
            scores = [
                masked_scores(
                    block,
                    dot_nt(queries, qkv[tile * TILE : (tile + 1) * TILE, lanes[1]]),
                    tile,
                    codes_q,
                    codes_k,
                )
                for tile in range(block + 1)
            ]
            top = functools.reduce(jnp.maximum, [jnp.max(x, axis=1, keepdims=True) for x in scores])
            powers = [jnp.exp(x - top) for x in scores]
            total = functools.reduce(jnp.add, [jnp.sum(e, axis=1, keepdims=True) for e in powers])
            share = 1.0 / total
            outs.append(
                functools.reduce(
                    jnp.add,
                    [
                        dot_nn((e * share).astype(BF), qkv[tile * TILE : (tile + 1) * TILE, lanes[2]])
                        for tile, e in enumerate(powers)
                    ],
                )
            )
            levels.append(top + jnp.log(total))
        mixed[rows, lanes_of(pair)] = join_heads(outs[0], outs[1]).astype(BF)
        stats[rows, lanes_of(pair)] = join_heads(levels[0], levels[1])


def lanes_of(pair):
    return pl.ds(pl.multiple_of(pair * 128, 128), 128)


def forward_kernel(
    sizes,
    own_qkv,
    own_out,
    own_up,
    own_down,
    prefix_in,
    later_in,
    prefix_cot,
    later_cot,
    active_ref,
    gain1,
    bias1,
    out_bias,
    gain2,
    bias2,
    shift,
    factor,
    up_bias,
    codes_q,
    codes_k,
    w_qkv,
    w_out,
    w_up,
    w_down,
    h1,
    df,
    h2,
    qkv,
    mixed,
    stats,
    attn,
    acted,
    slope,
    down_grad,
    wbuf,
    lhs,
    qkv_v,
    mixed_v,
    stats_v,
    x_v,
    cot_v,
    h1_v,
    df_v,
    h2_v,
    terms_v,
    near_v,
    pass_v,
    far_v,
    attn_v,
    acted_v,
    slope_v,
    grad_v,
    gather_send,
    gather_recv,
    spread_send,
    spread_recv,
    sum_send,
    sum_recv,
    local_sem,
):
    seq_size, pre_part, later_part = sizes
    part = pre_part + later_part
    cols = own_qkv.shape[1] // 3
    ff_cols = own_up.shape[1]
    wide = wide_masks(seq_size)
    pre = lax.axis_index("pre")
    near_id = {"pre": xor(pre, 1)}
    far_id = {"pre": xor(pre, 2)}

    def gather(i, own, land):
        return Gather(own, land, own.shape[0], gather_send.at[i], gather_recv.at[i], local_sem.at[i])

    get_qkv = gather(0, own_qkv, w_qkv)
    get_out = gather(1, own_out, w_out)
    get_up = gather(2, own_up, w_up)
    get_down = gather(3, own_down, w_down)
    get_h1 = Spread(h1_v, h1, part, spread_send.at[0], spread_recv.at[0], local_sem.at[4])
    get_df = Spread(df_v, df, part, spread_send.at[1], spread_recv.at[1], local_sem.at[5])
    get_h2 = Spread(h2_v, h2, part, spread_send.at[2], spread_recv.at[2], local_sem.at[6])

    greet(wide)
    get_qkv.begin(1, *wide)
    get_qkv.keep()
    get_out.begin(1, *wide)
    get_out.keep()
    local_copies(
        [
            (prefix_in, x_v.at[:pre_part, :]),
            (later_in, x_v.at[pre_part:, :]),
            (prefix_cot, cot_v.at[:pre_part, :]),
            (later_cot, cot_v.at[pre_part:, :]),
        ],
        local_sem.at[8:12],
    )
    chunk = 32

    @pl.loop(0, part // chunk)
    def _(i):
        rows = rows_of(i, chunk)
        value, _, _ = layer_norm_parts(x_v[rows, :].astype(F32), gain1[...], bias1[...])
        h1_v[rows, :] = value.astype(BF)

    get_h1.begin()

    @pl.loop(0, part // chunk)
    def _(i):
        rows = rows_of(i, chunk)
        df_v[rows, :] = (active_ref[rows, :] * cot_v[rows, :].astype(F32)).astype(BF)

    get_df.begin()
    get_qkv.forward(wide[0])
    get_h1.forward()
    for mask in wide[1:-1]:
        get_qkv.forward(mask)
    get_up.begin(1, *wide)
    get_up.keep()
    get_qkv.forward(wide[-1])
    get_h1.finish()
    get_df.forward()
    load = pltpu.make_async_copy(h1, lhs, local_sem.at[12])
    load.start()
    get_qkv.finish(wide)
    local_copies([(w_qkv, wbuf.at[:, : 3 * cols])], local_sem.at[8:9])
    load.wait()
    for mask in wide:
        get_out.forward(mask)

    @pl.loop(0, 4)
    def _(r):
        member = lax.rem(r, 2) * (xor(pre, 1) - pre) + lax.div(r, 2) * (xor(pre, 2) - pre) + pre
        head_rows = rows_of(member, pre_part)
        tail_rows = pl.ds(pl.multiple_of(4 * pre_part + member * later_part, 64), later_part)

        @pl.loop(0, 3)
        def _(j):
            lanes = pl.ds(pl.multiple_of(j * cols, cols), cols)
            value = dot_nn(lhs[rows_of(r, part), :], wbuf[:, lanes])
            value = ((value + shift[:, lanes]) * factor[:, lanes]).astype(BF)
            qkv_v[head_rows, lanes] = value[:pre_part]
            qkv_v[tail_rows, lanes] = value[pre_part:]

    save_qkv = pltpu.make_async_copy(qkv_v, qkv, local_sem.at[13])
    save_qkv.start()
    get_up.forward(wide[0])
    get_df.finish()
    pairs = cols // 128

    @pl.loop(0, pairs)
    def _(pair):
        attend_pair(pair, cols, qkv_v, codes_q[...], codes_k[...], mixed_v, stats_v)

    save_stats = pltpu.make_async_copy(stats_v, stats, local_sem.at[14])
    save_stats.start()
    for mask in wide[1:-1]:
        get_up.forward(mask)
    get_down.begin(1, *wide)
    get_down.keep()
    get_out.finish(wide)
    local_copies([(w_out, wbuf.at[:cols, :])], local_sem.at[8:9])

    def position_rows(r):
        member = xor(pre, r) if r else pre
        return (
            rows_of(member, pre_part),
            pl.ds(pl.multiple_of(4 * pre_part + member * later_part, 64), later_part),
        )

    def out_term(r, store):
        head_rows, tail_rows = position_rows(r)

        @pl.loop(0, D // 512)
        def _(j):
            lanes = rows_of(j, 512)
            store(
                lanes,
                dot_nn(mixed_v[head_rows, :], wbuf[:cols, lanes]),
                dot_nn(mixed_v[tail_rows, :], wbuf[:cols, lanes]),
            )

    def keep_term(slot):
        def store(lanes, head, tail):
            terms_v[slot, :pre_part, lanes] = head.astype(BF)
            terms_v[slot, pre_part:, lanes] = tail.astype(BF)

        return store

    near = [
        remote(terms_v.at[i], near_v.at[i], sum_send.at[i], sum_recv.at[i], **near_id)
        for i in range(2)
    ]
    far = remote(pass_v, far_v, sum_send.at[2], sum_recv.at[2], **far_id)
    out_term(3, keep_term(0))
    near[0].start()
    out_term(1, keep_term(1))
    near[1].start()
    near[0].wait_recv()

    def pass_term(lanes, head, tail):
        pass_v[:pre_part, lanes] = (head + near_v[0, :pre_part, lanes].astype(F32)).astype(BF)
        pass_v[pre_part:, lanes] = (tail + near_v[0, pre_part:, lanes].astype(F32)).astype(BF)

    out_term(2, pass_term)
    far.start()
    near[1].wait_recv()

    def own_term(lanes, head, tail):
        bias = out_bias[:, lanes]
        attn_v[:pre_part, lanes] = head + near_v[1, :pre_part, lanes].astype(F32) + bias
        attn_v[pre_part:, lanes] = tail + near_v[1, pre_part:, lanes].astype(F32) + bias

    out_term(0, own_term)
    moves = []
    for r in range(4):
        head_rows, tail_rows = position_rows(r)
        moves.append((mixed_v.at[head_rows, :], mixed.at[r * part : r * part + pre_part, :]))
        moves.append((mixed_v.at[tail_rows, :], mixed.at[r * part + pre_part : (r + 1) * part, :]))
    local_copies(moves, local_sem.at[16:24])
    get_up.forward(wide[-1])
    far.wait_recv()

    @pl.loop(0, part // chunk)
    def _(i):
        rows = rows_of(i, chunk)
        branch = attn_v[rows, :] + far_v[rows, :].astype(F32)
        attn_v[rows, :] = branch
        value, _, _ = layer_norm_parts(x_v[rows, :].astype(F32) + branch, gain2[...], bias2[...])
        h2_v[rows, :] = value.astype(BF)

    get_h2.begin()
    save_attn = pltpu.make_async_copy(attn_v, attn, local_sem.at[15])
    save_attn.start()
    get_down.forward(wide[0])
    get_up.finish(wide)
    load = pltpu.make_async_copy(w_up, wbuf, local_sem.at[12])
    load.start()
    get_h2.forward()
    get_h2.finish()
    local_copies([(h2, lhs)], local_sem.at[8:9])
    load.wait()

    @pl.loop(0, 4)
    def _(r):
        rows = rows_of(r, part)

        @pl.loop(0, ff_cols // 512)
        def _(j):
            lanes = rows_of(j, 512)
            upper = dot_nn(lhs[rows, :], wbuf[:, lanes]) + up_bias[:, lanes]
            cumulative = 0.5 * (1.0 + lax.erf(upper * (1.0 / math.sqrt(2.0))))
            density = jnp.exp(-0.5 * upper * upper) * (1.0 / math.sqrt(2.0 * math.pi))
            acted_v[rows, lanes] = (upper * cumulative).astype(BF)
            slope_v[rows, lanes] = (cumulative + upper * density).astype(BF)

    saves = [
        pltpu.make_async_copy(acted_v, acted, local_sem.at[12]),
        pltpu.make_async_copy(slope_v, slope, local_sem.at[8]),
    ]
    for save in saves:
        save.start()
    for mask in wide[1:-1]:
        get_down.forward(mask)
    local_copies([(df, lhs)], local_sem.at[9:10])

    @pl.loop(0, D // 256)
    def _(i):
        lanes = rows_of(i, 256)
        turned = lhs[:, lanes].T

        @pl.loop(0, ff_cols // 512)
        def _(j):
            grad_v[:, rows_of(j, 512)] = dot_nn(turned, acted_v[:, rows_of(j, 512)]).astype(BF)

        save = pltpu.make_async_copy(grad_v, down_grad.at[lanes, :], local_sem.at[9])
        save.start()
        save.wait()

    get_down.forward(wide[-1])
    get_down.finish(wide)
    for save in (*saves, save_qkv, save_stats, save_attn):
        save.wait()
    for item in (get_qkv, get_out, get_up, get_down, get_h1, get_df, get_h2):
        item.drain()
    for copy in (*near, far):
        copy.wait_send()


def forward_pass(seq_size, pre_part, later_part, *operands):
    own_qkv, own_out, own_up = operands[:3]
    part = pre_part + later_part
    length = 4 * part
    width = own_qkv.shape[1]
    cols = width // 3
    ff_cols = own_up.shape[1]
    hbm = pl.BlockSpec(memory_space=pl.ANY)
    vmem = pl.BlockSpec(memory_space=pltpu.VMEM)

    def out(shape, kind=BF):
        return jax.ShapeDtypeStruct(shape, kind)

    outs = (
        out((D, width)),
        out((cols, D)),
        out((D, ff_cols)),
        out((D, ff_cols)),
        out((length, D)),
        out((length, D)),
        out((length, D)),
        out((length, width)),
        out((length, cols)),
        out((length, cols), F32),
        out((part, D), F32),
        out((length, ff_cols)),
        out((length, ff_cols)),
        out((D, ff_cols)),
    )
    dma = pltpu.SemaphoreType.DMA
    return pl.pallas_call(
        functools.partial(forward_kernel, (seq_size, pre_part, later_part)),
        out_shape=outs,
        in_specs=[hbm] * 8 + [vmem] * (len(operands) - 8),
        out_specs=[hbm] * len(outs),
        scratch_shapes=[
            pltpu.VMEM((D, max(ff_cols, width)), BF),
            pltpu.VMEM((length, D), BF),
            pltpu.VMEM((length, width), BF),
            pltpu.VMEM((length, cols), BF),
            pltpu.VMEM((length, cols), F32),
            pltpu.VMEM((part, D), BF),
            pltpu.VMEM((part, D), BF),
            pltpu.VMEM((part, D), BF),
            pltpu.VMEM((part, D), BF),
            pltpu.VMEM((part, D), BF),
            pltpu.VMEM((2, part, D), BF),
            pltpu.VMEM((2, part, D), BF),
            pltpu.VMEM((part, D), BF),
            pltpu.VMEM((part, D), BF),
            pltpu.VMEM((part, D), F32),
            pltpu.VMEM((length, ff_cols), BF),
            pltpu.VMEM((length, ff_cols), BF),
            pltpu.VMEM((256, ff_cols), BF),
            dma((4, seq_size)),
            dma((4, seq_size)),
            dma((3, 4)),
            dma((3, 4)),
            dma((3,)),
            dma((3,)),
            dma((24,)),
        ],
        compiler_params=pltpu.CompilerParams(
            collective_id=0, has_side_effects=True, vmem_limit_bytes=62 * 2**20
        ),
        cost_estimate=pl.CostEstimate(
            flops=2 * length * D * (width + cols + 2 * ff_cols),
            bytes_accessed=8 * D * ff_cols,
            transcendentals=length * ff_cols,
        ),
        name="forward_pass",
    )(*operands)


class Pool:
    def __init__(self, buffers, count):
        self.buffers, self.count = buffers, count
        self.pending = [None] * count
        self.turn = 0

    def take(self):
        index = self.turn % self.count
        self.turn += 1
        if self.pending[index] is not None:
            self.pending[index].wait_send()
            self.pending[index] = None
        return index

    def drain(self):
        for copy in self.pending:
            if copy is not None:
                copy.wait_send()


class Reduce:
    def __init__(self, grad, near, wide_land, rows, width, sems, work):
        self.grad, self.near, self.wide_land = grad, near, wide_land
        self.rows, self.width = rows, width
        self.near_send, self.near_recv, self.wide_send, self.wide_recv = sems
        self.left, self.right, self.total, self.out, self.pool, self.sem = work
        self.seq = lax.axis_index("seq")
        self.sent = []

    def block(self, mask):
        return self.grad.at[rows_of(xor(self.seq, mask), self.rows), :]

    def near_slot(self, mask):
        return self.near.at[mask // 2 * self.rows : (mask // 2 + 1) * self.rows, :]

    def wide_slot(self, mask):
        return self.wide_land.at[mask // 2 * self.rows : (mask // 2 + 1) * self.rows, :]

    def near_copy(self, mask):
        return remote(
            self.block(mask + 1),
            self.near_slot(mask),
            self.near_send.at[mask // 2],
            self.near_recv.at[mask // 2],
            seq=xor(self.seq, 1),
        )

    def wide_copy(self, src, mask):
        return remote(
            src,
            self.wide_slot(mask),
            self.wide_send.at[mask // 2],
            self.wide_recv.at[mask // 2],
            seq=xor(self.seq, mask),
        )

    def begin(self, *masks):
        for mask in masks:
            copy = self.near_copy(mask)
            copy.start()
            self.sent.append(copy)

    def views(self, index=None):
        left = self.left.at[: self.rows, : self.width]
        right = self.right.at[: self.rows, : self.width]
        return left, right

    def step(self, mask):
        left, right = self.views()
        own = pltpu.make_async_copy(self.block(mask), left, self.sem.at[0])
        own.start()
        self.near_copy(mask).wait_recv()
        other = pltpu.make_async_copy(self.near_slot(mask), right, self.sem.at[1])
        other.start()
        index = self.pool.take()
        own.wait()
        other.wait()
        chunk = min(32, self.rows)

        @pl.loop(0, self.rows // chunk)
        def _(i):
            at = (rows_of(i, chunk), slice(0, self.width))
            value = self.left[at].astype(F32) + self.right[at].astype(F32)
            self.out[index, at[0], at[1]] = value.astype(BF)

        copy = self.wide_copy(self.out.at[index, : self.rows, : self.width], mask)
        copy.start()
        self.pool.pending[index] = copy

    def settle(self, wide):
        self.near_copy(0).wait_recv()
        for mask in wide:
            self.wide_copy(self.out.at[0, : self.rows, : self.width], mask).wait_recv()

    def final(self, wide, result):
        left, right = self.views()
        chunk = min(32, self.rows)
        local_copies([(self.block(0), left), (self.near_slot(0), right)], self.sem)
        masks = list(wide)

        @pl.loop(0, self.rows // chunk)
        def _(i):
            at = (rows_of(i, chunk), slice(0, self.width))
            self.total[at] = self.left[at].astype(F32) + self.right[at].astype(F32)

        while masks:
            now, masks = masks[:2], masks[2:]
            views = [(self.wide_slot(mask), view) for mask, view in zip(now, (left, right))]
            local_copies(views, self.sem)
            refs = (self.left, self.right)[: len(now)]
            last = not masks

            @pl.loop(0, self.rows // chunk)
            def _(i):
                at = (rows_of(i, chunk), slice(0, self.width))
                value = self.total[at]
                for ref in refs:
                    value = value + ref[at].astype(F32)
                if last:
                    result[at] = value.astype(BF)
                else:
                    self.total[at] = value

    def drain(self):
        for copy in self.sent:
            copy.wait_send()


class Sum:
    def __init__(self, terms, near, passed, far, send_sem, recv_sem):
        pre = lax.axis_index("pre")
        near_id, far_id = {"pre": xor(pre, 1)}, {"pre": xor(pre, 2)}
        self.terms, self.near, self.passed = terms, near, passed
        self.near_copies = [
            remote(terms.at[i], near.at[i], send_sem.at[i], recv_sem.at[i], **near_id)
            for i in range(2)
        ]
        self.far_copy = remote(passed, far, send_sem.at[2], recv_sem.at[2], **far_id)

    def run(self, term, keep):
        def store_in(slot):
            def store(rows, lanes, value):
                self.terms[slot, rows, lanes] = value.astype(BF)

            return store

        term(3, store_in(0))
        self.near_copies[0].start()
        term(1, store_in(1))
        self.near_copies[1].start()
        self.near_copies[0].wait_recv()

        def store(rows, lanes, value):
            self.passed[rows, lanes] = (value + self.near[0, rows, lanes].astype(F32)).astype(BF)

        term(2, store)
        self.far_copy.start()
        self.near_copies[1].wait_recv()

        def store(rows, lanes, value):
            keep(rows, lanes, value + self.near[1, rows, lanes].astype(F32))

        term(0, store)

    def drain(self):
        for copy in (*self.near_copies, self.far_copy):
            copy.wait_send()


def columns_grad(left, right, rows, width, tile, save):
    @pl.loop(0, rows // 256)
    def _(i):
        turned = left[:, rows_of(i, 256)].T

        @pl.loop(0, width // 512)
        def _(j):
            tile[:, rows_of(j, 512)] = dot_nn(turned, right[:, rows_of(j, 512)]).astype(BF)

        copy = save(rows_of(i, 256))
        copy.start()
        copy.wait()


def add_rows(target, index, value):
    target[index : index + 1, : value.shape[1]] += jnp.sum(value, axis=0, keepdims=True)


def feed_back_kernel(
    sizes,
    w_down,
    w_up,
    df,
    h2,
    slope,
    attn,
    down_grad,
    prefix_in,
    later_in,
    prefix_cot,
    later_cot,
    active_ref,
    gain2,
    near_down,
    wide_down,
    up_grad,
    dattn,
    middle_grad,
    sums,
    up_sums,
    wbuf,
    lhs,
    slope_v,
    du_v,
    x_v,
    cot_v,
    attn_v,
    acc_v,
    dattn_v,
    terms_v,
    near_v,
    pass_v,
    far_v,
    left_v,
    right_v,
    total_v,
    out_v,
    grad_v,
    twin_send,
    twin_recv,
    wide_send,
    wide_recv,
    spread_send,
    spread_recv,
    sum_send,
    sum_recv,
    local_sem,
):
    seq_size, pre_part, later_part = sizes
    part = pre_part + later_part
    length = 4 * part
    ff_cols = w_up.shape[1]
    wide = wide_masks(seq_size)
    late = sorted(wide, key=lambda m: (m == 2, m))
    pool = Pool(out_v, 3)
    work = (left_v, right_v, total_v, out_v, pool, local_sem.at[0:2])
    put_down = Reduce(
        down_grad,
        near_down,
        wide_down,
        D // seq_size,
        ff_cols,
        (twin_send, twin_recv, wide_send, wide_recv),
        work,
    )
    get_dattn = Spread(dattn_v, dattn, part, spread_send, spread_recv, local_sem.at[2])
    sum_dh2 = Sum(terms_v, near_v, pass_v, far_v, sum_send, sum_recv)

    greet(wide)
    put_down.begin(*late, 0)
    loads = [
        pltpu.make_async_copy(src, dst, local_sem.at[3 + i])
        for i, (src, dst) in enumerate(
            [
                (w_down, wbuf),
                (df, lhs),
                (slope, slope_v),
                (prefix_in, x_v.at[:pre_part, :]),
                (later_in, x_v.at[pre_part:, :]),
                (prefix_cot, cot_v.at[:pre_part, :]),
                (later_cot, cot_v.at[pre_part:, :]),
                (attn, attn_v),
            ]
        )
    ]
    for load in loads:
        load.start()
    for load in loads:
        load.wait()

    @pl.loop(0, 4)
    def _(r):
        rows = rows_of(r, part)

        @pl.loop(0, ff_cols // 512)
        def _(j):
            lanes = rows_of(j, 512)
            value = dot_nn(lhs[rows, :], wbuf[:, lanes])
            du_v[rows, lanes] = (value * slope_v[rows, lanes].astype(F32)).astype(BF)

    load = pltpu.make_async_copy(w_up, wbuf, local_sem.at[3])
    load.start()
    load_h2 = pltpu.make_async_copy(h2, lhs, local_sem.at[4])
    load_h2.start()
    put_down.step(late[0])
    load.wait()

    def dh2_term(r, store):
        @pl.loop(0, D // 512)
        def _(j):
            store(
                slice(0, part),
                rows_of(j, 512),
                dot_nt(du_v[r * part : (r + 1) * part, :], wbuf[rows_of(j, 512), :]),
            )

    def keep_dh2(rows, lanes, value):
        acc_v[rows, lanes] = value

    sum_dh2.run(dh2_term, keep_dh2)
    for mask in late[1:-1]:
        put_down.step(mask)
    load_h2.wait()
    columns_grad(
        lhs,
        du_v,
        D,
        ff_cols,
        grad_v,
        lambda rows: pltpu.make_async_copy(grad_v, up_grad.at[rows, :], local_sem.at[3]),
    )
    sums[...] = jnp.zeros_like(sums)
    up_sums[...] = jnp.zeros_like(up_sums)
    if len(late) > 1:
        put_down.step(late[-1])
    sum_dh2.far_copy.wait_recv()
    chunk = 32

    @pl.loop(0, part // chunk)
    def _(i):
        rows = rows_of(i, chunk)
        grad = acc_v[rows, :] + far_v[rows, :].astype(F32)
        middle = x_v[rows, :].astype(F32) + attn_v[rows, :]
        _, normed, scaling = layer_norm_parts(middle, gain2[...], 0.0)
        back = norm_back(grad, normed, scaling, gain2[...])
        acc_v[rows, :] = back
        direct = active_ref[rows, :] * cot_v[rows, :].astype(F32)
        value = (direct + back).astype(BF)
        dattn_v[rows, :] = value
        add_rows(sums, 0, value.astype(F32))
        add_rows(sums, 1, grad * normed)
        add_rows(sums, 2, grad)
        add_rows(sums, 3, direct)

    get_dattn.begin()
    save = pltpu.make_async_copy(acc_v, middle_grad, local_sem.at[3])
    save.start()

    @pl.loop(0, length // chunk)
    def _(i):
        add_rows(up_sums, 0, du_v[rows_of(i, chunk), :].astype(F32))

    get_dattn.forward()
    put_down.settle(wide)
    get_dattn.finish()
    save.wait()
    for item in (put_down, get_dattn, sum_dh2, pool):
        item.drain()


def feed_back(seq_size, pre_part, later_part, *operands):
    part = pre_part + later_part
    length = 4 * part
    w_up = operands[1]
    ff_cols = w_up.shape[1]
    own_d = D // seq_size
    hbm = pl.BlockSpec(memory_space=pl.ANY)
    vmem = pl.BlockSpec(memory_space=pltpu.VMEM)

    def out(shape, kind=BF):
        return jax.ShapeDtypeStruct(shape, kind)

    half = seq_size // 2
    outs = (
        out((half * own_d, ff_cols)),
        out((half * own_d, ff_cols)),
        out((D, ff_cols)),
        out((length, D)),
        out((part, D), F32),
        out((8, D), F32),
        out((8, ff_cols), F32),
    )
    dma = pltpu.SemaphoreType.DMA
    return pl.pallas_call(
        functools.partial(feed_back_kernel, (seq_size, pre_part, later_part)),
        out_shape=outs,
        in_specs=[hbm] * 11 + [vmem] * (len(operands) - 11),
        out_specs=[hbm] * 5 + [vmem] * 2,
        scratch_shapes=[
            pltpu.VMEM((D, ff_cols), BF),
            pltpu.VMEM((length, D), BF),
            pltpu.VMEM((length, ff_cols), BF),
            pltpu.VMEM((length, ff_cols), BF),
            pltpu.VMEM((part, D), BF),
            pltpu.VMEM((part, D), BF),
            pltpu.VMEM((part, D), F32),
            pltpu.VMEM((part, D), F32),
            pltpu.VMEM((part, D), BF),
            pltpu.VMEM((2, part, D), BF),
            pltpu.VMEM((2, part, D), BF),
            pltpu.VMEM((part, D), BF),
            pltpu.VMEM((part, D), BF),
            pltpu.VMEM((own_d, ff_cols), BF),
            pltpu.VMEM((own_d, ff_cols), BF),
            pltpu.VMEM((own_d, ff_cols), F32),
            pltpu.VMEM((3, own_d, ff_cols), BF),
            pltpu.VMEM((256, ff_cols), BF),
            dma((half,)),
            dma((half,)),
            dma((half,)),
            dma((half,)),
            dma((4,)),
            dma((4,)),
            dma((3,)),
            dma((3,)),
            dma((12,)),
        ],
        compiler_params=pltpu.CompilerParams(
            collective_id=1, has_side_effects=True, vmem_limit_bytes=62 * 2**20
        ),
        cost_estimate=pl.CostEstimate(
            flops=2 * length * D * 3 * ff_cols,
            bytes_accessed=8 * D * ff_cols,
            transcendentals=length,
        ),
        name="feed_back",
    )(*operands)


def attend_back_pair(pair, cols, qkv, do, stats, codes_q, codes_k, dq_all, dk_all, dv_all, dqkv):
    lanes = [pl.ds(pl.multiple_of(third * cols + pair * 128, 128), 128) for third in range(3)]
    dk_all[...] = jnp.zeros_like(dk_all)
    dv_all[...] = jnp.zeros_like(dv_all)
    blocks = qkv.shape[0] // TILE
    for block in range(blocks):
        rows = slice(block * TILE, (block + 1) * TILE)
        both_q = qkv[rows, lanes[0]]
        both_do = do[rows, lanes_of(pair)]
        both_levels = stats[rows, lanes_of(pair)]
        parts = []
        for head in range(2):
            queries = head_lanes(both_q, head)
            grads = head_lanes(both_do, head)
            level = both_levels[:, head * HEAD_DIM : head * HEAD_DIM + 1]
            probs = []
            dprobs = []
            for tile in range(block + 1):
                keys = slice(tile * TILE, (tile + 1) * TILE)
                scores = masked_scores(
                    block, dot_nt(queries, qkv[keys, lanes[1]]), tile, codes_q, codes_k
                )
                probs.append(jnp.exp(scores - level))
                dprobs.append(dot_nt(grads, qkv[keys, lanes[2]]))
            delta = functools.reduce(
                jnp.add, [jnp.sum(a * b, axis=1, keepdims=True) for a, b in zip(probs, dprobs)]
            )
            dq = None
            for tile in range(block + 1):
                keys = slice(tile * TILE, (tile + 1) * TILE)
                ds = (probs[tile] * (dprobs[tile] - delta)).astype(BF)
                part = dot_nn(ds, qkv[keys, lanes[1]])
                dq = part if dq is None else dq + part
                dk_all[keys, :] += dot_tn(ds, queries)
                dv_all[keys, :] += dot_tn(probs[tile].astype(BF), grads)
            parts.append(dq)
        dq_all[rows, :] = join_heads(*parts) * (1.0 / math.sqrt(HEAD_DIM))
    for lane, source in zip(lanes, (dq_all, dk_all, dv_all)):
        dqkv[:, lane] = source[...].astype(BF)


def attend_back_kernel(
    sizes,
    w_qkv,
    w_out,
    w_down,
    h1,
    qkv,
    stats,
    mixed,
    acted,
    dattn,
    middle_grad,
    attn,
    up_grad,
    down_grad,
    near_down,
    wide_down,
    prefix_in,
    later_in,
    prefix_cot,
    later_cot,
    active_ref,
    gain1,
    down_bias,
    codes_q,
    codes_k,
    fin_down,
    fin_up,
    fin_qkv,
    fin_out,
    near_up,
    wide_up,
    near_out,
    wide_out,
    near_qkv,
    wide_qkv,
    out_grad,
    qkv_grad,
    prefix_out,
    later_out,
    prefix_grad,
    later_grad,
    sums,
    qkv_sums,
    wbuf,
    lhs,
    qkv_v,
    stats_v,
    do_v,
    mixed_v,
    dqkv_v,
    dq_v,
    dk_v,
    dv_v,
    x_v,
    cot_v,
    attn_v,
    middle_v,
    acc_v,
    terms_v,
    near_v,
    pass_v,
    far_v,
    left_v,
    right_v,
    total_v,
    out_v,
    grad_v,
    res_down,
    res_up,
    res_qkv,
    res_out,
    twin_send,
    twin_recv,
    wide_send,
    wide_recv,
    spread_send,
    spread_recv,
    sum_send,
    sum_recv,
    local_sem,
):
    seq_size, pre_part, later_part = sizes
    part = pre_part + later_part
    length = 4 * part
    width = w_qkv.shape[1]
    cols = width // 3
    ff_cols = w_down.shape[1]
    own_d = D // seq_size
    own_o = cols // seq_size
    pre = lax.axis_index("pre")
    wide = wide_masks(seq_size)
    late = sorted(wide, key=lambda m: (m == 2, m))
    pool = Pool(out_v, 3)
    work = (left_v, right_v, total_v, out_v, pool, local_sem.at[0:2])

    def reduce_of(i, grad, near, wide_land, rows, columns):
        sems = (twin_send.at[i], twin_recv.at[i], wide_send.at[i], wide_recv.at[i])
        return Reduce(grad, near, wide_land, rows, columns, sems, work)

    put_down = reduce_of(0, down_grad, near_down, wide_down, own_d, ff_cols)
    put_up = reduce_of(0, up_grad, near_up, wide_up, own_d, ff_cols)
    put_out = reduce_of(1, out_grad, near_out, wide_out, own_o, D)
    put_qkv = reduce_of(2, qkv_grad, near_qkv, wide_qkv, own_d, width)

    def spread_of(i, own, land):
        return Spread(own, land, own_d, spread_send.at[i], spread_recv.at[i], local_sem.at[2 + i])

    get_down = spread_of(0, res_down, fin_down)
    get_up = spread_of(1, res_up, fin_up)
    get_qkv = spread_of(2, res_qkv, fin_qkv)
    sum_f = Sum(terms_v, near_v, pass_v, far_v, sum_send.at[0], sum_recv.at[0])
    sum_dh1 = Sum(terms_v, near_v, pass_v, far_v, sum_send.at[1], sum_recv.at[1])
    chunk = 32

    greet(wide)
    put_up.begin(*late, 0)

    def load_all(first, *pairs):
        copies = [
            pltpu.make_async_copy(src, dst, local_sem.at[first + i])
            for i, (src, dst) in enumerate(pairs)
        ]
        for copy in copies:
            copy.start()
        return copies

    def wait_all(copies):
        for copy in copies:
            copy.wait()

    loads = load_all(5, (w_down, wbuf), (acted, lhs))
    more = load_all(
        8,
        (prefix_in, x_v.at[:pre_part, :]),
        (later_in, x_v.at[pre_part:, :]),
        (prefix_cot, cot_v.at[:pre_part, :]),
        (later_cot, cot_v.at[pre_part:, :]),
        (attn, attn_v),
        (middle_grad, middle_v),
        (qkv, qkv_v),
        (stats, stats_v),
        (mixed, mixed_v),
    )
    sums[...] = jnp.zeros_like(sums)
    qkv_sums[...] = jnp.zeros_like(qkv_sums)
    wait_all(loads)

    def f_term(r, store):
        @pl.loop(0, D // 512)
        def _(j):
            store(
                slice(0, part),
                rows_of(j, 512),
                dot_nt(lhs[r * part : (r + 1) * part, :], wbuf[rows_of(j, 512), :]),
            )

    def keep(rows, lanes, value):
        acc_v[rows, lanes] = value

    sum_f.run(f_term, keep)
    loads = load_all(5, (w_out, wbuf.at[:cols, :]), (dattn, lhs))
    wait_all(more)
    put_up.step(late[0])
    wait_all(loads)

    def position_rows(r):
        member = lax.rem(r, 2) * (xor(pre, 1) - pre) + lax.div(r, 2) * (xor(pre, 2) - pre) + pre
        return (
            rows_of(member, pre_part),
            pl.ds(pl.multiple_of(4 * pre_part + member * later_part, 64), later_part),
        )

    @pl.loop(0, 4)
    def _(r):
        head_rows, tail_rows = position_rows(r)
        value = dot_nt(lhs[rows_of(r, part), :], wbuf[:cols, :]).astype(BF)
        do_v[head_rows, :] = value[:pre_part]
        do_v[tail_rows, :] = value[pre_part:]

    columns_grad(
        mixed_v,
        lhs,
        cols,
        D,
        grad_v,
        lambda rows: pltpu.make_async_copy(grad_v.at[:, :D], out_grad.at[rows, :], local_sem.at[5]),
    )
    put_out.begin(*late, 0)
    loads = load_all(5, (w_qkv, wbuf.at[:, :width]))
    for r in range(4):
        head_rows, tail_rows = position_rows(jnp.int32(r))
        loads += load_all(
            8 + 2 * r,
            (h1.at[r * part : r * part + pre_part, :], lhs.at[head_rows, :]),
            (h1.at[r * part + pre_part : (r + 1) * part, :], lhs.at[tail_rows, :]),
        )
    pairs = cols // 128

    def attention(first, last):
        @pl.loop(first, last)
        def _(pair):
            attend_back_pair(
                pair,
                cols,
                qkv_v,
                do_v,
                stats_v,
                codes_q[...],
                codes_k[...],
                dq_v,
                dk_v,
                dv_v,
                dqkv_v,
            )

    attention(0, pairs // 2)
    for mask in late[1:-1]:
        put_up.step(mask)
    sum_f.far_copy.wait_recv()
    sum_f.drain()

    @pl.loop(0, part // chunk)
    def _(i):
        rows = rows_of(i, chunk)
        live = active_ref[rows, :]
        ffn = acc_v[rows, :] + far_v[rows, :].astype(F32) + down_bias[...]
        branch = attn_v[rows, :]
        result = x_v[rows, :].astype(F32) + live * (branch + ffn)
        add_rows(sums, 2, live * result * result)
        add_rows(sums, 3, live * branch * branch)
        add_rows(sums, 4, live * ffn * ffn)
        pass_v[rows, :] = result.astype(BF)

    put_down.final(wide, res_down)
    get_down.begin()
    attention(pairs // 2, pairs)
    get_down.forward()
    wait_all(loads)
    columns_grad(
        lhs,
        dqkv_v,
        D,
        width,
        grad_v,
        lambda rows: pltpu.make_async_copy(
            grad_v.at[:, :width], qkv_grad.at[rows, :], local_sem.at[5]
        ),
    )
    put_qkv.begin(*late, 0)
    put_up.step(late[-1])
    get_down.finish()
    saves = load_all(6, (pass_v.at[:pre_part, :], prefix_out), (pass_v.at[pre_part:, :], later_out))
    wait_all(saves)

    def dh1_term(r, store):
        head_rows, tail_rows = position_rows(jnp.int32(r))

        @pl.loop(0, D // 512)
        def _(j):
            weights = wbuf[rows_of(j, 512), :width]
            store(slice(0, pre_part), rows_of(j, 512), dot_nt(dqkv_v[head_rows, :], weights))
            store(slice(pre_part, part), rows_of(j, 512), dot_nt(dqkv_v[tail_rows, :], weights))

    sum_dh1.run(dh1_term, keep)

    @pl.loop(0, length // chunk)
    def _(i):
        add_rows(qkv_sums, 0, dqkv_v[rows_of(i, chunk), :].astype(F32))

    for mask in late:
        put_out.step(mask)
    sum_dh1.far_copy.wait_recv()

    @pl.loop(0, part // chunk)
    def _(i):
        rows = rows_of(i, chunk)
        grad = acc_v[rows, :] + far_v[rows, :].astype(F32)
        _, normed, scaling = layer_norm_parts(x_v[rows, :].astype(F32), gain1[...], 0.0)
        back = norm_back(grad, normed, scaling, gain1[...])
        add_rows(sums, 0, grad * normed)
        add_rows(sums, 1, grad)
        value = cot_v[rows, :].astype(F32) + middle_v[rows, :] + back
        terms_rows = value.astype(BF)
        x_v[rows, :] = terms_rows

    saves = load_all(6, (x_v.at[:pre_part, :], prefix_grad), (x_v.at[pre_part:, :], later_grad))
    put_up.settle(wide)
    put_up.final(wide, res_up)
    get_up.begin()
    put_qkv.step(late[0])
    put_out.settle(wide)
    put_out.final(wide, res_out)
    wait_all(saves)
    saves = load_all(6, (res_out, fin_out))
    for mask in late[1:]:
        put_qkv.step(mask)
    get_up.forward()
    put_qkv.settle(wide)
    put_qkv.final(wide, res_qkv)
    get_qkv.begin()
    get_up.finish()
    get_qkv.forward()
    get_qkv.finish()
    wait_all(saves)
    for item in (put_up, put_out, put_qkv, get_down, get_up, get_qkv, sum_dh1, pool):
        item.drain()


def attend_back(seq_size, pre_part, later_part, *operands):
    part = pre_part + later_part
    length = 4 * part
    width = operands[0].shape[1]
    cols = width // 3
    ff_cols = operands[2].shape[1]
    own_d = D // seq_size
    own_o = cols // seq_size
    half = seq_size // 2
    hbm = pl.BlockSpec(memory_space=pl.ANY)
    vmem = pl.BlockSpec(memory_space=pltpu.VMEM)

    def out(shape, kind=BF):
        return jax.ShapeDtypeStruct(shape, kind)

    outs = (
        out((4 * own_d, ff_cols)),
        out((4 * own_d, ff_cols)),
        out((4 * own_d, width)),
        out((own_o, D)),
        out((half * own_d, ff_cols)),
        out((half * own_d, ff_cols)),
        out((half * own_o, D)),
        out((half * own_o, D)),
        out((half * own_d, width)),
        out((half * own_d, width)),
        out((cols, D)),
        out((D, width)),
        out((pre_part, D)),
        out((later_part, D)),
        out((pre_part, D)),
        out((later_part, D)),
        out((8, D), F32),
        out((8, width), F32),
    )
    most = max(ff_cols, D, width)
    dma = pltpu.SemaphoreType.DMA
    return pl.pallas_call(
        functools.partial(attend_back_kernel, (seq_size, pre_part, later_part)),
        out_shape=outs,
        in_specs=[hbm] * 19 + [vmem] * (len(operands) - 19),
        out_specs=[hbm] * 16 + [vmem] * 2,
        scratch_shapes=[
            pltpu.VMEM((D, most), BF),
            pltpu.VMEM((length, D), BF),
            pltpu.VMEM((length, width), BF),
            pltpu.VMEM((length, cols), F32),
            pltpu.VMEM((length, cols), BF),
            pltpu.VMEM((length, cols), BF),
            pltpu.VMEM((length, width), BF),
            pltpu.VMEM((length, 128), F32),
            pltpu.VMEM((length, 128), F32),
            pltpu.VMEM((length, 128), F32),
            pltpu.VMEM((part, D), BF),
            pltpu.VMEM((part, D), BF),
            pltpu.VMEM((part, D), F32),
            pltpu.VMEM((part, D), F32),
            pltpu.VMEM((part, D), F32),
            pltpu.VMEM((2, part, D), BF),
            pltpu.VMEM((2, part, D), BF),
            pltpu.VMEM((part, D), BF),
            pltpu.VMEM((part, D), BF),
            pltpu.VMEM((own_d, most), BF),
            pltpu.VMEM((own_d, most), BF),
            pltpu.VMEM((own_d, most), F32),
            pltpu.VMEM((3, own_d, most), BF),
            pltpu.VMEM((256, most), BF),
            pltpu.VMEM((own_d, ff_cols), BF),
            pltpu.VMEM((own_d, ff_cols), BF),
            pltpu.VMEM((own_d, width), BF),
            pltpu.VMEM((own_o, D), BF),
            dma((3, half)),
            dma((3, half)),
            dma((3, half)),
            dma((3, half)),
            dma((3, 4)),
            dma((3, 4)),
            dma((2, 3)),
            dma((2, 3)),
            dma((20,)),
        ],
        compiler_params=pltpu.CompilerParams(
            collective_id=2, has_side_effects=True, vmem_limit_bytes=63 * 2**20
        ),
        cost_estimate=pl.CostEstimate(
            flops=2 * length * D * (2 * width + ff_cols),
            bytes_accessed=8 * D * ff_cols,
            transcendentals=length * length,
        ),
        name="attend_back",
    )(*operands)


class Seq:
    def __init__(self):
        self.size = lax.axis_size("seq")
        self.place = lax.axis_index("seq")

    def swap(self, value, mask):
        return lax.ppermute(value, "seq", [(i, i ^ mask) for i in range(self.size)])

    def gather(self, own):
        blocks = [own, self.swap(own, 1)]
        for mask in range(2, self.size, 2):
            blocks.append(self.swap(own, mask))
            blocks.append(self.swap(blocks[-1], 1))
        return blocks

    def reorder(self, value, axis):
        block = value.shape[axis] // self.size
        return jnp.concatenate(
            [
                lax.dynamic_slice_in_dim(value, jnp.bitwise_xor(self.place, i) * block, block, axis)
                for i in range(self.size)
            ],
            axis=axis,
        )


def over_pre(value, mask):
    return lax.ppermute(value, "pre", [(i, i ^ mask) for i in range(lax.axis_size("pre"))])


def gather_pre(own):
    far = over_pre(own, 2)
    near = over_pre(own, 1)
    return [own, near, far, over_pre(far, 1)]


def sum_all(value):
    for mask in (1, 2):
        value = value + over_pre(value, mask)
    size = lax.axis_size("seq")
    mask = 1
    while mask < size:
        value = value + lax.ppermute(value, "seq", [(i, i ^ mask) for i in range(size)])
        mask *= 2
    return value


def absolute_pre(blocks, place):
    first = place % 2 == 0
    low = place < 2
    a = [jnp.where(first, blocks[0], blocks[1]), jnp.where(first, blocks[1], blocks[0])]
    b = [jnp.where(first, blocks[2], blocks[3]), jnp.where(first, blocks[3], blocks[2])]
    return [jnp.where(low, u, w) for u, w in zip(a, b)] + [jnp.where(low, w, u) for u, w in zip(a, b)]


def on_device(
    prefix_in,
    later_in,
    doc_lengths,
    doc_exit,
    token_skip,
    first_gain,
    first_bias,
    qkv_weight,
    query_bias,
    value_bias,
    out_weight,
    out_bias,
    second_gain,
    second_bias,
    up_weight,
    up_bias,
    down_weight,
    down_bias,
    prefix_cot,
    later_cot,
):
    scale = 1.0 / math.sqrt(HEAD_DIM)
    pre_part = prefix_in.shape[1]
    later_part = later_in.shape[1]
    part = pre_part + later_part
    parts = lax.axis_size("pre")
    place = lax.axis_index("pre")
    seq = Seq()
    seq_count = seq.size
    seq_place = seq.place
    own_d = D // seq_count
    cols = D // parts
    ff_cols = FF // parts
    length = parts * part

    packed = jnp.concatenate(
        [
            first_gain,
            first_bias,
            query_bias,
            value_bias,
            out_bias,
            second_gain,
            second_bias,
            down_bias,
            up_bias,
        ]
    ).reshape(-1, 128)
    small = seq.reorder(jnp.stack(seq.gather(packed)).reshape(seq_count, -1), 0).astype(F32)
    vectors = [small[:, i * own_d : (i + 1) * own_d].reshape(1, D) for i in range(8)]
    full_up_bias = small[:, 8 * own_d :].reshape(1, FF)
    (gain1, bias1, qb, vb, ob, gain2, bias2, db) = vectors

    def section(weight, start, width):
        return lax.dynamic_slice_in_dim(weight, start + place * width, width, 1)

    own_qkv = jnp.concatenate([section(qkv_weight, i * D, cols) for i in range(3)], axis=1)
    block_rows = own_d // parts
    out_block = lax.dynamic_slice_in_dim(out_weight, place * block_rows, block_rows, 0)
    shuffle = [
        ((b % parts) * seq_count + b // parts, (b // seq_count) * seq_count + b % seq_count)
        for b in range(parts * seq_count)
    ]
    own_out = lax.ppermute(out_block, ("pre", "seq"), shuffle)
    doc_id, live = token_tables(doc_lengths, doc_exit, token_skip)
    live_here = lax.dynamic_slice_in_dim(live[0], place * later_part, later_part, 0)
    active = jnp.concatenate([jnp.ones((pre_part,), F32), live_here.astype(F32)])[:, None]
    codes_q = jnp.concatenate([jnp.full((PRE,), -1, jnp.int32), doc_id[0]])[:, None]
    codes_k = jnp.concatenate(
        [jnp.full((PRE,), -1, jnp.int32), jnp.where(live[0], doc_id[0], -2)]
    )[None, :]

    def own_columns(vector, width):
        return lax.dynamic_slice_in_dim(vector, place * width, width, 1)

    shift = jnp.concatenate(
        [own_columns(qb, cols), jnp.zeros((1, cols), F32), own_columns(vb, cols)], axis=1
    )
    factor = jnp.concatenate([jnp.full((1, cols), scale, F32), jnp.ones((1, 2 * cols), F32)], axis=1)
    (w_qkv, w_out, w_up, w_down, h1, df, h2, qkv, mixed, stats, attn, acted, slope, down_grad) = forward_pass(
        seq_count,
        pre_part,
        later_part,
        own_qkv,
        own_out,
        section(up_weight, 0, ff_cols),
        section(down_weight, 0, ff_cols),
        prefix_in[0],
        later_in[0],
        prefix_cot[0],
        later_cot[0],
        active,
        gain1,
        bias1,
        ob,
        gain2,
        bias2,
        shift,
        factor,
        own_columns(full_up_bias, ff_cols),
        codes_q,
        codes_k,
    )

    rows_in = (prefix_in[0], later_in[0], prefix_cot[0], later_cot[0], active)
    near_down, wide_down, up_grad, dattn, middle_grad, sums2, up_sums = feed_back(
        seq_count,
        pre_part,
        later_part,
        w_down,
        w_up,
        df,
        h2,
        slope,
        attn,
        down_grad,
        *rows_in,
        gain2,
    )
    (fin_down, fin_up, fin_qkv, fin_out, *_, prefix_out, later_out, prefix_grad, later_grad, sums1, qkv_sums) = attend_back(
        seq_count,
        pre_part,
        later_part,
        w_qkv,
        w_out,
        w_down,
        h1,
        qkv,
        stats,
        mixed,
        acted,
        dattn,
        middle_grad,
        attn,
        up_grad,
        down_grad,
        near_down,
        wide_down,
        *rows_in,
        gain1,
        db,
        codes_q,
        codes_k,
    )

    def shared(blocks):
        rows = blocks.shape[0] // parts
        return absolute_pre([blocks[i * rows : (i + 1) * rows] for i in range(parts)], place)

    down_full = jnp.concatenate(shared(fin_down), axis=1).astype(F32)
    up_full = jnp.concatenate(shared(fin_up), axis=1).astype(F32)
    out_own = lax.ppermute(fin_out, ("pre", "seq"), [(b, a) for a, b in shuffle])
    out_full = jnp.concatenate(absolute_pre(gather_pre(out_own), place), axis=0).astype(F32)
    qkv_blocks = shared(fin_qkv)
    qkv_full = jnp.concatenate(
        [block[:, i * cols : (i + 1) * cols] for i in range(3) for block in qkv_blocks], axis=1
    ).astype(F32)

    def placed(vector, width):
        zeros = jnp.zeros((width * parts,), F32)
        return lax.dynamic_update_slice_in_dim(zeros, vector, place * width, 0)

    squares = jnp.stack([jnp.sum(sums1[2]), jnp.sum(sums1[3]), jnp.sum(sums1[4]), jnp.sum(active)])
    sums = [
        sums1[0],
        sums1[1],
        placed(qkv_sums[0, :cols], cols),
        placed(qkv_sums[0, 2 * cols :], cols),
        sums2[0],
        sums2[1],
        sums2[2],
        sums2[3],
        placed(up_sums[0], ff_cols),
        jnp.concatenate([squares, jnp.zeros((124,), F32)]),
    ]
    flat = sum_all(jnp.concatenate(sums).reshape(-1, 128)).reshape(-1)
    totals = [flat[i * D : (i + 1) * D] for i in range(8)]
    total_ub = flat[8 * D : 8 * D + FF]
    total_squares = flat[8 * D + FF : 8 * D + FF + 4]

    def own_share(vector):
        width = vector.shape[0] // seq_count
        return lax.dynamic_slice_in_dim(vector, seq_place * width, width, 0)

    residual_rms = jnp.sqrt(total_squares[:3] / (total_squares[3] * D))
    return (
        prefix_out[None],
        later_out[None],
        prefix_grad[None],
        later_grad[None],
        own_share(totals[0]),
        own_share(totals[1]),
        qkv_full,
        own_share(totals[2]),
        own_share(totals[3]),
        out_full,
        own_share(totals[4]),
        own_share(totals[5]),
        own_share(totals[6]),
        up_full,
        own_share(total_ub),
        down_full,
        own_share(totals[7]),
        residual_rms,
    )


def solution(mesh):
    placed = (
        P("seq", "pre", None),
        P("seq", "pre", None),
        P("seq", None),
        P("seq", None),
        P("seq", None),
        P("seq"),
        P("seq"),
        P("seq", None),
        P("seq"),
        P("seq"),
        P("seq", None),
        P("seq"),
        P("seq"),
        P("seq"),
        P("seq", None),
        P("seq"),
        P("seq", None),
        P("seq"),
        P("seq", "pre", None),
        P("seq", "pre", None),
    )
    return jax.shard_map(
        on_device,
        mesh=mesh,
        in_specs=placed,
        out_specs=(
            P("seq", "pre", None),
            P("seq", "pre", None),
            P("seq", "pre", None),
            P("seq", "pre", None),
            P("seq"),
            P("seq"),
            P("seq", None),
            P("seq"),
            P("seq"),
            P("seq", None),
            P("seq"),
            P("seq"),
            P("seq"),
            P("seq", None),
            P("seq"),
            P("seq", None),
            P("seq"),
            P(),
        ),
        check_vma=False,
    )
```

```python
import functools
import math

import jax
import jax.numpy as jnp
from jax import lax
from jax.experimental import pallas as pl
from jax.experimental.pallas import tpu as pltpu
from jax.sharding import PartitionSpec as P

D = 2048
HEADS = 32
HEAD_DIM = 64
FF = 8192
LAYER = 12
PRE = 512

EPS = 1e-05
NEG = -1e30
BF = jnp.bfloat16
F32 = jnp.float32
TILE = 256


def layer_norm_parts(values, gain, bias):
    mean = jnp.mean(values, axis=-1, keepdims=True)
    centred = values - mean
    variance = jnp.mean(centred * centred, axis=-1, keepdims=True)
    scaling = lax.rsqrt(variance + EPS)
    normed = centred * scaling
    return (normed * gain + bias, normed, scaling)


def norm_back(grad, normed, scaling, gain):
    scaled = grad * gain
    inner = jnp.mean(scaled, axis=-1, keepdims=True)
    cross = jnp.mean(scaled * normed, axis=-1, keepdims=True)
    return scaling * (scaled - inner - normed * cross)


def token_tables(doc_lengths, doc_exit, token_skip):
    order = jnp.arange(doc_lengths.shape[-1], dtype=jnp.int32)
    earlier = order[None, :] < order[:, None]
    starts = jnp.sum(
        jnp.where(earlier, doc_lengths[..., None, :], 0), axis=-1, dtype=jnp.int32
    )
    places = jnp.arange(token_skip.shape[-1], dtype=jnp.int32)
    doc_id = (
        jnp.sum(
            (places[:, None] >= starts[..., None, :]).astype(jnp.int32), axis=-1, dtype=jnp.int32
        )
        - 1
    )
    live_doc = doc_exit > LAYER
    live = jnp.any((doc_id[..., None] == order) & live_doc[..., None, :], axis=-1) & (
        token_skip == 0
    )
    return (doc_id, live)


def dot_nt(a, b):
    return lax.dot_general(a, b, (((1,), (1,)), ((), ())), preferred_element_type=F32)


def dot_nn(a, b):
    return lax.dot_general(a, b, (((1,), (0,)), ((), ())), preferred_element_type=F32)


def dot_tn(a, b):
    return lax.dot_general(a, b, (((0,), (0,)), ((), ())), preferred_element_type=F32)


def masked_scores(block, scores, tile, codes_q, codes_k):
    rows = lax.broadcasted_iota(jnp.int32, (TILE, TILE), 0)
    cols = lax.broadcasted_iota(jnp.int32, (TILE, TILE), 1)
    allowed = None
    if tile == block:
        allowed = cols <= rows
    if tile * TILE >= PRE:
        same = (
            codes_q[block * TILE : (block + 1) * TILE, :]
            == codes_k[:, tile * TILE : (tile + 1) * TILE]
        )
        allowed = same if allowed is None else allowed & same
    if allowed is None:
        return scores
    return jnp.where(allowed, scores, NEG)


def xor(value, mask):
    bit = 1
    while bit <= mask:
        if mask & bit:
            value = value + bit * (1 - 2 * lax.rem(lax.div(value, jnp.int32(bit)), jnp.int32(2)))
        bit *= 2
    return value


def remote(src, dst, send_sem, recv_sem, **target):
    return pltpu.make_async_remote_copy(
        src_ref=src,
        dst_ref=dst,
        send_sem=send_sem,
        recv_sem=recv_sem,
        device_id=target,
        device_id_type=pl.DeviceIdType.MESH,
    )


def greet(masks, relay=None):
    barrier = pltpu.get_barrier_semaphore()
    seq = lax.axis_index("seq")
    pre = lax.axis_index("pre")

    def signal(**target):
        pl.semaphore_signal(
            barrier, inc=1, device_id=target, device_id_type=pl.DeviceIdType.MESH
        )

    for mask in masks:
        signal(seq=xor(seq, mask))
    for mask in (1, 2):
        signal(pre=xor(pre, mask))
    count = len(masks) + 2
    if relay is not None:

        @pl.when(relay.moves)
        def _():
            signal(seq=relay.there[0], pre=relay.there[1])
            signal(seq=relay.back[0], pre=relay.back[1])

        count = count + 2 * relay.moves.astype(jnp.int32)
    pl.semaphore_wait(barrier, count)


class Relay:
    def __init__(self, size, send_sem, recv_sem, local_sem):
        seq, pre = lax.axis_index("seq"), lax.axis_index("pre")
        held = seq * 4 + pre
        used = pre * size + seq
        self.there = (lax.rem(held, size), lax.div(held, size))
        self.back = (lax.div(used, 4), lax.rem(used, 4))
        self.moves = held != used
        self.sems = (send_sem, recv_sem, local_sem)

    def copies(self, src, dst, target):
        send_sem, recv_sem, local_sem = self.sems
        return (
            remote(src, dst, send_sem, recv_sem, seq=target[0], pre=target[1]),
            pltpu.make_async_copy(src, dst, local_sem),
        )

    def begin(self, src, dst, target):
        away, here = self.copies(src, dst, target)
        pl.when(self.moves)(away.start)
        pl.when(jnp.logical_not(self.moves))(here.start)

    def finish(self, src, dst, target):
        away, here = self.copies(src, dst, target)

        @pl.when(self.moves)
        def _():
            away.wait_recv()
            away.wait_send()

        pl.when(jnp.logical_not(self.moves))(here.wait)


def rows_of(index, count):
    return pl.ds(pl.multiple_of(index * count, count), count)


def far_line(lines, line, turn):
    low = lines - 1 - turn
    low = low - (low <= line).astype(jnp.int32)
    high = turn + (turn >= line).astype(jnp.int32)
    return jnp.where(line < lines // 2, low, high)


def early_rows(rows):
    return (rows * 3 + 128) // 256 * 16


class Copies:
    def __init__(self):
        self.items = []

    def start(self, copy, when=None):
        if when is None:
            copy.start()
        else:
            pl.when(when)(copy.start)
        self.items.append((copy, when))

    def drain(self):
        for copy, when in self.items:
            if when is None:
                copy.wait_send()
            else:
                pl.when(when)(copy.wait_send)


class Gather:
    def __init__(self, own, land, rows, send_sem, recv_sem, local_sem, size):
        self.own, self.land, self.rows = own, land, rows
        self.early = early_rows(rows)
        self.send_sem, self.recv_sem, self.local_sem = send_sem, recv_sem, local_sem
        self.seq = lax.axis_index("seq")
        self.lines = size // 2
        self.line = lax.div(self.seq, jnp.int32(2))
        self.twin = xor(self.seq, 1)
        self.sent = Copies()
        self.local = None

    def view(self, place, kind):
        first = {0: 0, 1: self.rows - self.early, 2: 0, 3: self.rows - self.early}[kind]
        count = {0: self.rows, 1: self.early, 2: self.rows - self.early, 3: self.early}[kind]
        return self.land.at[pl.ds(pl.multiple_of(place * self.rows + first, 16), count), :]

    def copy(self, place, kind, send, recv, to, own=False):
        there = self.view(place, kind)
        src = there
        if own:
            first = self.rows - self.early if kind in (1, 3) else 0
            count = there.shape[0]
            src = self.own.at[first : first + count, :]
        return remote(
            src, there, self.send_sem.at[kind, send], self.recv_sem.at[kind, recv], seq=to
        )

    def beside(self, up):
        return (self.line < self.lines - 1, self.seq + 2) if up else (self.line > 0, self.seq - 2)

    def begin(self):
        if self.early:
            self.sent.start(self.copy(self.seq, 3, 0, 0, self.twin, True))
        for up in (True, False):
            there, to = self.beside(up)
            spare = self.lines + (0 if up else 1)
            self.sent.start(self.copy(self.seq, 0, spare, self.line, to, True), there)
        self.sent.start(self.copy(self.seq, 2, self.line, self.line, self.twin, True))
        self.local = pltpu.make_async_copy(self.own, self.view(self.seq, 0), self.local_sem)
        self.local.start()

    def rest(self):
        if not self.early:
            return
        self.copy(self.twin, 3, 0, 0, self.twin).wait_recv()
        for up in (True, False):
            there, to = self.beside(up)
            spare = self.lines + (0 if up else 1)
            self.sent.start(self.copy(self.twin, 1, spare, self.line, to), there)

    def event(self, turn):
        line = far_line(self.lines, self.line, jnp.int32(self.lines - 2 - turn))
        step = jnp.where(line < self.line, 2, -2)
        after = jnp.where(line < self.line, self.line < self.lines - 1, self.line > 0)
        place = line * 2 + lax.rem(self.seq, jnp.int32(2))
        other = xor(place, 1)
        to = jnp.clip(self.seq + step, 0, 2 * self.lines - 1)
        self.copy(place, 0, line, line, self.twin).wait_recv()
        self.sent.start(self.copy(place, 0, line, line, to), after)
        self.sent.start(self.copy(place, 2, line, line, self.twin))
        if self.early:
            self.copy(other, 1, line, line, self.twin).wait_recv()
            self.sent.start(self.copy(other, 1, line, line, to), after)

    def finish(self):
        self.local.wait()
        for line in range(self.lines):
            self.copy(line * 2, 2, line, line, self.twin).wait_recv()

    def drain(self):
        self.sent.drain()


class Spread:
    def __init__(self, own, land, rows, send_sem, recv_sem, local_sem):
        self.own, self.land, self.rows = own, land, rows
        self.send_sem, self.recv_sem, self.local_sem = send_sem, recv_sem, local_sem
        self.pre = lax.axis_index("pre")
        self.sent = []

    def slot(self, index):
        return self.land.at[index * self.rows : (index + 1) * self.rows, :]

    def copy(self, src, slot, mask):
        return remote(
            src, self.slot(slot), self.send_sem.at[slot], self.recv_sem.at[slot], pre=xor(self.pre, mask)
        )

    def begin(self):
        for mask in (2, 1):
            copy = self.copy(self.own, mask, mask)
            copy.start()
            self.sent.append(copy)
        self.local = pltpu.make_async_copy(self.own, self.slot(0), self.local_sem)
        self.local.start()

    def forward(self):
        self.copy(self.own, 2, 2).wait_recv()
        copy = self.copy(self.slot(2), 3, 1)
        copy.start()
        self.sent.append(copy)

    def finish_near(self):
        self.local.wait()
        self.copy(self.own, 1, 1).wait_recv()

    def finish_far(self):
        self.copy(self.own, 3, 1).wait_recv()

    def finish(self):
        self.finish_near()
        self.finish_far()

    def drain(self):
        for copy in self.sent:
            copy.wait_send()


def local_copies(pairs, sem):
    copies = [pltpu.make_async_copy(src, dst, sem.at[i]) for i, (src, dst) in enumerate(pairs)]
    for copy in copies:
        copy.start()
    for copy in copies:
        copy.wait()


def wide_masks(size):
    masks = list(range(2, size, 2))
    return sorted(masks, key=lambda m: (m != 2, -m))


def head_lanes(value, head):
    lane = lax.broadcasted_iota(jnp.int32, value.shape, 1)
    inside = (lane < HEAD_DIM) if head == 0 else (lane >= HEAD_DIM)
    return jnp.where(inside, value, jnp.zeros_like(value))


def join_heads(first, second):
    lane = lax.broadcasted_iota(jnp.int32, (first.shape[0], 2 * HEAD_DIM), 1)
    return jnp.where(lane < HEAD_DIM, first, second)


def attend_pair(pair, cols, qkv, codes_q, codes_k, mixed, stats):
    lanes = [pl.ds(pl.multiple_of(third * cols + pair * 128, 128), 128) for third in range(3)]
    blocks = qkv.shape[0] // TILE
    for block in range(blocks):
        rows = slice(block * TILE, (block + 1) * TILE)
        both = qkv[rows, lanes[0]]
        outs, levels = [], []
        for head in range(2):
            queries = head_lanes(both, head)
            scores = [
                masked_scores(
                    block,
                    dot_nt(queries, qkv[tile * TILE : (tile + 1) * TILE, lanes[1]]),
                    tile,
                    codes_q,
                    codes_k,
                )
                for tile in range(block + 1)
            ]
            top = functools.reduce(jnp.maximum, [jnp.max(x, axis=1, keepdims=True) for x in scores])
            powers = [jnp.exp(x - top) for x in scores]
            total = functools.reduce(jnp.add, [jnp.sum(e, axis=1, keepdims=True) for e in powers])
            share = 1.0 / total
            outs.append(
                functools.reduce(
                    jnp.add,
                    [
                        dot_nn((e * share).astype(BF), qkv[tile * TILE : (tile + 1) * TILE, lanes[2]])
                        for tile, e in enumerate(powers)
                    ],
                )
            )
            levels.append(top + jnp.log(total))
        mixed[rows, lanes_of(pair)] = join_heads(outs[0], outs[1]).astype(BF)
        stats[rows, lanes_of(pair)] = join_heads(levels[0], levels[1])


def lanes_of(pair):
    return pl.ds(pl.multiple_of(pair * 128, 128), 128)


def forward_kernel(
    sizes,
    small,
    qkv_weight,
    out_weight,
    up_weight,
    down_weight,
    prefix_in,
    later_in,
    prefix_cot,
    later_cot,
    active_ref,
    codes_q,
    codes_k,
    w_qkv,
    w_out,
    w_up,
    w_down,
    h1,
    df,
    h2,
    qkv,
    mixed,
    stats,
    attn,
    acted,
    slope,
    down_grad,
    vectors,
    wbuf,
    lhs,
    qkv_v,
    mixed_v,
    stats_v,
    x_v,
    cot_v,
    h1_v,
    df_v,
    h2_v,
    terms_v,
    near_v,
    pass_v,
    far_v,
    attn_v,
    acted_v,
    slope_v,
    grad_v,
    own_qkv,
    own_up,
    own_down,
    own_out,
    small_v,
    slope_bias,
    gather_send,
    gather_recv,
    small_send,
    small_recv,
    spread_send,
    spread_recv,
    sum_send,
    sum_recv,
    relay_sem,
    local_sem,
):
    seq_size, pre_part, later_part = sizes
    part = pre_part + later_part
    cols = qkv_weight.shape[1] // 12
    ff_cols = up_weight.shape[1] // 4
    own_d = D // seq_size
    wide = wide_masks(seq_size)
    pre = lax.axis_index("pre")
    seq = lax.axis_index("seq")
    near_id = {"pre": xor(pre, 1)}
    far_id = {"pre": xor(pre, 2)}

    def gather(i, own, land):
        sems = (gather_send.at[i], gather_recv.at[i], local_sem.at[i])
        return Gather(own, land, own.shape[0], *sems, seq_size)

    def own_section(weight, first, columns):
        return weight.at[:, pl.ds(pl.multiple_of(first + pre * columns, columns), columns)]

    get_qkv = gather(0, own_qkv, w_qkv)
    get_out = gather(1, own_out, w_out)
    get_up = gather(2, own_up, w_up)
    get_down = gather(3, own_down, w_down)
    get_h1 = Spread(h1_v, h1, part, spread_send.at[0], spread_recv.at[0], local_sem.at[4])
    get_df = Spread(df_v, df, part, spread_send.at[1], spread_recv.at[1], local_sem.at[5])
    get_h2 = Spread(h2_v, h2, part, spread_send.at[2], spread_recv.at[2], local_sem.at[6])
    relay = Relay(seq_size, relay_sem.at[0], relay_sem.at[1], relay_sem.at[2])
    out_rows = own_d // 4
    relayed = (out_weight.at[rows_of(pre, out_rows), :], own_out, relay.there)

    cuts = [
        pltpu.make_async_copy(
            own_section(qkv_weight, i * D, cols),
            own_qkv.at[:, i * cols : (i + 1) * cols],
            local_sem.at[12 + i],
        )
        for i in range(3)
    ]
    late_cuts = [
        pltpu.make_async_copy(own_section(weight, 0, ff_cols), own, local_sem.at[15 + i])
        for i, (weight, own) in enumerate(((up_weight, own_up), (down_weight, own_down)))
    ]
    for cut in (*cuts, *late_cuts):
        cut.start()
    greet(range(1, seq_size), relay)
    small_copies = [
        remote(
            small, small_v.at[seq], small_send.at[mask], small_recv.at[mask], seq=xor(seq, mask)
        )
        for mask in range(1, seq_size)
    ]
    for copy in small_copies:
        copy.start()
    keep_small = pltpu.make_async_copy(small, small_v.at[seq], local_sem.at[7])
    keep_small.start()
    relay.begin(*relayed)
    for cut in cuts:
        cut.wait()
    get_qkv.begin()
    for cut in late_cuts:
        cut.wait()
    local_copies(
        [
            (prefix_in, x_v.at[:pre_part, :]),
            (later_in, x_v.at[pre_part:, :]),
            (prefix_cot, cot_v.at[:pre_part, :]),
            (later_cot, cot_v.at[pre_part:, :]),
        ],
        local_sem.at[8:12],
    )
    keep_small.wait()
    for copy in small_copies:
        copy.wait_recv()
    for member in range(seq_size):
        vectors[:, member * own_d : (member + 1) * own_d] = small_v[member]
    gain1, bias1, out_bias, gain2, bias2 = [vectors[i : i + 1, :] for i in (0, 1, 4, 5, 6)]
    own_lanes = pl.ds(pl.multiple_of(pre * cols, cols), cols)
    query_bias, value_bias = vectors[2:3, own_lanes], vectors[3:4, own_lanes]
    up_shares = vectors[8:12, own_lanes]
    up_bias = jnp.concatenate(
        [
            up_shares[k : k + 1, i * own_d : (i + 1) * own_d]
            for i in range(seq_size // 4)
            for k in range(4)
        ],
        axis=1,
    )
    chunk = 32

    @pl.loop(0, part // chunk)
    def _(i):
        rows = rows_of(i, chunk)
        value, _, _ = layer_norm_parts(x_v[rows, :].astype(F32), gain1, bias1)
        h1_v[rows, :] = value.astype(BF)

    get_h1.begin()

    @pl.loop(0, part // chunk)
    def _(i):
        rows = rows_of(i, chunk)
        df_v[rows, :] = (active_ref[rows, :] * cot_v[rows, :].astype(F32)).astype(BF)

    get_df.begin()
    slope_bias[...] = up_bias
    turns = range(seq_size // 2 - 1)
    get_qkv.rest()
    for turn in turns:
        get_qkv.event(turn)
        if turn == 0:
            relay.finish(*relayed)
            get_out.begin()
            get_h1.forward()
        if turn == turns[-2]:
            get_up.begin()
    get_h1.finish()
    get_df.forward()
    get_out.rest()
    load = pltpu.make_async_copy(h1, lhs, local_sem.at[12])
    load.start()
    get_qkv.finish()
    local_copies([(w_qkv, wbuf.at[:, : 3 * cols])], local_sem.at[8:9])
    load.wait()

    @pl.loop(0, 4)
    def _(r):
        member = lax.rem(r, 2) * (xor(pre, 1) - pre) + lax.div(r, 2) * (xor(pre, 2) - pre) + pre
        head_rows = rows_of(member, pre_part)
        tail_rows = pl.ds(pl.multiple_of(4 * pre_part + member * later_part, 64), later_part)

        for j in range(3):
            lanes = slice(j * cols, (j + 1) * cols)
            value = dot_nn(lhs[rows_of(r, part), :], wbuf[:, lanes])
            if j == 0:
                value = (value + query_bias) * (1.0 / math.sqrt(HEAD_DIM))
            if j == 2:
                value = value + value_bias
            value = value.astype(BF)
            qkv_v[head_rows, lanes] = value[:pre_part]
            qkv_v[tail_rows, lanes] = value[pre_part:]

    save_qkv = pltpu.make_async_copy(qkv_v, qkv, local_sem.at[13])
    save_qkv.start()
    for turn in turns:
        get_out.event(turn)
    get_up.rest()
    get_df.finish()
    pairs = cols // 128

    def attention(first, last):
        @pl.loop(first, last)
        def _(pair):
            attend_pair(pair, cols, qkv_v, codes_q[...], codes_k[...], mixed_v, stats_v)

    attention(0, pairs // 2)
    get_up.event(0)
    get_down.begin()
    attention(pairs // 2, pairs)
    save_stats = pltpu.make_async_copy(stats_v, stats, local_sem.at[14])
    save_stats.start()
    get_out.finish()
    local_copies([(w_out, wbuf.at[:cols, :])], local_sem.at[8:9])

    def position_rows(r):
        member = xor(pre, r) if r else pre
        return (
            rows_of(member, pre_part),
            pl.ds(pl.multiple_of(4 * pre_part + member * later_part, 64), later_part),
        )

    def out_term(r, store):
        head_rows, tail_rows = position_rows(r)

        @pl.loop(0, D // 512)
        def _(j):
            lanes = rows_of(j, 512)
            store(
                lanes,
                dot_nn(mixed_v[head_rows, :], wbuf[:cols, lanes]),
                dot_nn(mixed_v[tail_rows, :], wbuf[:cols, lanes]),
            )

    def keep_term(slot):
        def store(lanes, head, tail):
            terms_v[slot, :pre_part, lanes] = head.astype(BF)
            terms_v[slot, pre_part:, lanes] = tail.astype(BF)

        return store

    near = [
        remote(terms_v.at[i], near_v.at[i], sum_send.at[i], sum_recv.at[i], **near_id)
        for i in range(2)
    ]
    far = remote(pass_v, far_v, sum_send.at[2], sum_recv.at[2], **far_id)
    out_term(3, keep_term(0))
    near[0].start()
    out_term(1, keep_term(1))
    near[1].start()
    near[0].wait_recv()

    def pass_term(lanes, head, tail):
        pass_v[:pre_part, lanes] = (head + near_v[0, :pre_part, lanes].astype(F32)).astype(BF)
        pass_v[pre_part:, lanes] = (tail + near_v[0, pre_part:, lanes].astype(F32)).astype(BF)

    out_term(2, pass_term)
    far.start()
    near[1].wait_recv()

    def own_term(lanes, head, tail):
        bias = vectors[4:5, lanes]
        attn_v[:pre_part, lanes] = head + near_v[1, :pre_part, lanes].astype(F32) + bias
        attn_v[pre_part:, lanes] = tail + near_v[1, pre_part:, lanes].astype(F32) + bias

    out_term(0, own_term)
    moves = []
    for r in range(4):
        head_rows, tail_rows = position_rows(r)
        moves.append((mixed_v.at[head_rows, :], mixed.at[r * part : r * part + pre_part, :]))
        moves.append((mixed_v.at[tail_rows, :], mixed.at[r * part + pre_part : (r + 1) * part, :]))
    local_copies(moves, local_sem.at[16:24])
    for turn in turns[1:]:
        get_up.event(turn)
    far.wait_recv()

    @pl.loop(0, part // chunk)
    def _(i):
        rows = rows_of(i, chunk)
        branch = attn_v[rows, :] + far_v[rows, :].astype(F32)
        attn_v[rows, :] = branch
        value, _, _ = layer_norm_parts(x_v[rows, :].astype(F32) + branch, gain2, bias2)
        h2_v[rows, :] = value.astype(BF)

    get_h2.begin()
    save_attn = pltpu.make_async_copy(attn_v, attn, local_sem.at[15])
    save_attn.start()
    get_down.rest()
    get_up.finish()
    load = pltpu.make_async_copy(w_up, wbuf, local_sem.at[12])
    load.start()
    get_h2.finish_near()
    half = slice(0, 2 * part)
    local_copies([(h2.at[half, :], lhs.at[half, :])], local_sem.at[8:9])
    load.wait()

    def up_rows(r):
        rows = rows_of(r, part)

        @pl.loop(0, ff_cols // 512)
        def _(j):
            lanes = rows_of(j, 512)
            upper = dot_nn(lhs[rows, :], wbuf[:, lanes]) + slope_bias[:, lanes]
            cumulative = 0.5 * (1.0 + lax.erf(upper * (1.0 / math.sqrt(2.0))))
            density = jnp.exp(-0.5 * upper * upper) * (1.0 / math.sqrt(2.0 * math.pi))
            acted_v[rows, lanes] = (upper * cumulative).astype(BF)
            slope_v[rows, lanes] = (cumulative + upper * density).astype(BF)

    pl.loop(0, 2)(up_rows)
    get_h2.forward()
    get_down.event(0)
    get_h2.finish_far()
    half = slice(2 * part, 4 * part)
    local_copies([(h2.at[half, :], lhs.at[half, :])], local_sem.at[8:9])
    pl.loop(2, 4)(up_rows)

    saves = [
        pltpu.make_async_copy(acted_v, acted, local_sem.at[12]),
        pltpu.make_async_copy(slope_v, slope, local_sem.at[8]),
    ]
    for save in saves:
        save.start()
    for turn in turns[1:-1]:
        get_down.event(turn)
    local_copies([(df, lhs)], local_sem.at[9:10])

    @pl.loop(0, D // 256)
    def _(i):
        lanes = rows_of(i, 256)
        turned = lhs[:, lanes].T

        @pl.loop(0, ff_cols // 512)
        def _(j):
            grad_v[:, rows_of(j, 512)] = dot_nn(turned, acted_v[:, rows_of(j, 512)]).astype(BF)

        save = pltpu.make_async_copy(grad_v, down_grad.at[lanes, :], local_sem.at[9])
        save.start()
        save.wait()

    get_down.event(turns[-1])
    get_down.finish()
    for save in (*saves, save_qkv, save_stats, save_attn):
        save.wait()
    for item in (get_qkv, get_out, get_up, get_down, get_h1, get_df, get_h2):
        item.drain()
    for copy in (*near, far, *small_copies):
        copy.wait_send()


def forward_pass(seq_size, pre_part, later_part, *operands):
    part = pre_part + later_part
    length = 4 * part
    width = 3 * D // 4
    cols = width // 3
    ff_cols = FF // 4
    own_d = D // seq_size
    hbm = pl.BlockSpec(memory_space=pl.ANY)
    vmem = pl.BlockSpec(memory_space=pltpu.VMEM)

    def out(shape, kind=BF):
        return jax.ShapeDtypeStruct(shape, kind)

    outs = (
        out((D, width)),
        out((cols, D)),
        out((D, ff_cols)),
        out((D, ff_cols)),
        out((length, D)),
        out((length, D)),
        out((length, D)),
        out((length, width)),
        out((length, cols)),
        out((length, cols), F32),
        out((part, D), F32),
        out((length, ff_cols)),
        out((length, ff_cols)),
        out((D, ff_cols)),
        out((16, D), F32),
    )
    dma = pltpu.SemaphoreType.DMA
    return pl.pallas_call(
        functools.partial(forward_kernel, (seq_size, pre_part, later_part)),
        out_shape=outs,
        in_specs=[hbm] * 9 + [vmem] * (len(operands) - 9),
        out_specs=[hbm] * (len(outs) - 1) + [vmem],
        scratch_shapes=[
            pltpu.VMEM((D, max(ff_cols, width)), BF),
            pltpu.VMEM((length, D), BF),
            pltpu.VMEM((length, width), BF),
            pltpu.VMEM((length, cols), BF),
            pltpu.VMEM((length, cols), F32),
            pltpu.VMEM((part, D), BF),
            pltpu.VMEM((part, D), BF),
            pltpu.VMEM((part, D), BF),
            pltpu.VMEM((part, D), BF),
            pltpu.VMEM((part, D), BF),
            pltpu.VMEM((2, part, D), BF),
            pltpu.VMEM((2, part, D), BF),
            pltpu.VMEM((part, D), BF),
            pltpu.VMEM((part, D), BF),
            pltpu.VMEM((part, D), F32),
            pltpu.VMEM((length, ff_cols), BF),
            pltpu.VMEM((length, ff_cols), BF),
            pltpu.VMEM((256, ff_cols), BF),
            pltpu.VMEM((own_d, width), BF),
            pltpu.VMEM((own_d, ff_cols), BF),
            pltpu.VMEM((own_d, ff_cols), BF),
            pltpu.VMEM((own_d // 4, D), BF),
            pltpu.VMEM((seq_size, 16, own_d), F32),
            pltpu.VMEM((1, ff_cols), F32),
            dma((4, 4, seq_size // 2 + 2)),
            dma((4, 4, seq_size // 2)),
            dma((seq_size,)),
            dma((seq_size,)),
            dma((3, 4)),
            dma((3, 4)),
            dma((3,)),
            dma((3,)),
            dma((3,)),
            dma((24,)),
        ],
        compiler_params=pltpu.CompilerParams(
            collective_id=0, has_side_effects=True, vmem_limit_bytes=62 * 2**20
        ),
        cost_estimate=pl.CostEstimate(
            flops=2 * length * D * (width + cols + 2 * ff_cols),
            bytes_accessed=8 * D * ff_cols,
            transcendentals=length * ff_cols,
        ),
        name="forward_pass",
    )(*operands)


class Pool:
    def __init__(self, buffers, count):
        self.buffers, self.count = buffers, count
        self.pending = [None] * count
        self.turn = 0

    def take(self):
        index = self.turn % self.count
        self.turn += 1
        if self.pending[index] is not None:
            self.pending[index].wait_send()
            self.pending[index] = None
        return index

    def drain(self):
        for copy in self.pending:
            if copy is not None:
                copy.wait_send()


class Reduce:
    def __init__(self, grad, near, wide_land, rows, width, sems, work):
        self.grad, self.near, self.wide_land = grad, near, wide_land
        self.rows, self.width = rows, width
        self.near_send, self.near_recv, self.wide_send, self.wide_recv = sems
        self.left, self.right, self.total, self.out, self.pool, self.sem = work
        self.seq = lax.axis_index("seq")
        self.sent = []

    def block(self, mask):
        return self.grad.at[rows_of(xor(self.seq, mask), self.rows), :]

    def near_slot(self, mask):
        return self.near.at[mask // 2 * self.rows : (mask // 2 + 1) * self.rows, :]

    def wide_slot(self, mask):
        return self.wide_land.at[mask // 2 * self.rows : (mask // 2 + 1) * self.rows, :]

    def near_copy(self, mask):
        return remote(
            self.block(mask + 1),
            self.near_slot(mask),
            self.near_send.at[mask // 2],
            self.near_recv.at[mask // 2],
            seq=xor(self.seq, 1),
        )

    def wide_copy(self, src, mask):
        return remote(
            src,
            self.wide_slot(mask),
            self.wide_send.at[mask // 2],
            self.wide_recv.at[mask // 2],
            seq=xor(self.seq, mask),
        )

    def begin(self, *masks):
        for mask in masks:
            copy = self.near_copy(mask)
            copy.start()
            self.sent.append(copy)

    def views(self, index=None):
        left = self.left.at[: self.rows, : self.width]
        right = self.right.at[: self.rows, : self.width]
        return left, right

    def step(self, mask, early=None):
        left, right = self.views()
        own = pltpu.make_async_copy(self.block(mask), left, self.sem.at[0])
        own.start()
        if early is None:
            self.near_copy(mask).wait_recv()
            source = self.near_slot(mask)
        else:
            source = early.at[mask // 2 * self.rows : (mask // 2 + 1) * self.rows, :]
        other = pltpu.make_async_copy(source, right, self.sem.at[1])
        other.start()
        index = self.pool.take()
        own.wait()
        other.wait()
        chunk = min(32, self.rows)

        @pl.loop(0, self.rows // chunk)
        def _(i):
            at = (rows_of(i, chunk), slice(0, self.width))
            value = self.left[at].astype(F32) + self.right[at].astype(F32)
            self.out[index, at[0], at[1]] = value.astype(BF)

        copy = self.wide_copy(self.out.at[index, : self.rows, : self.width], mask)
        copy.start()
        self.pool.pending[index] = copy

    def settle(self, wide):
        self.near_copy(0).wait_recv()
        for mask in wide:
            self.wide_copy(self.out.at[0, : self.rows, : self.width], mask).wait_recv()

    def final(self, wide, result):
        left, right = self.views()
        chunk = min(32, self.rows)
        local_copies([(self.block(0), left), (self.near_slot(0), right)], self.sem)
        masks = list(wide)

        @pl.loop(0, self.rows // chunk)
        def _(i):
            at = (rows_of(i, chunk), slice(0, self.width))
            self.total[at] = self.left[at].astype(F32) + self.right[at].astype(F32)

        while masks:
            now, masks = masks[:2], masks[2:]
            views = [(self.wide_slot(mask), view) for mask, view in zip(now, (left, right))]
            local_copies(views, self.sem)
            refs = (self.left, self.right)[: len(now)]
            last = not masks

            @pl.loop(0, self.rows // chunk)
            def _(i):
                at = (rows_of(i, chunk), slice(0, self.width))
                value = self.total[at]
                for ref in refs:
                    value = value + ref[at].astype(F32)
                if last:
                    result[at] = value.astype(BF)
                else:
                    self.total[at] = value

    def drain(self):
        for copy in self.sent:
            copy.wait_send()


class Sum:
    def __init__(self, terms, near, passed, far, send_sem, recv_sem):
        pre = lax.axis_index("pre")
        near_id, far_id = {"pre": xor(pre, 1)}, {"pre": xor(pre, 2)}
        self.terms, self.near, self.passed = terms, near, passed
        self.near_copies = [
            remote(terms.at[i], near.at[i], send_sem.at[i], recv_sem.at[i], **near_id)
            for i in range(2)
        ]
        self.far_copy = remote(passed, far, send_sem.at[2], recv_sem.at[2], **far_id)

    def run(self, term, keep):
        def store_in(slot):
            def store(rows, lanes, value):
                self.terms[slot, rows, lanes] = value.astype(BF)

            return store

        term(3, store_in(0))
        self.near_copies[0].start()
        term(1, store_in(1))
        self.near_copies[1].start()
        self.near_copies[0].wait_recv()

        def store(rows, lanes, value):
            self.passed[rows, lanes] = (value + self.near[0, rows, lanes].astype(F32)).astype(BF)

        term(2, store)
        self.far_copy.start()
        self.near_copies[1].wait_recv()

        def store(rows, lanes, value):
            keep(rows, lanes, value + self.near[1, rows, lanes].astype(F32))

        term(0, store)

    def drain(self):
        for copy in (*self.near_copies, self.far_copy):
            copy.wait_send()


def columns_grad(left, right, rows, width, tile, save):
    @pl.loop(0, rows // 256)
    def _(i):
        turned = left[:, rows_of(i, 256)].T

        @pl.loop(0, width // 512)
        def _(j):
            tile[:, rows_of(j, 512)] = dot_nn(turned, right[:, rows_of(j, 512)]).astype(BF)

        copy = save(rows_of(i, 256))
        copy.start()
        copy.wait()


def add_rows(target, index, value):
    target[index : index + 1, : value.shape[1]] += jnp.sum(value, axis=0, keepdims=True)


def feed_back_kernel(
    sizes,
    w_down,
    w_up,
    acted,
    df,
    h2,
    slope,
    attn,
    down_grad,
    prefix_in,
    later_in,
    prefix_cot,
    later_cot,
    active_ref,
    vectors,
    near_down,
    wide_down,
    near_up,
    up_grad,
    dattn,
    middle_grad,
    prefix_out,
    later_out,
    sums,
    up_sums,
    wbuf,
    lhs,
    acted_v,
    slope_v,
    du_v,
    x_v,
    cot_v,
    attn_v,
    acc_v,
    ffn_v,
    dattn_v,
    terms_v,
    near_v,
    pass_v,
    far_v,
    ffn_near_v,
    ffn_far_v,
    left_v,
    right_v,
    total_v,
    out_v,
    grad_v,
    twin_send,
    twin_recv,
    wide_send,
    wide_recv,
    early_send,
    early_recv,
    spread_send,
    spread_recv,
    sum_send,
    sum_recv,
    local_sem,
):
    seq_size, pre_part, later_part = sizes
    part = pre_part + later_part
    length = 4 * part
    ff_cols = w_up.shape[1]
    gain2 = vectors[5:6, :]
    wide = wide_masks(seq_size)
    late = sorted(wide, key=lambda m: (m == 2, m))
    pool = Pool(out_v, 3)
    work = (left_v, right_v, total_v, out_v, pool, local_sem.at[0:2])
    put_down = Reduce(
        down_grad,
        near_down,
        wide_down,
        D // seq_size,
        ff_cols,
        (twin_send, twin_recv, wide_send, wide_recv),
        work,
    )
    put_up = Reduce(
        up_grad,
        near_up,
        None,
        D // seq_size,
        ff_cols,
        (early_send, early_recv, None, None),
        work,
    )
    get_dattn = Spread(dattn_v, dattn, part, spread_send, spread_recv, local_sem.at[2])
    sum_f = Sum(terms_v, ffn_near_v, pass_v, ffn_far_v, sum_send.at[0], sum_recv.at[0])
    sum_dh2 = Sum(terms_v, near_v, pass_v, far_v, sum_send.at[1], sum_recv.at[1])

    greet((1, *wide))
    put_down.begin(*late, 0)
    loads = [
        pltpu.make_async_copy(src, dst, local_sem.at[3 + i])
        for i, (src, dst) in enumerate(
            [
                (w_down, wbuf),
                (acted, acted_v),
                (df, lhs),
                (slope, slope_v),
                (prefix_in, x_v.at[:pre_part, :]),
                (later_in, x_v.at[pre_part:, :]),
                (prefix_cot, cot_v.at[:pre_part, :]),
                (later_cot, cot_v.at[pre_part:, :]),
                (attn, attn_v),
            ]
        )
    ]
    for load in loads:
        load.start()
    sums[...] = jnp.zeros_like(sums)
    up_sums[...] = jnp.zeros_like(up_sums)
    for load in loads[:2]:
        load.wait()

    def f_term(r, store):
        @pl.loop(0, D // 512)
        def _(j):
            store(
                slice(0, part),
                rows_of(j, 512),
                dot_nt(acted_v[r * part : (r + 1) * part, :], wbuf[rows_of(j, 512), :]),
            )

    def keep_f(rows, lanes, value):
        ffn_v[rows, lanes] = value

    sum_f.run(f_term, keep_f)
    for load in loads[2:]:
        load.wait()
    put_down.step(late[0])

    @pl.loop(0, 4)
    def _(r):
        rows = rows_of(r, part)

        @pl.loop(0, ff_cols // 512)
        def _(j):
            lanes = rows_of(j, 512)
            value = dot_nn(lhs[rows, :], wbuf[:, lanes])
            du_v[rows, lanes] = (value * slope_v[rows, lanes].astype(F32)).astype(BF)

    load = pltpu.make_async_copy(w_up, wbuf, local_sem.at[3])
    load.start()
    load_h2 = pltpu.make_async_copy(h2, lhs, local_sem.at[4])
    load_h2.start()
    for copy in sum_f.near_copies:
        copy.wait_send()
    for mask in late[1:-1]:
        put_down.step(mask)
    sum_f.far_copy.wait_send()
    load.wait()

    def dh2_term(r, store):
        @pl.loop(0, D // 512)
        def _(j):
            store(
                slice(0, part),
                rows_of(j, 512),
                dot_nt(du_v[r * part : (r + 1) * part, :], wbuf[rows_of(j, 512), :]),
            )

    def keep_dh2(rows, lanes, value):
        acc_v[rows, lanes] = value

    sum_dh2.run(dh2_term, keep_dh2)
    load_h2.wait()
    columns_grad(
        lhs,
        du_v,
        D,
        ff_cols,
        grad_v,
        lambda rows: pltpu.make_async_copy(grad_v, up_grad.at[rows, :], local_sem.at[3]),
    )
    put_up.begin(late[0])
    if len(late) > 1:
        put_down.step(late[-1])
    chunk = 32
    sum_f.far_copy.wait_recv()

    @pl.loop(0, part // chunk)
    def _(i):
        rows = rows_of(i, chunk)
        live = active_ref[rows, :]
        ffn = ffn_v[rows, :] + ffn_far_v[rows, :].astype(F32) + vectors[7:8, :]
        branch = attn_v[rows, :]
        result = x_v[rows, :].astype(F32) + live * (branch + ffn)
        add_rows(sums, 4, live * result * result)
        add_rows(sums, 5, live * branch * branch)
        add_rows(sums, 6, live * ffn * ffn)
        acted_v[rows, :] = result.astype(BF)

    saves = [
        pltpu.make_async_copy(acted_v.at[:pre_part, :], prefix_out, local_sem.at[4]),
        pltpu.make_async_copy(acted_v.at[pre_part:part, :], later_out, local_sem.at[5]),
    ]
    for save in saves:
        save.start()
    sum_dh2.far_copy.wait_recv()

    @pl.loop(0, part // chunk)
    def _(i):
        rows = rows_of(i, chunk)
        grad = acc_v[rows, :] + far_v[rows, :].astype(F32)
        middle = x_v[rows, :].astype(F32) + attn_v[rows, :]
        _, normed, scaling = layer_norm_parts(middle, gain2, 0.0)
        back = norm_back(grad, normed, scaling, gain2)
        acc_v[rows, :] = back
        direct = active_ref[rows, :] * cot_v[rows, :].astype(F32)
        value = (direct + back).astype(BF)
        dattn_v[rows, :] = value
        add_rows(sums, 0, value.astype(F32))
        add_rows(sums, 1, grad * normed)
        add_rows(sums, 2, grad)
        add_rows(sums, 3, direct)

    get_dattn.begin()
    saves.append(pltpu.make_async_copy(acc_v, middle_grad, local_sem.at[3]))
    saves[-1].start()

    @pl.loop(0, length // chunk)
    def _(i):
        add_rows(up_sums, 0, du_v[rows_of(i, chunk), :].astype(F32))

    get_dattn.forward()
    put_down.settle(wide)
    get_dattn.finish()
    for save in saves:
        save.wait()
    put_up.near_copy(late[0]).wait_recv()
    for item in (put_down, put_up, get_dattn, sum_dh2, pool):
        item.drain()


def feed_back(seq_size, pre_part, later_part, *operands):
    part = pre_part + later_part
    length = 4 * part
    w_up = operands[1]
    ff_cols = w_up.shape[1]
    own_d = D // seq_size
    hbm = pl.BlockSpec(memory_space=pl.ANY)
    vmem = pl.BlockSpec(memory_space=pltpu.VMEM)

    def out(shape, kind=BF):
        return jax.ShapeDtypeStruct(shape, kind)

    half = seq_size // 2
    outs = (
        out((half * own_d, ff_cols)),
        out((half * own_d, ff_cols)),
        out((half * own_d, ff_cols)),
        out((D, ff_cols)),
        out((length, D)),
        out((part, D), F32),
        out((pre_part, D)),
        out((later_part, D)),
        out((8, D), F32),
        out((8, ff_cols), F32),
    )
    dma = pltpu.SemaphoreType.DMA
    return pl.pallas_call(
        functools.partial(feed_back_kernel, (seq_size, pre_part, later_part)),
        out_shape=outs,
        in_specs=[hbm] * 12 + [vmem] * (len(operands) - 12),
        out_specs=[hbm] * 8 + [vmem] * 2,
        scratch_shapes=[
            pltpu.VMEM((D, ff_cols), BF),
            pltpu.VMEM((length, D), BF),
            pltpu.VMEM((length, ff_cols), BF),
            pltpu.VMEM((length, ff_cols), BF),
            pltpu.VMEM((length, ff_cols), BF),
            pltpu.VMEM((part, D), BF),
            pltpu.VMEM((part, D), BF),
            pltpu.VMEM((part, D), F32),
            pltpu.VMEM((part, D), F32),
            pltpu.VMEM((part, D), F32),
            pltpu.VMEM((part, D), BF),
            pltpu.VMEM((2, part, D), BF),
            pltpu.VMEM((2, part, D), BF),
            pltpu.VMEM((part, D), BF),
            pltpu.VMEM((part, D), BF),
            pltpu.VMEM((2, part, D), BF),
            pltpu.VMEM((part, D), BF),
            pltpu.VMEM((own_d, ff_cols), BF),
            pltpu.VMEM((own_d, ff_cols), BF),
            pltpu.VMEM((own_d, ff_cols), F32),
            pltpu.VMEM((3, own_d, ff_cols), BF),
            pltpu.VMEM((256, ff_cols), BF),
            dma((half,)),
            dma((half,)),
            dma((half,)),
            dma((half,)),
            dma((half,)),
            dma((half,)),
            dma((4,)),
            dma((4,)),
            dma((2, 3)),
            dma((2, 3)),
            dma((16,)),
        ],
        compiler_params=pltpu.CompilerParams(
            collective_id=1, has_side_effects=True, vmem_limit_bytes=62 * 2**20
        ),
        cost_estimate=pl.CostEstimate(
            flops=2 * length * D * 3 * ff_cols,
            bytes_accessed=8 * D * ff_cols,
            transcendentals=length,
        ),
        name="feed_back",
    )(*operands)


def attend_back_pair(pair, cols, qkv, do, stats, codes_q, codes_k, dq_all, dk_all, dv_all, dqkv):
    lanes = [pl.ds(pl.multiple_of(third * cols + pair * 128, 128), 128) for third in range(3)]
    dk_all[...] = jnp.zeros_like(dk_all)
    dv_all[...] = jnp.zeros_like(dv_all)
    blocks = qkv.shape[0] // TILE
    for block in range(blocks):
        rows = slice(block * TILE, (block + 1) * TILE)
        both_q = qkv[rows, lanes[0]]
        both_do = do[rows, lanes_of(pair)]
        both_levels = stats[rows, lanes_of(pair)]
        parts = []
        for head in range(2):
            queries = head_lanes(both_q, head)
            grads = head_lanes(both_do, head)
            level = both_levels[:, head * HEAD_DIM : head * HEAD_DIM + 1]
            probs = []
            dprobs = []
            for tile in range(block + 1):
                keys = slice(tile * TILE, (tile + 1) * TILE)
                scores = masked_scores(
                    block, dot_nt(queries, qkv[keys, lanes[1]]), tile, codes_q, codes_k
                )
                probs.append(jnp.exp(scores - level))
                dprobs.append(dot_nt(grads, qkv[keys, lanes[2]]))
            delta = functools.reduce(
                jnp.add, [jnp.sum(a * b, axis=1, keepdims=True) for a, b in zip(probs, dprobs)]
            )
            dq = None
            for tile in range(block + 1):
                keys = slice(tile * TILE, (tile + 1) * TILE)
                ds = (probs[tile] * (dprobs[tile] - delta)).astype(BF)
                part = dot_nn(ds, qkv[keys, lanes[1]])
                dq = part if dq is None else dq + part
                dk_all[keys, :] += dot_tn(ds, queries)
                dv_all[keys, :] += dot_tn(probs[tile].astype(BF), grads)
            parts.append(dq)
        dq_all[rows, :] = join_heads(*parts) * (1.0 / math.sqrt(HEAD_DIM))
    for lane, source in zip(lanes, (dq_all, dk_all, dv_all)):
        dqkv[:, lane] = source[...].astype(BF)


def attend_back_kernel(
    sizes,
    w_qkv,
    w_out,
    h1,
    qkv,
    stats,
    mixed,
    dattn,
    middle_grad,
    up_grad,
    down_grad,
    near_down,
    wide_down,
    early_up,
    prefix_in,
    later_in,
    prefix_cot,
    later_cot,
    active_ref,
    vectors,
    feed_sums,
    up_sums,
    codes_q,
    codes_k,
    fin_down,
    fin_up,
    fin_qkv,
    fin_out,
    near_up,
    wide_up,
    near_out,
    wide_out,
    near_qkv,
    wide_qkv,
    out_grad,
    qkv_grad,
    prefix_grad,
    later_grad,
    sums,
    wbuf,
    lhs,
    qkv_v,
    stats_v,
    do_v,
    mixed_v,
    dqkv_v,
    dq_v,
    dk_v,
    dv_v,
    x_v,
    cot_v,
    middle_v,
    acc_v,
    terms_v,
    near_v,
    pass_v,
    far_v,
    left_v,
    right_v,
    total_v,
    out_v,
    grad_v,
    res_down,
    res_up,
    res_qkv,
    res_out,
    moved_out,
    qkv_sums,
    sums_land,
    total_send,
    total_recv,
    relay_sem,
    twin_send,
    twin_recv,
    wide_send,
    wide_recv,
    spread_send,
    spread_recv,
    sum_send,
    sum_recv,
    local_sem,
):
    seq_size, pre_part, later_part = sizes
    part = pre_part + later_part
    length = 4 * part
    width = w_qkv.shape[1]
    cols = width // 3
    ff_cols = up_grad.shape[1]
    own_d = D // seq_size
    own_o = cols // seq_size
    pre = lax.axis_index("pre")
    wide = wide_masks(seq_size)
    late = sorted(wide, key=lambda m: (m == 2, m))
    pool = Pool(out_v, 3)
    work = (left_v, right_v, total_v, out_v, pool, local_sem.at[0:2])

    def reduce_of(i, grad, near, wide_land, rows, columns):
        sems = (twin_send.at[i], twin_recv.at[i], wide_send.at[i], wide_recv.at[i])
        return Reduce(grad, near, wide_land, rows, columns, sems, work)

    put_down = reduce_of(0, down_grad, near_down, wide_down, own_d, ff_cols)
    put_up = reduce_of(0, up_grad, near_up, wide_up, own_d, ff_cols)
    put_out = reduce_of(1, out_grad, near_out, wide_out, own_o, D)
    put_qkv = reduce_of(2, qkv_grad, near_qkv, wide_qkv, own_d, width)

    def spread_of(i, own, land):
        return Spread(own, land, own_d, spread_send.at[i], spread_recv.at[i], local_sem.at[2 + i])

    get_down = spread_of(0, res_down, fin_down)
    get_up = spread_of(1, res_up, fin_up)
    get_qkv = spread_of(2, res_qkv, fin_qkv)
    sum_dh1 = Sum(terms_v, near_v, pass_v, far_v, sum_send, sum_recv)
    chunk = 32

    relay = Relay(seq_size, relay_sem.at[0], relay_sem.at[1], relay_sem.at[2])
    relayed = (res_out, moved_out, relay.back)
    get_out = Spread(
        moved_out, fin_out, own_o, spread_send.at[3], spread_recv.at[3], local_sem.at[20]
    )
    bits = [1 << i for i in range(seq_size.bit_length() - 1)]
    greet(sorted({*wide, *bits}), relay)
    put_up.begin(*late[1:])
    stages = [
        remote(sums, sums_land.at[i], total_send.at[i], total_recv.at[i], **target)
        for i, target in enumerate(
            [{"pre": xor(pre, 1)}, {"pre": xor(pre, 2)}]
            + [{"seq": xor(lax.axis_index("seq"), bit)} for bit in bits]
        )
    ]

    def add_stage(i, onward=True):
        stages[i].wait_recv()
        stages[i].wait_send()
        sums[...] += sums_land[i]
        if onward:
            stages[i + 1].start()

    def load_all(first, *pairs):
        copies = [
            pltpu.make_async_copy(src, dst, local_sem.at[first + i])
            for i, (src, dst) in enumerate(pairs)
        ]
        for copy in copies:
            copy.start()
        return copies

    def wait_all(copies):
        for copy in copies:
            copy.wait()

    loads = load_all(5, (w_out, wbuf.at[:cols, :]), (dattn, lhs))
    more = load_all(
        8,
        (prefix_in, x_v.at[:pre_part, :]),
        (later_in, x_v.at[pre_part:, :]),
        (prefix_cot, cot_v.at[:pre_part, :]),
        (later_cot, cot_v.at[pre_part:, :]),
        (middle_grad, middle_v),
        (qkv, qkv_v),
        (stats, stats_v),
        (mixed, mixed_v),
    )
    sums[...] = jnp.zeros_like(sums)
    qkv_sums[...] = jnp.zeros_like(qkv_sums)
    put_up.step(late[0], early_up)
    put_down.final(wide, res_down)
    get_down.begin()
    def keep(rows, lanes, value):
        acc_v[rows, lanes] = value

    wait_all(loads)
    wait_all(more)

    def position_rows(r):
        member = lax.rem(r, 2) * (xor(pre, 1) - pre) + lax.div(r, 2) * (xor(pre, 2) - pre) + pre
        return (
            rows_of(member, pre_part),
            pl.ds(pl.multiple_of(4 * pre_part + member * later_part, 64), later_part),
        )

    @pl.loop(0, 4)
    def _(r):
        head_rows, tail_rows = position_rows(r)
        value = dot_nt(lhs[rows_of(r, part), :], wbuf[:cols, :]).astype(BF)
        do_v[head_rows, :] = value[:pre_part]
        do_v[tail_rows, :] = value[pre_part:]

    columns_grad(
        mixed_v,
        lhs,
        cols,
        D,
        grad_v,
        lambda rows: pltpu.make_async_copy(grad_v.at[:, :D], out_grad.at[rows, :], local_sem.at[5]),
    )
    put_out.begin(*late, 0)
    put_up.begin(0)
    loads = load_all(5, (w_qkv, wbuf.at[:, :width]))
    for r in range(4):
        head_rows, tail_rows = position_rows(jnp.int32(r))
        loads += load_all(
            8 + 2 * r,
            (h1.at[r * part : r * part + pre_part, :], lhs.at[head_rows, :]),
            (h1.at[r * part + pre_part : (r + 1) * part, :], lhs.at[tail_rows, :]),
        )
    pairs = cols // 128

    def attention(first, last):
        @pl.loop(first, last)
        def _(pair):
            attend_back_pair(
                pair,
                cols,
                qkv_v,
                do_v,
                stats_v,
                codes_q[...],
                codes_k[...],
                dq_v,
                dk_v,
                dv_v,
                dqkv_v,
            )

    for mask in late[1:-1]:
        put_up.step(mask)
    attention(0, pairs // 2)
    if len(late) > 1:
        put_up.step(late[-1])
    get_down.forward()
    attention(pairs // 2, pairs)
    for mask in late:
        put_out.step(mask)
    wait_all(loads)
    columns_grad(
        lhs,
        dqkv_v,
        D,
        width,
        grad_v,
        lambda rows: pltpu.make_async_copy(
            grad_v.at[:, :width], qkv_grad.at[rows, :], local_sem.at[5]
        ),
    )
    put_qkv.begin(*late, 0)
    get_down.finish()

    def dh1_term(r, store):
        head_rows, tail_rows = position_rows(jnp.int32(r))

        @pl.loop(0, D // 512)
        def _(j):
            weights = wbuf[rows_of(j, 512), :width]
            store(slice(0, pre_part), rows_of(j, 512), dot_nt(dqkv_v[head_rows, :], weights))
            store(slice(pre_part, part), rows_of(j, 512), dot_nt(dqkv_v[tail_rows, :], weights))

    sum_dh1.run(dh1_term, keep)

    @pl.loop(0, length // chunk)
    def _(i):
        add_rows(qkv_sums, 0, dqkv_v[rows_of(i, chunk), :].astype(F32))

    put_up.settle(wide)
    put_up.final(wide, res_up)
    get_up.begin()
    put_qkv.step(late[0])
    sum_dh1.far_copy.wait_recv()

    @pl.loop(0, part // chunk)
    def _(i):
        rows = rows_of(i, chunk)
        grad = acc_v[rows, :] + far_v[rows, :].astype(F32)
        _, normed, scaling = layer_norm_parts(x_v[rows, :].astype(F32), vectors[0:1, :], 0.0)
        back = norm_back(grad, normed, scaling, vectors[0:1, :])
        add_rows(sums, 0, grad * normed)
        add_rows(sums, 1, grad)
        value = cot_v[rows, :].astype(F32) + middle_v[rows, :] + back
        terms_rows = value.astype(BF)
        x_v[rows, :] = terms_rows

    saves = load_all(6, (x_v.at[:pre_part, :], prefix_grad), (x_v.at[pre_part:, :], later_grad))
    own_lanes = pl.ds(pl.multiple_of(pre * cols, cols), cols)
    sums[2:5, :] = feed_sums[4:7, :]
    sums[5:9, :] = feed_sums[:4, :]
    sums[9:10, own_lanes] = qkv_sums[0:1, :cols]
    sums[10:11, own_lanes] = qkv_sums[0:1, 2 * cols :]
    for k in range(4):
        sums[11 + k : 12 + k, own_lanes] = jnp.concatenate(
            [
                up_sums[0:1, (i * 4 + k) * own_d : (i * 4 + k + 1) * own_d]
                for i in range(seq_size // 4)
            ],
            axis=1,
        )
    sums[15:16, :] = jnp.zeros((1, D), F32) + jnp.sum(active_ref[...])
    stages[0].start()
    put_out.settle(wide)
    put_out.final(wide, res_out)
    relay.begin(*relayed)
    add_stage(0)
    wait_all(saves)
    for mask in late[1:]:
        put_qkv.step(mask)
    add_stage(1, False)
    get_up.forward()
    relay.finish(*relayed)
    get_out.begin()
    put_qkv.settle(wide)
    put_qkv.final(wide, res_qkv)
    get_qkv.begin()
    stages[2].start()
    get_out.forward()
    get_up.finish()
    for i in range(2, len(stages)):
        add_stage(i, i + 1 < len(stages))
    get_out.finish()
    get_qkv.forward()
    get_qkv.finish()
    for item in (put_up, put_out, put_qkv, get_down, get_up, get_out, get_qkv, sum_dh1, pool):
        item.drain()


def attend_back(seq_size, pre_part, later_part, *operands):
    part = pre_part + later_part
    length = 4 * part
    width = operands[0].shape[1]
    cols = width // 3
    ff_cols = FF // 4
    own_d = D // seq_size
    own_o = cols // seq_size
    half = seq_size // 2
    hbm = pl.BlockSpec(memory_space=pl.ANY)
    vmem = pl.BlockSpec(memory_space=pltpu.VMEM)

    def out(shape, kind=BF):
        return jax.ShapeDtypeStruct(shape, kind)

    outs = (
        out((4 * own_d, ff_cols)),
        out((4 * own_d, ff_cols)),
        out((4 * own_d, width)),
        out((4 * own_o, D)),
        out((half * own_d, ff_cols)),
        out((half * own_d, ff_cols)),
        out((half * own_o, D)),
        out((half * own_o, D)),
        out((half * own_d, width)),
        out((half * own_d, width)),
        out((cols, D)),
        out((D, width)),
        out((pre_part, D)),
        out((later_part, D)),
        out((16, D), F32),
    )
    most = max(ff_cols, D, width)
    stages = 1 + seq_size.bit_length()
    dma = pltpu.SemaphoreType.DMA
    return pl.pallas_call(
        functools.partial(attend_back_kernel, (seq_size, pre_part, later_part)),
        out_shape=outs,
        in_specs=[hbm] * 17 + [vmem] * (len(operands) - 17),
        out_specs=[hbm] * 14 + [vmem],
        scratch_shapes=[
            pltpu.VMEM((D, most), BF),
            pltpu.VMEM((length, D), BF),
            pltpu.VMEM((length, width), BF),
            pltpu.VMEM((length, cols), F32),
            pltpu.VMEM((length, cols), BF),
            pltpu.VMEM((length, cols), BF),
            pltpu.VMEM((length, width), BF),
            pltpu.VMEM((length, 128), F32),
            pltpu.VMEM((length, 128), F32),
            pltpu.VMEM((length, 128), F32),
            pltpu.VMEM((part, D), BF),
            pltpu.VMEM((part, D), BF),
            pltpu.VMEM((part, D), F32),
            pltpu.VMEM((part, D), F32),
            pltpu.VMEM((2, part, D), BF),
            pltpu.VMEM((2, part, D), BF),
            pltpu.VMEM((part, D), BF),
            pltpu.VMEM((part, D), BF),
            pltpu.VMEM((own_d, most), BF),
            pltpu.VMEM((own_d, most), BF),
            pltpu.VMEM((own_d, most), F32),
            pltpu.VMEM((3, own_d, most), BF),
            pltpu.VMEM((256, most), BF),
            pltpu.VMEM((own_d, ff_cols), BF),
            pltpu.VMEM((own_d, ff_cols), BF),
            pltpu.VMEM((own_d, width), BF),
            pltpu.VMEM((own_o, D), BF),
            pltpu.VMEM((own_o, D), BF),
            pltpu.VMEM((8, width), F32),
            pltpu.VMEM((stages, 16, D), F32),
            dma((stages,)),
            dma((stages,)),
            dma((3,)),
            dma((3, half)),
            dma((3, half)),
            dma((3, half)),
            dma((3, half)),
            dma((4, 4)),
            dma((4, 4)),
            dma((3,)),
            dma((3,)),
            dma((24,)),
        ],
        compiler_params=pltpu.CompilerParams(
            collective_id=2, has_side_effects=True, vmem_limit_bytes=63 * 2**20
        ),
        cost_estimate=pl.CostEstimate(
            flops=2 * length * D * (2 * width + ff_cols),
            bytes_accessed=8 * D * ff_cols,
            transcendentals=length * length,
        ),
        name="attend_back",
    )(*operands)


def absolute_pre(blocks, place):
    first = place % 2 == 0
    low = place < 2
    a = [jnp.where(first, blocks[0], blocks[1]), jnp.where(first, blocks[1], blocks[0])]
    b = [jnp.where(first, blocks[2], blocks[3]), jnp.where(first, blocks[3], blocks[2])]
    return [jnp.where(low, u, w) for u, w in zip(a, b)] + [jnp.where(low, w, u) for u, w in zip(a, b)]


def on_device(
    prefix_in,
    later_in,
    doc_lengths,
    doc_exit,
    token_skip,
    first_gain,
    first_bias,
    qkv_weight,
    query_bias,
    value_bias,
    out_weight,
    out_bias,
    second_gain,
    second_bias,
    up_weight,
    up_bias,
    down_weight,
    down_bias,
    prefix_cot,
    later_cot,
):
    pre_part = prefix_in.shape[1]
    later_part = later_in.shape[1]
    part = pre_part + later_part
    parts = lax.axis_size("pre")
    place = lax.axis_index("pre")
    seq_count = lax.axis_size("seq")
    seq_place = lax.axis_index("seq")
    own_d = D // seq_count
    cols = D // parts

    small = jnp.concatenate(
        [
            jnp.stack(
                [
                    first_gain,
                    first_bias,
                    query_bias,
                    value_bias,
                    out_bias,
                    second_gain,
                    second_bias,
                    down_bias,
                ]
            ),
            up_bias.reshape(4, own_d),
            jnp.zeros((4, own_d), BF),
        ]
    ).astype(F32)
    doc_id, live = token_tables(doc_lengths, doc_exit, token_skip)
    live_here = lax.dynamic_slice_in_dim(live[0], place * later_part, later_part, 0)
    active = jnp.concatenate([jnp.ones((pre_part,), F32), live_here.astype(F32)])[:, None]
    codes_q = jnp.concatenate([jnp.full((PRE,), -1, jnp.int32), doc_id[0]])[:, None]
    codes_k = jnp.concatenate(
        [jnp.full((PRE,), -1, jnp.int32), jnp.where(live[0], doc_id[0], -2)]
    )[None, :]

    (w_qkv, w_out, w_up, w_down, h1, df, h2, qkv, mixed, stats, attn, acted, slope, down_grad, vectors) = forward_pass(
        seq_count,
        pre_part,
        later_part,
        small,
        qkv_weight,
        out_weight,
        up_weight,
        down_weight,
        prefix_in[0],
        later_in[0],
        prefix_cot[0],
        later_cot[0],
        active,
        codes_q,
        codes_k,
    )

    rows_in = (prefix_in[0], later_in[0], prefix_cot[0], later_cot[0], active)
    (near_down, wide_down, early_up, up_grad, dattn, middle_grad, prefix_out, later_out, feed_sums, up_sums) = feed_back(
        seq_count,
        pre_part,
        later_part,
        w_down,
        w_up,
        acted,
        df,
        h2,
        slope,
        attn,
        down_grad,
        *rows_in,
        vectors,
    )
    (fin_down, fin_up, fin_qkv, fin_out, *_, prefix_grad, later_grad, sums) = attend_back(
        seq_count,
        pre_part,
        later_part,
        w_qkv,
        w_out,
        h1,
        qkv,
        stats,
        mixed,
        dattn,
        middle_grad,
        up_grad,
        down_grad,
        near_down,
        wide_down,
        early_up,
        *rows_in,
        vectors,
        feed_sums,
        up_sums,
        codes_q,
        codes_k,
    )

    def shared(blocks):
        rows = blocks.shape[0] // parts
        return absolute_pre([blocks[i * rows : (i + 1) * rows] for i in range(parts)], place)

    down_full = jnp.concatenate(shared(fin_down), axis=1).astype(F32)
    up_full = jnp.concatenate(shared(fin_up), axis=1).astype(F32)
    out_full = jnp.concatenate(shared(fin_out), axis=0).astype(F32)
    qkv_blocks = shared(fin_qkv)
    qkv_full = jnp.concatenate(
        [block[:, i * cols : (i + 1) * cols] for i in range(3) for block in qkv_blocks], axis=1
    ).astype(F32)

    mine = lax.dynamic_slice_in_dim(sums, seq_place * own_d, own_d, 1)
    residual_rms = jnp.sqrt(jnp.sum(sums[2:5], axis=1) / (sums[15, 0] * D))
    return (
        prefix_out[None],
        later_out[None],
        prefix_grad[None],
        later_grad[None],
        mine[0],
        mine[1],
        qkv_full,
        mine[9],
        mine[10],
        out_full,
        mine[5],
        mine[6],
        mine[7],
        up_full,
        mine[11:15].reshape(-1),
        down_full,
        mine[8],
        residual_rms,
    )


def solution(mesh):
    placed = (
        P("seq", "pre", None),
        P("seq", "pre", None),
        P("seq", None),
        P("seq", None),
        P("seq", None),
        P("seq"),
        P("seq"),
        P("seq", None),
        P("seq"),
        P("seq"),
        P("seq", None),
        P("seq"),
        P("seq"),
        P("seq"),
        P("seq", None),
        P("seq"),
        P("seq", None),
        P("seq"),
        P("seq", "pre", None),
        P("seq", "pre", None),
    )
    return jax.shard_map(
        on_device,
        mesh=mesh,
        in_specs=placed,
        out_specs=(
            P("seq", "pre", None),
            P("seq", "pre", None),
            P("seq", "pre", None),
            P("seq", "pre", None),
            P("seq"),
            P("seq"),
            P("seq", None),
            P("seq"),
            P("seq"),
            P("seq", None),
            P("seq"),
            P("seq"),
            P("seq"),
            P("seq", None),
            P("seq"),
            P("seq", None),
            P("seq"),
            P(),
        ),
        check_vma=False,
    )
```

```python
import functools
import math

import jax
import jax.numpy as jnp
from jax import lax
from jax.experimental import pallas as pl
from jax.experimental.pallas import tpu as pltpu
from jax.sharding import PartitionSpec as P

D = 2048
HEADS = 32
HEAD_DIM = 64
FF = 8192
LAYER = 12
PRE = 512

EPS = 1e-05
NEG = -1e30
BF = jnp.bfloat16
F32 = jnp.float32
TILE = 256


def layer_norm_parts(values, gain, bias):
    mean = jnp.mean(values, axis=-1, keepdims=True)
    centred = values - mean
    variance = jnp.mean(centred * centred, axis=-1, keepdims=True)
    scaling = lax.rsqrt(variance + EPS)
    normed = centred * scaling
    return (normed * gain + bias, normed, scaling)


def norm_back(grad, normed, scaling, gain):
    scaled = grad * gain
    inner = jnp.mean(scaled, axis=-1, keepdims=True)
    cross = jnp.mean(scaled * normed, axis=-1, keepdims=True)
    return scaling * (scaled - inner - normed * cross)


def token_tables(doc_lengths, doc_exit, token_skip):
    order = jnp.arange(doc_lengths.shape[-1], dtype=jnp.int32)
    earlier = order[None, :] < order[:, None]
    starts = jnp.sum(
        jnp.where(earlier, doc_lengths[..., None, :], 0), axis=-1, dtype=jnp.int32
    )
    places = jnp.arange(token_skip.shape[-1], dtype=jnp.int32)
    doc_id = (
        jnp.sum(
            (places[:, None] >= starts[..., None, :]).astype(jnp.int32), axis=-1, dtype=jnp.int32
        )
        - 1
    )
    live_doc = doc_exit > LAYER
    live = jnp.any((doc_id[..., None] == order) & live_doc[..., None, :], axis=-1) & (
        token_skip == 0
    )
    return (doc_id, live)


def dot_nt(a, b):
    return lax.dot_general(a, b, (((1,), (1,)), ((), ())), preferred_element_type=F32)


def dot_nn(a, b):
    return lax.dot_general(a, b, (((1,), (0,)), ((), ())), preferred_element_type=F32)


def dot_tn(a, b):
    return lax.dot_general(a, b, (((0,), (0,)), ((), ())), preferred_element_type=F32)


def masked_scores(block, scores, tile, codes_q, codes_k):
    rows = lax.broadcasted_iota(jnp.int32, (TILE, TILE), 0)
    cols = lax.broadcasted_iota(jnp.int32, (TILE, TILE), 1)
    allowed = None
    if tile == block:
        allowed = cols <= rows
    if tile * TILE >= PRE:
        same = (
            codes_q[block * TILE : (block + 1) * TILE, :]
            == codes_k[:, tile * TILE : (tile + 1) * TILE]
        )
        allowed = same if allowed is None else allowed & same
    if allowed is None:
        return scores
    return jnp.where(allowed, scores, NEG)


def xor(value, mask):
    bit = 1
    while bit <= mask:
        if mask & bit:
            value = value + bit * (1 - 2 * lax.rem(lax.div(value, jnp.int32(bit)), jnp.int32(2)))
        bit *= 2
    return value


def remote(src, dst, send_sem, recv_sem, **target):
    return pltpu.make_async_remote_copy(
        src_ref=src,
        dst_ref=dst,
        send_sem=send_sem,
        recv_sem=recv_sem,
        device_id=target,
        device_id_type=pl.DeviceIdType.MESH,
    )


def greet(masks, relay=None):
    barrier = pltpu.get_barrier_semaphore()
    seq = lax.axis_index("seq")
    pre = lax.axis_index("pre")

    def signal(**target):
        pl.semaphore_signal(
            barrier, inc=1, device_id=target, device_id_type=pl.DeviceIdType.MESH
        )

    for mask in masks:
        signal(seq=xor(seq, mask))
    for mask in (1, 2):
        signal(pre=xor(pre, mask))
    count = len(masks) + 2
    if relay is not None:

        @pl.when(relay.moves)
        def _():
            signal(seq=relay.there[0], pre=relay.there[1])
            signal(seq=relay.back[0], pre=relay.back[1])

        count = count + 2 * relay.moves.astype(jnp.int32)
    pl.semaphore_wait(barrier, count)


class Relay:
    def __init__(self, size, send_sem, recv_sem, local_sem):
        seq, pre = lax.axis_index("seq"), lax.axis_index("pre")
        held = seq * 4 + pre
        used = pre * size + seq
        self.there = (lax.rem(held, size), lax.div(held, size))
        self.back = (lax.div(used, 4), lax.rem(used, 4))
        self.moves = held != used
        self.sems = (send_sem, recv_sem, local_sem)

    def copies(self, src, dst, target):
        send_sem, recv_sem, local_sem = self.sems
        return (
            remote(src, dst, send_sem, recv_sem, seq=target[0], pre=target[1]),
            pltpu.make_async_copy(src, dst, local_sem),
        )

    def begin(self, src, dst, target):
        away, here = self.copies(src, dst, target)
        pl.when(self.moves)(away.start)
        pl.when(jnp.logical_not(self.moves))(here.start)

    def finish(self, src, dst, target):
        away, here = self.copies(src, dst, target)

        @pl.when(self.moves)
        def _():
            away.wait_recv()
            away.wait_send()

        pl.when(jnp.logical_not(self.moves))(here.wait)


def rows_of(index, count):
    return pl.ds(pl.multiple_of(index * count, count), count)


def far_line(lines, line, turn):
    low = lines - 1 - turn
    low = low - (low <= line).astype(jnp.int32)
    high = turn + (turn >= line).astype(jnp.int32)
    return jnp.where(line < lines // 2, low, high)


def early_rows(rows):
    return (rows * 3 + 128) // 256 * 16


class Copies:
    def __init__(self):
        self.items = []

    def start(self, copy, when=None):
        if when is None:
            copy.start()
        else:
            pl.when(when)(copy.start)
        self.items.append((copy, when))

    def drain(self):
        for copy, when in self.items:
            if when is None:
                copy.wait_send()
            else:
                pl.when(when)(copy.wait_send)


class Gather:
    def __init__(self, own, land, rows, send_sem, recv_sem, local_sem, size):
        self.own, self.land, self.rows = own, land, rows
        self.early = early_rows(rows)
        self.send_sem, self.recv_sem, self.local_sem = send_sem, recv_sem, local_sem
        self.seq = lax.axis_index("seq")
        self.lines = size // 2
        self.line = lax.div(self.seq, jnp.int32(2))
        self.twin = xor(self.seq, 1)
        self.sent = Copies()
        self.local = None

    def view(self, place, kind):
        first = {0: 0, 1: self.rows - self.early, 2: 0, 3: self.rows - self.early}[kind]
        count = {0: self.rows, 1: self.early, 2: self.rows - self.early, 3: self.early}[kind]
        return self.land.at[pl.ds(pl.multiple_of(place * self.rows + first, 16), count), :]

    def copy(self, place, kind, send, recv, to, own=False):
        there = self.view(place, kind)
        src = there
        if own:
            first = self.rows - self.early if kind in (1, 3) else 0
            count = there.shape[0]
            src = self.own.at[first : first + count, :]
        return remote(
            src, there, self.send_sem.at[kind, send], self.recv_sem.at[kind, recv], seq=to
        )

    def beside(self, up):
        return (self.line < self.lines - 1, self.seq + 2) if up else (self.line > 0, self.seq - 2)

    def begin(self):
        if self.early:
            self.sent.start(self.copy(self.seq, 3, 0, 0, self.twin, True))
        for up in (True, False):
            there, to = self.beside(up)
            spare = self.lines + (0 if up else 1)
            self.sent.start(self.copy(self.seq, 0, spare, self.line, to, True), there)
        self.sent.start(self.copy(self.seq, 2, self.line, self.line, self.twin, True))
        self.local = pltpu.make_async_copy(self.own, self.view(self.seq, 0), self.local_sem)
        self.local.start()

    def rest(self):
        if not self.early:
            return
        self.copy(self.twin, 3, 0, 0, self.twin).wait_recv()
        for up in (True, False):
            there, to = self.beside(up)
            spare = self.lines + (0 if up else 1)
            self.sent.start(self.copy(self.twin, 1, spare, self.line, to), there)

    def event(self, turn):
        line = far_line(self.lines, self.line, jnp.int32(self.lines - 2 - turn))
        step = jnp.where(line < self.line, 2, -2)
        after = jnp.where(line < self.line, self.line < self.lines - 1, self.line > 0)
        place = line * 2 + lax.rem(self.seq, jnp.int32(2))
        other = xor(place, 1)
        to = jnp.clip(self.seq + step, 0, 2 * self.lines - 1)
        self.copy(place, 0, line, line, self.twin).wait_recv()
        self.sent.start(self.copy(place, 0, line, line, to), after)
        self.sent.start(self.copy(place, 2, line, line, self.twin))
        if self.early:
            self.copy(other, 1, line, line, self.twin).wait_recv()
            self.sent.start(self.copy(other, 1, line, line, to), after)

    def finish(self):
        self.local.wait()
        for line in range(self.lines):
            self.copy(line * 2, 2, line, line, self.twin).wait_recv()

    def drain(self):
        self.sent.drain()


class Spread:
    def __init__(self, own, land, rows, send_sem, recv_sem, local_sem):
        self.own, self.land, self.rows = own, land, rows
        self.send_sem, self.recv_sem, self.local_sem = send_sem, recv_sem, local_sem
        self.pre = lax.axis_index("pre")
        self.sent = []

    def slot(self, index):
        return self.land.at[index * self.rows : (index + 1) * self.rows, :]

    def copy(self, src, slot, mask):
        return remote(
            src, self.slot(slot), self.send_sem.at[slot], self.recv_sem.at[slot], pre=xor(self.pre, mask)
        )

    def begin(self):
        for mask in (2, 1):
            copy = self.copy(self.own, mask, mask)
            copy.start()
            self.sent.append(copy)
        self.local = pltpu.make_async_copy(self.own, self.slot(0), self.local_sem)
        self.local.start()

    def forward(self):
        self.copy(self.own, 2, 2).wait_recv()
        copy = self.copy(self.slot(2), 3, 1)
        copy.start()
        self.sent.append(copy)

    def finish_near(self):
        self.local.wait()
        self.copy(self.own, 1, 1).wait_recv()

    def finish_far(self):
        self.copy(self.own, 3, 1).wait_recv()

    def finish(self):
        self.finish_near()
        self.finish_far()

    def drain(self):
        for copy in self.sent:
            copy.wait_send()


def local_copies(pairs, sem):
    copies = [pltpu.make_async_copy(src, dst, sem.at[i]) for i, (src, dst) in enumerate(pairs)]
    for copy in copies:
        copy.start()
    for copy in copies:
        copy.wait()


def wide_masks(size):
    masks = list(range(2, size, 2))
    return sorted(masks, key=lambda m: (m != 2, -m))


def head_lanes(value, head):
    lane = lax.broadcasted_iota(jnp.int32, value.shape, 1)
    inside = (lane < HEAD_DIM) if head == 0 else (lane >= HEAD_DIM)
    return jnp.where(inside, value, jnp.zeros_like(value))


def join_heads(first, second):
    lane = lax.broadcasted_iota(jnp.int32, (first.shape[0], 2 * HEAD_DIM), 1)
    return jnp.where(lane < HEAD_DIM, first, second)


def attend_pair(pair, cols, qkv, codes_q, codes_k, mixed, stats):
    lanes = [pl.ds(pl.multiple_of(third * cols + pair * 128, 128), 128) for third in range(3)]
    blocks = qkv.shape[0] // TILE
    for block in range(blocks):
        rows = slice(block * TILE, (block + 1) * TILE)
        both = qkv[rows, lanes[0]]
        outs, levels = [], []
        for head in range(2):
            queries = head_lanes(both, head)
            scores = [
                masked_scores(
                    block,
                    dot_nt(queries, qkv[tile * TILE : (tile + 1) * TILE, lanes[1]]),
                    tile,
                    codes_q,
                    codes_k,
                )
                for tile in range(block + 1)
            ]
            top = functools.reduce(jnp.maximum, [jnp.max(x, axis=1, keepdims=True) for x in scores])
            powers = [jnp.exp(x - top) for x in scores]
            total = functools.reduce(jnp.add, [jnp.sum(e, axis=1, keepdims=True) for e in powers])
            share = 1.0 / total
            outs.append(
                functools.reduce(
                    jnp.add,
                    [
                        dot_nn((e * share).astype(BF), qkv[tile * TILE : (tile + 1) * TILE, lanes[2]])
                        for tile, e in enumerate(powers)
                    ],
                )
            )
            levels.append(top + jnp.log(total))
        mixed[rows, lanes_of(pair)] = join_heads(outs[0], outs[1]).astype(BF)
        stats[rows, lanes_of(pair)] = join_heads(levels[0], levels[1])


def lanes_of(pair):
    return pl.ds(pl.multiple_of(pair * 128, 128), 128)


def forward_kernel(
    sizes,
    small,
    qkv_weight,
    out_weight,
    up_weight,
    down_weight,
    prefix_in,
    later_in,
    prefix_cot,
    later_cot,
    active_ref,
    codes_q,
    codes_k,
    w_qkv,
    w_out,
    w_up,
    w_down,
    h1,
    df,
    h2,
    qkv,
    mixed,
    stats,
    attn,
    acted,
    slope,
    down_grad,
    vectors,
    wbuf,
    lhs,
    qkv_v,
    mixed_v,
    stats_v,
    x_v,
    cot_v,
    h1_v,
    df_v,
    h2_v,
    terms_v,
    near_v,
    pass_v,
    far_v,
    attn_v,
    acted_v,
    slope_v,
    grad_v,
    own_qkv,
    own_up,
    own_down,
    own_out,
    small_v,
    slope_bias,
    gather_send,
    gather_recv,
    small_send,
    small_recv,
    spread_send,
    spread_recv,
    sum_send,
    sum_recv,
    relay_sem,
    local_sem,
):
    seq_size, pre_part, later_part = sizes
    part = pre_part + later_part
    cols = qkv_weight.shape[1] // 12
    ff_cols = up_weight.shape[1] // 4
    own_d = D // seq_size
    wide = wide_masks(seq_size)
    pre = lax.axis_index("pre")
    seq = lax.axis_index("seq")
    near_id = {"pre": xor(pre, 1)}
    far_id = {"pre": xor(pre, 2)}

    def gather(i, own, land):
        sems = (gather_send.at[i], gather_recv.at[i], local_sem.at[i])
        return Gather(own, land, own.shape[0], *sems, seq_size)

    def own_section(weight, first, columns):
        return weight.at[:, pl.ds(pl.multiple_of(first + pre * columns, columns), columns)]

    get_qkv = gather(0, own_qkv, w_qkv)
    get_out = gather(1, own_out, w_out)
    get_up = gather(2, own_up, w_up)
    get_down = gather(3, own_down, w_down)
    get_h1 = Spread(h1_v, h1, part, spread_send.at[0], spread_recv.at[0], local_sem.at[4])
    get_df = Spread(df_v, df, part, spread_send.at[1], spread_recv.at[1], local_sem.at[5])
    get_h2 = Spread(h2_v, h2, part, spread_send.at[2], spread_recv.at[2], local_sem.at[6])
    relay = Relay(seq_size, relay_sem.at[0], relay_sem.at[1], relay_sem.at[2])
    out_rows = own_d // 4
    relayed = (out_weight.at[rows_of(pre, out_rows), :], own_out, relay.there)

    cuts = [
        pltpu.make_async_copy(
            own_section(qkv_weight, i * D, cols),
            own_qkv.at[:, i * cols : (i + 1) * cols],
            local_sem.at[12 + i],
        )
        for i in range(3)
    ]
    late_cuts = [
        pltpu.make_async_copy(own_section(weight, 0, ff_cols), own, local_sem.at[15 + i])
        for i, (weight, own) in enumerate(((up_weight, own_up), (down_weight, own_down)))
    ]
    for cut in (*cuts, *late_cuts):
        cut.start()
    greet(range(1, seq_size), relay)
    small_copies = [
        remote(
            small, small_v.at[seq], small_send.at[mask], small_recv.at[mask], seq=xor(seq, mask)
        )
        for mask in range(1, seq_size)
    ]
    for copy in small_copies:
        copy.start()
    keep_small = pltpu.make_async_copy(small, small_v.at[seq], local_sem.at[7])
    keep_small.start()
    relay.begin(*relayed)
    for cut in cuts:
        cut.wait()
    get_qkv.begin()
    for cut in late_cuts:
        cut.wait()
    local_copies(
        [
            (prefix_in, x_v.at[:pre_part, :]),
            (later_in, x_v.at[pre_part:, :]),
            (prefix_cot, cot_v.at[:pre_part, :]),
            (later_cot, cot_v.at[pre_part:, :]),
        ],
        local_sem.at[8:12],
    )
    keep_small.wait()
    for copy in small_copies:
        copy.wait_recv()
    for member in range(seq_size):
        vectors[:, member * own_d : (member + 1) * own_d] = small_v[member]
    gain1, bias1, out_bias, gain2, bias2 = [vectors[i : i + 1, :] for i in (0, 1, 4, 5, 6)]
    own_lanes = pl.ds(pl.multiple_of(pre * cols, cols), cols)
    query_bias, value_bias = vectors[2:3, own_lanes], vectors[3:4, own_lanes]
    up_shares = vectors[8:12, own_lanes]
    up_bias = jnp.concatenate(
        [
            up_shares[k : k + 1, i * own_d : (i + 1) * own_d]
            for i in range(seq_size // 4)
            for k in range(4)
        ],
        axis=1,
    )
    chunk = 32

    @pl.loop(0, part // chunk)
    def _(i):
        rows = rows_of(i, chunk)
        value, _, _ = layer_norm_parts(x_v[rows, :].astype(F32), gain1, bias1)
        h1_v[rows, :] = value.astype(BF)

    get_h1.begin()

    @pl.loop(0, part // chunk)
    def _(i):
        rows = rows_of(i, chunk)
        df_v[rows, :] = (active_ref[rows, :] * cot_v[rows, :].astype(F32)).astype(BF)

    get_df.begin()
    slope_bias[...] = up_bias
    turns = range(seq_size // 2 - 1)
    get_qkv.rest()
    for turn in turns:
        get_qkv.event(turn)
        if turn == 0:
            relay.finish(*relayed)
            get_out.begin()
            get_h1.forward()
        if turn == turns[-2]:
            get_up.begin()
    get_h1.finish()
    get_df.forward()
    get_out.rest()
    load = pltpu.make_async_copy(h1, lhs, local_sem.at[12])
    load.start()
    get_qkv.finish()
    local_copies([(w_qkv, wbuf.at[:, : 3 * cols])], local_sem.at[8:9])
    load.wait()

    @pl.loop(0, 4)
    def _(r):
        member = lax.rem(r, 2) * (xor(pre, 1) - pre) + lax.div(r, 2) * (xor(pre, 2) - pre) + pre
        head_rows = rows_of(member, pre_part)
        tail_rows = pl.ds(pl.multiple_of(4 * pre_part + member * later_part, 64), later_part)

        for j in range(3):
            lanes = slice(j * cols, (j + 1) * cols)
            value = dot_nn(lhs[rows_of(r, part), :], wbuf[:, lanes])
            if j == 0:
                value = (value + query_bias) * (1.0 / math.sqrt(HEAD_DIM))
            if j == 2:
                value = value + value_bias
            value = value.astype(BF)
            qkv_v[head_rows, lanes] = value[:pre_part]
            qkv_v[tail_rows, lanes] = value[pre_part:]

    save_qkv = pltpu.make_async_copy(qkv_v, qkv, local_sem.at[13])
    save_qkv.start()
    for turn in turns:
        get_out.event(turn)
    get_up.rest()
    get_df.finish()
    pairs = cols // 128

    def attention(first, last):
        @pl.loop(first, last)
        def _(pair):
            attend_pair(pair, cols, qkv_v, codes_q[...], codes_k[...], mixed_v, stats_v)

    attention(0, pairs // 2)
    get_up.event(0)
    get_down.begin()
    attention(pairs // 2, pairs)
    save_stats = pltpu.make_async_copy(stats_v, stats, local_sem.at[14])
    save_stats.start()
    get_out.finish()
    local_copies([(w_out, wbuf.at[:cols, :])], local_sem.at[8:9])

    def position_rows(r):
        member = xor(pre, r) if r else pre
        return (
            rows_of(member, pre_part),
            pl.ds(pl.multiple_of(4 * pre_part + member * later_part, 64), later_part),
        )

    def out_term(r, store):
        head_rows, tail_rows = position_rows(r)

        @pl.loop(0, D // 512)
        def _(j):
            lanes = rows_of(j, 512)
            store(
                lanes,
                dot_nn(mixed_v[head_rows, :], wbuf[:cols, lanes]),
                dot_nn(mixed_v[tail_rows, :], wbuf[:cols, lanes]),
            )

    def keep_term(slot):
        def store(lanes, head, tail):
            terms_v[slot, :pre_part, lanes] = head.astype(BF)
            terms_v[slot, pre_part:, lanes] = tail.astype(BF)

        return store

    near = [
        remote(terms_v.at[i], near_v.at[i], sum_send.at[i], sum_recv.at[i], **near_id)
        for i in range(2)
    ]
    far = remote(pass_v, far_v, sum_send.at[2], sum_recv.at[2], **far_id)
    out_term(3, keep_term(0))
    near[0].start()
    out_term(1, keep_term(1))
    near[1].start()
    near[0].wait_recv()

    def pass_term(lanes, head, tail):
        pass_v[:pre_part, lanes] = (head + near_v[0, :pre_part, lanes].astype(F32)).astype(BF)
        pass_v[pre_part:, lanes] = (tail + near_v[0, pre_part:, lanes].astype(F32)).astype(BF)

    out_term(2, pass_term)
    far.start()
    near[1].wait_recv()

    def own_term(lanes, head, tail):
        bias = vectors[4:5, lanes]
        attn_v[:pre_part, lanes] = head + near_v[1, :pre_part, lanes].astype(F32) + bias
        attn_v[pre_part:, lanes] = tail + near_v[1, pre_part:, lanes].astype(F32) + bias

    out_term(0, own_term)
    moves = []
    for r in range(4):
        head_rows, tail_rows = position_rows(r)
        moves.append((mixed_v.at[head_rows, :], mixed.at[r * part : r * part + pre_part, :]))
        moves.append((mixed_v.at[tail_rows, :], mixed.at[r * part + pre_part : (r + 1) * part, :]))
    local_copies(moves, local_sem.at[16:24])
    for turn in turns[1:]:
        get_up.event(turn)
    far.wait_recv()

    @pl.loop(0, part // chunk)
    def _(i):
        rows = rows_of(i, chunk)
        branch = attn_v[rows, :] + far_v[rows, :].astype(F32)
        attn_v[rows, :] = branch
        value, _, _ = layer_norm_parts(x_v[rows, :].astype(F32) + branch, gain2, bias2)
        h2_v[rows, :] = value.astype(BF)

    get_h2.begin()
    save_attn = pltpu.make_async_copy(attn_v, attn, local_sem.at[15])
    save_attn.start()
    get_down.rest()
    get_up.finish()
    load = pltpu.make_async_copy(w_up, wbuf, local_sem.at[12])
    load.start()
    get_h2.finish_near()
    half = slice(0, 2 * part)
    local_copies([(h2.at[half, :], lhs.at[half, :])], local_sem.at[8:9])
    load.wait()

    def up_rows(r):
        rows = rows_of(r, part)

        @pl.loop(0, ff_cols // 512)
        def _(j):
            lanes = rows_of(j, 512)
            upper = dot_nn(lhs[rows, :], wbuf[:, lanes]) + slope_bias[:, lanes]
            cumulative = 0.5 * (1.0 + lax.erf(upper * (1.0 / math.sqrt(2.0))))
            density = jnp.exp(-0.5 * upper * upper) * (1.0 / math.sqrt(2.0 * math.pi))
            acted_v[rows, lanes] = (upper * cumulative).astype(BF)
            slope_v[rows, lanes] = (cumulative + upper * density).astype(BF)

    pl.loop(0, 2)(up_rows)
    get_h2.forward()
    get_down.event(0)
    get_h2.finish_far()
    half = slice(2 * part, 4 * part)
    local_copies([(h2.at[half, :], lhs.at[half, :])], local_sem.at[8:9])
    pl.loop(2, 4)(up_rows)

    saves = [
        pltpu.make_async_copy(acted_v, acted, local_sem.at[12]),
        pltpu.make_async_copy(slope_v, slope, local_sem.at[8]),
    ]
    for save in saves:
        save.start()
    for turn in turns[1:-1]:
        get_down.event(turn)
    local_copies([(df, lhs)], local_sem.at[9:10])

    @pl.loop(0, D // 256)
    def _(i):
        lanes = rows_of(i, 256)
        turned = lhs[:, lanes].T

        @pl.loop(0, ff_cols // 512)
        def _(j):
            grad_v[:, rows_of(j, 512)] = dot_nn(turned, acted_v[:, rows_of(j, 512)]).astype(BF)

        save = pltpu.make_async_copy(grad_v, down_grad.at[lanes, :], local_sem.at[9])
        save.start()
        save.wait()

    get_down.event(turns[-1])
    get_down.finish()
    for save in (*saves, save_qkv, save_stats, save_attn):
        save.wait()
    for item in (get_qkv, get_out, get_up, get_down, get_h1, get_df, get_h2):
        item.drain()
    for copy in (*near, far, *small_copies):
        copy.wait_send()


def forward_pass(seq_size, pre_part, later_part, *operands):
    part = pre_part + later_part
    length = 4 * part
    width = 3 * D // 4
    cols = width // 3
    ff_cols = FF // 4
    own_d = D // seq_size
    hbm = pl.BlockSpec(memory_space=pl.ANY)
    vmem = pl.BlockSpec(memory_space=pltpu.VMEM)

    def out(shape, kind=BF):
        return jax.ShapeDtypeStruct(shape, kind)

    outs = (
        out((D, width)),
        out((cols, D)),
        out((D, ff_cols)),
        out((D, ff_cols)),
        out((length, D)),
        out((length, D)),
        out((length, D)),
        out((length, width)),
        out((length, cols)),
        out((length, cols), F32),
        out((part, D), F32),
        out((length, ff_cols)),
        out((length, ff_cols)),
        out((D, ff_cols)),
        out((16, D), F32),
    )
    dma = pltpu.SemaphoreType.DMA
    return pl.pallas_call(
        functools.partial(forward_kernel, (seq_size, pre_part, later_part)),
        out_shape=outs,
        in_specs=[hbm] * 9 + [vmem] * (len(operands) - 9),
        out_specs=[hbm] * (len(outs) - 1) + [vmem],
        scratch_shapes=[
            pltpu.VMEM((D, max(ff_cols, width)), BF),
            pltpu.VMEM((length, D), BF),
            pltpu.VMEM((length, width), BF),
            pltpu.VMEM((length, cols), BF),
            pltpu.VMEM((length, cols), F32),
            pltpu.VMEM((part, D), BF),
            pltpu.VMEM((part, D), BF),
            pltpu.VMEM((part, D), BF),
            pltpu.VMEM((part, D), BF),
            pltpu.VMEM((part, D), BF),
            pltpu.VMEM((2, part, D), BF),
            pltpu.VMEM((2, part, D), BF),
            pltpu.VMEM((part, D), BF),
            pltpu.VMEM((part, D), BF),
            pltpu.VMEM((part, D), F32),
            pltpu.VMEM((length, ff_cols), BF),
            pltpu.VMEM((length, ff_cols), BF),
            pltpu.VMEM((256, ff_cols), BF),
            pltpu.VMEM((own_d, width), BF),
            pltpu.VMEM((own_d, ff_cols), BF),
            pltpu.VMEM((own_d, ff_cols), BF),
            pltpu.VMEM((own_d // 4, D), BF),
            pltpu.VMEM((seq_size, 16, own_d), F32),
            pltpu.VMEM((1, ff_cols), F32),
            dma((4, 4, seq_size // 2 + 2)),
            dma((4, 4, seq_size // 2)),
            dma((seq_size,)),
            dma((seq_size,)),
            dma((3, 4)),
            dma((3, 4)),
            dma((3,)),
            dma((3,)),
            dma((3,)),
            dma((24,)),
        ],
        compiler_params=pltpu.CompilerParams(
            collective_id=0, has_side_effects=True, vmem_limit_bytes=62 * 2**20
        ),
        cost_estimate=pl.CostEstimate(
            flops=2 * length * D * (width + cols + 2 * ff_cols),
            bytes_accessed=8 * D * ff_cols,
            transcendentals=length * ff_cols,
        ),
        name="forward_pass",
    )(*operands)


class Pool:
    def __init__(self, buffers, count):
        self.buffers, self.count = buffers, count
        self.pending = [Copies() for _ in range(count)]
        self.turn = 0

    def take(self):
        index = self.turn % self.count
        self.turn += 1
        self.pending[index].drain()
        self.pending[index] = Copies()
        return index

    def drain(self):
        for copies in self.pending:
            copies.drain()


class Reduce:
    def __init__(self, grad, near, chain, tail, rows, width, sems, work, size, split=False):
        self.grad, self.near, self.chain, self.tail = grad, near, chain, tail
        self.rows, self.width = rows, width
        self.early = early_rows(rows) if split else 0
        self.first = rows - self.early
        self.whole = rows + self.early
        self.near_send, self.near_recv, self.chain_send, self.chain_recv, self.tail_sem = sems
        self.left, self.right, self.third, self.fourth, self.out, self.pool, self.sem = work
        self.seq = lax.axis_index("seq")
        self.lines = size // 2
        self.line = lax.div(self.seq, jnp.int32(2))
        self.side = lax.rem(self.seq, jnp.int32(2))
        self.sent = Copies()

    def target(self, turn):
        if turn == self.lines - 1:
            return self.line
        return far_line(self.lines, self.line, jnp.int32(turn))

    def block(self, line, other, first, count):
        place = line * 2 + ((1 - self.side) if other else self.side)
        return self.grad.at[pl.ds(pl.multiple_of(place * self.rows + first, 16), count), :]

    def near_slot(self, line, near=None):
        near = self.near if near is None else near
        return near.at[pl.ds(pl.multiple_of(line * self.first, 16), self.first), :]

    def chain_slot(self, slot):
        return self.chain.at[pl.ds(pl.multiple_of(slot * self.whole, 16), self.whole), :]

    def near_copy(self, turn):
        line = self.target(turn)
        return remote(
            self.block(line, True, 0, self.first),
            self.near_slot(line),
            self.near_send.at[turn],
            self.near_recv.at[line],
            seq=xor(self.seq, 1),
        )

    def chain_copy(self, src, turn, slot, to):
        return remote(
            src, self.chain_slot(slot), self.chain_send.at[turn], self.chain_recv.at[slot], seq=to
        )

    def begin(self, *turns):
        for turn in turns:
            self.sent.start(self.near_copy(turn))

    def view(self, ref, first, count):
        return ref.at[first : first + count, : self.width]

    def load_own(self, line):
        copies = [
            pltpu.make_async_copy(
                self.block(line, False, 0, self.rows), self.view(self.left, 0, self.rows), self.sem.at[0]
            )
        ]
        if self.early:
            copies.append(
                pltpu.make_async_copy(
                    self.block(line, True, self.first, self.early),
                    self.view(self.left, self.rows, self.early),
                    self.sem.at[1],
                )
            )
        for copy in copies:
            copy.start()
        return copies

    def load(self, src, ref, count, sem):
        copy = pltpu.make_async_copy(src, self.view(ref, 0, count), self.sem.at[sem])
        copy.start()
        return copy

    def rows_loop(self, first, last, value, store):
        if first == last:
            return

        @pl.loop(first // 16, last // 16)
        def _(i):
            at = (rows_of(i, 16), slice(0, self.width))
            store(at, value(at))

    def step(self, turn, when=None, early=None):
        line = self.target(turn)
        up = line > self.line
        ahead = jnp.where(up, line - self.line, self.line - line)
        base = jnp.where(up, 0, self.lines - 1)
        more = jnp.where(up, self.line > 0, self.line < self.lines - 1)
        slot_in = jnp.minimum(base + ahead, 2 * (self.lines - 1) - 1)
        slot_out = base + ahead - 1
        to = jnp.clip(self.seq + jnp.where(up, 2, -2), 0, 2 * self.lines - 1)
        index = self.pool.take()
        out = self.out.at[index]
        leave = self.chain_copy(out.at[: self.whole, : self.width], turn, slot_out, to)

        def store(at, value):
            out[at] = value.astype(BF)

        def body():
            copies = self.load_own(line)
            if early is None:
                self.near_copy(turn).wait_recv()
            copies.append(self.load(self.near_slot(line, early), self.right, self.first, 2))

            def both(at):
                return self.left[at].astype(F32) + self.right[at].astype(F32)

            def own(at):
                return self.left[at].astype(F32)

            @pl.when(more)
            def _():
                self.chain_copy(out.at[: self.whole, : self.width], turn, slot_in, to).wait_recv()
                third = self.load(self.chain_slot(slot_in), self.third, self.whole, 3)
                for copy in (*copies, third):
                    copy.wait()
                self.rows_loop(
                    0, self.first, lambda at: both(at) + self.third[at].astype(F32), store
                )
                self.rows_loop(
                    self.first, self.whole, lambda at: own(at) + self.third[at].astype(F32), store
                )

            @pl.when(jnp.logical_not(more))
            def _():
                for copy in copies:
                    copy.wait()
                self.rows_loop(0, self.first, both, store)
                self.rows_loop(self.first, self.whole, own, store)

            leave.start()

        if when is None:
            body()
        else:
            pl.when(when)(body)
        self.pool.pending[index].items.append((leave, when))

    def sides(self):
        return ((self.line > 0, 0), (self.line < self.lines - 1, self.lines - 1))

    def settle(self):
        self.near_copy(self.lines - 1).wait_recv()
        for there, slot in self.sides():
            pl.when(there)(
                self.chain_copy(self.view(self.third, 0, self.whole), 0, slot, self.seq).wait_recv
            )

    def tail_copy(self, src):
        return remote(src, self.tail, self.tail_sem.at[0], self.tail_sem.at[1], seq=xor(self.seq, 1))

    def final(self, result):
        copies = self.load_own(self.line)
        copies.append(self.load(self.near_slot(self.line), self.right, self.first, 2))
        side = jnp.where(self.line > 0, 0, self.lines - 1)
        copies.append(self.load(self.chain_slot(side), self.third, self.whole, 3))
        mid = (self.line > 0) & (self.line < self.lines - 1)
        fourth = pltpu.make_async_copy(
            self.chain_slot(self.lines - 1), self.view(self.fourth, 0, self.whole), self.sem.at[4]
        )
        pl.when(mid)(fourth.start)
        index = self.pool.take()
        out = self.out.at[index]

        def put(at, value):
            result[at] = value.astype(BF)

        def put_tail(at, value):
            out[at] = value.astype(BF)

        def loops(refs):
            def sum_of(at):
                return functools.reduce(jnp.add, [ref[at].astype(F32) for ref in refs])

            self.rows_loop(0, self.first, lambda at: sum_of(at) + self.right[at].astype(F32), put)
            self.rows_loop(self.first, self.rows, sum_of, put)
            self.rows_loop(self.rows, self.whole, sum_of, put_tail)

        for copy in copies:
            copy.wait()

        @pl.when(mid)
        def _():
            fourth.wait()
            loops((self.left, self.third, self.fourth))

        pl.when(jnp.logical_not(mid))(lambda: loops((self.left, self.third)))
        if self.early:
            self.pool.pending[index].start(
                self.tail_copy(out.at[self.rows : self.whole, : self.width])
            )

    def last(self, result):
        if not self.early:
            return
        self.tail_copy(self.view(self.third, 0, self.early)).wait_recv()
        self.load(self.tail, self.third, self.early, 3).wait()

        @pl.loop(0, self.early // 16)
        def _(i):
            lanes = slice(0, self.width)
            rows = pl.ds(pl.multiple_of(self.first + i * 16, 16), 16)
            value = result[rows, lanes].astype(F32) + self.third[rows_of(i, 16), lanes].astype(F32)
            result[rows, lanes] = value.astype(BF)

    def drain(self):
        self.sent.drain()


class Sum:
    def __init__(self, terms, near, passed, far, send_sem, recv_sem):
        pre = lax.axis_index("pre")
        near_id, far_id = {"pre": xor(pre, 1)}, {"pre": xor(pre, 2)}
        self.terms, self.near, self.passed = terms, near, passed
        self.near_copies = [
            remote(terms.at[i], near.at[i], send_sem.at[i], recv_sem.at[i], **near_id)
            for i in range(2)
        ]
        self.far_copy = remote(passed, far, send_sem.at[2], recv_sem.at[2], **far_id)

    def run(self, term, keep):
        def store_in(slot):
            def store(rows, lanes, value):
                self.terms[slot, rows, lanes] = value.astype(BF)

            return store

        term(3, store_in(0))
        self.near_copies[0].start()
        term(1, store_in(1))
        self.near_copies[1].start()
        self.near_copies[0].wait_recv()

        def store(rows, lanes, value):
            self.passed[rows, lanes] = (value + self.near[0, rows, lanes].astype(F32)).astype(BF)

        term(2, store)
        self.far_copy.start()
        self.near_copies[1].wait_recv()

        def store(rows, lanes, value):
            keep(rows, lanes, value + self.near[1, rows, lanes].astype(F32))

        term(0, store)

    def drain(self):
        for copy in (*self.near_copies, self.far_copy):
            copy.wait_send()


def columns_grad(left, right, rows, width, tile, save):
    @pl.loop(0, rows // 256)
    def _(i):
        turned = left[:, rows_of(i, 256)].T

        @pl.loop(0, width // 512)
        def _(j):
            tile[:, rows_of(j, 512)] = dot_nn(turned, right[:, rows_of(j, 512)]).astype(BF)

        copy = save(rows_of(i, 256))
        copy.start()
        copy.wait()


def add_rows(target, index, value):
    target[index : index + 1, : value.shape[1]] += jnp.sum(value, axis=0, keepdims=True)


def feed_back_kernel(
    sizes,
    w_down,
    w_up,
    acted,
    df,
    h2,
    slope,
    attn,
    down_grad,
    prefix_in,
    later_in,
    prefix_cot,
    later_cot,
    active_ref,
    vectors,
    near_down,
    chain_down,
    near_up,
    up_grad,
    dattn,
    middle_grad,
    prefix_out,
    later_out,
    sums,
    up_sums,
    wbuf,
    lhs,
    acted_v,
    slope_v,
    du_v,
    x_v,
    cot_v,
    attn_v,
    acc_v,
    ffn_v,
    dattn_v,
    terms_v,
    near_v,
    pass_v,
    far_v,
    ffn_near_v,
    ffn_far_v,
    left_v,
    right_v,
    third_v,
    out_v,
    grad_v,
    twin_send,
    twin_recv,
    chain_send,
    chain_recv,
    early_send,
    early_recv,
    spread_send,
    spread_recv,
    sum_send,
    sum_recv,
    local_sem,
):
    seq_size, pre_part, later_part = sizes
    part = pre_part + later_part
    length = 4 * part
    ff_cols = w_up.shape[1]
    gain2 = vectors[5:6, :]
    wide = wide_masks(seq_size)
    lines = seq_size // 2
    line = lax.div(lax.axis_index("seq"), jnp.int32(2))
    end = (line == 0) | (line == lines - 1)
    mid = jnp.logical_not(end)
    turns = range(lines - 1)
    pool = Pool(out_v, 3)
    work = (left_v, right_v, third_v, None, out_v, pool, local_sem.at[12:16])
    put_down = Reduce(
        down_grad,
        near_down,
        chain_down,
        None,
        D // seq_size,
        ff_cols,
        (twin_send, twin_recv, chain_send, chain_recv, None),
        work,
        seq_size,
    )
    put_up = Reduce(
        up_grad,
        near_up,
        None,
        None,
        D // seq_size,
        ff_cols,
        (early_send, early_recv, None, None, None),
        work,
        seq_size,
    )
    get_dattn = Spread(dattn_v, dattn, part, spread_send, spread_recv, local_sem.at[2])
    sum_f = Sum(terms_v, ffn_near_v, pass_v, ffn_far_v, sum_send.at[0], sum_recv.at[0])
    sum_dh2 = Sum(terms_v, near_v, pass_v, far_v, sum_send.at[1], sum_recv.at[1])

    greet((1, *wide))
    put_down.begin(*turns, lines - 1)
    loads = [
        pltpu.make_async_copy(src, dst, local_sem.at[3 + i])
        for i, (src, dst) in enumerate(
            [
                (w_down, wbuf),
                (acted, acted_v),
                (df, lhs),
                (slope, slope_v),
                (prefix_in, x_v.at[:pre_part, :]),
                (later_in, x_v.at[pre_part:, :]),
                (prefix_cot, cot_v.at[:pre_part, :]),
                (later_cot, cot_v.at[pre_part:, :]),
                (attn, attn_v),
            ]
        )
    ]
    for load in loads:
        load.start()
    sums[...] = jnp.zeros_like(sums)
    up_sums[...] = jnp.zeros_like(up_sums)
    for load in loads[:2]:
        load.wait()

    def f_term(r, store):
        @pl.loop(0, D // 512)
        def _(j):
            store(
                slice(0, part),
                rows_of(j, 512),
                dot_nt(acted_v[r * part : (r + 1) * part, :], wbuf[rows_of(j, 512), :]),
            )

    def keep_f(rows, lanes, value):
        ffn_v[rows, lanes] = value

    sum_f.run(f_term, keep_f)
    for load in loads[2:]:
        load.wait()
    put_down.step(0, end)

    @pl.loop(0, 4)
    def _(r):
        rows = rows_of(r, part)

        @pl.loop(0, ff_cols // 512)
        def _(j):
            lanes = rows_of(j, 512)
            value = dot_nn(lhs[rows, :], wbuf[:, lanes])
            du_v[rows, lanes] = (value * slope_v[rows, lanes].astype(F32)).astype(BF)

    load = pltpu.make_async_copy(w_up, wbuf, local_sem.at[3])
    load.start()
    load_h2 = pltpu.make_async_copy(h2, lhs, local_sem.at[4])
    load_h2.start()
    for copy in sum_f.near_copies:
        copy.wait_send()
    sum_f.far_copy.wait_send()
    load.wait()

    def dh2_term(r, store):
        @pl.loop(0, D // 512)
        def _(j):
            store(
                slice(0, part),
                rows_of(j, 512),
                dot_nt(du_v[r * part : (r + 1) * part, :], wbuf[rows_of(j, 512), :]),
            )

    def keep_dh2(rows, lanes, value):
        acc_v[rows, lanes] = value

    sum_dh2.run(dh2_term, keep_dh2)
    put_down.step(1, end)
    put_down.step(0, mid)
    load_h2.wait()
    columns_grad(
        lhs,
        du_v,
        D,
        ff_cols,
        grad_v,
        lambda rows: pltpu.make_async_copy(grad_v, up_grad.at[rows, :], local_sem.at[3]),
    )
    put_up.begin(0)
    for turn in turns[2:]:
        put_down.step(turn, end)
    chunk = 32
    sum_f.far_copy.wait_recv()

    @pl.loop(0, part // chunk)
    def _(i):
        rows = rows_of(i, chunk)
        live = active_ref[rows, :]
        ffn = ffn_v[rows, :] + ffn_far_v[rows, :].astype(F32) + vectors[7:8, :]
        branch = attn_v[rows, :]
        result = x_v[rows, :].astype(F32) + live * (branch + ffn)
        add_rows(sums, 4, live * result * result)
        add_rows(sums, 5, live * branch * branch)
        add_rows(sums, 6, live * ffn * ffn)
        acted_v[rows, :] = result.astype(BF)

    saves = [
        pltpu.make_async_copy(acted_v.at[:pre_part, :], prefix_out, local_sem.at[4]),
        pltpu.make_async_copy(acted_v.at[pre_part:part, :], later_out, local_sem.at[5]),
    ]
    for save in saves:
        save.start()
    for turn in turns[1:]:
        put_down.step(turn, mid)
    sum_dh2.far_copy.wait_recv()

    @pl.loop(0, part // chunk)
    def _(i):
        rows = rows_of(i, chunk)
        grad = acc_v[rows, :] + far_v[rows, :].astype(F32)
        middle = x_v[rows, :].astype(F32) + attn_v[rows, :]
        _, normed, scaling = layer_norm_parts(middle, gain2, 0.0)
        back = norm_back(grad, normed, scaling, gain2)
        acc_v[rows, :] = back
        direct = active_ref[rows, :] * cot_v[rows, :].astype(F32)
        value = (direct + back).astype(BF)
        dattn_v[rows, :] = value
        add_rows(sums, 0, value.astype(F32))
        add_rows(sums, 1, grad * normed)
        add_rows(sums, 2, grad)
        add_rows(sums, 3, direct)

    get_dattn.begin()
    saves.append(pltpu.make_async_copy(acc_v, middle_grad, local_sem.at[3]))
    saves[-1].start()

    @pl.loop(0, length // chunk)
    def _(i):
        add_rows(up_sums, 0, du_v[rows_of(i, chunk), :].astype(F32))

    get_dattn.forward()
    put_down.settle()
    get_dattn.finish()
    for save in saves:
        save.wait()
    put_up.near_copy(0).wait_recv()
    for item in (put_down, put_up, get_dattn, sum_dh2, pool):
        item.drain()


def feed_back(seq_size, pre_part, later_part, *operands):
    part = pre_part + later_part
    length = 4 * part
    w_up = operands[1]
    ff_cols = w_up.shape[1]
    own_d = D // seq_size
    hbm = pl.BlockSpec(memory_space=pl.ANY)
    vmem = pl.BlockSpec(memory_space=pltpu.VMEM)

    def out(shape, kind=BF):
        return jax.ShapeDtypeStruct(shape, kind)

    lines = seq_size // 2
    near_rows = lines * own_d
    whole = own_d
    chains = 2 * (lines - 1)
    outs = (
        out((near_rows, ff_cols)),
        out((chains * whole, ff_cols)),
        out((near_rows, ff_cols)),
        out((D, ff_cols)),
        out((length, D)),
        out((part, D), F32),
        out((pre_part, D)),
        out((later_part, D)),
        out((8, D), F32),
        out((8, ff_cols), F32),
    )
    dma = pltpu.SemaphoreType.DMA
    return pl.pallas_call(
        functools.partial(feed_back_kernel, (seq_size, pre_part, later_part)),
        out_shape=outs,
        in_specs=[hbm] * 12 + [vmem] * (len(operands) - 12),
        out_specs=[hbm] * 8 + [vmem] * 2,
        scratch_shapes=[
            pltpu.VMEM((D, ff_cols), BF),
            pltpu.VMEM((length, D), BF),
            pltpu.VMEM((length, ff_cols), BF),
            pltpu.VMEM((length, ff_cols), BF),
            pltpu.VMEM((length, ff_cols), BF),
            pltpu.VMEM((part, D), BF),
            pltpu.VMEM((part, D), BF),
            pltpu.VMEM((part, D), F32),
            pltpu.VMEM((part, D), F32),
            pltpu.VMEM((part, D), F32),
            pltpu.VMEM((part, D), BF),
            pltpu.VMEM((2, part, D), BF),
            pltpu.VMEM((2, part, D), BF),
            pltpu.VMEM((part, D), BF),
            pltpu.VMEM((part, D), BF),
            pltpu.VMEM((2, part, D), BF),
            pltpu.VMEM((part, D), BF),
            pltpu.VMEM((whole, ff_cols), BF),
            pltpu.VMEM((own_d, ff_cols), BF),
            pltpu.VMEM((whole, ff_cols), BF),
            pltpu.VMEM((3, whole, ff_cols), BF),
            pltpu.VMEM((256, ff_cols), BF),
            dma((lines,)),
            dma((lines,)),
            dma((lines,)),
            dma((chains,)),
            dma((lines,)),
            dma((lines,)),
            dma((4,)),
            dma((4,)),
            dma((2, 3)),
            dma((2, 3)),
            dma((16,)),
        ],
        compiler_params=pltpu.CompilerParams(
            collective_id=1, has_side_effects=True, vmem_limit_bytes=62 * 2**20
        ),
        cost_estimate=pl.CostEstimate(
            flops=2 * length * D * 3 * ff_cols,
            bytes_accessed=8 * D * ff_cols,
            transcendentals=length,
        ),
        name="feed_back",
    )(*operands)


def attend_back_pair(pair, cols, qkv, do, stats, codes_q, codes_k, dq_all, dk_all, dv_all, dqkv):
    lanes = [pl.ds(pl.multiple_of(third * cols + pair * 128, 128), 128) for third in range(3)]
    dk_all[...] = jnp.zeros_like(dk_all)
    dv_all[...] = jnp.zeros_like(dv_all)
    blocks = qkv.shape[0] // TILE
    for block in range(blocks):
        rows = slice(block * TILE, (block + 1) * TILE)
        both_q = qkv[rows, lanes[0]]
        both_do = do[rows, lanes_of(pair)]
        both_levels = stats[rows, lanes_of(pair)]
        parts = []
        for head in range(2):
            queries = head_lanes(both_q, head)
            grads = head_lanes(both_do, head)
            level = both_levels[:, head * HEAD_DIM : head * HEAD_DIM + 1]
            probs = []
            dprobs = []
            for tile in range(block + 1):
                keys = slice(tile * TILE, (tile + 1) * TILE)
                scores = masked_scores(
                    block, dot_nt(queries, qkv[keys, lanes[1]]), tile, codes_q, codes_k
                )
                probs.append(jnp.exp(scores - level))
                dprobs.append(dot_nt(grads, qkv[keys, lanes[2]]))
            delta = functools.reduce(
                jnp.add, [jnp.sum(a * b, axis=1, keepdims=True) for a, b in zip(probs, dprobs)]
            )
            dq = None
            for tile in range(block + 1):
                keys = slice(tile * TILE, (tile + 1) * TILE)
                ds = (probs[tile] * (dprobs[tile] - delta)).astype(BF)
                part = dot_nn(ds, qkv[keys, lanes[1]])
                dq = part if dq is None else dq + part
                dk_all[keys, :] += dot_tn(ds, queries)
                dv_all[keys, :] += dot_tn(probs[tile].astype(BF), grads)
            parts.append(dq)
        dq_all[rows, :] = join_heads(*parts) * (1.0 / math.sqrt(HEAD_DIM))
    for lane, source in zip(lanes, (dq_all, dk_all, dv_all)):
        dqkv[:, lane] = source[...].astype(BF)


def attend_back_kernel(
    sizes,
    w_qkv,
    w_out,
    h1,
    qkv,
    stats,
    mixed,
    dattn,
    middle_grad,
    up_grad,
    down_grad,
    near_down,
    chain_down,
    early_up,
    prefix_in,
    later_in,
    prefix_cot,
    later_cot,
    active_ref,
    vectors,
    feed_sums,
    up_sums,
    codes_q,
    codes_k,
    fin_down,
    fin_up,
    fin_qkv,
    fin_out,
    tail_down,
    near_up,
    chain_up,
    tail_up,
    near_out,
    chain_out,
    tail_out,
    near_qkv,
    chain_qkv,
    tail_qkv,
    out_grad,
    qkv_grad,
    prefix_grad,
    later_grad,
    sums,
    wbuf,
    lhs,
    qkv_v,
    stats_v,
    do_v,
    mixed_v,
    dqkv_v,
    dq_v,
    dk_v,
    dv_v,
    x_v,
    cot_v,
    middle_v,
    acc_v,
    terms_v,
    near_v,
    pass_v,
    far_v,
    left_v,
    right_v,
    third_v,
    fourth_v,
    out_v,
    grad_v,
    res_down,
    res_up,
    res_qkv,
    res_out,
    moved_out,
    qkv_sums,
    sums_land,
    total_send,
    total_recv,
    relay_sem,
    twin_send,
    twin_recv,
    chain_send,
    chain_recv,
    tail_sem,
    spread_send,
    spread_recv,
    sum_send,
    sum_recv,
    local_sem,
):
    seq_size, pre_part, later_part = sizes
    part = pre_part + later_part
    length = 4 * part
    width = w_qkv.shape[1]
    cols = width // 3
    ff_cols = up_grad.shape[1]
    own_d = D // seq_size
    own_o = cols // seq_size
    pre = lax.axis_index("pre")
    wide = wide_masks(seq_size)
    lines = seq_size // 2
    line = lax.div(lax.axis_index("seq"), jnp.int32(2))
    end = (line == 0) | (line == lines - 1)
    mid = jnp.logical_not(end)
    turns = range(lines - 1)
    pool = Pool(out_v, 3)
    work = (left_v, right_v, third_v, fourth_v, out_v, pool, local_sem.at[24:29])

    def reduce_of(i, grad, near, chain, tail, rows, columns, split=False):
        j = max(i, 1) - 1
        sems = (twin_send.at[j], twin_recv.at[j], chain_send.at[j], chain_recv.at[j], tail_sem.at[i])
        return Reduce(grad, near, chain, tail, rows, columns, sems, work, seq_size, split)

    put_down = reduce_of(0, down_grad, near_down, chain_down, tail_down, own_d, ff_cols)
    put_up = reduce_of(1, up_grad, near_up, chain_up, tail_up, own_d, ff_cols)
    put_out = reduce_of(2, out_grad, near_out, chain_out, tail_out, own_o, D)
    put_qkv = reduce_of(3, qkv_grad, near_qkv, chain_qkv, tail_qkv, own_d, width)

    def spread_of(i, own, land):
        return Spread(own, land, own_d, spread_send.at[i], spread_recv.at[i], local_sem.at[2 + i])

    get_down = spread_of(0, res_down, fin_down)
    get_up = spread_of(1, res_up, fin_up)
    get_qkv = spread_of(2, res_qkv, fin_qkv)
    sum_dh1 = Sum(terms_v, near_v, pass_v, far_v, sum_send, sum_recv)
    chunk = 32

    relay = Relay(seq_size, relay_sem.at[0], relay_sem.at[1], relay_sem.at[2])
    relayed = (res_out, moved_out, relay.back)
    get_out = Spread(
        moved_out, fin_out, own_o, spread_send.at[3], spread_recv.at[3], local_sem.at[20]
    )
    bits = [1 << i for i in range(seq_size.bit_length() - 1)]
    greet(sorted({*wide, *bits}), relay)
    put_up.begin(*turns[1:])
    stages = [
        remote(sums, sums_land.at[i], total_send.at[i], total_recv.at[i], **target)
        for i, target in enumerate(
            [{"pre": xor(pre, 1)}, {"pre": xor(pre, 2)}]
            + [{"seq": xor(lax.axis_index("seq"), bit)} for bit in bits]
        )
    ]

    def add_stage(i, onward=True):
        stages[i].wait_recv()
        stages[i].wait_send()
        sums[...] += sums_land[i]
        if onward:
            stages[i + 1].start()

    def load_all(first, *pairs):
        copies = [
            pltpu.make_async_copy(src, dst, local_sem.at[first + i])
            for i, (src, dst) in enumerate(pairs)
        ]
        for copy in copies:
            copy.start()
        return copies

    def wait_all(copies):
        for copy in copies:
            copy.wait()

    loads = load_all(5, (w_out, wbuf.at[:cols, :]), (dattn, lhs))
    more = load_all(
        8,
        (prefix_in, x_v.at[:pre_part, :]),
        (later_in, x_v.at[pre_part:, :]),
        (prefix_cot, cot_v.at[:pre_part, :]),
        (later_cot, cot_v.at[pre_part:, :]),
        (middle_grad, middle_v),
        (qkv, qkv_v),
        (stats, stats_v),
        (mixed, mixed_v),
    )
    sums[...] = jnp.zeros_like(sums)
    qkv_sums[...] = jnp.zeros_like(qkv_sums)
    put_up.step(0, end, early_up)
    put_down.final(res_down)
    get_down.begin()
    def keep(rows, lanes, value):
        acc_v[rows, lanes] = value

    wait_all(loads)
    wait_all(more)

    def position_rows(r):
        member = lax.rem(r, 2) * (xor(pre, 1) - pre) + lax.div(r, 2) * (xor(pre, 2) - pre) + pre
        return (
            rows_of(member, pre_part),
            pl.ds(pl.multiple_of(4 * pre_part + member * later_part, 64), later_part),
        )

    @pl.loop(0, 4)
    def _(r):
        head_rows, tail_rows = position_rows(r)
        value = dot_nt(lhs[rows_of(r, part), :], wbuf[:cols, :]).astype(BF)
        do_v[head_rows, :] = value[:pre_part]
        do_v[tail_rows, :] = value[pre_part:]

    columns_grad(
        mixed_v,
        lhs,
        cols,
        D,
        grad_v,
        lambda rows: pltpu.make_async_copy(grad_v.at[:, :D], out_grad.at[rows, :], local_sem.at[5]),
    )
    put_out.begin(*turns)
    put_up.begin(lines - 1)
    put_out.begin(lines - 1)
    loads = load_all(5, (w_qkv, wbuf.at[:, :width]))
    for r in range(4):
        head_rows, tail_rows = position_rows(jnp.int32(r))
        loads += load_all(
            8 + 2 * r,
            (h1.at[r * part : r * part + pre_part, :], lhs.at[head_rows, :]),
            (h1.at[r * part + pre_part : (r + 1) * part, :], lhs.at[tail_rows, :]),
        )
    pairs = cols // 128

    def attention(first, last):
        @pl.loop(first, last)
        def _(pair):
            attend_back_pair(
                pair,
                cols,
                qkv_v,
                do_v,
                stats_v,
                codes_q[...],
                codes_k[...],
                dq_v,
                dk_v,
                dv_v,
                dqkv_v,
            )

    put_up.step(0, mid, early_up)
    attention(0, pairs // 2)
    put_up.step(1, end)
    attention(pairs // 2, pairs)
    for turn in turns[2:]:
        put_up.step(turn, end)
    for turn in turns[1:]:
        put_up.step(turn, mid)
    get_down.forward()
    wait_all(loads)
    columns_grad(
        lhs,
        dqkv_v,
        D,
        width,
        grad_v,
        lambda rows: pltpu.make_async_copy(
            grad_v.at[:, :width], qkv_grad.at[rows, :], local_sem.at[5]
        ),
    )
    put_qkv.begin(*turns, lines - 1)
    get_down.finish()
    for turn in turns:
        put_out.step(turn, end)

    def dh1_term(r, store):
        head_rows, tail_rows = position_rows(jnp.int32(r))

        @pl.loop(0, D // 512)
        def _(j):
            weights = wbuf[rows_of(j, 512), :width]
            store(slice(0, pre_part), rows_of(j, 512), dot_nt(dqkv_v[head_rows, :], weights))
            store(slice(pre_part, part), rows_of(j, 512), dot_nt(dqkv_v[tail_rows, :], weights))

    sum_dh1.run(dh1_term, keep)

    @pl.loop(0, length // chunk)
    def _(i):
        add_rows(qkv_sums, 0, dqkv_v[rows_of(i, chunk), :].astype(F32))

    put_qkv.step(0, end)
    for turn in turns:
        put_out.step(turn, mid)
    put_up.settle()
    put_up.final(res_up)
    put_qkv.step(1, end)
    put_up.last(res_up)
    get_up.begin()
    put_qkv.step(0, mid)
    sum_dh1.far_copy.wait_recv()

    @pl.loop(0, part // chunk)
    def _(i):
        rows = rows_of(i, chunk)
        grad = acc_v[rows, :] + far_v[rows, :].astype(F32)
        _, normed, scaling = layer_norm_parts(x_v[rows, :].astype(F32), vectors[0:1, :], 0.0)
        back = norm_back(grad, normed, scaling, vectors[0:1, :])
        add_rows(sums, 0, grad * normed)
        add_rows(sums, 1, grad)
        value = cot_v[rows, :].astype(F32) + middle_v[rows, :] + back
        terms_rows = value.astype(BF)
        x_v[rows, :] = terms_rows

    saves = load_all(6, (x_v.at[:pre_part, :], prefix_grad), (x_v.at[pre_part:, :], later_grad))
    own_lanes = pl.ds(pl.multiple_of(pre * cols, cols), cols)
    sums[2:5, :] = feed_sums[4:7, :]
    sums[5:9, :] = feed_sums[:4, :]
    sums[9:10, own_lanes] = qkv_sums[0:1, :cols]
    sums[10:11, own_lanes] = qkv_sums[0:1, 2 * cols :]
    for k in range(4):
        sums[11 + k : 12 + k, own_lanes] = jnp.concatenate(
            [
                up_sums[0:1, (i * 4 + k) * own_d : (i * 4 + k + 1) * own_d]
                for i in range(seq_size // 4)
            ],
            axis=1,
        )
    sums[15:16, :] = jnp.zeros((1, D), F32) + jnp.sum(active_ref[...])
    stages[0].start()
    for turn in turns[2:]:
        put_qkv.step(turn, end)
    put_out.settle()
    put_out.final(res_out)
    add_stage(0)
    wait_all(saves)
    put_out.last(res_out)
    relay.begin(*relayed)
    for turn in turns[1:]:
        put_qkv.step(turn, mid)
    add_stage(1, False)
    get_up.forward()
    relay.finish(*relayed)
    get_out.begin()
    put_qkv.settle()
    put_qkv.final(res_qkv)
    put_qkv.last(res_qkv)
    get_qkv.begin()
    stages[2].start()
    get_out.forward()
    get_up.finish()
    for i in range(2, len(stages)):
        add_stage(i, i + 1 < len(stages))
    get_out.finish()
    get_qkv.forward()
    get_qkv.finish()
    for item in (put_up, put_out, put_qkv, get_down, get_up, get_out, get_qkv, sum_dh1, pool):
        item.drain()


def attend_back(seq_size, pre_part, later_part, *operands):
    part = pre_part + later_part
    length = 4 * part
    width = operands[0].shape[1]
    cols = width // 3
    ff_cols = FF // 4
    own_d = D // seq_size
    own_o = cols // seq_size
    lines = seq_size // 2
    chains = 2 * (lines - 1)
    early_d, early_o = 0, 0
    least = 16

    def landings(rows, early, columns):
        return (
            out((lines * (rows - early), columns)),
            out((chains * (rows + early), columns)),
            out((max(early, least), columns)),
        )

    hbm = pl.BlockSpec(memory_space=pl.ANY)
    vmem = pl.BlockSpec(memory_space=pltpu.VMEM)

    def out(shape, kind=BF):
        return jax.ShapeDtypeStruct(shape, kind)

    outs = (
        out((4 * own_d, ff_cols)),
        out((4 * own_d, ff_cols)),
        out((4 * own_d, width)),
        out((4 * own_o, D)),
        out((max(early_d, least), ff_cols)),
        *landings(own_d, early_d, ff_cols),
        *landings(own_o, early_o, D),
        *landings(own_d, 0, width),
        out((cols, D)),
        out((D, width)),
        out((pre_part, D)),
        out((later_part, D)),
        out((16, D), F32),
    )
    most = max(ff_cols, D, width)
    stages = 1 + seq_size.bit_length()
    dma = pltpu.SemaphoreType.DMA
    return pl.pallas_call(
        functools.partial(attend_back_kernel, (seq_size, pre_part, later_part)),
        out_shape=outs,
        in_specs=[hbm] * 17 + [vmem] * (len(operands) - 17),
        out_specs=[hbm] * (len(outs) - 1) + [vmem],
        scratch_shapes=[
            pltpu.VMEM((D, most), BF),
            pltpu.VMEM((length, D), BF),
            pltpu.VMEM((length, width), BF),
            pltpu.VMEM((length, cols), F32),
            pltpu.VMEM((length, cols), BF),
            pltpu.VMEM((length, cols), BF),
            pltpu.VMEM((length, width), BF),
            pltpu.VMEM((length, 128), F32),
            pltpu.VMEM((length, 128), F32),
            pltpu.VMEM((length, 128), F32),
            pltpu.VMEM((part, D), BF),
            pltpu.VMEM((part, D), BF),
            pltpu.VMEM((part, D), F32),
            pltpu.VMEM((part, D), F32),
            pltpu.VMEM((2, part, D), BF),
            pltpu.VMEM((2, part, D), BF),
            pltpu.VMEM((part, D), BF),
            pltpu.VMEM((part, D), BF),
            pltpu.VMEM((own_d + early_d, most), BF),
            pltpu.VMEM((own_d, most), BF),
            pltpu.VMEM((own_d + early_d, most), BF),
            pltpu.VMEM((own_d + early_d, most), BF),
            pltpu.VMEM((3, own_d + early_d, most), BF),
            pltpu.VMEM((256, most), BF),
            pltpu.VMEM((own_d, ff_cols), BF),
            pltpu.VMEM((own_d, ff_cols), BF),
            pltpu.VMEM((own_d, width), BF),
            pltpu.VMEM((own_o, D), BF),
            pltpu.VMEM((own_o, D), BF),
            pltpu.VMEM((8, width), F32),
            pltpu.VMEM((stages, 16, D), F32),
            dma((stages,)),
            dma((stages,)),
            dma((3,)),
            dma((3, lines)),
            dma((3, lines)),
            dma((3, lines)),
            dma((3, chains)),
            dma((4, 2)),
            dma((4, 4)),
            dma((4, 4)),
            dma((3,)),
            dma((3,)),
            dma((29,)),
        ],
        compiler_params=pltpu.CompilerParams(
            collective_id=2, has_side_effects=True, vmem_limit_bytes=63 * 2**20
        ),
        cost_estimate=pl.CostEstimate(
            flops=2 * length * D * (2 * width + ff_cols),
            bytes_accessed=8 * D * ff_cols,
            transcendentals=length * length,
        ),
        name="attend_back",
    )(*operands)


def absolute_pre(blocks, place):
    first = place % 2 == 0
    low = place < 2
    a = [jnp.where(first, blocks[0], blocks[1]), jnp.where(first, blocks[1], blocks[0])]
    b = [jnp.where(first, blocks[2], blocks[3]), jnp.where(first, blocks[3], blocks[2])]
    return [jnp.where(low, u, w) for u, w in zip(a, b)] + [jnp.where(low, w, u) for u, w in zip(a, b)]


def on_device(
    prefix_in,
    later_in,
    doc_lengths,
    doc_exit,
    token_skip,
    first_gain,
    first_bias,
    qkv_weight,
    query_bias,
    value_bias,
    out_weight,
    out_bias,
    second_gain,
    second_bias,
    up_weight,
    up_bias,
    down_weight,
    down_bias,
    prefix_cot,
    later_cot,
):
    pre_part = prefix_in.shape[1]
    later_part = later_in.shape[1]
    part = pre_part + later_part
    parts = lax.axis_size("pre")
    place = lax.axis_index("pre")
    seq_count = lax.axis_size("seq")
    seq_place = lax.axis_index("seq")
    own_d = D // seq_count
    cols = D // parts

    small = jnp.concatenate(
        [
            jnp.stack(
                [
                    first_gain,
                    first_bias,
                    query_bias,
                    value_bias,
                    out_bias,
                    second_gain,
                    second_bias,
                    down_bias,
                ]
            ),
            up_bias.reshape(4, own_d),
            jnp.zeros((4, own_d), BF),
        ]
    ).astype(F32)
    doc_id, live = token_tables(doc_lengths, doc_exit, token_skip)
    live_here = lax.dynamic_slice_in_dim(live[0], place * later_part, later_part, 0)
    active = jnp.concatenate([jnp.ones((pre_part,), F32), live_here.astype(F32)])[:, None]
    codes_q = jnp.concatenate([jnp.full((PRE,), -1, jnp.int32), doc_id[0]])[:, None]
    codes_k = jnp.concatenate(
        [jnp.full((PRE,), -1, jnp.int32), jnp.where(live[0], doc_id[0], -2)]
    )[None, :]

    (w_qkv, w_out, w_up, w_down, h1, df, h2, qkv, mixed, stats, attn, acted, slope, down_grad, vectors) = forward_pass(
        seq_count,
        pre_part,
        later_part,
        small,
        qkv_weight,
        out_weight,
        up_weight,
        down_weight,
        prefix_in[0],
        later_in[0],
        prefix_cot[0],
        later_cot[0],
        active,
        codes_q,
        codes_k,
    )

    rows_in = (prefix_in[0], later_in[0], prefix_cot[0], later_cot[0], active)
    (near_down, chain_down, early_up, up_grad, dattn, middle_grad, prefix_out, later_out, feed_sums, up_sums) = feed_back(
        seq_count,
        pre_part,
        later_part,
        w_down,
        w_up,
        acted,
        df,
        h2,
        slope,
        attn,
        down_grad,
        *rows_in,
        vectors,
    )
    (fin_down, fin_up, fin_qkv, fin_out, *_, prefix_grad, later_grad, sums) = attend_back(
        seq_count,
        pre_part,
        later_part,
        w_qkv,
        w_out,
        h1,
        qkv,
        stats,
        mixed,
        dattn,
        middle_grad,
        up_grad,
        down_grad,
        near_down,
        chain_down,
        early_up,
        *rows_in,
        vectors,
        feed_sums,
        up_sums,
        codes_q,
        codes_k,
    )

    def shared(blocks):
        rows = blocks.shape[0] // parts
        return absolute_pre([blocks[i * rows : (i + 1) * rows] for i in range(parts)], place)

    down_full = jnp.concatenate(shared(fin_down), axis=1).astype(F32)
    up_full = jnp.concatenate(shared(fin_up), axis=1).astype(F32)
    out_full = jnp.concatenate(shared(fin_out), axis=0).astype(F32)
    qkv_blocks = shared(fin_qkv)
    qkv_full = jnp.concatenate(
        [block[:, i * cols : (i + 1) * cols] for i in range(3) for block in qkv_blocks], axis=1
    ).astype(F32)

    mine = lax.dynamic_slice_in_dim(sums, seq_place * own_d, own_d, 1)
    residual_rms = jnp.sqrt(jnp.sum(sums[2:5], axis=1) / (sums[15, 0] * D))
    return (
        prefix_out[None],
        later_out[None],
        prefix_grad[None],
        later_grad[None],
        mine[0],
        mine[1],
        qkv_full,
        mine[9],
        mine[10],
        out_full,
        mine[5],
        mine[6],
        mine[7],
        up_full,
        mine[11:15].reshape(-1),
        down_full,
        mine[8],
        residual_rms,
    )


def solution(mesh):
    placed = (
        P("seq", "pre", None),
        P("seq", "pre", None),
        P("seq", None),
        P("seq", None),
        P("seq", None),
        P("seq"),
        P("seq"),
        P("seq", None),
        P("seq"),
        P("seq"),
        P("seq", None),
        P("seq"),
        P("seq"),
        P("seq"),
        P("seq", None),
        P("seq"),
        P("seq", None),
        P("seq"),
        P("seq", "pre", None),
        P("seq", "pre", None),
    )
    return jax.shard_map(
        on_device,
        mesh=mesh,
        in_specs=placed,
        out_specs=(
            P("seq", "pre", None),
            P("seq", "pre", None),
            P("seq", "pre", None),
            P("seq", "pre", None),
            P("seq"),
            P("seq"),
            P("seq", None),
            P("seq"),
            P("seq"),
            P("seq", None),
            P("seq"),
            P("seq"),
            P("seq"),
            P("seq", None),
            P("seq"),
            P("seq", None),
            P("seq"),
            P(),
        ),
        check_vma=False,
    )
```

```python
import functools
import math

import jax
import jax.numpy as jnp
from jax import lax
from jax.experimental import pallas as pl
from jax.experimental.pallas import tpu as pltpu
from jax.sharding import PartitionSpec as P

D = 2048
HEADS = 32
HEAD_DIM = 64
FF = 8192
LAYER = 12
PRE = 512

EPS = 1e-05
NEG = -1e30
BF = jnp.bfloat16
F32 = jnp.float32
TILE = 256


def layer_norm_parts(values, gain, bias):
    mean = jnp.mean(values, axis=-1, keepdims=True)
    centred = values - mean
    variance = jnp.mean(centred * centred, axis=-1, keepdims=True)
    scaling = lax.rsqrt(variance + EPS)
    normed = centred * scaling
    return (normed * gain + bias, normed, scaling)


def norm_back(grad, normed, scaling, gain):
    scaled = grad * gain
    inner = jnp.mean(scaled, axis=-1, keepdims=True)
    cross = jnp.mean(scaled * normed, axis=-1, keepdims=True)
    return scaling * (scaled - inner - normed * cross)


def token_tables(doc_lengths, doc_exit, token_skip):
    order = jnp.arange(doc_lengths.shape[-1], dtype=jnp.int32)
    earlier = order[None, :] < order[:, None]
    starts = jnp.sum(
        jnp.where(earlier, doc_lengths[..., None, :], 0), axis=-1, dtype=jnp.int32
    )
    places = jnp.arange(token_skip.shape[-1], dtype=jnp.int32)
    doc_id = (
        jnp.sum(
            (places[:, None] >= starts[..., None, :]).astype(jnp.int32), axis=-1, dtype=jnp.int32
        )
        - 1
    )
    live_doc = doc_exit > LAYER
    live = jnp.any((doc_id[..., None] == order) & live_doc[..., None, :], axis=-1) & (
        token_skip == 0
    )
    return (doc_id, live)


def dot_nt(a, b):
    return lax.dot_general(a, b, (((1,), (1,)), ((), ())), preferred_element_type=F32)


def dot_nn(a, b):
    return lax.dot_general(a, b, (((1,), (0,)), ((), ())), preferred_element_type=F32)


def dot_tn(a, b):
    return lax.dot_general(a, b, (((0,), (0,)), ((), ())), preferred_element_type=F32)


def masked_scores(block, scores, tile, codes_q, codes_k):
    rows = lax.broadcasted_iota(jnp.int32, (TILE, TILE), 0)
    cols = lax.broadcasted_iota(jnp.int32, (TILE, TILE), 1)
    allowed = None
    if tile == block:
        allowed = cols <= rows
    if tile * TILE >= PRE:
        same = (
            codes_q[block * TILE : (block + 1) * TILE, :]
            == codes_k[:, tile * TILE : (tile + 1) * TILE]
        )
        allowed = same if allowed is None else allowed & same
    if allowed is None:
        return scores
    return jnp.where(allowed, scores, NEG)


def xor(value, mask):
    bit = 1
    while bit <= mask:
        if mask & bit:
            value = value + bit * (1 - 2 * lax.rem(lax.div(value, jnp.int32(bit)), jnp.int32(2)))
        bit *= 2
    return value


def remote(src, dst, send_sem, recv_sem, **target):
    return pltpu.make_async_remote_copy(
        src_ref=src,
        dst_ref=dst,
        send_sem=send_sem,
        recv_sem=recv_sem,
        device_id=target,
        device_id_type=pl.DeviceIdType.MESH,
    )


def greet(masks, relay=None):
    barrier = pltpu.get_barrier_semaphore()
    seq = lax.axis_index("seq")
    pre = lax.axis_index("pre")

    def signal(**target):
        pl.semaphore_signal(
            barrier, inc=1, device_id=target, device_id_type=pl.DeviceIdType.MESH
        )

    for mask in masks:
        signal(seq=xor(seq, mask))
    for mask in (1, 2):
        signal(pre=xor(pre, mask))
    count = len(masks) + 2
    if relay is not None:

        @pl.when(relay.moves)
        def _():
            signal(seq=relay.there[0], pre=relay.there[1])
            signal(seq=relay.back[0], pre=relay.back[1])

        count = count + 2 * relay.moves.astype(jnp.int32)
    pl.semaphore_wait(barrier, count)


class Relay:
    def __init__(self, size, send_sem, recv_sem, local_sem):
        seq, pre = lax.axis_index("seq"), lax.axis_index("pre")
        held = seq * 4 + pre
        used = pre * size + seq
        self.there = (lax.rem(held, size), lax.div(held, size))
        self.back = (lax.div(used, 4), lax.rem(used, 4))
        self.moves = held != used
        self.sems = (send_sem, recv_sem, local_sem)

    def copies(self, src, dst, target):
        send_sem, recv_sem, local_sem = self.sems
        return (
            remote(src, dst, send_sem, recv_sem, seq=target[0], pre=target[1]),
            pltpu.make_async_copy(src, dst, local_sem),
        )

    def begin(self, src, dst, target):
        away, here = self.copies(src, dst, target)
        pl.when(self.moves)(away.start)
        pl.when(jnp.logical_not(self.moves))(here.start)

    def finish(self, src, dst, target):
        away, here = self.copies(src, dst, target)

        @pl.when(self.moves)
        def _():
            away.wait_recv()
            away.wait_send()

        pl.when(jnp.logical_not(self.moves))(here.wait)


def rows_of(index, count):
    return pl.ds(pl.multiple_of(index * count, count), count)


def far_line(lines, line, turn):
    low = lines - 1 - turn
    low = low - (low <= line).astype(jnp.int32)
    high = turn + (turn >= line).astype(jnp.int32)
    return jnp.where(line < lines // 2, low, high)


def early_rows(rows):
    return (rows * 3 + 128) // 256 * 16


class Copies:
    def __init__(self):
        self.items = []

    def start(self, copy, when=None):
        if when is None:
            copy.start()
        else:
            pl.when(when)(copy.start)
        self.items.append((copy, when))

    def drain(self):
        for copy, when in self.items:
            if when is None:
                copy.wait_send()
            else:
                pl.when(when)(copy.wait_send)


class Gather:
    def __init__(self, own, land, rows, send_sem, recv_sem, local_sem, size):
        self.own, self.land, self.rows = own, land, rows
        self.early = early_rows(rows)
        self.send_sem, self.recv_sem, self.local_sem = send_sem, recv_sem, local_sem
        self.seq = lax.axis_index("seq")
        self.lines = size // 2
        self.line = lax.div(self.seq, jnp.int32(2))
        self.twin = xor(self.seq, 1)
        self.sent = Copies()
        self.local = None

    def view(self, place, kind):
        first = {0: 0, 1: self.rows - self.early, 2: 0, 3: self.rows - self.early}[kind]
        count = {0: self.rows, 1: self.early, 2: self.rows - self.early, 3: self.early}[kind]
        return self.land.at[pl.ds(pl.multiple_of(place * self.rows + first, 16), count), :]

    def copy(self, place, kind, send, recv, to, own=False):
        there = self.view(place, kind)
        src = there
        if own:
            first = self.rows - self.early if kind in (1, 3) else 0
            count = there.shape[0]
            src = self.own.at[first : first + count, :]
        return remote(
            src, there, self.send_sem.at[kind, send], self.recv_sem.at[kind, recv], seq=to
        )

    def beside(self, up):
        return (self.line < self.lines - 1, self.seq + 2) if up else (self.line > 0, self.seq - 2)

    def begin(self):
        if self.early:
            self.sent.start(self.copy(self.seq, 3, 0, 0, self.twin, True))
        for up in (True, False):
            there, to = self.beside(up)
            spare = self.lines + (0 if up else 1)
            self.sent.start(self.copy(self.seq, 0, spare, self.line, to, True), there)
        self.sent.start(self.copy(self.seq, 2, self.line, self.line, self.twin, True))
        self.local = pltpu.make_async_copy(self.own, self.view(self.seq, 0), self.local_sem)
        self.local.start()

    def rest(self):
        if not self.early:
            return
        self.copy(self.twin, 3, 0, 0, self.twin).wait_recv()
        for up in (True, False):
            there, to = self.beside(up)
            spare = self.lines + (0 if up else 1)
            self.sent.start(self.copy(self.twin, 1, spare, self.line, to), there)

    def event(self, turn, when=None):
        line = far_line(self.lines, self.line, jnp.int32(self.lines - 2 - turn))
        step = jnp.where(line < self.line, 2, -2)
        after = jnp.where(line < self.line, self.line < self.lines - 1, self.line > 0)
        place = line * 2 + lax.rem(self.seq, jnp.int32(2))
        other = xor(place, 1)
        to = jnp.clip(self.seq + step, 0, 2 * self.lines - 1)
        onward = self.copy(place, 0, line, line, to)
        aside = self.copy(place, 2, line, line, self.twin)
        both = self.copy(other, 1, line, line, to) if self.early else None

        def body():
            self.copy(place, 0, line, line, self.twin).wait_recv()
            pl.when(after)(onward.start)
            aside.start()
            if both is not None:
                self.copy(other, 1, line, line, self.twin).wait_recv()
                pl.when(after)(both.start)

        if when is None:
            body()
        else:
            pl.when(when)(body)
            after = after & when
        self.sent.items += [(onward, after), (aside, when)]
        if both is not None:
            self.sent.items.append((both, after))

    def poll(self, turn):
        last = self.lines - 2
        end = (self.line == 0) | (self.line == self.lines - 1)
        self.event(turn, end if turn else None)
        if turn < last:
            self.event(turn + 1, jnp.logical_not(end))

    def finish(self):
        self.local.wait()
        for line in range(self.lines):
            self.copy(line * 2, 2, line, line, self.twin).wait_recv()

    def drain(self):
        self.sent.drain()


class Spread:
    def __init__(self, own, land, rows, send_sem, recv_sem, local_sem):
        self.own, self.land, self.rows = own, land, rows
        self.send_sem, self.recv_sem, self.local_sem = send_sem, recv_sem, local_sem
        self.pre = lax.axis_index("pre")
        self.sent = []

    def slot(self, index):
        return self.land.at[index * self.rows : (index + 1) * self.rows, :]

    def copy(self, src, slot, mask):
        return remote(
            src, self.slot(slot), self.send_sem.at[slot], self.recv_sem.at[slot], pre=xor(self.pre, mask)
        )

    def begin(self):
        for mask in (2, 1):
            copy = self.copy(self.own, mask, mask)
            copy.start()
            self.sent.append(copy)
        self.local = pltpu.make_async_copy(self.own, self.slot(0), self.local_sem)
        self.local.start()

    def forward(self):
        self.copy(self.own, 2, 2).wait_recv()
        copy = self.copy(self.slot(2), 3, 1)
        copy.start()
        self.sent.append(copy)

    def finish_near(self):
        self.local.wait()
        self.copy(self.own, 1, 1).wait_recv()

    def finish_far(self):
        self.copy(self.own, 3, 1).wait_recv()

    def finish(self):
        self.finish_near()
        self.finish_far()

    def drain(self):
        for copy in self.sent:
            copy.wait_send()


def local_copies(pairs, sem):
    copies = [pltpu.make_async_copy(src, dst, sem.at[i]) for i, (src, dst) in enumerate(pairs)]
    for copy in copies:
        copy.start()
    for copy in copies:
        copy.wait()


def wide_masks(size):
    masks = list(range(2, size, 2))
    return sorted(masks, key=lambda m: (m != 2, -m))


def head_lanes(value, head):
    lane = lax.broadcasted_iota(jnp.int32, value.shape, 1)
    inside = (lane < HEAD_DIM) if head == 0 else (lane >= HEAD_DIM)
    return jnp.where(inside, value, jnp.zeros_like(value))


def join_heads(first, second):
    lane = lax.broadcasted_iota(jnp.int32, (first.shape[0], 2 * HEAD_DIM), 1)
    return jnp.where(lane < HEAD_DIM, first, second)


def attend_pair(pair, cols, qkv, codes_q, codes_k, mixed, stats):
    lanes = [pl.ds(pl.multiple_of(third * cols + pair * 128, 128), 128) for third in range(3)]
    blocks = qkv.shape[0] // TILE
    for block in range(blocks):
        rows = slice(block * TILE, (block + 1) * TILE)
        both = qkv[rows, lanes[0]]
        outs, levels = [], []
        for head in range(2):
            queries = head_lanes(both, head)
            scores = [
                masked_scores(
                    block,
                    dot_nt(queries, qkv[tile * TILE : (tile + 1) * TILE, lanes[1]]),
                    tile,
                    codes_q,
                    codes_k,
                )
                for tile in range(block + 1)
            ]
            top = functools.reduce(jnp.maximum, [jnp.max(x, axis=1, keepdims=True) for x in scores])
            powers = [jnp.exp(x - top) for x in scores]
            total = functools.reduce(jnp.add, [jnp.sum(e, axis=1, keepdims=True) for e in powers])
            share = 1.0 / total
            outs.append(
                functools.reduce(
                    jnp.add,
                    [
                        dot_nn((e * share).astype(BF), qkv[tile * TILE : (tile + 1) * TILE, lanes[2]])
                        for tile, e in enumerate(powers)
                    ],
                )
            )
            levels.append(top + jnp.log(total))
        mixed[rows, lanes_of(pair)] = join_heads(outs[0], outs[1]).astype(BF)
        stats[rows, lanes_of(pair)] = join_heads(levels[0], levels[1])


def lanes_of(pair):
    return pl.ds(pl.multiple_of(pair * 128, 128), 128)


def forward_kernel(
    sizes,
    small,
    qkv_weight,
    out_weight,
    up_weight,
    down_weight,
    prefix_in,
    later_in,
    prefix_cot,
    later_cot,
    active_ref,
    codes_q,
    codes_k,
    w_qkv,
    w_out,
    w_up,
    w_down,
    h1,
    df,
    h2,
    qkv,
    mixed,
    stats,
    attn,
    acted,
    slope,
    down_grad,
    vectors,
    wbuf,
    lhs,
    qkv_v,
    mixed_v,
    stats_v,
    x_v,
    cot_v,
    h1_v,
    df_v,
    h2_v,
    terms_v,
    near_v,
    pass_v,
    far_v,
    attn_v,
    acted_v,
    slope_v,
    grad_v,
    own_qkv,
    own_up,
    own_down,
    own_out,
    small_v,
    slope_bias,
    gather_send,
    gather_recv,
    small_send,
    small_recv,
    spread_send,
    spread_recv,
    sum_send,
    sum_recv,
    relay_sem,
    local_sem,
):
    seq_size, pre_part, later_part = sizes
    part = pre_part + later_part
    cols = qkv_weight.shape[1] // 12
    ff_cols = up_weight.shape[1] // 4
    own_d = D // seq_size
    wide = wide_masks(seq_size)
    pre = lax.axis_index("pre")
    seq = lax.axis_index("seq")
    near_id = {"pre": xor(pre, 1)}
    far_id = {"pre": xor(pre, 2)}

    def gather(i, own, land):
        sems = (gather_send.at[i], gather_recv.at[i], local_sem.at[i])
        return Gather(own, land, own.shape[0], *sems, seq_size)

    def own_section(weight, first, columns):
        return weight.at[:, pl.ds(pl.multiple_of(first + pre * columns, columns), columns)]

    get_qkv = gather(0, own_qkv, w_qkv)
    get_out = gather(1, own_out, w_out)
    get_up = gather(2, own_up, w_up)
    get_down = gather(3, own_down, w_down)
    get_h1 = Spread(h1_v, h1, part, spread_send.at[0], spread_recv.at[0], local_sem.at[4])
    get_df = Spread(df_v, df, part, spread_send.at[1], spread_recv.at[1], local_sem.at[5])
    get_h2 = Spread(h2_v, h2, part, spread_send.at[2], spread_recv.at[2], local_sem.at[6])
    relay = Relay(seq_size, relay_sem.at[0], relay_sem.at[1], relay_sem.at[2])
    out_rows = own_d // 4
    relayed = (out_weight.at[rows_of(pre, out_rows), :], own_out, relay.there)

    cuts = [
        pltpu.make_async_copy(
            own_section(qkv_weight, i * D, cols),
            own_qkv.at[:, i * cols : (i + 1) * cols],
            local_sem.at[12 + i],
        )
        for i in range(3)
    ]
    late_cuts = [
        pltpu.make_async_copy(own_section(weight, 0, ff_cols), own, local_sem.at[15 + i])
        for i, (weight, own) in enumerate(((up_weight, own_up), (down_weight, own_down)))
    ]
    for cut in (*cuts, *late_cuts):
        cut.start()
    greet(range(1, seq_size), relay)
    small_copies = [
        remote(
            small, small_v.at[seq], small_send.at[mask], small_recv.at[mask], seq=xor(seq, mask)
        )
        for mask in range(1, seq_size)
    ]
    for copy in small_copies:
        copy.start()
    keep_small = pltpu.make_async_copy(small, small_v.at[seq], local_sem.at[7])
    keep_small.start()
    relay.begin(*relayed)
    for cut in cuts:
        cut.wait()
    get_qkv.begin()
    for cut in late_cuts:
        cut.wait()
    local_copies(
        [
            (prefix_in, x_v.at[:pre_part, :]),
            (later_in, x_v.at[pre_part:, :]),
            (prefix_cot, cot_v.at[:pre_part, :]),
            (later_cot, cot_v.at[pre_part:, :]),
        ],
        local_sem.at[8:12],
    )
    keep_small.wait()
    for copy in small_copies:
        copy.wait_recv()
    for member in range(seq_size):
        vectors[:, member * own_d : (member + 1) * own_d] = small_v[member]
    gain1, bias1, out_bias, gain2, bias2 = [vectors[i : i + 1, :] for i in (0, 1, 4, 5, 6)]
    own_lanes = pl.ds(pl.multiple_of(pre * cols, cols), cols)
    query_bias, value_bias = vectors[2:3, own_lanes], vectors[3:4, own_lanes]
    up_shares = vectors[8:12, own_lanes]
    up_bias = jnp.concatenate(
        [
            up_shares[k : k + 1, i * own_d : (i + 1) * own_d]
            for i in range(seq_size // 4)
            for k in range(4)
        ],
        axis=1,
    )
    chunk = 32

    @pl.loop(0, part // chunk)
    def _(i):
        rows = rows_of(i, chunk)
        value, _, _ = layer_norm_parts(x_v[rows, :].astype(F32), gain1, bias1)
        h1_v[rows, :] = value.astype(BF)

    get_h1.begin()

    @pl.loop(0, part // chunk)
    def _(i):
        rows = rows_of(i, chunk)
        df_v[rows, :] = (active_ref[rows, :] * cot_v[rows, :].astype(F32)).astype(BF)

    get_df.begin()
    slope_bias[...] = up_bias
    turns = range(seq_size // 2 - 1)
    get_qkv.rest()
    for turn in turns:
        get_qkv.poll(turn)
        if turn == 0:
            relay.finish(*relayed)
            get_out.begin()
            get_h1.forward()
        if turn == turns[-2]:
            get_up.begin()
    get_h1.finish()
    get_df.forward()
    get_out.rest()
    load = pltpu.make_async_copy(h1, lhs, local_sem.at[12])
    load.start()
    get_qkv.finish()
    local_copies([(w_qkv, wbuf.at[:, : 3 * cols])], local_sem.at[8:9])
    load.wait()

    @pl.loop(0, 4)
    def _(r):
        member = lax.rem(r, 2) * (xor(pre, 1) - pre) + lax.div(r, 2) * (xor(pre, 2) - pre) + pre
        head_rows = rows_of(member, pre_part)
        tail_rows = pl.ds(pl.multiple_of(4 * pre_part + member * later_part, 64), later_part)

        for j in range(3):
            lanes = slice(j * cols, (j + 1) * cols)
            value = dot_nn(lhs[rows_of(r, part), :], wbuf[:, lanes])
            if j == 0:
                value = (value + query_bias) * (1.0 / math.sqrt(HEAD_DIM))
            if j == 2:
                value = value + value_bias
            value = value.astype(BF)
            qkv_v[head_rows, lanes] = value[:pre_part]
            qkv_v[tail_rows, lanes] = value[pre_part:]

    save_qkv = pltpu.make_async_copy(qkv_v, qkv, local_sem.at[13])
    save_qkv.start()
    for turn in turns:
        get_out.poll(turn)
    get_up.rest()
    get_df.finish()
    pairs = cols // 128

    def attention(first, last):
        @pl.loop(first, last)
        def _(pair):
            attend_pair(pair, cols, qkv_v, codes_q[...], codes_k[...], mixed_v, stats_v)

    attention(0, pairs // 2)
    get_up.poll(0)
    get_down.begin()
    attention(pairs // 2, pairs)
    save_stats = pltpu.make_async_copy(stats_v, stats, local_sem.at[14])
    save_stats.start()
    get_out.finish()
    local_copies([(w_out, wbuf.at[:cols, :])], local_sem.at[8:9])

    def position_rows(r):
        member = xor(pre, r) if r else pre
        return (
            rows_of(member, pre_part),
            pl.ds(pl.multiple_of(4 * pre_part + member * later_part, 64), later_part),
        )

    def out_term(r, store):
        head_rows, tail_rows = position_rows(r)

        @pl.loop(0, D // 512)
        def _(j):
            lanes = rows_of(j, 512)
            store(
                lanes,
                dot_nn(mixed_v[head_rows, :], wbuf[:cols, lanes]),
                dot_nn(mixed_v[tail_rows, :], wbuf[:cols, lanes]),
            )

    def keep_term(slot):
        def store(lanes, head, tail):
            terms_v[slot, :pre_part, lanes] = head.astype(BF)
            terms_v[slot, pre_part:, lanes] = tail.astype(BF)

        return store

    near = [
        remote(terms_v.at[i], near_v.at[i], sum_send.at[i], sum_recv.at[i], **near_id)
        for i in range(2)
    ]
    far = remote(pass_v, far_v, sum_send.at[2], sum_recv.at[2], **far_id)
    out_term(3, keep_term(0))
    near[0].start()
    out_term(1, keep_term(1))
    near[1].start()
    near[0].wait_recv()

    def pass_term(lanes, head, tail):
        pass_v[:pre_part, lanes] = (head + near_v[0, :pre_part, lanes].astype(F32)).astype(BF)
        pass_v[pre_part:, lanes] = (tail + near_v[0, pre_part:, lanes].astype(F32)).astype(BF)

    out_term(2, pass_term)
    far.start()
    near[1].wait_recv()

    def own_term(lanes, head, tail):
        bias = vectors[4:5, lanes]
        attn_v[:pre_part, lanes] = head + near_v[1, :pre_part, lanes].astype(F32) + bias
        attn_v[pre_part:, lanes] = tail + near_v[1, pre_part:, lanes].astype(F32) + bias

    out_term(0, own_term)
    moves = []
    for r in range(4):
        head_rows, tail_rows = position_rows(r)
        moves.append((mixed_v.at[head_rows, :], mixed.at[r * part : r * part + pre_part, :]))
        moves.append((mixed_v.at[tail_rows, :], mixed.at[r * part + pre_part : (r + 1) * part, :]))
    local_copies(moves, local_sem.at[16:24])
    for turn in turns[1:]:
        get_up.poll(turn)
    far.wait_recv()

    @pl.loop(0, part // chunk)
    def _(i):
        rows = rows_of(i, chunk)
        branch = attn_v[rows, :] + far_v[rows, :].astype(F32)
        attn_v[rows, :] = branch
        value, _, _ = layer_norm_parts(x_v[rows, :].astype(F32) + branch, gain2, bias2)
        h2_v[rows, :] = value.astype(BF)

    get_h2.begin()
    save_attn = pltpu.make_async_copy(attn_v, attn, local_sem.at[15])
    save_attn.start()
    get_down.rest()
    get_up.finish()
    load = pltpu.make_async_copy(w_up, wbuf, local_sem.at[12])
    load.start()
    get_h2.finish_near()
    half = slice(0, 2 * part)
    local_copies([(h2.at[half, :], lhs.at[half, :])], local_sem.at[8:9])
    load.wait()

    def up_rows(r):
        rows = rows_of(r, part)

        @pl.loop(0, ff_cols // 512)
        def _(j):
            lanes = rows_of(j, 512)
            upper = dot_nn(lhs[rows, :], wbuf[:, lanes]) + slope_bias[:, lanes]
            cumulative = 0.5 * (1.0 + lax.erf(upper * (1.0 / math.sqrt(2.0))))
            density = jnp.exp(-0.5 * upper * upper) * (1.0 / math.sqrt(2.0 * math.pi))
            acted_v[rows, lanes] = (upper * cumulative).astype(BF)
            slope_v[rows, lanes] = (cumulative + upper * density).astype(BF)

    pl.loop(0, 2)(up_rows)
    get_down.poll(0)
    get_h2.forward()
    get_h2.finish_far()
    for turn in turns[1:-1]:
        get_down.poll(turn)
    half = slice(2 * part, 4 * part)
    local_copies([(h2.at[half, :], lhs.at[half, :])], local_sem.at[8:9])
    pl.loop(2, 4)(up_rows)

    saves = [
        pltpu.make_async_copy(acted_v, acted, local_sem.at[12]),
        pltpu.make_async_copy(slope_v, slope, local_sem.at[8]),
    ]
    for save in saves:
        save.start()
    get_down.poll(turns[-1])
    local_copies([(df, lhs)], local_sem.at[9:10])

    @pl.loop(0, D // 256)
    def _(i):
        lanes = rows_of(i, 256)
        turned = lhs[:, lanes].T

        @pl.loop(0, ff_cols // 512)
        def _(j):
            grad_v[:, rows_of(j, 512)] = dot_nn(turned, acted_v[:, rows_of(j, 512)]).astype(BF)

        save = pltpu.make_async_copy(grad_v, down_grad.at[lanes, :], local_sem.at[9])
        save.start()
        save.wait()

    get_down.finish()
    for save in (*saves, save_qkv, save_stats, save_attn):
        save.wait()
    for item in (get_qkv, get_out, get_up, get_down, get_h1, get_df, get_h2):
        item.drain()
    for copy in (*near, far, *small_copies):
        copy.wait_send()


def forward_pass(seq_size, pre_part, later_part, *operands):
    part = pre_part + later_part
    length = 4 * part
    width = 3 * D // 4
    cols = width // 3
    ff_cols = FF // 4
    own_d = D // seq_size
    hbm = pl.BlockSpec(memory_space=pl.ANY)
    vmem = pl.BlockSpec(memory_space=pltpu.VMEM)

    def out(shape, kind=BF):
        return jax.ShapeDtypeStruct(shape, kind)

    outs = (
        out((D, width)),
        out((cols, D)),
        out((D, ff_cols)),
        out((D, ff_cols)),
        out((length, D)),
        out((length, D)),
        out((length, D)),
        out((length, width)),
        out((length, cols)),
        out((length, cols), F32),
        out((part, D), F32),
        out((length, ff_cols)),
        out((length, ff_cols)),
        out((D, ff_cols)),
        out((16, D), F32),
    )
    dma = pltpu.SemaphoreType.DMA
    return pl.pallas_call(
        functools.partial(forward_kernel, (seq_size, pre_part, later_part)),
        out_shape=outs,
        in_specs=[hbm] * 9 + [vmem] * (len(operands) - 9),
        out_specs=[hbm] * (len(outs) - 1) + [vmem],
        scratch_shapes=[
            pltpu.VMEM((D, max(ff_cols, width)), BF),
            pltpu.VMEM((length, D), BF),
            pltpu.VMEM((length, width), BF),
            pltpu.VMEM((length, cols), BF),
            pltpu.VMEM((length, cols), F32),
            pltpu.VMEM((part, D), BF),
            pltpu.VMEM((part, D), BF),
            pltpu.VMEM((part, D), BF),
            pltpu.VMEM((part, D), BF),
            pltpu.VMEM((part, D), BF),
            pltpu.VMEM((2, part, D), BF),
            pltpu.VMEM((2, part, D), BF),
            pltpu.VMEM((part, D), BF),
            pltpu.VMEM((part, D), BF),
            pltpu.VMEM((part, D), F32),
            pltpu.VMEM((length, ff_cols), BF),
            pltpu.VMEM((length, ff_cols), BF),
            pltpu.VMEM((256, ff_cols), BF),
            pltpu.VMEM((own_d, width), BF),
            pltpu.VMEM((own_d, ff_cols), BF),
            pltpu.VMEM((own_d, ff_cols), BF),
            pltpu.VMEM((own_d // 4, D), BF),
            pltpu.VMEM((seq_size, 16, own_d), F32),
            pltpu.VMEM((1, ff_cols), F32),
            dma((4, 4, seq_size // 2 + 2)),
            dma((4, 4, seq_size // 2)),
            dma((seq_size,)),
            dma((seq_size,)),
            dma((3, 4)),
            dma((3, 4)),
            dma((3,)),
            dma((3,)),
            dma((3,)),
            dma((24,)),
        ],
        compiler_params=pltpu.CompilerParams(
            collective_id=0, has_side_effects=True, vmem_limit_bytes=62 * 2**20
        ),
        cost_estimate=pl.CostEstimate(
            flops=2 * length * D * (width + cols + 2 * ff_cols),
            bytes_accessed=8 * D * ff_cols,
            transcendentals=length * ff_cols,
        ),
        name="forward_pass",
    )(*operands)


class Pool:
    def __init__(self, buffers, count):
        self.buffers, self.count = buffers, count
        self.pending = [Copies() for _ in range(count)]
        self.turn = 0

    def take(self):
        index = self.turn % self.count
        self.turn += 1
        self.pending[index].drain()
        self.pending[index] = Copies()
        return index

    def drain(self):
        for copies in self.pending:
            copies.drain()


class Reduce:
    def __init__(self, grad, near, chain, tail, rows, width, sems, work, size, split=False):
        self.grad, self.near, self.chain, self.tail = grad, near, chain, tail
        self.rows, self.width = rows, width
        self.early = early_rows(rows) if split else 0
        self.first = rows - self.early
        self.whole = rows + self.early
        self.near_send, self.near_recv, self.chain_send, self.chain_recv, self.tail_sem = sems
        self.left, self.right, self.third, self.fourth, self.out, self.pool, self.sem = work
        self.seq = lax.axis_index("seq")
        self.lines = size // 2
        self.line = lax.div(self.seq, jnp.int32(2))
        self.side = lax.rem(self.seq, jnp.int32(2))
        self.sent = Copies()

    def target(self, turn):
        if turn == self.lines - 1:
            return self.line
        return far_line(self.lines, self.line, jnp.int32(turn))

    def block(self, line, other, first, count):
        place = line * 2 + ((1 - self.side) if other else self.side)
        return self.grad.at[pl.ds(pl.multiple_of(place * self.rows + first, 16), count), :]

    def near_slot(self, line, near=None):
        near = self.near if near is None else near
        return near.at[pl.ds(pl.multiple_of(line * self.first, 16), self.first), :]

    def chain_slot(self, slot):
        return self.chain.at[pl.ds(pl.multiple_of(slot * self.whole, 16), self.whole), :]

    def near_copy(self, turn):
        line = self.target(turn)
        return remote(
            self.block(line, True, 0, self.first),
            self.near_slot(line),
            self.near_send.at[turn],
            self.near_recv.at[line],
            seq=xor(self.seq, 1),
        )

    def chain_copy(self, src, turn, slot, to):
        return remote(
            src, self.chain_slot(slot), self.chain_send.at[turn], self.chain_recv.at[slot], seq=to
        )

    def begin(self, *turns):
        for turn in turns:
            self.sent.start(self.near_copy(turn))

    def view(self, ref, first, count):
        return ref.at[first : first + count, : self.width]

    def load_own(self, line):
        copies = [
            pltpu.make_async_copy(
                self.block(line, False, 0, self.rows), self.view(self.left, 0, self.rows), self.sem.at[0]
            )
        ]
        if self.early:
            copies.append(
                pltpu.make_async_copy(
                    self.block(line, True, self.first, self.early),
                    self.view(self.left, self.rows, self.early),
                    self.sem.at[1],
                )
            )
        for copy in copies:
            copy.start()
        return copies

    def load(self, src, ref, count, sem):
        copy = pltpu.make_async_copy(src, self.view(ref, 0, count), self.sem.at[sem])
        copy.start()
        return copy

    def rows_loop(self, first, last, value, store):
        if first == last:
            return

        @pl.loop(first // 16, last // 16)
        def _(i):
            at = (rows_of(i, 16), slice(0, self.width))
            store(at, value(at))

    def step(self, turn, when=None, early=None):
        line = self.target(turn)
        up = line > self.line
        ahead = jnp.where(up, line - self.line, self.line - line)
        base = jnp.where(up, 0, self.lines - 1)
        more = jnp.where(up, self.line > 0, self.line < self.lines - 1)
        slot_in = jnp.minimum(base + ahead, 2 * (self.lines - 1) - 1)
        slot_out = base + ahead - 1
        to = jnp.clip(self.seq + jnp.where(up, 2, -2), 0, 2 * self.lines - 1)
        index = self.pool.take()
        out = self.out.at[index]
        leave = self.chain_copy(out.at[: self.whole, : self.width], turn, slot_out, to)

        def store(at, value):
            out[at] = value.astype(BF)

        def body():
            copies = self.load_own(line)
            if early is None:
                self.near_copy(turn).wait_recv()
            copies.append(self.load(self.near_slot(line, early), self.right, self.first, 2))

            def both(at):
                return self.left[at].astype(F32) + self.right[at].astype(F32)

            def own(at):
                return self.left[at].astype(F32)

            @pl.when(more)
            def _():
                self.chain_copy(out.at[: self.whole, : self.width], turn, slot_in, to).wait_recv()
                third = self.load(self.chain_slot(slot_in), self.third, self.whole, 3)
                for copy in (*copies, third):
                    copy.wait()
                self.rows_loop(
                    0, self.first, lambda at: both(at) + self.third[at].astype(F32), store
                )
                self.rows_loop(
                    self.first, self.whole, lambda at: own(at) + self.third[at].astype(F32), store
                )

            @pl.when(jnp.logical_not(more))
            def _():
                for copy in copies:
                    copy.wait()
                self.rows_loop(0, self.first, both, store)
                self.rows_loop(self.first, self.whole, own, store)

            leave.start()

        if when is None:
            body()
        else:
            pl.when(when)(body)
        self.pool.pending[index].items.append((leave, when))

    def sides(self):
        return ((self.line > 0, 0), (self.line < self.lines - 1, self.lines - 1))

    def settle(self):
        self.near_copy(self.lines - 1).wait_recv()
        for there, slot in self.sides():
            pl.when(there)(
                self.chain_copy(self.view(self.third, 0, self.whole), 0, slot, self.seq).wait_recv
            )

    def tail_copy(self, src):
        return remote(src, self.tail, self.tail_sem.at[0], self.tail_sem.at[1], seq=xor(self.seq, 1))

    def final(self, result):
        copies = self.load_own(self.line)
        copies.append(self.load(self.near_slot(self.line), self.right, self.first, 2))
        side = jnp.where(self.line > 0, 0, self.lines - 1)
        copies.append(self.load(self.chain_slot(side), self.third, self.whole, 3))
        mid = (self.line > 0) & (self.line < self.lines - 1)
        fourth = pltpu.make_async_copy(
            self.chain_slot(self.lines - 1), self.view(self.fourth, 0, self.whole), self.sem.at[4]
        )
        pl.when(mid)(fourth.start)
        index = self.pool.take()
        out = self.out.at[index]

        def put(at, value):
            result[at] = value.astype(BF)

        def put_tail(at, value):
            out[at] = value.astype(BF)

        def loops(refs):
            def sum_of(at):
                return functools.reduce(jnp.add, [ref[at].astype(F32) for ref in refs])

            self.rows_loop(0, self.first, lambda at: sum_of(at) + self.right[at].astype(F32), put)
            self.rows_loop(self.first, self.rows, sum_of, put)
            self.rows_loop(self.rows, self.whole, sum_of, put_tail)

        for copy in copies:
            copy.wait()

        @pl.when(mid)
        def _():
            fourth.wait()
            loops((self.left, self.third, self.fourth))

        pl.when(jnp.logical_not(mid))(lambda: loops((self.left, self.third)))
        if self.early:
            self.pool.pending[index].start(
                self.tail_copy(out.at[self.rows : self.whole, : self.width])
            )

    def last(self, result):
        if not self.early:
            return
        self.tail_copy(self.view(self.third, 0, self.early)).wait_recv()
        self.load(self.tail, self.third, self.early, 3).wait()

        @pl.loop(0, self.early // 16)
        def _(i):
            lanes = slice(0, self.width)
            rows = pl.ds(pl.multiple_of(self.first + i * 16, 16), 16)
            value = result[rows, lanes].astype(F32) + self.third[rows_of(i, 16), lanes].astype(F32)
            result[rows, lanes] = value.astype(BF)

    def drain(self):
        self.sent.drain()


class Sum:
    def __init__(self, terms, near, passed, far, send_sem, recv_sem):
        pre = lax.axis_index("pre")
        near_id, far_id = {"pre": xor(pre, 1)}, {"pre": xor(pre, 2)}
        self.terms, self.near, self.passed = terms, near, passed
        self.near_copies = [
            remote(terms.at[i], near.at[i], send_sem.at[i], recv_sem.at[i], **near_id)
            for i in range(2)
        ]
        self.far_copy = remote(passed, far, send_sem.at[2], recv_sem.at[2], **far_id)

    def run(self, term, keep):
        def store_in(slot):
            def store(rows, lanes, value):
                self.terms[slot, rows, lanes] = value.astype(BF)

            return store

        term(3, store_in(0))
        self.near_copies[0].start()
        term(1, store_in(1))
        self.near_copies[1].start()
        self.near_copies[0].wait_recv()

        def store(rows, lanes, value):
            self.passed[rows, lanes] = (value + self.near[0, rows, lanes].astype(F32)).astype(BF)

        term(2, store)
        self.far_copy.start()
        self.near_copies[1].wait_recv()

        def store(rows, lanes, value):
            keep(rows, lanes, value + self.near[1, rows, lanes].astype(F32))

        term(0, store)

    def drain(self):
        for copy in (*self.near_copies, self.far_copy):
            copy.wait_send()


def columns_grad(left, right, rows, width, tile, save):
    @pl.loop(0, rows // 256)
    def _(i):
        turned = left[:, rows_of(i, 256)].T

        @pl.loop(0, width // 512)
        def _(j):
            tile[:, rows_of(j, 512)] = dot_nn(turned, right[:, rows_of(j, 512)]).astype(BF)

        copy = save(rows_of(i, 256))
        copy.start()
        copy.wait()


def add_rows(target, index, value):
    target[index : index + 1, : value.shape[1]] += jnp.sum(value, axis=0, keepdims=True)


def feed_back_kernel(
    sizes,
    w_down,
    w_up,
    acted,
    df,
    h2,
    slope,
    attn,
    down_grad,
    prefix_in,
    later_in,
    prefix_cot,
    later_cot,
    active_ref,
    vectors,
    near_down,
    chain_down,
    near_up,
    up_grad,
    dattn,
    middle_grad,
    prefix_out,
    later_out,
    sums,
    up_sums,
    wbuf,
    lhs,
    acted_v,
    slope_v,
    du_v,
    x_v,
    cot_v,
    attn_v,
    acc_v,
    ffn_v,
    dattn_v,
    terms_v,
    near_v,
    pass_v,
    far_v,
    ffn_near_v,
    ffn_far_v,
    left_v,
    right_v,
    third_v,
    out_v,
    grad_v,
    twin_send,
    twin_recv,
    chain_send,
    chain_recv,
    early_send,
    early_recv,
    spread_send,
    spread_recv,
    sum_send,
    sum_recv,
    local_sem,
):
    seq_size, pre_part, later_part = sizes
    part = pre_part + later_part
    length = 4 * part
    ff_cols = w_up.shape[1]
    gain2 = vectors[5:6, :]
    wide = wide_masks(seq_size)
    lines = seq_size // 2
    line = lax.div(lax.axis_index("seq"), jnp.int32(2))
    end = (line == 0) | (line == lines - 1)
    mid = jnp.logical_not(end)
    turns = range(lines - 1)
    pool = Pool(out_v, 3)
    work = (left_v, right_v, third_v, None, out_v, pool, local_sem.at[12:16])
    put_down = Reduce(
        down_grad,
        near_down,
        chain_down,
        None,
        D // seq_size,
        ff_cols,
        (twin_send, twin_recv, chain_send, chain_recv, None),
        work,
        seq_size,
    )
    put_up = Reduce(
        up_grad,
        near_up,
        None,
        None,
        D // seq_size,
        ff_cols,
        (early_send, early_recv, None, None, None),
        work,
        seq_size,
    )
    get_dattn = Spread(dattn_v, dattn, part, spread_send, spread_recv, local_sem.at[2])
    sum_f = Sum(terms_v, ffn_near_v, pass_v, ffn_far_v, sum_send.at[0], sum_recv.at[0])
    sum_dh2 = Sum(terms_v, near_v, pass_v, far_v, sum_send.at[1], sum_recv.at[1])

    greet((1, *wide))
    put_down.begin(*turns, lines - 1)
    loads = [
        pltpu.make_async_copy(src, dst, local_sem.at[3 + i])
        for i, (src, dst) in enumerate(
            [
                (w_down, wbuf),
                (acted, acted_v),
                (df, lhs),
                (slope, slope_v),
                (prefix_in, x_v.at[:pre_part, :]),
                (later_in, x_v.at[pre_part:, :]),
                (prefix_cot, cot_v.at[:pre_part, :]),
                (later_cot, cot_v.at[pre_part:, :]),
                (attn, attn_v),
            ]
        )
    ]
    for load in loads:
        load.start()
    sums[...] = jnp.zeros_like(sums)
    up_sums[...] = jnp.zeros_like(up_sums)
    for load in loads[:2]:
        load.wait()

    def f_term(r, store):
        @pl.loop(0, D // 512)
        def _(j):
            store(
                slice(0, part),
                rows_of(j, 512),
                dot_nt(acted_v[r * part : (r + 1) * part, :], wbuf[rows_of(j, 512), :]),
            )

    def keep_f(rows, lanes, value):
        ffn_v[rows, lanes] = value

    sum_f.run(f_term, keep_f)
    for load in loads[2:]:
        load.wait()
    put_down.step(0, end)

    @pl.loop(0, 4)
    def _(r):
        rows = rows_of(r, part)

        @pl.loop(0, ff_cols // 512)
        def _(j):
            lanes = rows_of(j, 512)
            value = dot_nn(lhs[rows, :], wbuf[:, lanes])
            du_v[rows, lanes] = (value * slope_v[rows, lanes].astype(F32)).astype(BF)

    load = pltpu.make_async_copy(w_up, wbuf, local_sem.at[3])
    load.start()
    load_h2 = pltpu.make_async_copy(h2, lhs, local_sem.at[4])
    load_h2.start()
    for copy in sum_f.near_copies:
        copy.wait_send()
    sum_f.far_copy.wait_send()
    load.wait()

    def dh2_term(r, store):
        @pl.loop(0, D // 512)
        def _(j):
            store(
                slice(0, part),
                rows_of(j, 512),
                dot_nt(du_v[r * part : (r + 1) * part, :], wbuf[rows_of(j, 512), :]),
            )

    def keep_dh2(rows, lanes, value):
        acc_v[rows, lanes] = value

    sum_dh2.run(dh2_term, keep_dh2)
    put_down.step(1, end)
    put_down.step(0, mid)
    load_h2.wait()
    columns_grad(
        lhs,
        du_v,
        D,
        ff_cols,
        grad_v,
        lambda rows: pltpu.make_async_copy(grad_v, up_grad.at[rows, :], local_sem.at[3]),
    )
    put_up.begin(0)
    for turn in turns[2:]:
        put_down.step(turn, end)
    chunk = 32
    sum_f.far_copy.wait_recv()

    @pl.loop(0, part // chunk)
    def _(i):
        rows = rows_of(i, chunk)
        live = active_ref[rows, :]
        ffn = ffn_v[rows, :] + ffn_far_v[rows, :].astype(F32) + vectors[7:8, :]
        branch = attn_v[rows, :]
        result = x_v[rows, :].astype(F32) + live * (branch + ffn)
        add_rows(sums, 4, live * result * result)
        add_rows(sums, 5, live * branch * branch)
        add_rows(sums, 6, live * ffn * ffn)
        acted_v[rows, :] = result.astype(BF)

    saves = [
        pltpu.make_async_copy(acted_v.at[:pre_part, :], prefix_out, local_sem.at[4]),
        pltpu.make_async_copy(acted_v.at[pre_part:part, :], later_out, local_sem.at[5]),
    ]
    for save in saves:
        save.start()
    for turn in turns[1:]:
        put_down.step(turn, mid)
    sum_dh2.far_copy.wait_recv()

    @pl.loop(0, part // chunk)
    def _(i):
        rows = rows_of(i, chunk)
        grad = acc_v[rows, :] + far_v[rows, :].astype(F32)
        middle = x_v[rows, :].astype(F32) + attn_v[rows, :]
        _, normed, scaling = layer_norm_parts(middle, gain2, 0.0)
        back = norm_back(grad, normed, scaling, gain2)
        acc_v[rows, :] = back
        direct = active_ref[rows, :] * cot_v[rows, :].astype(F32)
        value = (direct + back).astype(BF)
        dattn_v[rows, :] = value
        add_rows(sums, 0, value.astype(F32))
        add_rows(sums, 1, grad * normed)
        add_rows(sums, 2, grad)
        add_rows(sums, 3, direct)

    get_dattn.begin()
    saves.append(pltpu.make_async_copy(acc_v, middle_grad, local_sem.at[3]))
    saves[-1].start()

    @pl.loop(0, length // chunk)
    def _(i):
        add_rows(up_sums, 0, du_v[rows_of(i, chunk), :].astype(F32))

    get_dattn.forward()
    put_down.settle()
    get_dattn.finish()
    for save in saves:
        save.wait()
    put_up.near_copy(0).wait_recv()
    for item in (put_down, put_up, get_dattn, sum_dh2, pool):
        item.drain()


def feed_back(seq_size, pre_part, later_part, *operands):
    part = pre_part + later_part
    length = 4 * part
    w_up = operands[1]
    ff_cols = w_up.shape[1]
    own_d = D // seq_size
    hbm = pl.BlockSpec(memory_space=pl.ANY)
    vmem = pl.BlockSpec(memory_space=pltpu.VMEM)

    def out(shape, kind=BF):
        return jax.ShapeDtypeStruct(shape, kind)

    lines = seq_size // 2
    near_rows = lines * own_d
    whole = own_d
    chains = 2 * (lines - 1)
    outs = (
        out((near_rows, ff_cols)),
        out((chains * whole, ff_cols)),
        out((near_rows, ff_cols)),
        out((D, ff_cols)),
        out((length, D)),
        out((part, D), F32),
        out((pre_part, D)),
        out((later_part, D)),
        out((8, D), F32),
        out((8, ff_cols), F32),
    )
    dma = pltpu.SemaphoreType.DMA
    return pl.pallas_call(
        functools.partial(feed_back_kernel, (seq_size, pre_part, later_part)),
        out_shape=outs,
        in_specs=[hbm] * 12 + [vmem] * (len(operands) - 12),
        out_specs=[hbm] * 8 + [vmem] * 2,
        scratch_shapes=[
            pltpu.VMEM((D, ff_cols), BF),
            pltpu.VMEM((length, D), BF),
            pltpu.VMEM((length, ff_cols), BF),
            pltpu.VMEM((length, ff_cols), BF),
            pltpu.VMEM((length, ff_cols), BF),
            pltpu.VMEM((part, D), BF),
            pltpu.VMEM((part, D), BF),
            pltpu.VMEM((part, D), F32),
            pltpu.VMEM((part, D), F32),
            pltpu.VMEM((part, D), F32),
            pltpu.VMEM((part, D), BF),
            pltpu.VMEM((2, part, D), BF),
            pltpu.VMEM((2, part, D), BF),
            pltpu.VMEM((part, D), BF),
            pltpu.VMEM((part, D), BF),
            pltpu.VMEM((2, part, D), BF),
            pltpu.VMEM((part, D), BF),
            pltpu.VMEM((whole, ff_cols), BF),
            pltpu.VMEM((own_d, ff_cols), BF),
            pltpu.VMEM((whole, ff_cols), BF),
            pltpu.VMEM((3, whole, ff_cols), BF),
            pltpu.VMEM((256, ff_cols), BF),
            dma((lines,)),
            dma((lines,)),
            dma((lines,)),
            dma((chains,)),
            dma((lines,)),
            dma((lines,)),
            dma((4,)),
            dma((4,)),
            dma((2, 3)),
            dma((2, 3)),
            dma((16,)),
        ],
        compiler_params=pltpu.CompilerParams(
            collective_id=1, has_side_effects=True, vmem_limit_bytes=62 * 2**20
        ),
        cost_estimate=pl.CostEstimate(
            flops=2 * length * D * 3 * ff_cols,
            bytes_accessed=8 * D * ff_cols,
            transcendentals=length,
        ),
        name="feed_back",
    )(*operands)


def attend_back_pair(pair, cols, qkv, do, stats, codes_q, codes_k, dq_all, dk_all, dv_all, dqkv):
    lanes = [pl.ds(pl.multiple_of(third * cols + pair * 128, 128), 128) for third in range(3)]
    dk_all[...] = jnp.zeros_like(dk_all)
    dv_all[...] = jnp.zeros_like(dv_all)
    blocks = qkv.shape[0] // TILE
    for block in range(blocks):
        rows = slice(block * TILE, (block + 1) * TILE)
        both_q = qkv[rows, lanes[0]]
        both_do = do[rows, lanes_of(pair)]
        both_levels = stats[rows, lanes_of(pair)]
        parts = []
        for head in range(2):
            queries = head_lanes(both_q, head)
            grads = head_lanes(both_do, head)
            level = both_levels[:, head * HEAD_DIM : head * HEAD_DIM + 1]
            probs = []
            dprobs = []
            for tile in range(block + 1):
                keys = slice(tile * TILE, (tile + 1) * TILE)
                scores = masked_scores(
                    block, dot_nt(queries, qkv[keys, lanes[1]]), tile, codes_q, codes_k
                )
                probs.append(jnp.exp(scores - level))
                dprobs.append(dot_nt(grads, qkv[keys, lanes[2]]))
            delta = functools.reduce(
                jnp.add, [jnp.sum(a * b, axis=1, keepdims=True) for a, b in zip(probs, dprobs)]
            )
            dq = None
            for tile in range(block + 1):
                keys = slice(tile * TILE, (tile + 1) * TILE)
                ds = (probs[tile] * (dprobs[tile] - delta)).astype(BF)
                part = dot_nn(ds, qkv[keys, lanes[1]])
                dq = part if dq is None else dq + part
                dk_all[keys, :] += dot_tn(ds, queries)
                dv_all[keys, :] += dot_tn(probs[tile].astype(BF), grads)
            parts.append(dq)
        dq_all[rows, :] = join_heads(*parts) * (1.0 / math.sqrt(HEAD_DIM))
    for lane, source in zip(lanes, (dq_all, dk_all, dv_all)):
        dqkv[:, lane] = source[...].astype(BF)


def attend_back_kernel(
    sizes,
    w_qkv,
    w_out,
    h1,
    qkv,
    stats,
    mixed,
    dattn,
    middle_grad,
    up_grad,
    down_grad,
    near_down,
    chain_down,
    early_up,
    prefix_in,
    later_in,
    prefix_cot,
    later_cot,
    active_ref,
    vectors,
    feed_sums,
    up_sums,
    codes_q,
    codes_k,
    fin_down,
    fin_up,
    fin_qkv,
    fin_out,
    tail_down,
    near_up,
    chain_up,
    tail_up,
    near_out,
    chain_out,
    tail_out,
    near_qkv,
    chain_qkv,
    tail_qkv,
    out_grad,
    qkv_grad,
    prefix_grad,
    later_grad,
    sums,
    wbuf,
    lhs,
    qkv_v,
    stats_v,
    do_v,
    mixed_v,
    dqkv_v,
    dq_v,
    dk_v,
    dv_v,
    x_v,
    cot_v,
    middle_v,
    acc_v,
    terms_v,
    near_v,
    pass_v,
    far_v,
    left_v,
    right_v,
    third_v,
    fourth_v,
    out_v,
    grad_v,
    res_down,
    res_up,
    res_qkv,
    res_out,
    moved_out,
    qkv_sums,
    sums_land,
    total_send,
    total_recv,
    relay_sem,
    twin_send,
    twin_recv,
    chain_send,
    chain_recv,
    tail_sem,
    spread_send,
    spread_recv,
    sum_send,
    sum_recv,
    local_sem,
):
    seq_size, pre_part, later_part = sizes
    part = pre_part + later_part
    length = 4 * part
    width = w_qkv.shape[1]
    cols = width // 3
    ff_cols = up_grad.shape[1]
    own_d = D // seq_size
    own_o = cols // seq_size
    pre = lax.axis_index("pre")
    wide = wide_masks(seq_size)
    lines = seq_size // 2
    line = lax.div(lax.axis_index("seq"), jnp.int32(2))
    end = (line == 0) | (line == lines - 1)
    mid = jnp.logical_not(end)
    turns = range(lines - 1)
    pool = Pool(out_v, 3)
    work = (left_v, right_v, third_v, fourth_v, out_v, pool, local_sem.at[24:29])

    def reduce_of(i, grad, near, chain, tail, rows, columns, split=False):
        j = max(i, 1) - 1
        sems = (twin_send.at[j], twin_recv.at[j], chain_send.at[j], chain_recv.at[j], tail_sem.at[i])
        return Reduce(grad, near, chain, tail, rows, columns, sems, work, seq_size, split)

    put_down = reduce_of(0, down_grad, near_down, chain_down, tail_down, own_d, ff_cols)
    put_up = reduce_of(1, up_grad, near_up, chain_up, tail_up, own_d, ff_cols)
    put_out = reduce_of(2, out_grad, near_out, chain_out, tail_out, own_o, D)
    put_qkv = reduce_of(3, qkv_grad, near_qkv, chain_qkv, tail_qkv, own_d, width)

    def spread_of(i, own, land):
        return Spread(own, land, own_d, spread_send.at[i], spread_recv.at[i], local_sem.at[2 + i])

    get_down = spread_of(0, res_down, fin_down)
    get_up = spread_of(1, res_up, fin_up)
    get_qkv = spread_of(2, res_qkv, fin_qkv)
    sum_dh1 = Sum(terms_v, near_v, pass_v, far_v, sum_send, sum_recv)
    chunk = 32

    relay = Relay(seq_size, relay_sem.at[0], relay_sem.at[1], relay_sem.at[2])
    relayed = (res_out, moved_out, relay.back)
    get_out = Spread(
        moved_out, fin_out, own_o, spread_send.at[3], spread_recv.at[3], local_sem.at[20]
    )
    bits = [1 << i for i in range(seq_size.bit_length() - 1)]
    greet(sorted({*wide, *bits}), relay)
    put_up.begin(*turns[1:])
    stages = [
        remote(sums, sums_land.at[i], total_send.at[i], total_recv.at[i], **target)
        for i, target in enumerate(
            [{"pre": xor(pre, 1)}, {"pre": xor(pre, 2)}]
            + [{"seq": xor(lax.axis_index("seq"), bit)} for bit in bits]
        )
    ]

    def add_stage(i, onward=True):
        stages[i].wait_recv()
        stages[i].wait_send()
        sums[...] += sums_land[i]
        if onward:
            stages[i + 1].start()

    def load_all(first, *pairs):
        copies = [
            pltpu.make_async_copy(src, dst, local_sem.at[first + i])
            for i, (src, dst) in enumerate(pairs)
        ]
        for copy in copies:
            copy.start()
        return copies

    def wait_all(copies):
        for copy in copies:
            copy.wait()

    loads = load_all(5, (w_out, wbuf.at[:cols, :]), (dattn, lhs))
    more = load_all(
        8,
        (prefix_in, x_v.at[:pre_part, :]),
        (later_in, x_v.at[pre_part:, :]),
        (prefix_cot, cot_v.at[:pre_part, :]),
        (later_cot, cot_v.at[pre_part:, :]),
        (middle_grad, middle_v),
        (qkv, qkv_v),
        (stats, stats_v),
        (mixed, mixed_v),
    )
    sums[...] = jnp.zeros_like(sums)
    qkv_sums[...] = jnp.zeros_like(qkv_sums)
    put_up.step(0, end, early_up)
    put_down.final(res_down)
    get_down.begin()
    def keep(rows, lanes, value):
        acc_v[rows, lanes] = value

    wait_all(loads)
    wait_all(more)

    def position_rows(r):
        member = lax.rem(r, 2) * (xor(pre, 1) - pre) + lax.div(r, 2) * (xor(pre, 2) - pre) + pre
        return (
            rows_of(member, pre_part),
            pl.ds(pl.multiple_of(4 * pre_part + member * later_part, 64), later_part),
        )

    @pl.loop(0, 4)
    def _(r):
        head_rows, tail_rows = position_rows(r)
        value = dot_nt(lhs[rows_of(r, part), :], wbuf[:cols, :]).astype(BF)
        do_v[head_rows, :] = value[:pre_part]
        do_v[tail_rows, :] = value[pre_part:]

    columns_grad(
        mixed_v,
        lhs,
        cols,
        D,
        grad_v,
        lambda rows: pltpu.make_async_copy(grad_v.at[:, :D], out_grad.at[rows, :], local_sem.at[5]),
    )
    put_out.begin(*turns)
    put_up.begin(lines - 1)
    put_out.begin(lines - 1)
    loads = load_all(5, (w_qkv, wbuf.at[:, :width]))
    for r in range(4):
        head_rows, tail_rows = position_rows(jnp.int32(r))
        loads += load_all(
            8 + 2 * r,
            (h1.at[r * part : r * part + pre_part, :], lhs.at[head_rows, :]),
            (h1.at[r * part + pre_part : (r + 1) * part, :], lhs.at[tail_rows, :]),
        )
    pairs = cols // 128

    def attention(first, last):
        @pl.loop(first, last)
        def _(pair):
            attend_back_pair(
                pair,
                cols,
                qkv_v,
                do_v,
                stats_v,
                codes_q[...],
                codes_k[...],
                dq_v,
                dk_v,
                dv_v,
                dqkv_v,
            )

    put_up.step(0, mid, early_up)
    attention(0, pairs // 2)
    put_up.step(1, end)
    attention(pairs // 2, pairs)
    for turn in turns[2:]:
        put_up.step(turn, end)
    for turn in turns[1:]:
        put_up.step(turn, mid)
    get_down.forward()
    wait_all(loads)
    columns_grad(
        lhs,
        dqkv_v,
        D,
        width,
        grad_v,
        lambda rows: pltpu.make_async_copy(
            grad_v.at[:, :width], qkv_grad.at[rows, :], local_sem.at[5]
        ),
    )
    put_qkv.begin(*turns, lines - 1)
    get_down.finish()
    for turn in turns:
        put_out.step(turn, end)

    def dh1_term(r, store):
        head_rows, tail_rows = position_rows(jnp.int32(r))

        @pl.loop(0, D // 512)
        def _(j):
            weights = wbuf[rows_of(j, 512), :width]
            store(slice(0, pre_part), rows_of(j, 512), dot_nt(dqkv_v[head_rows, :], weights))
            store(slice(pre_part, part), rows_of(j, 512), dot_nt(dqkv_v[tail_rows, :], weights))

    sum_dh1.run(dh1_term, keep)

    @pl.loop(0, length // chunk)
    def _(i):
        add_rows(qkv_sums, 0, dqkv_v[rows_of(i, chunk), :].astype(F32))

    put_qkv.step(0, end)
    for turn in turns:
        put_out.step(turn, mid)
    put_up.settle()
    put_up.final(res_up)
    put_qkv.step(1, end)
    put_up.last(res_up)
    get_up.begin()
    put_qkv.step(0, mid)
    sum_dh1.far_copy.wait_recv()

    @pl.loop(0, part // chunk)
    def _(i):
        rows = rows_of(i, chunk)
        grad = acc_v[rows, :] + far_v[rows, :].astype(F32)
        _, normed, scaling = layer_norm_parts(x_v[rows, :].astype(F32), vectors[0:1, :], 0.0)
        back = norm_back(grad, normed, scaling, vectors[0:1, :])
        add_rows(sums, 0, grad * normed)
        add_rows(sums, 1, grad)
        value = cot_v[rows, :].astype(F32) + middle_v[rows, :] + back
        terms_rows = value.astype(BF)
        x_v[rows, :] = terms_rows

    saves = load_all(6, (x_v.at[:pre_part, :], prefix_grad), (x_v.at[pre_part:, :], later_grad))
    own_lanes = pl.ds(pl.multiple_of(pre * cols, cols), cols)
    sums[2:5, :] = feed_sums[4:7, :]
    sums[5:9, :] = feed_sums[:4, :]
    sums[9:10, own_lanes] = qkv_sums[0:1, :cols]
    sums[10:11, own_lanes] = qkv_sums[0:1, 2 * cols :]
    for k in range(4):
        sums[11 + k : 12 + k, own_lanes] = jnp.concatenate(
            [
                up_sums[0:1, (i * 4 + k) * own_d : (i * 4 + k + 1) * own_d]
                for i in range(seq_size // 4)
            ],
            axis=1,
        )
    sums[15:16, :] = jnp.zeros((1, D), F32) + jnp.sum(active_ref[...])
    stages[0].start()
    for turn in turns[2:]:
        put_qkv.step(turn, end)
    put_out.settle()
    put_out.final(res_out)
    add_stage(0)
    wait_all(saves)
    put_out.last(res_out)
    relay.begin(*relayed)
    for turn in turns[1:]:
        put_qkv.step(turn, mid)
    add_stage(1, False)
    get_up.forward()
    relay.finish(*relayed)
    get_out.begin()
    put_qkv.settle()
    put_qkv.final(res_qkv)
    put_qkv.last(res_qkv)
    get_qkv.begin()
    stages[2].start()
    get_out.forward()
    get_up.finish()
    for i in range(2, len(stages)):
        add_stage(i, i + 1 < len(stages))
    get_out.finish()
    get_qkv.forward()
    get_qkv.finish()
    for item in (put_up, put_out, put_qkv, get_down, get_up, get_out, get_qkv, sum_dh1, pool):
        item.drain()


def attend_back(seq_size, pre_part, later_part, *operands):
    part = pre_part + later_part
    length = 4 * part
    width = operands[0].shape[1]
    cols = width // 3
    ff_cols = FF // 4
    own_d = D // seq_size
    own_o = cols // seq_size
    lines = seq_size // 2
    chains = 2 * (lines - 1)
    early_d, early_o = 0, 0
    least = 16

    def landings(rows, early, columns):
        return (
            out((lines * (rows - early), columns)),
            out((chains * (rows + early), columns)),
            out((max(early, least), columns)),
        )

    hbm = pl.BlockSpec(memory_space=pl.ANY)
    vmem = pl.BlockSpec(memory_space=pltpu.VMEM)

    def out(shape, kind=BF):
        return jax.ShapeDtypeStruct(shape, kind)

    outs = (
        out((4 * own_d, ff_cols)),
        out((4 * own_d, ff_cols)),
        out((4 * own_d, width)),
        out((4 * own_o, D)),
        out((max(early_d, least), ff_cols)),
        *landings(own_d, early_d, ff_cols),
        *landings(own_o, early_o, D),
        *landings(own_d, 0, width),
        out((cols, D)),
        out((D, width)),
        out((pre_part, D)),
        out((later_part, D)),
        out((16, D), F32),
    )
    most = max(ff_cols, D, width)
    stages = 1 + seq_size.bit_length()
    dma = pltpu.SemaphoreType.DMA
    return pl.pallas_call(
        functools.partial(attend_back_kernel, (seq_size, pre_part, later_part)),
        out_shape=outs,
        in_specs=[hbm] * 17 + [vmem] * (len(operands) - 17),
        out_specs=[hbm] * (len(outs) - 1) + [vmem],
        scratch_shapes=[
            pltpu.VMEM((D, most), BF),
            pltpu.VMEM((length, D), BF),
            pltpu.VMEM((length, width), BF),
            pltpu.VMEM((length, cols), F32),
            pltpu.VMEM((length, cols), BF),
            pltpu.VMEM((length, cols), BF),
            pltpu.VMEM((length, width), BF),
            pltpu.VMEM((length, 128), F32),
            pltpu.VMEM((length, 128), F32),
            pltpu.VMEM((length, 128), F32),
            pltpu.VMEM((part, D), BF),
            pltpu.VMEM((part, D), BF),
            pltpu.VMEM((part, D), F32),
            pltpu.VMEM((part, D), F32),
            pltpu.VMEM((2, part, D), BF),
            pltpu.VMEM((2, part, D), BF),
            pltpu.VMEM((part, D), BF),
            pltpu.VMEM((part, D), BF),
            pltpu.VMEM((own_d + early_d, most), BF),
            pltpu.VMEM((own_d, most), BF),
            pltpu.VMEM((own_d + early_d, most), BF),
            pltpu.VMEM((own_d + early_d, most), BF),
            pltpu.VMEM((3, own_d + early_d, most), BF),
            pltpu.VMEM((256, most), BF),
            pltpu.VMEM((own_d, ff_cols), BF),
            pltpu.VMEM((own_d, ff_cols), BF),
            pltpu.VMEM((own_d, width), BF),
            pltpu.VMEM((own_o, D), BF),
            pltpu.VMEM((own_o, D), BF),
            pltpu.VMEM((8, width), F32),
            pltpu.VMEM((stages, 16, D), F32),
            dma((stages,)),
            dma((stages,)),
            dma((3,)),
            dma((3, lines)),
            dma((3, lines)),
            dma((3, lines)),
            dma((3, chains)),
            dma((4, 2)),
            dma((4, 4)),
            dma((4, 4)),
            dma((3,)),
            dma((3,)),
            dma((29,)),
        ],
        compiler_params=pltpu.CompilerParams(
            collective_id=2, has_side_effects=True, vmem_limit_bytes=63 * 2**20
        ),
        cost_estimate=pl.CostEstimate(
            flops=2 * length * D * (2 * width + ff_cols),
            bytes_accessed=8 * D * ff_cols,
            transcendentals=length * length,
        ),
        name="attend_back",
    )(*operands)


def assemble_kernel(place_ref, down, up, qkv, out, down_full, up_full, qkv_full, out_full):
    qkv_full[...] = qkv[...].astype(F32)

    @pl.when(pl.program_id(1) == 0)
    def _():
        down_full[...] = down[...].astype(F32)
        up_full[...] = up[...].astype(F32)
        out_full[...] = out[...].astype(F32)


def assemble(place, down, up, qkv, out):
    rows, ff_cols = down.shape[0] // 4, down.shape[1]
    cols = qkv.shape[1] // 3
    out_rows = out.shape[0] // 4

    def member(slot, place_ref):
        return jnp.bitwise_xor(slot, place_ref[0])

    wide_in = pl.BlockSpec((rows, ff_cols), lambda slot, third, p: (slot, 0))
    wide_out = pl.BlockSpec((rows, ff_cols), lambda slot, third, p: (0, member(slot, p)))
    return pl.pallas_call(
        assemble_kernel,
        out_shape=(
            jax.ShapeDtypeStruct((rows, 4 * ff_cols), F32),
            jax.ShapeDtypeStruct((rows, 4 * ff_cols), F32),
            jax.ShapeDtypeStruct((rows, 12 * cols), F32),
            jax.ShapeDtypeStruct((4 * out_rows, out.shape[1]), F32),
        ),
        grid_spec=pltpu.PrefetchScalarGridSpec(
            num_scalar_prefetch=1,
            grid=(4, 3),
            in_specs=[
                wide_in,
                wide_in,
                pl.BlockSpec((rows, cols), lambda slot, third, p: (slot, third)),
                pl.BlockSpec((out_rows, out.shape[1]), lambda slot, third, p: (slot, 0)),
            ],
            out_specs=[
                wide_out,
                wide_out,
                pl.BlockSpec(
                    (rows, cols), lambda slot, third, p: (0, third * 4 + member(slot, p))
                ),
                pl.BlockSpec(
                    (out_rows, out.shape[1]), lambda slot, third, p: (member(slot, p), 0)
                ),
            ],
        ),
        compiler_params=pltpu.CompilerParams(vmem_limit_bytes=62 * 2**20),
        name="assemble",
    )(place, down, up, qkv, out)


def on_device(
    prefix_in,
    later_in,
    doc_lengths,
    doc_exit,
    token_skip,
    first_gain,
    first_bias,
    qkv_weight,
    query_bias,
    value_bias,
    out_weight,
    out_bias,
    second_gain,
    second_bias,
    up_weight,
    up_bias,
    down_weight,
    down_bias,
    prefix_cot,
    later_cot,
):
    pre_part = prefix_in.shape[1]
    later_part = later_in.shape[1]
    part = pre_part + later_part
    parts = lax.axis_size("pre")
    place = lax.axis_index("pre")
    seq_count = lax.axis_size("seq")
    seq_place = lax.axis_index("seq")
    own_d = D // seq_count
    cols = D // parts

    vectors_in = [
        first_gain,
        first_bias,
        query_bias,
        value_bias,
        out_bias,
        second_gain,
        second_bias,
        down_bias,
    ] + [up_bias[k * own_d : (k + 1) * own_d] for k in range(4)]
    row = lax.broadcasted_iota(jnp.int32, (16, own_d), 0)
    small = jnp.zeros((16, own_d), F32)
    for i, vector in enumerate(vectors_in):
        small = jnp.where(row == i, vector.astype(F32)[None, :], small)

    doc_id, live = token_tables(doc_lengths, doc_exit, token_skip)
    live_here = lax.dynamic_slice_in_dim(live[0], place * later_part, later_part, 0)
    active = jnp.concatenate([jnp.ones((pre_part,), F32), live_here.astype(F32)])[:, None]
    codes_q = jnp.concatenate([jnp.full((PRE,), -1, jnp.int32), doc_id[0]])[:, None]
    codes_k = jnp.concatenate(
        [jnp.full((PRE,), -1, jnp.int32), jnp.where(live[0], doc_id[0], -2)]
    )[None, :]

    (w_qkv, w_out, w_up, w_down, h1, df, h2, qkv, mixed, stats, attn, acted, slope, down_grad, vectors) = forward_pass(
        seq_count,
        pre_part,
        later_part,
        small,
        qkv_weight,
        out_weight,
        up_weight,
        down_weight,
        prefix_in[0],
        later_in[0],
        prefix_cot[0],
        later_cot[0],
        active,
        codes_q,
        codes_k,
    )

    rows_in = (prefix_in[0], later_in[0], prefix_cot[0], later_cot[0], active)
    (near_down, chain_down, early_up, up_grad, dattn, middle_grad, prefix_out, later_out, feed_sums, up_sums) = feed_back(
        seq_count,
        pre_part,
        later_part,
        w_down,
        w_up,
        acted,
        df,
        h2,
        slope,
        attn,
        down_grad,
        *rows_in,
        vectors,
    )
    (fin_down, fin_up, fin_qkv, fin_out, *_, prefix_grad, later_grad, sums) = attend_back(
        seq_count,
        pre_part,
        later_part,
        w_qkv,
        w_out,
        h1,
        qkv,
        stats,
        mixed,
        dattn,
        middle_grad,
        up_grad,
        down_grad,
        near_down,
        chain_down,
        early_up,
        *rows_in,
        vectors,
        feed_sums,
        up_sums,
        codes_q,
        codes_k,
    )

    down_full, up_full, qkv_full, out_full = assemble(
        place.reshape(1).astype(jnp.int32), fin_down, fin_up, fin_qkv, fin_out
    )
    mine = lax.dynamic_slice_in_dim(sums, seq_place * own_d, own_d, 1)
    residual_rms = jnp.sqrt(jnp.sum(sums[2:5], axis=1) / (sums[15, 0] * D))
    return (
        prefix_out[None],
        later_out[None],
        prefix_grad[None],
        later_grad[None],
        mine[0],
        mine[1],
        qkv_full,
        mine[9],
        mine[10],
        out_full,
        mine[5],
        mine[6],
        mine[7],
        up_full,
        mine[11:15].reshape(-1),
        down_full,
        mine[8],
        residual_rms,
    )


def solution(mesh):
    placed = (
        P("seq", "pre", None),
        P("seq", "pre", None),
        P("seq", None),
        P("seq", None),
        P("seq", None),
        P("seq"),
        P("seq"),
        P("seq", None),
        P("seq"),
        P("seq"),
        P("seq", None),
        P("seq"),
        P("seq"),
        P("seq"),
        P("seq", None),
        P("seq"),
        P("seq", None),
        P("seq"),
        P("seq", "pre", None),
        P("seq", "pre", None),
    )
    return jax.shard_map(
        on_device,
        mesh=mesh,
        in_specs=placed,
        out_specs=(
            P("seq", "pre", None),
            P("seq", "pre", None),
            P("seq", "pre", None),
            P("seq", "pre", None),
            P("seq"),
            P("seq"),
            P("seq", None),
            P("seq"),
            P("seq"),
            P("seq", None),
            P("seq"),
            P("seq"),
            P("seq"),
            P("seq", None),
            P("seq"),
            P("seq", None),
            P("seq"),
            P(),
        ),
        check_vma=False,
    )
```

```python
import functools
import math

import jax
import jax.numpy as jnp
from jax import lax
from jax.experimental import pallas as pl
from jax.experimental.pallas import tpu as pltpu
from jax.sharding import PartitionSpec as P

D = 2048
HEADS = 32
HEAD_DIM = 64
FF = 8192
LAYER = 12
PRE = 512

EPS = 1e-05
NEG = -1e30
BF = jnp.bfloat16
F32 = jnp.float32
TILE = 256


def layer_norm_parts(values, gain, bias):
    mean = jnp.mean(values, axis=-1, keepdims=True)
    centred = values - mean
    variance = jnp.mean(centred * centred, axis=-1, keepdims=True)
    scaling = lax.rsqrt(variance + EPS)
    normed = centred * scaling
    return (normed * gain + bias, normed, scaling)


def norm_back(grad, normed, scaling, gain):
    scaled = grad * gain
    inner = jnp.mean(scaled, axis=-1, keepdims=True)
    cross = jnp.mean(scaled * normed, axis=-1, keepdims=True)
    return scaling * (scaled - inner - normed * cross)


def token_tables(doc_lengths, doc_exit, token_skip):
    order = jnp.arange(doc_lengths.shape[-1], dtype=jnp.int32)
    earlier = order[None, :] < order[:, None]
    starts = jnp.sum(
        jnp.where(earlier, doc_lengths[..., None, :], 0), axis=-1, dtype=jnp.int32
    )
    places = jnp.arange(token_skip.shape[-1], dtype=jnp.int32)
    doc_id = (
        jnp.sum(
            (places[:, None] >= starts[..., None, :]).astype(jnp.int32), axis=-1, dtype=jnp.int32
        )
        - 1
    )
    live_doc = doc_exit > LAYER
    live = jnp.any((doc_id[..., None] == order) & live_doc[..., None, :], axis=-1) & (
        token_skip == 0
    )
    return (doc_id, live)


def dot_nt(a, b):
    return lax.dot_general(a, b, (((1,), (1,)), ((), ())), preferred_element_type=F32)


def dot_nn(a, b):
    return lax.dot_general(a, b, (((1,), (0,)), ((), ())), preferred_element_type=F32)


def dot_tn(a, b):
    return lax.dot_general(a, b, (((0,), (0,)), ((), ())), preferred_element_type=F32)


def masked_scores(block, scores, tile, codes_q, codes_k):
    rows = lax.broadcasted_iota(jnp.int32, (TILE, TILE), 0)
    cols = lax.broadcasted_iota(jnp.int32, (TILE, TILE), 1)
    allowed = None
    if tile == block:
        allowed = cols <= rows
    if tile * TILE >= PRE:
        same = (
            codes_q[block * TILE : (block + 1) * TILE, :]
            == codes_k[:, tile * TILE : (tile + 1) * TILE]
        )
        allowed = same if allowed is None else allowed & same
    if allowed is None:
        return scores
    return jnp.where(allowed, scores, NEG)


def xor(value, mask):
    bit = 1
    while bit <= mask:
        if mask & bit:
            value = value + bit * (1 - 2 * lax.rem(lax.div(value, jnp.int32(bit)), jnp.int32(2)))
        bit *= 2
    return value


def remote(src, dst, send_sem, recv_sem, **target):
    return pltpu.make_async_remote_copy(
        src_ref=src,
        dst_ref=dst,
        send_sem=send_sem,
        recv_sem=recv_sem,
        device_id=target,
        device_id_type=pl.DeviceIdType.MESH,
    )


def greet(masks, relay=None):
    barrier = pltpu.get_barrier_semaphore()
    seq = lax.axis_index("seq")
    pre = lax.axis_index("pre")

    def signal(**target):
        pl.semaphore_signal(
            barrier, inc=1, device_id=target, device_id_type=pl.DeviceIdType.MESH
        )

    for mask in masks:
        signal(seq=xor(seq, mask))
    for mask in (1, 2):
        signal(pre=xor(pre, mask))
    count = len(masks) + 2
    if relay is not None:

        @pl.when(relay.moves)
        def _():
            signal(seq=relay.there[0], pre=relay.there[1])
            signal(seq=relay.back[0], pre=relay.back[1])

        count = count + 2 * relay.moves.astype(jnp.int32)
    pl.semaphore_wait(barrier, count)


class Relay:
    def __init__(self, size, send_sem, recv_sem, local_sem):
        seq, pre = lax.axis_index("seq"), lax.axis_index("pre")
        held = seq * 4 + pre
        used = pre * size + seq
        self.there = (lax.rem(held, size), lax.div(held, size))
        self.back = (lax.div(used, 4), lax.rem(used, 4))
        self.moves = held != used
        self.sems = (send_sem, recv_sem, local_sem)

    def copies(self, src, dst, target):
        send_sem, recv_sem, local_sem = self.sems
        return (
            remote(src, dst, send_sem, recv_sem, seq=target[0], pre=target[1]),
            pltpu.make_async_copy(src, dst, local_sem),
        )

    def begin(self, src, dst, target):
        away, here = self.copies(src, dst, target)
        pl.when(self.moves)(away.start)
        pl.when(jnp.logical_not(self.moves))(here.start)

    def finish(self, src, dst, target):
        away, here = self.copies(src, dst, target)

        @pl.when(self.moves)
        def _():
            away.wait_recv()
            away.wait_send()

        pl.when(jnp.logical_not(self.moves))(here.wait)


def rows_of(index, count):
    return pl.ds(pl.multiple_of(index * count, count), count)


def far_line(lines, line, turn):
    low = lines - 1 - turn
    low = low - (low <= line).astype(jnp.int32)
    high = turn + (turn >= line).astype(jnp.int32)
    return jnp.where(line < lines // 2, low, high)


def early_rows(rows):
    return (rows * 3 + 128) // 256 * 16


class Copies:
    def __init__(self):
        self.items = []

    def start(self, copy, when=None):
        if when is None:
            copy.start()
        else:
            pl.when(when)(copy.start)
        self.items.append((copy, when))

    def drain(self):
        for copy, when in self.items:
            if when is None:
                copy.wait_send()
            else:
                pl.when(when)(copy.wait_send)


class Gather:
    def __init__(self, own, land, rows, send_sem, recv_sem, local_sem, size):
        self.own, self.land, self.rows = own, land, rows
        self.early = early_rows(rows)
        self.send_sem, self.recv_sem, self.local_sem = send_sem, recv_sem, local_sem
        self.seq = lax.axis_index("seq")
        self.lines = size // 2
        self.line = lax.div(self.seq, jnp.int32(2))
        self.twin = xor(self.seq, 1)
        self.sent = Copies()
        self.local = None

    def view(self, place, kind):
        first = {0: 0, 1: self.rows - self.early, 2: 0, 3: self.rows - self.early}[kind]
        count = {0: self.rows, 1: self.early, 2: self.rows - self.early, 3: self.early}[kind]
        return self.land.at[pl.ds(pl.multiple_of(place * self.rows + first, 16), count), :]

    def copy(self, place, kind, send, recv, to, own=False):
        there = self.view(place, kind)
        src = there
        if own:
            first = self.rows - self.early if kind in (1, 3) else 0
            count = there.shape[0]
            src = self.own.at[first : first + count, :]
        return remote(
            src, there, self.send_sem.at[kind, send], self.recv_sem.at[kind, recv], seq=to
        )

    def beside(self, up):
        return (self.line < self.lines - 1, self.seq + 2) if up else (self.line > 0, self.seq - 2)

    def begin(self):
        if self.early:
            self.sent.start(self.copy(self.seq, 3, 0, 0, self.twin, True))
        for up in (True, False):
            there, to = self.beside(up)
            spare = self.lines + (0 if up else 1)
            self.sent.start(self.copy(self.seq, 0, spare, self.line, to, True), there)
        self.sent.start(self.copy(self.seq, 2, self.line, self.line, self.twin, True))
        self.local = pltpu.make_async_copy(self.own, self.view(self.seq, 0), self.local_sem)
        self.local.start()

    def rest(self):
        if not self.early:
            return
        self.copy(self.twin, 3, 0, 0, self.twin).wait_recv()
        for up in (True, False):
            there, to = self.beside(up)
            spare = self.lines + (0 if up else 1)
            self.sent.start(self.copy(self.twin, 1, spare, self.line, to), there)

    def event(self, turn, when=None):
        line = far_line(self.lines, self.line, jnp.int32(self.lines - 2 - turn))
        step = jnp.where(line < self.line, 2, -2)
        after = jnp.where(line < self.line, self.line < self.lines - 1, self.line > 0)
        place = line * 2 + lax.rem(self.seq, jnp.int32(2))
        other = xor(place, 1)
        to = jnp.clip(self.seq + step, 0, 2 * self.lines - 1)
        onward = self.copy(place, 0, line, line, to)
        aside = self.copy(place, 2, line, line, self.twin)
        both = self.copy(other, 1, line, line, to) if self.early else None

        def body():
            self.copy(place, 0, line, line, self.twin).wait_recv()
            pl.when(after)(onward.start)
            aside.start()
            if both is not None:
                self.copy(other, 1, line, line, self.twin).wait_recv()
                pl.when(after)(both.start)

        if when is None:
            body()
        else:
            pl.when(when)(body)
            after = after & when
        self.sent.items += [(onward, after), (aside, when)]
        if both is not None:
            self.sent.items.append((both, after))

    def poll(self, turn):
        last = self.lines - 2
        end = (self.line == 0) | (self.line == self.lines - 1)
        self.event(turn, end if turn else None)
        if turn < last:
            self.event(turn + 1, jnp.logical_not(end))

    def finish(self):
        self.local.wait()
        for line in range(self.lines):
            self.copy(line * 2, 2, line, line, self.twin).wait_recv()

    def drain(self):
        self.sent.drain()


class Spread:
    def __init__(self, own, land, rows, send_sem, recv_sem, local_sem):
        self.own, self.land, self.rows = own, land, rows
        self.send_sem, self.recv_sem, self.local_sem = send_sem, recv_sem, local_sem
        self.pre = lax.axis_index("pre")
        self.sent = []

    def slot(self, index):
        return self.land.at[index * self.rows : (index + 1) * self.rows, :]

    def copy(self, src, slot, mask):
        return remote(
            src, self.slot(slot), self.send_sem.at[slot], self.recv_sem.at[slot], pre=xor(self.pre, mask)
        )

    def begin(self):
        for mask in (2, 1):
            copy = self.copy(self.own, mask, mask)
            copy.start()
            self.sent.append(copy)
        self.local = pltpu.make_async_copy(self.own, self.slot(0), self.local_sem)
        self.local.start()

    def forward(self):
        self.copy(self.own, 2, 2).wait_recv()
        copy = self.copy(self.slot(2), 3, 1)
        copy.start()
        self.sent.append(copy)

    def finish_near(self):
        self.local.wait()
        self.copy(self.own, 1, 1).wait_recv()

    def finish_far(self):
        self.copy(self.own, 3, 1).wait_recv()

    def finish(self):
        self.finish_near()
        self.finish_far()

    def drain(self):
        for copy in self.sent:
            copy.wait_send()


def local_copies(pairs, sem):
    copies = [pltpu.make_async_copy(src, dst, sem.at[i]) for i, (src, dst) in enumerate(pairs)]
    for copy in copies:
        copy.start()
    for copy in copies:
        copy.wait()


def wide_masks(size):
    masks = list(range(2, size, 2))
    return sorted(masks, key=lambda m: (m != 2, -m))


def head_lanes(value, head):
    lane = lax.broadcasted_iota(jnp.int32, value.shape, 1)
    inside = (lane < HEAD_DIM) if head == 0 else (lane >= HEAD_DIM)
    return jnp.where(inside, value, jnp.zeros_like(value))


def join_heads(first, second):
    lane = lax.broadcasted_iota(jnp.int32, (first.shape[0], 2 * HEAD_DIM), 1)
    return jnp.where(lane < HEAD_DIM, first, second)


def attend_pair(pair, cols, qkv, codes_q, codes_k, mixed, stats):
    lanes = [pl.ds(pl.multiple_of(third * cols + pair * 128, 128), 128) for third in range(3)]
    blocks = qkv.shape[0] // TILE
    for block in range(blocks):
        rows = slice(block * TILE, (block + 1) * TILE)
        both = qkv[rows, lanes[0]]
        outs, levels = [], []
        for head in range(2):
            queries = head_lanes(both, head)
            scores = [
                masked_scores(
                    block,
                    dot_nt(queries, qkv[tile * TILE : (tile + 1) * TILE, lanes[1]]),
                    tile,
                    codes_q,
                    codes_k,
                )
                for tile in range(block + 1)
            ]
            top = functools.reduce(jnp.maximum, [jnp.max(x, axis=1, keepdims=True) for x in scores])
            powers = [jnp.exp(x - top) for x in scores]
            total = functools.reduce(jnp.add, [jnp.sum(e, axis=1, keepdims=True) for e in powers])
            share = 1.0 / total
            outs.append(
                functools.reduce(
                    jnp.add,
                    [
                        dot_nn((e * share).astype(BF), qkv[tile * TILE : (tile + 1) * TILE, lanes[2]])
                        for tile, e in enumerate(powers)
                    ],
                )
            )
            levels.append(top + jnp.log(total))
        mixed[rows, lanes_of(pair)] = join_heads(outs[0], outs[1]).astype(BF)
        stats[rows, lanes_of(pair)] = join_heads(levels[0], levels[1])


def lanes_of(pair):
    return pl.ds(pl.multiple_of(pair * 128, 128), 128)


def forward_kernel(
    sizes,
    small,
    qkv_weight,
    out_weight,
    up_weight,
    down_weight,
    prefix_in,
    later_in,
    prefix_cot,
    later_cot,
    active_ref,
    codes_q,
    codes_k,
    w_qkv,
    w_out,
    w_up,
    w_down,
    h1,
    df,
    h2,
    qkv,
    mixed,
    stats,
    attn,
    acted,
    slope,
    down_grad,
    vectors,
    wbuf,
    lhs,
    qkv_v,
    mixed_v,
    stats_v,
    x_v,
    cot_v,
    h1_v,
    df_v,
    h2_v,
    terms_v,
    near_v,
    pass_v,
    far_v,
    attn_v,
    acted_v,
    slope_v,
    grad_v,
    own_qkv,
    own_up,
    own_down,
    own_out,
    small_v,
    slope_bias,
    gather_send,
    gather_recv,
    small_send,
    small_recv,
    spread_send,
    spread_recv,
    sum_send,
    sum_recv,
    relay_sem,
    local_sem,
):
    seq_size, pre_part, later_part = sizes
    part = pre_part + later_part
    cols = qkv_weight.shape[1] // 12
    ff_cols = up_weight.shape[1] // 4
    own_d = D // seq_size
    wide = wide_masks(seq_size)
    pre = lax.axis_index("pre")
    seq = lax.axis_index("seq")
    near_id = {"pre": xor(pre, 1)}
    far_id = {"pre": xor(pre, 2)}

    def gather(i, own, land):
        sems = (gather_send.at[i], gather_recv.at[i], local_sem.at[i])
        return Gather(own, land, own.shape[0], *sems, seq_size)

    def own_section(weight, first, columns):
        return weight.at[:, pl.ds(pl.multiple_of(first + pre * columns, columns), columns)]

    get_qkv = gather(0, own_qkv, w_qkv)
    get_out = gather(1, own_out, w_out)
    get_up = gather(2, own_up, w_up)
    get_down = gather(3, own_down, w_down)
    get_h1 = Spread(h1_v, h1, part, spread_send.at[0], spread_recv.at[0], local_sem.at[4])
    get_df = Spread(df_v, df, part, spread_send.at[1], spread_recv.at[1], local_sem.at[5])
    get_h2 = Spread(h2_v, h2, part, spread_send.at[2], spread_recv.at[2], local_sem.at[6])
    relay = Relay(seq_size, relay_sem.at[0], relay_sem.at[1], relay_sem.at[2])
    out_rows = own_d // 4
    relayed = (out_weight.at[rows_of(pre, out_rows), :], own_out, relay.there)

    cuts = [
        pltpu.make_async_copy(
            own_section(qkv_weight, i * D, cols),
            own_qkv.at[:, i * cols : (i + 1) * cols],
            local_sem.at[12 + i],
        )
        for i in range(3)
    ]
    late_cuts = [
        pltpu.make_async_copy(own_section(weight, 0, ff_cols), own, local_sem.at[15 + i])
        for i, (weight, own) in enumerate(((up_weight, own_up), (down_weight, own_down)))
    ]
    for cut in (*cuts, *late_cuts):
        cut.start()
    greet(range(1, seq_size), relay)
    small_copies = [
        remote(
            small, small_v.at[seq], small_send.at[mask], small_recv.at[mask], seq=xor(seq, mask)
        )
        for mask in range(1, seq_size)
    ]
    for copy in small_copies:
        copy.start()
    keep_small = pltpu.make_async_copy(small, small_v.at[seq], local_sem.at[7])
    keep_small.start()
    relay.begin(*relayed)
    for cut in cuts:
        cut.wait()
    get_qkv.begin()
    for cut in late_cuts:
        cut.wait()
    local_copies(
        [
            (prefix_in, x_v.at[:pre_part, :]),
            (later_in, x_v.at[pre_part:, :]),
            (prefix_cot, cot_v.at[:pre_part, :]),
            (later_cot, cot_v.at[pre_part:, :]),
        ],
        local_sem.at[8:12],
    )
    keep_small.wait()
    for copy in small_copies:
        copy.wait_recv()
    for member in range(seq_size):
        vectors[:, member * own_d : (member + 1) * own_d] = small_v[member]
    gain1, bias1, out_bias, gain2, bias2 = [vectors[i : i + 1, :] for i in (0, 1, 4, 5, 6)]
    own_lanes = pl.ds(pl.multiple_of(pre * cols, cols), cols)
    query_bias, value_bias = vectors[2:3, own_lanes], vectors[3:4, own_lanes]
    up_shares = vectors[8:12, own_lanes]
    up_bias = jnp.concatenate(
        [
            up_shares[k : k + 1, i * own_d : (i + 1) * own_d]
            for i in range(seq_size // 4)
            for k in range(4)
        ],
        axis=1,
    )
    chunk = 32

    @pl.loop(0, part // chunk)
    def _(i):
        rows = rows_of(i, chunk)
        value, _, _ = layer_norm_parts(x_v[rows, :].astype(F32), gain1, bias1)
        h1_v[rows, :] = value.astype(BF)

    get_h1.begin()

    @pl.loop(0, part // chunk)
    def _(i):
        rows = rows_of(i, chunk)
        df_v[rows, :] = (active_ref[rows, :] * cot_v[rows, :].astype(F32)).astype(BF)

    get_df.begin()
    slope_bias[...] = up_bias
    turns = range(seq_size // 2 - 1)
    get_qkv.rest()
    for turn in turns:
        get_qkv.poll(turn)
        if turn == 0:
            relay.finish(*relayed)
            get_out.begin()
            get_h1.forward()
        if turn == turns[-2]:
            get_up.begin()
    get_h1.finish()
    get_df.forward()
    get_out.rest()
    load = pltpu.make_async_copy(h1, lhs, local_sem.at[12])
    load.start()
    get_qkv.finish()
    local_copies([(w_qkv, wbuf.at[:, : 3 * cols])], local_sem.at[8:9])
    load.wait()

    @pl.loop(0, 4)
    def _(r):
        member = lax.rem(r, 2) * (xor(pre, 1) - pre) + lax.div(r, 2) * (xor(pre, 2) - pre) + pre
        head_rows = rows_of(member, pre_part)
        tail_rows = pl.ds(pl.multiple_of(4 * pre_part + member * later_part, 64), later_part)

        for j in range(3):
            lanes = slice(j * cols, (j + 1) * cols)
            value = dot_nn(lhs[rows_of(r, part), :], wbuf[:, lanes])
            if j == 0:
                value = (value + query_bias) * (1.0 / math.sqrt(HEAD_DIM))
            if j == 2:
                value = value + value_bias
            value = value.astype(BF)
            qkv_v[head_rows, lanes] = value[:pre_part]
            qkv_v[tail_rows, lanes] = value[pre_part:]

    save_qkv = pltpu.make_async_copy(qkv_v, qkv, local_sem.at[13])
    save_qkv.start()
    for turn in turns:
        get_out.poll(turn)
    get_up.rest()
    get_df.finish()
    pairs = cols // 128

    def attention(first, last):
        @pl.loop(first, last)
        def _(pair):
            attend_pair(pair, cols, qkv_v, codes_q[...], codes_k[...], mixed_v, stats_v)

    attention(0, pairs // 2)
    get_up.poll(0)
    get_down.begin()
    attention(pairs // 2, pairs)
    save_stats = pltpu.make_async_copy(stats_v, stats, local_sem.at[14])
    save_stats.start()
    get_out.finish()
    local_copies([(w_out, wbuf.at[:cols, :])], local_sem.at[8:9])

    def position_rows(r):
        member = xor(pre, r) if r else pre
        return (
            rows_of(member, pre_part),
            pl.ds(pl.multiple_of(4 * pre_part + member * later_part, 64), later_part),
        )

    def out_term(r, store):
        head_rows, tail_rows = position_rows(r)

        @pl.loop(0, D // 512)
        def _(j):
            lanes = rows_of(j, 512)
            store(
                lanes,
                dot_nn(mixed_v[head_rows, :], wbuf[:cols, lanes]),
                dot_nn(mixed_v[tail_rows, :], wbuf[:cols, lanes]),
            )

    def keep_term(slot):
        def store(lanes, head, tail):
            terms_v[slot, :pre_part, lanes] = head.astype(BF)
            terms_v[slot, pre_part:, lanes] = tail.astype(BF)

        return store

    near = [
        remote(terms_v.at[i], near_v.at[i], sum_send.at[i], sum_recv.at[i], **near_id)
        for i in range(2)
    ]
    far = remote(pass_v, far_v, sum_send.at[2], sum_recv.at[2], **far_id)
    out_term(3, keep_term(0))
    near[0].start()
    out_term(1, keep_term(1))
    near[1].start()
    near[0].wait_recv()

    def pass_term(lanes, head, tail):
        pass_v[:pre_part, lanes] = (head + near_v[0, :pre_part, lanes].astype(F32)).astype(BF)
        pass_v[pre_part:, lanes] = (tail + near_v[0, pre_part:, lanes].astype(F32)).astype(BF)

    out_term(2, pass_term)
    far.start()
    near[1].wait_recv()

    def own_term(lanes, head, tail):
        bias = vectors[4:5, lanes]
        attn_v[:pre_part, lanes] = head + near_v[1, :pre_part, lanes].astype(F32) + bias
        attn_v[pre_part:, lanes] = tail + near_v[1, pre_part:, lanes].astype(F32) + bias

    out_term(0, own_term)
    moves = []
    for r in range(4):
        head_rows, tail_rows = position_rows(r)
        moves.append((mixed_v.at[head_rows, :], mixed.at[r * part : r * part + pre_part, :]))
        moves.append((mixed_v.at[tail_rows, :], mixed.at[r * part + pre_part : (r + 1) * part, :]))
    local_copies(moves, local_sem.at[16:24])
    for turn in turns[1:]:
        get_up.poll(turn)
    far.wait_recv()

    @pl.loop(0, part // chunk)
    def _(i):
        rows = rows_of(i, chunk)
        branch = attn_v[rows, :] + far_v[rows, :].astype(F32)
        attn_v[rows, :] = branch
        value, _, _ = layer_norm_parts(x_v[rows, :].astype(F32) + branch, gain2, bias2)
        h2_v[rows, :] = value.astype(BF)

    get_h2.begin()
    save_attn = pltpu.make_async_copy(attn_v, attn, local_sem.at[15])
    save_attn.start()
    get_down.rest()
    get_up.finish()
    load = pltpu.make_async_copy(w_up, wbuf, local_sem.at[12])
    load.start()
    get_h2.finish_near()
    half = slice(0, 2 * part)
    local_copies([(h2.at[half, :], lhs.at[half, :])], local_sem.at[8:9])
    load.wait()

    def up_rows(r):
        rows = rows_of(r, part)

        @pl.loop(0, ff_cols // 512)
        def _(j):
            lanes = rows_of(j, 512)
            upper = dot_nn(lhs[rows, :], wbuf[:, lanes]) + slope_bias[:, lanes]
            cumulative = 0.5 * (1.0 + lax.erf(upper * (1.0 / math.sqrt(2.0))))
            density = jnp.exp(-0.5 * upper * upper) * (1.0 / math.sqrt(2.0 * math.pi))
            acted_v[rows, lanes] = (upper * cumulative).astype(BF)
            slope_v[rows, lanes] = (cumulative + upper * density).astype(BF)

    pl.loop(0, 2)(up_rows)
    get_down.poll(0)
    get_h2.forward()
    get_h2.finish_far()
    for turn in turns[1:-1]:
        get_down.poll(turn)
    half = slice(2 * part, 4 * part)
    local_copies([(h2.at[half, :], lhs.at[half, :])], local_sem.at[8:9])
    pl.loop(2, 4)(up_rows)

    saves = [
        pltpu.make_async_copy(acted_v, acted, local_sem.at[12]),
        pltpu.make_async_copy(slope_v, slope, local_sem.at[8]),
    ]
    for save in saves:
        save.start()
    get_down.poll(turns[-1])
    local_copies([(df, lhs)], local_sem.at[9:10])

    @pl.loop(0, D // 256)
    def _(i):
        lanes = rows_of(i, 256)
        turned = lhs[:, lanes].T

        @pl.loop(0, ff_cols // 512)
        def _(j):
            grad_v[:, rows_of(j, 512)] = dot_nn(turned, acted_v[:, rows_of(j, 512)]).astype(BF)

        save = pltpu.make_async_copy(grad_v, down_grad.at[lanes, :], local_sem.at[9])
        save.start()
        save.wait()

    get_down.finish()
    for save in (*saves, save_qkv, save_stats, save_attn):
        save.wait()
    for item in (get_qkv, get_out, get_up, get_down, get_h1, get_df, get_h2):
        item.drain()
    for copy in (*near, far, *small_copies):
        copy.wait_send()


def forward_pass(seq_size, pre_part, later_part, *operands):
    part = pre_part + later_part
    length = 4 * part
    width = 3 * D // 4
    cols = width // 3
    ff_cols = FF // 4
    own_d = D // seq_size
    hbm = pl.BlockSpec(memory_space=pl.ANY)
    vmem = pl.BlockSpec(memory_space=pltpu.VMEM)

    def out(shape, kind=BF):
        return jax.ShapeDtypeStruct(shape, kind)

    outs = (
        out((D, width)),
        out((cols, D)),
        out((D, ff_cols)),
        out((D, ff_cols)),
        out((length, D)),
        out((length, D)),
        out((length, D)),
        out((length, width)),
        out((length, cols)),
        out((length, cols), F32),
        out((part, D), F32),
        out((length, ff_cols)),
        out((length, ff_cols)),
        out((D, ff_cols)),
        out((16, D), F32),
    )
    dma = pltpu.SemaphoreType.DMA
    return pl.pallas_call(
        functools.partial(forward_kernel, (seq_size, pre_part, later_part)),
        out_shape=outs,
        in_specs=[hbm] * 9 + [vmem] * (len(operands) - 9),
        out_specs=[hbm] * (len(outs) - 1) + [vmem],
        scratch_shapes=[
            pltpu.VMEM((D, max(ff_cols, width)), BF),
            pltpu.VMEM((length, D), BF),
            pltpu.VMEM((length, width), BF),
            pltpu.VMEM((length, cols), BF),
            pltpu.VMEM((length, cols), F32),
            pltpu.VMEM((part, D), BF),
            pltpu.VMEM((part, D), BF),
            pltpu.VMEM((part, D), BF),
            pltpu.VMEM((part, D), BF),
            pltpu.VMEM((part, D), BF),
            pltpu.VMEM((2, part, D), BF),
            pltpu.VMEM((2, part, D), BF),
            pltpu.VMEM((part, D), BF),
            pltpu.VMEM((part, D), BF),
            pltpu.VMEM((part, D), F32),
            pltpu.VMEM((length, ff_cols), BF),
            pltpu.VMEM((length, ff_cols), BF),
            pltpu.VMEM((256, ff_cols), BF),
            pltpu.VMEM((own_d, width), BF),
            pltpu.VMEM((own_d, ff_cols), BF),
            pltpu.VMEM((own_d, ff_cols), BF),
            pltpu.VMEM((own_d // 4, D), BF),
            pltpu.VMEM((seq_size, 16, own_d), F32),
            pltpu.VMEM((1, ff_cols), F32),
            dma((4, 4, seq_size // 2 + 2)),
            dma((4, 4, seq_size // 2)),
            dma((seq_size,)),
            dma((seq_size,)),
            dma((3, 4)),
            dma((3, 4)),
            dma((3,)),
            dma((3,)),
            dma((3,)),
            dma((24,)),
        ],
        compiler_params=pltpu.CompilerParams(
            collective_id=0, has_side_effects=True, vmem_limit_bytes=62 * 2**20
        ),
        cost_estimate=pl.CostEstimate(
            flops=2 * length * D * (width + cols + 2 * ff_cols),
            bytes_accessed=8 * D * ff_cols,
            transcendentals=length * ff_cols,
        ),
        name="forward_pass",
    )(*operands)


class Pool:
    def __init__(self, buffers, count):
        self.buffers, self.count = buffers, count
        self.pending = [Copies() for _ in range(count)]
        self.turn = 0

    def take(self):
        index = self.turn % self.count
        self.turn += 1
        self.pending[index].drain()
        self.pending[index] = Copies()
        return index

    def drain(self):
        for copies in self.pending:
            copies.drain()


class Reduce:
    def __init__(self, grad, near, chain, tail, rows, width, sems, work, size, split=False):
        self.grad, self.near, self.chain, self.tail = grad, near, chain, tail
        self.rows, self.width = rows, width
        self.early = early_rows(rows) if split else 0
        self.first = rows - self.early
        self.whole = rows + self.early
        self.near_send, self.near_recv, self.chain_send, self.chain_recv, self.tail_sem = sems
        self.left, self.right, self.third, self.fourth, self.out, self.pool, self.sem = work
        self.seq = lax.axis_index("seq")
        self.lines = size // 2
        self.line = lax.div(self.seq, jnp.int32(2))
        self.side = lax.rem(self.seq, jnp.int32(2))
        self.sent = Copies()

    def target(self, turn):
        if turn == self.lines - 1:
            return self.line
        return far_line(self.lines, self.line, jnp.int32(turn))

    def block(self, line, other, first, count):
        place = line * 2 + ((1 - self.side) if other else self.side)
        return self.grad.at[pl.ds(pl.multiple_of(place * self.rows + first, 16), count), :]

    def near_slot(self, line, near=None):
        near = self.near if near is None else near
        return near.at[pl.ds(pl.multiple_of(line * self.first, 16), self.first), :]

    def chain_slot(self, slot):
        return self.chain.at[pl.ds(pl.multiple_of(slot * self.whole, 16), self.whole), :]

    def near_copy(self, turn):
        line = self.target(turn)
        return remote(
            self.block(line, True, 0, self.first),
            self.near_slot(line),
            self.near_send.at[turn],
            self.near_recv.at[line],
            seq=xor(self.seq, 1),
        )

    def chain_copy(self, src, turn, slot, to):
        return remote(
            src, self.chain_slot(slot), self.chain_send.at[turn], self.chain_recv.at[slot], seq=to
        )

    def begin(self, *turns):
        for turn in turns:
            self.sent.start(self.near_copy(turn))

    def view(self, ref, first, count):
        return ref.at[first : first + count, : self.width]

    def load_own(self, line):
        copies = [
            pltpu.make_async_copy(
                self.block(line, False, 0, self.rows), self.view(self.left, 0, self.rows), self.sem.at[0]
            )
        ]
        if self.early:
            copies.append(
                pltpu.make_async_copy(
                    self.block(line, True, self.first, self.early),
                    self.view(self.left, self.rows, self.early),
                    self.sem.at[1],
                )
            )
        for copy in copies:
            copy.start()
        return copies

    def load(self, src, ref, count, sem):
        copy = pltpu.make_async_copy(src, self.view(ref, 0, count), self.sem.at[sem])
        copy.start()
        return copy

    def rows_loop(self, first, last, value, store):
        if first == last:
            return

        @pl.loop(first // 16, last // 16)
        def _(i):
            at = (rows_of(i, 16), slice(0, self.width))
            store(at, value(at))

    def step(self, turn, when=None, early=None):
        line = self.target(turn)
        up = line > self.line
        ahead = jnp.where(up, line - self.line, self.line - line)
        base = jnp.where(up, 0, self.lines - 1)
        more = jnp.where(up, self.line > 0, self.line < self.lines - 1)
        slot_in = jnp.minimum(base + ahead, 2 * (self.lines - 1) - 1)
        slot_out = base + ahead - 1
        to = jnp.clip(self.seq + jnp.where(up, 2, -2), 0, 2 * self.lines - 1)
        index = self.pool.take()
        out = self.out.at[index]
        leave = self.chain_copy(out.at[: self.whole, : self.width], turn, slot_out, to)

        def store(at, value):
            out[at] = value.astype(BF)

        def body():
            copies = self.load_own(line)
            if early is None:
                self.near_copy(turn).wait_recv()
            copies.append(self.load(self.near_slot(line, early), self.right, self.first, 2))

            def both(at):
                return self.left[at].astype(F32) + self.right[at].astype(F32)

            def own(at):
                return self.left[at].astype(F32)

            @pl.when(more)
            def _():
                self.chain_copy(out.at[: self.whole, : self.width], turn, slot_in, to).wait_recv()
                third = self.load(self.chain_slot(slot_in), self.third, self.whole, 3)
                for copy in (*copies, third):
                    copy.wait()
                self.rows_loop(
                    0, self.first, lambda at: both(at) + self.third[at].astype(F32), store
                )
                self.rows_loop(
                    self.first, self.whole, lambda at: own(at) + self.third[at].astype(F32), store
                )

            @pl.when(jnp.logical_not(more))
            def _():
                for copy in copies:
                    copy.wait()
                self.rows_loop(0, self.first, both, store)
                self.rows_loop(self.first, self.whole, own, store)

            leave.start()

        if when is None:
            body()
        else:
            pl.when(when)(body)
        self.pool.pending[index].items.append((leave, when))

    def sides(self):
        return ((self.line > 0, 0), (self.line < self.lines - 1, self.lines - 1))

    def settle(self):
        self.near_copy(self.lines - 1).wait_recv()
        for there, slot in self.sides():
            pl.when(there)(
                self.chain_copy(self.view(self.third, 0, self.whole), 0, slot, self.seq).wait_recv
            )

    def tail_copy(self, src):
        return remote(src, self.tail, self.tail_sem.at[0], self.tail_sem.at[1], seq=xor(self.seq, 1))

    def final(self, result):
        copies = self.load_own(self.line)
        copies.append(self.load(self.near_slot(self.line), self.right, self.first, 2))
        side = jnp.where(self.line > 0, 0, self.lines - 1)
        copies.append(self.load(self.chain_slot(side), self.third, self.whole, 3))
        mid = (self.line > 0) & (self.line < self.lines - 1)
        fourth = pltpu.make_async_copy(
            self.chain_slot(self.lines - 1), self.view(self.fourth, 0, self.whole), self.sem.at[4]
        )
        pl.when(mid)(fourth.start)
        index = self.pool.take()
        out = self.out.at[index]

        def put(at, value):
            result[at] = value.astype(BF)

        def put_tail(at, value):
            out[at] = value.astype(BF)

        def loops(refs):
            def sum_of(at):
                return functools.reduce(jnp.add, [ref[at].astype(F32) for ref in refs])

            self.rows_loop(0, self.first, lambda at: sum_of(at) + self.right[at].astype(F32), put)
            self.rows_loop(self.first, self.rows, sum_of, put)
            self.rows_loop(self.rows, self.whole, sum_of, put_tail)

        for copy in copies:
            copy.wait()

        @pl.when(mid)
        def _():
            fourth.wait()
            loops((self.left, self.third, self.fourth))

        pl.when(jnp.logical_not(mid))(lambda: loops((self.left, self.third)))
        if self.early:
            self.pool.pending[index].start(
                self.tail_copy(out.at[self.rows : self.whole, : self.width])
            )

    def last(self, result):
        if not self.early:
            return
        self.tail_copy(self.view(self.third, 0, self.early)).wait_recv()
        self.load(self.tail, self.third, self.early, 3).wait()

        @pl.loop(0, self.early // 16)
        def _(i):
            lanes = slice(0, self.width)
            rows = pl.ds(pl.multiple_of(self.first + i * 16, 16), 16)
            value = result[rows, lanes].astype(F32) + self.third[rows_of(i, 16), lanes].astype(F32)
            result[rows, lanes] = value.astype(BF)

    def drain(self):
        self.sent.drain()


class Sum:
    def __init__(self, terms, near, passed, far, send_sem, recv_sem):
        pre = lax.axis_index("pre")
        near_id, far_id = {"pre": xor(pre, 1)}, {"pre": xor(pre, 2)}
        self.terms, self.near, self.passed = terms, near, passed
        self.near_copies = [
            remote(terms.at[i], near.at[i], send_sem.at[i], recv_sem.at[i], **near_id)
            for i in range(2)
        ]
        self.far_copy = remote(passed, far, send_sem.at[2], recv_sem.at[2], **far_id)

    def run(self, term, keep):
        def store_in(slot):
            def store(rows, lanes, value):
                self.terms[slot, rows, lanes] = value.astype(BF)

            return store

        term(3, store_in(0))
        self.near_copies[0].start()
        term(1, store_in(1))
        self.near_copies[1].start()
        self.near_copies[0].wait_recv()

        def store(rows, lanes, value):
            self.passed[rows, lanes] = (value + self.near[0, rows, lanes].astype(F32)).astype(BF)

        term(2, store)
        self.far_copy.start()
        self.near_copies[1].wait_recv()

        def store(rows, lanes, value):
            keep(rows, lanes, value + self.near[1, rows, lanes].astype(F32))

        term(0, store)

    def drain(self):
        for copy in (*self.near_copies, self.far_copy):
            copy.wait_send()


def columns_grad(left, right, rows, width, tile, save):
    @pl.loop(0, rows // 256)
    def _(i):
        turned = left[:, rows_of(i, 256)].T

        @pl.loop(0, width // 512)
        def _(j):
            tile[:, rows_of(j, 512)] = dot_nn(turned, right[:, rows_of(j, 512)]).astype(BF)

        copy = save(rows_of(i, 256))
        copy.start()
        copy.wait()


def add_rows(target, index, value):
    target[index : index + 1, : value.shape[1]] += jnp.sum(value, axis=0, keepdims=True)


def feed_back_kernel(
    sizes,
    w_down,
    w_up,
    acted,
    df,
    h2,
    slope,
    attn,
    down_grad,
    prefix_in,
    later_in,
    prefix_cot,
    later_cot,
    active_ref,
    vectors,
    near_down,
    chain_down,
    near_up,
    up_grad,
    dattn,
    middle_grad,
    prefix_out,
    later_out,
    sums,
    up_sums,
    wbuf,
    lhs,
    acted_v,
    slope_v,
    du_v,
    x_v,
    cot_v,
    attn_v,
    acc_v,
    ffn_v,
    dattn_v,
    terms_v,
    near_v,
    pass_v,
    far_v,
    ffn_near_v,
    ffn_far_v,
    left_v,
    right_v,
    third_v,
    out_v,
    grad_v,
    twin_send,
    twin_recv,
    chain_send,
    chain_recv,
    early_send,
    early_recv,
    spread_send,
    spread_recv,
    sum_send,
    sum_recv,
    local_sem,
):
    seq_size, pre_part, later_part = sizes
    part = pre_part + later_part
    length = 4 * part
    ff_cols = w_up.shape[1]
    gain2 = vectors[5:6, :]
    wide = wide_masks(seq_size)
    lines = seq_size // 2
    line = lax.div(lax.axis_index("seq"), jnp.int32(2))
    end = (line == 0) | (line == lines - 1)
    mid = jnp.logical_not(end)
    turns = range(lines - 1)
    pool = Pool(out_v, 3)
    work = (left_v, right_v, third_v, None, out_v, pool, local_sem.at[12:16])
    put_down = Reduce(
        down_grad,
        near_down,
        chain_down,
        None,
        D // seq_size,
        ff_cols,
        (twin_send, twin_recv, chain_send, chain_recv, None),
        work,
        seq_size,
    )
    put_up = Reduce(
        up_grad,
        near_up,
        None,
        None,
        D // seq_size,
        ff_cols,
        (early_send, early_recv, None, None, None),
        work,
        seq_size,
    )
    get_dattn = Spread(dattn_v, dattn, part, spread_send, spread_recv, local_sem.at[2])
    sum_f = Sum(terms_v, ffn_near_v, pass_v, ffn_far_v, sum_send.at[0], sum_recv.at[0])
    sum_dh2 = Sum(terms_v, near_v, pass_v, far_v, sum_send.at[1], sum_recv.at[1])

    greet((1, *wide))
    put_down.begin(*turns, lines - 1)
    loads = [
        pltpu.make_async_copy(src, dst, local_sem.at[3 + i])
        for i, (src, dst) in enumerate(
            [
                (w_down, wbuf),
                (acted, acted_v),
                (df, lhs),
                (slope, slope_v),
                (prefix_in, x_v.at[:pre_part, :]),
                (later_in, x_v.at[pre_part:, :]),
                (prefix_cot, cot_v.at[:pre_part, :]),
                (later_cot, cot_v.at[pre_part:, :]),
                (attn, attn_v),
            ]
        )
    ]
    for load in loads:
        load.start()
    sums[...] = jnp.zeros_like(sums)
    up_sums[...] = jnp.zeros_like(up_sums)
    for load in loads[:2]:
        load.wait()

    def f_term(r, store):
        @pl.loop(0, D // 512)
        def _(j):
            store(
                slice(0, part),
                rows_of(j, 512),
                dot_nt(acted_v[r * part : (r + 1) * part, :], wbuf[rows_of(j, 512), :]),
            )

    def keep_f(rows, lanes, value):
        ffn_v[rows, lanes] = value

    sum_f.run(f_term, keep_f)
    for load in loads[2:]:
        load.wait()
    put_down.step(0, end)

    @pl.loop(0, 4)
    def _(r):
        rows = rows_of(r, part)

        @pl.loop(0, ff_cols // 512)
        def _(j):
            lanes = rows_of(j, 512)
            value = dot_nn(lhs[rows, :], wbuf[:, lanes])
            du_v[rows, lanes] = (value * slope_v[rows, lanes].astype(F32)).astype(BF)

    load = pltpu.make_async_copy(w_up, wbuf, local_sem.at[3])
    load.start()
    load_h2 = pltpu.make_async_copy(h2, lhs, local_sem.at[4])
    load_h2.start()
    for copy in sum_f.near_copies:
        copy.wait_send()
    sum_f.far_copy.wait_send()
    load.wait()

    def dh2_term(r, store):
        @pl.loop(0, D // 512)
        def _(j):
            store(
                slice(0, part),
                rows_of(j, 512),
                dot_nt(du_v[r * part : (r + 1) * part, :], wbuf[rows_of(j, 512), :]),
            )

    def keep_dh2(rows, lanes, value):
        acc_v[rows, lanes] = value

    sum_dh2.run(dh2_term, keep_dh2)
    put_down.step(1, end)
    put_down.step(0, mid)
    load_h2.wait()
    columns_grad(
        lhs,
        du_v,
        D,
        ff_cols,
        grad_v,
        lambda rows: pltpu.make_async_copy(grad_v, up_grad.at[rows, :], local_sem.at[3]),
    )
    put_up.begin(0)
    for turn in turns[2:]:
        put_down.step(turn, end)
    chunk = 32
    sum_f.far_copy.wait_recv()

    @pl.loop(0, part // chunk)
    def _(i):
        rows = rows_of(i, chunk)
        live = active_ref[rows, :]
        ffn = ffn_v[rows, :] + ffn_far_v[rows, :].astype(F32) + vectors[7:8, :]
        branch = attn_v[rows, :]
        result = x_v[rows, :].astype(F32) + live * (branch + ffn)
        add_rows(sums, 4, live * result * result)
        add_rows(sums, 5, live * branch * branch)
        add_rows(sums, 6, live * ffn * ffn)
        acted_v[rows, :] = result.astype(BF)

    saves = [
        pltpu.make_async_copy(acted_v.at[:pre_part, :], prefix_out, local_sem.at[4]),
        pltpu.make_async_copy(acted_v.at[pre_part:part, :], later_out, local_sem.at[5]),
    ]
    for save in saves:
        save.start()
    for turn in turns[1:]:
        put_down.step(turn, mid)
    sum_dh2.far_copy.wait_recv()

    @pl.loop(0, part // chunk)
    def _(i):
        rows = rows_of(i, chunk)
        grad = acc_v[rows, :] + far_v[rows, :].astype(F32)
        middle = x_v[rows, :].astype(F32) + attn_v[rows, :]
        _, normed, scaling = layer_norm_parts(middle, gain2, 0.0)
        back = norm_back(grad, normed, scaling, gain2)
        acc_v[rows, :] = back
        direct = active_ref[rows, :] * cot_v[rows, :].astype(F32)
        value = (direct + back).astype(BF)
        dattn_v[rows, :] = value
        add_rows(sums, 0, value.astype(F32))
        add_rows(sums, 1, grad * normed)
        add_rows(sums, 2, grad)
        add_rows(sums, 3, direct)

    get_dattn.begin()
    saves.append(pltpu.make_async_copy(acc_v, middle_grad, local_sem.at[3]))
    saves[-1].start()

    @pl.loop(0, length // chunk)
    def _(i):
        add_rows(up_sums, 0, du_v[rows_of(i, chunk), :].astype(F32))

    get_dattn.forward()
    put_down.settle()
    get_dattn.finish()
    for save in saves:
        save.wait()
    put_up.near_copy(0).wait_recv()
    for item in (put_down, put_up, get_dattn, sum_dh2, pool):
        item.drain()


def feed_back(seq_size, pre_part, later_part, *operands):
    part = pre_part + later_part
    length = 4 * part
    w_up = operands[1]
    ff_cols = w_up.shape[1]
    own_d = D // seq_size
    hbm = pl.BlockSpec(memory_space=pl.ANY)
    vmem = pl.BlockSpec(memory_space=pltpu.VMEM)

    def out(shape, kind=BF):
        return jax.ShapeDtypeStruct(shape, kind)

    lines = seq_size // 2
    near_rows = lines * own_d
    whole = own_d
    chains = 2 * (lines - 1)
    outs = (
        out((near_rows, ff_cols)),
        out((chains * whole, ff_cols)),
        out((near_rows, ff_cols)),
        out((D, ff_cols)),
        out((length, D)),
        out((part, D), F32),
        out((pre_part, D)),
        out((later_part, D)),
        out((8, D), F32),
        out((8, ff_cols), F32),
    )
    dma = pltpu.SemaphoreType.DMA
    return pl.pallas_call(
        functools.partial(feed_back_kernel, (seq_size, pre_part, later_part)),
        out_shape=outs,
        in_specs=[hbm] * 12 + [vmem] * (len(operands) - 12),
        out_specs=[hbm] * 8 + [vmem] * 2,
        scratch_shapes=[
            pltpu.VMEM((D, ff_cols), BF),
            pltpu.VMEM((length, D), BF),
            pltpu.VMEM((length, ff_cols), BF),
            pltpu.VMEM((length, ff_cols), BF),
            pltpu.VMEM((length, ff_cols), BF),
            pltpu.VMEM((part, D), BF),
            pltpu.VMEM((part, D), BF),
            pltpu.VMEM((part, D), F32),
            pltpu.VMEM((part, D), F32),
            pltpu.VMEM((part, D), F32),
            pltpu.VMEM((part, D), BF),
            pltpu.VMEM((2, part, D), BF),
            pltpu.VMEM((2, part, D), BF),
            pltpu.VMEM((part, D), BF),
            pltpu.VMEM((part, D), BF),
            pltpu.VMEM((2, part, D), BF),
            pltpu.VMEM((part, D), BF),
            pltpu.VMEM((whole, ff_cols), BF),
            pltpu.VMEM((own_d, ff_cols), BF),
            pltpu.VMEM((whole, ff_cols), BF),
            pltpu.VMEM((3, whole, ff_cols), BF),
            pltpu.VMEM((256, ff_cols), BF),
            dma((lines,)),
            dma((lines,)),
            dma((lines,)),
            dma((chains,)),
            dma((lines,)),
            dma((lines,)),
            dma((4,)),
            dma((4,)),
            dma((2, 3)),
            dma((2, 3)),
            dma((16,)),
        ],
        compiler_params=pltpu.CompilerParams(
            collective_id=1, has_side_effects=True, vmem_limit_bytes=62 * 2**20
        ),
        cost_estimate=pl.CostEstimate(
            flops=2 * length * D * 3 * ff_cols,
            bytes_accessed=8 * D * ff_cols,
            transcendentals=length,
        ),
        name="feed_back",
    )(*operands)


def attend_back_pair(pair, cols, qkv, do, stats, codes_q, codes_k, dq_all, dk_all, dv_all, dqkv):
    lanes = [pl.ds(pl.multiple_of(third * cols + pair * 128, 128), 128) for third in range(3)]
    dk_all[...] = jnp.zeros_like(dk_all)
    dv_all[...] = jnp.zeros_like(dv_all)
    blocks = qkv.shape[0] // TILE
    for block in range(blocks):
        rows = slice(block * TILE, (block + 1) * TILE)
        both_q = qkv[rows, lanes[0]]
        both_do = do[rows, lanes_of(pair)]
        both_levels = stats[rows, lanes_of(pair)]
        parts = []
        for head in range(2):
            queries = head_lanes(both_q, head)
            grads = head_lanes(both_do, head)
            level = both_levels[:, head * HEAD_DIM : head * HEAD_DIM + 1]
            probs = []
            dprobs = []
            for tile in range(block + 1):
                keys = slice(tile * TILE, (tile + 1) * TILE)
                scores = masked_scores(
                    block, dot_nt(queries, qkv[keys, lanes[1]]), tile, codes_q, codes_k
                )
                probs.append(jnp.exp(scores - level))
                dprobs.append(dot_nt(grads, qkv[keys, lanes[2]]))
            delta = functools.reduce(
                jnp.add, [jnp.sum(a * b, axis=1, keepdims=True) for a, b in zip(probs, dprobs)]
            )
            dq = None
            for tile in range(block + 1):
                keys = slice(tile * TILE, (tile + 1) * TILE)
                ds = (probs[tile] * (dprobs[tile] - delta)).astype(BF)
                part = dot_nn(ds, qkv[keys, lanes[1]])
                dq = part if dq is None else dq + part
                dk_all[keys, :] += dot_tn(ds, queries)
                dv_all[keys, :] += dot_tn(probs[tile].astype(BF), grads)
            parts.append(dq)
        dq_all[rows, :] = join_heads(*parts) * (1.0 / math.sqrt(HEAD_DIM))
    for lane, source in zip(lanes, (dq_all, dk_all, dv_all)):
        dqkv[:, lane] = source[...].astype(BF)


def attend_back_kernel(
    sizes,
    w_qkv,
    w_out,
    h1,
    qkv,
    stats,
    mixed,
    dattn,
    middle_grad,
    up_grad,
    down_grad,
    near_down,
    chain_down,
    early_up,
    prefix_in,
    later_in,
    prefix_cot,
    later_cot,
    active_ref,
    vectors,
    feed_sums,
    up_sums,
    codes_q,
    codes_k,
    fin_down,
    fin_up,
    fin_qkv,
    fin_out,
    tail_down,
    near_up,
    chain_up,
    tail_up,
    near_out,
    chain_out,
    tail_out,
    near_qkv,
    chain_qkv,
    tail_qkv,
    out_grad,
    qkv_grad,
    prefix_grad,
    later_grad,
    sums,
    wbuf,
    lhs,
    qkv_v,
    stats_v,
    do_v,
    mixed_v,
    dqkv_v,
    dq_v,
    dk_v,
    dv_v,
    x_v,
    cot_v,
    middle_v,
    acc_v,
    terms_v,
    near_v,
    pass_v,
    far_v,
    left_v,
    right_v,
    third_v,
    fourth_v,
    out_v,
    grad_v,
    res_down,
    res_up,
    res_qkv,
    res_out,
    moved_out,
    qkv_sums,
    sums_land,
    total_send,
    total_recv,
    relay_sem,
    twin_send,
    twin_recv,
    chain_send,
    chain_recv,
    tail_sem,
    spread_send,
    spread_recv,
    sum_send,
    sum_recv,
    local_sem,
):
    seq_size, pre_part, later_part = sizes
    part = pre_part + later_part
    length = 4 * part
    width = w_qkv.shape[1]
    cols = width // 3
    ff_cols = up_grad.shape[1]
    own_d = D // seq_size
    own_o = cols // seq_size
    pre = lax.axis_index("pre")
    wide = wide_masks(seq_size)
    lines = seq_size // 2
    line = lax.div(lax.axis_index("seq"), jnp.int32(2))
    end = (line == 0) | (line == lines - 1)
    mid = jnp.logical_not(end)
    turns = range(lines - 1)
    pool = Pool(out_v, 3)
    work = (left_v, right_v, third_v, fourth_v, out_v, pool, local_sem.at[24:29])

    def reduce_of(i, grad, near, chain, tail, rows, columns, split=False):
        j = max(i, 1) - 1
        sems = (twin_send.at[j], twin_recv.at[j], chain_send.at[j], chain_recv.at[j], tail_sem.at[i])
        return Reduce(grad, near, chain, tail, rows, columns, sems, work, seq_size, split)

    put_down = reduce_of(0, down_grad, near_down, chain_down, tail_down, own_d, ff_cols)
    put_up = reduce_of(1, up_grad, near_up, chain_up, tail_up, own_d, ff_cols)
    put_out = reduce_of(2, out_grad, near_out, chain_out, tail_out, own_o, D)
    put_qkv = reduce_of(3, qkv_grad, near_qkv, chain_qkv, tail_qkv, own_d, width)

    def spread_of(i, own, land):
        return Spread(own, land, own_d, spread_send.at[i], spread_recv.at[i], local_sem.at[2 + i])

    get_down = spread_of(0, res_down, fin_down)
    get_up = spread_of(1, res_up, fin_up)
    get_qkv = spread_of(2, res_qkv, fin_qkv)
    sum_dh1 = Sum(terms_v, near_v, pass_v, far_v, sum_send, sum_recv)
    chunk = 32

    relay = Relay(seq_size, relay_sem.at[0], relay_sem.at[1], relay_sem.at[2])
    relayed = (res_out, moved_out, relay.back)
    get_out = Spread(
        moved_out, fin_out, own_o, spread_send.at[3], spread_recv.at[3], local_sem.at[20]
    )
    bits = [1 << i for i in range(seq_size.bit_length() - 1)]
    greet(sorted({*wide, *bits}), relay)
    put_up.begin(*turns[1:])
    stages = [
        remote(sums, sums_land.at[i], total_send.at[i], total_recv.at[i], **target)
        for i, target in enumerate(
            [{"pre": xor(pre, 1)}, {"pre": xor(pre, 2)}]
            + [{"seq": xor(lax.axis_index("seq"), bit)} for bit in bits]
        )
    ]

    def add_stage(i, onward=True):
        stages[i].wait_recv()
        stages[i].wait_send()
        sums[...] += sums_land[i]
        if onward:
            stages[i + 1].start()

    def load_all(first, *pairs):
        copies = [
            pltpu.make_async_copy(src, dst, local_sem.at[first + i])
            for i, (src, dst) in enumerate(pairs)
        ]
        for copy in copies:
            copy.start()
        return copies

    def wait_all(copies):
        for copy in copies:
            copy.wait()

    loads = load_all(5, (w_out, wbuf.at[:cols, :]), (dattn, lhs))
    more = load_all(
        8,
        (prefix_in, x_v.at[:pre_part, :]),
        (later_in, x_v.at[pre_part:, :]),
        (prefix_cot, cot_v.at[:pre_part, :]),
        (later_cot, cot_v.at[pre_part:, :]),
        (middle_grad, middle_v),
        (qkv, qkv_v),
        (stats, stats_v),
        (mixed, mixed_v),
    )
    sums[...] = jnp.zeros_like(sums)
    qkv_sums[...] = jnp.zeros_like(qkv_sums)
    put_up.step(0, end, early_up)
    put_down.final(res_down)
    get_down.begin()
    def keep(rows, lanes, value):
        acc_v[rows, lanes] = value

    wait_all(loads)
    wait_all(more)

    def position_rows(r):
        member = lax.rem(r, 2) * (xor(pre, 1) - pre) + lax.div(r, 2) * (xor(pre, 2) - pre) + pre
        return (
            rows_of(member, pre_part),
            pl.ds(pl.multiple_of(4 * pre_part + member * later_part, 64), later_part),
        )

    @pl.loop(0, 4)
    def _(r):
        head_rows, tail_rows = position_rows(r)
        value = dot_nt(lhs[rows_of(r, part), :], wbuf[:cols, :]).astype(BF)
        do_v[head_rows, :] = value[:pre_part]
        do_v[tail_rows, :] = value[pre_part:]

    columns_grad(
        mixed_v,
        lhs,
        cols,
        D,
        grad_v,
        lambda rows: pltpu.make_async_copy(grad_v.at[:, :D], out_grad.at[rows, :], local_sem.at[5]),
    )
    put_out.begin(*turns)
    put_up.begin(lines - 1)
    put_out.begin(lines - 1)
    loads = load_all(5, (w_qkv, wbuf.at[:, :width]))
    for r in range(4):
        head_rows, tail_rows = position_rows(jnp.int32(r))
        loads += load_all(
            8 + 2 * r,
            (h1.at[r * part : r * part + pre_part, :], lhs.at[head_rows, :]),
            (h1.at[r * part + pre_part : (r + 1) * part, :], lhs.at[tail_rows, :]),
        )
    pairs = cols // 128

    def attention(first, last):
        @pl.loop(first, last)
        def _(pair):
            attend_back_pair(
                pair,
                cols,
                qkv_v,
                do_v,
                stats_v,
                codes_q[...],
                codes_k[...],
                dq_v,
                dk_v,
                dv_v,
                dqkv_v,
            )

    put_up.step(0, mid, early_up)
    attention(0, pairs // 2)
    put_up.step(1, end)
    attention(pairs // 2, pairs)
    for turn in turns[2:]:
        put_up.step(turn, end)
    for turn in turns[1:]:
        put_up.step(turn, mid)
    get_down.forward()
    wait_all(loads)
    columns_grad(
        lhs,
        dqkv_v,
        D,
        width,
        grad_v,
        lambda rows: pltpu.make_async_copy(
            grad_v.at[:, :width], qkv_grad.at[rows, :], local_sem.at[5]
        ),
    )
    put_qkv.begin(*turns, lines - 1)
    get_down.finish()
    for turn in turns:
        put_out.step(turn, end)

    def dh1_term(r, store):
        head_rows, tail_rows = position_rows(jnp.int32(r))

        @pl.loop(0, D // 512)
        def _(j):
            weights = wbuf[rows_of(j, 512), :width]
            store(slice(0, pre_part), rows_of(j, 512), dot_nt(dqkv_v[head_rows, :], weights))
            store(slice(pre_part, part), rows_of(j, 512), dot_nt(dqkv_v[tail_rows, :], weights))

    sum_dh1.run(dh1_term, keep)

    @pl.loop(0, length // chunk)
    def _(i):
        add_rows(qkv_sums, 0, dqkv_v[rows_of(i, chunk), :].astype(F32))

    put_qkv.step(0, end)
    for turn in turns:
        put_out.step(turn, mid)
    put_up.settle()
    put_up.final(res_up)
    put_qkv.step(1, end)
    put_up.last(res_up)
    get_up.begin()
    put_qkv.step(0, mid)
    sum_dh1.far_copy.wait_recv()

    @pl.loop(0, part // chunk)
    def _(i):
        rows = rows_of(i, chunk)
        grad = acc_v[rows, :] + far_v[rows, :].astype(F32)
        _, normed, scaling = layer_norm_parts(x_v[rows, :].astype(F32), vectors[0:1, :], 0.0)
        back = norm_back(grad, normed, scaling, vectors[0:1, :])
        add_rows(sums, 0, grad * normed)
        add_rows(sums, 1, grad)
        value = cot_v[rows, :].astype(F32) + middle_v[rows, :] + back
        terms_rows = value.astype(BF)
        x_v[rows, :] = terms_rows

    saves = load_all(6, (x_v.at[:pre_part, :], prefix_grad), (x_v.at[pre_part:, :], later_grad))
    own_lanes = pl.ds(pl.multiple_of(pre * cols, cols), cols)
    sums[2:5, :] = feed_sums[4:7, :]
    sums[5:9, :] = feed_sums[:4, :]
    sums[9:10, own_lanes] = qkv_sums[0:1, :cols]
    sums[10:11, own_lanes] = qkv_sums[0:1, 2 * cols :]
    for k in range(4):
        sums[11 + k : 12 + k, own_lanes] = jnp.concatenate(
            [
                up_sums[0:1, (i * 4 + k) * own_d : (i * 4 + k + 1) * own_d]
                for i in range(seq_size // 4)
            ],
            axis=1,
        )
    sums[15:16, :] = jnp.zeros((1, D), F32) + jnp.sum(active_ref[...])
    stages[0].start()
    for turn in turns[2:]:
        put_qkv.step(turn, end)
    put_out.settle()
    put_out.final(res_out)
    add_stage(0)
    wait_all(saves)
    put_out.last(res_out)
    relay.begin(*relayed)
    for turn in turns[1:]:
        put_qkv.step(turn, mid)
    add_stage(1, False)
    get_up.forward()
    relay.finish(*relayed)
    get_out.begin()
    put_qkv.settle()
    put_qkv.final(res_qkv)
    put_qkv.last(res_qkv)
    get_qkv.begin()
    stages[2].start()
    get_out.forward()
    get_up.finish()
    for i in range(2, len(stages)):
        add_stage(i, i + 1 < len(stages))
    get_out.finish()
    get_qkv.forward()
    get_qkv.finish()
    for item in (put_up, put_out, put_qkv, get_down, get_up, get_out, get_qkv, sum_dh1, pool):
        item.drain()


def attend_back(seq_size, pre_part, later_part, *operands):
    part = pre_part + later_part
    length = 4 * part
    width = operands[0].shape[1]
    cols = width // 3
    ff_cols = FF // 4
    own_d = D // seq_size
    own_o = cols // seq_size
    lines = seq_size // 2
    chains = 2 * (lines - 1)
    early_d, early_o = 0, 0
    least = 16

    def landings(rows, early, columns):
        return (
            out((lines * (rows - early), columns)),
            out((chains * (rows + early), columns)),
            out((max(early, least), columns)),
        )

    hbm = pl.BlockSpec(memory_space=pl.ANY)
    vmem = pl.BlockSpec(memory_space=pltpu.VMEM)

    def out(shape, kind=BF):
        return jax.ShapeDtypeStruct(shape, kind)

    outs = (
        out((4 * own_d, ff_cols)),
        out((4 * own_d, ff_cols)),
        out((4 * own_d, width)),
        out((4 * own_o, D)),
        out((max(early_d, least), ff_cols)),
        *landings(own_d, early_d, ff_cols),
        *landings(own_o, early_o, D),
        *landings(own_d, 0, width),
        out((cols, D)),
        out((D, width)),
        out((pre_part, D)),
        out((later_part, D)),
        out((16, D), F32),
    )
    most = max(ff_cols, D, width)
    stages = 1 + seq_size.bit_length()
    dma = pltpu.SemaphoreType.DMA
    return pl.pallas_call(
        functools.partial(attend_back_kernel, (seq_size, pre_part, later_part)),
        out_shape=outs,
        in_specs=[hbm] * 17 + [vmem] * (len(operands) - 17),
        out_specs=[hbm] * (len(outs) - 1) + [vmem],
        scratch_shapes=[
            pltpu.VMEM((D, most), BF),
            pltpu.VMEM((length, D), BF),
            pltpu.VMEM((length, width), BF),
            pltpu.VMEM((length, cols), F32),
            pltpu.VMEM((length, cols), BF),
            pltpu.VMEM((length, cols), BF),
            pltpu.VMEM((length, width), BF),
            pltpu.VMEM((length, 128), F32),
            pltpu.VMEM((length, 128), F32),
            pltpu.VMEM((length, 128), F32),
            pltpu.VMEM((part, D), BF),
            pltpu.VMEM((part, D), BF),
            pltpu.VMEM((part, D), F32),
            pltpu.VMEM((part, D), F32),
            pltpu.VMEM((2, part, D), BF),
            pltpu.VMEM((2, part, D), BF),
            pltpu.VMEM((part, D), BF),
            pltpu.VMEM((part, D), BF),
            pltpu.VMEM((own_d + early_d, most), BF),
            pltpu.VMEM((own_d, most), BF),
            pltpu.VMEM((own_d + early_d, most), BF),
            pltpu.VMEM((own_d + early_d, most), BF),
            pltpu.VMEM((3, own_d + early_d, most), BF),
            pltpu.VMEM((256, most), BF),
            pltpu.VMEM((own_d, ff_cols), BF),
            pltpu.VMEM((own_d, ff_cols), BF),
            pltpu.VMEM((own_d, width), BF),
            pltpu.VMEM((own_o, D), BF),
            pltpu.VMEM((own_o, D), BF),
            pltpu.VMEM((8, width), F32),
            pltpu.VMEM((stages, 16, D), F32),
            dma((stages,)),
            dma((stages,)),
            dma((3,)),
            dma((3, lines)),
            dma((3, lines)),
            dma((3, lines)),
            dma((3, chains)),
            dma((4, 2)),
            dma((4, 4)),
            dma((4, 4)),
            dma((3,)),
            dma((3,)),
            dma((29,)),
        ],
        compiler_params=pltpu.CompilerParams(
            collective_id=2, has_side_effects=True, vmem_limit_bytes=63 * 2**20
        ),
        cost_estimate=pl.CostEstimate(
            flops=2 * length * D * (2 * width + ff_cols),
            bytes_accessed=8 * D * ff_cols,
            transcendentals=length * length,
        ),
        name="attend_back",
    )(*operands)


def assemble_kernel(place_ref, down, up, qkv, out, down_full, up_full, qkv_full, out_full):
    for source, target in ((qkv, qkv_full), (down, down_full), (up, up_full), (out, out_full)):
        target[...] = source[...].astype(F32)


def assemble(place, down, up, qkv, out):
    rows, ff_cols = down.shape[0] // 4, down.shape[1]
    cols = qkv.shape[1] // 3
    out_rows = out.shape[0] // 4

    def member(slot, place_ref):
        return jnp.bitwise_xor(slot, place_ref[0])

    wide = ff_cols // 4
    wide_in = pl.BlockSpec((rows, wide), lambda slot, q, p: (slot, q))
    wide_out = pl.BlockSpec((rows, wide), lambda slot, q, p: (0, member(slot, p) * 4 + q))
    out_cols = out.shape[1] // 4
    return pl.pallas_call(
        assemble_kernel,
        out_shape=(
            jax.ShapeDtypeStruct((rows, 4 * ff_cols), F32),
            jax.ShapeDtypeStruct((rows, 4 * ff_cols), F32),
            jax.ShapeDtypeStruct((rows, 12 * cols), F32),
            jax.ShapeDtypeStruct((4 * out_rows, out.shape[1]), F32),
        ),
        grid_spec=pltpu.PrefetchScalarGridSpec(
            num_scalar_prefetch=1,
            grid=(4, 4),
            in_specs=[
                wide_in,
                wide_in,
                pl.BlockSpec((rows, cols), lambda slot, q, p: (slot, jnp.minimum(q, 2))),
                pl.BlockSpec((out_rows, out_cols), lambda slot, q, p: (slot, q)),
            ],
            out_specs=[
                wide_out,
                wide_out,
                pl.BlockSpec(
                    (rows, cols),
                    lambda slot, q, p: (0, jnp.minimum(q, 2) * 4 + member(slot, p)),
                ),
                pl.BlockSpec(
                    (out_rows, out_cols), lambda slot, q, p: (member(slot, p), q)
                ),
            ],
        ),
        compiler_params=pltpu.CompilerParams(vmem_limit_bytes=62 * 2**20),
        name="assemble",
    )(place, down, up, qkv, out)


def on_device(
    prefix_in,
    later_in,
    doc_lengths,
    doc_exit,
    token_skip,
    first_gain,
    first_bias,
    qkv_weight,
    query_bias,
    value_bias,
    out_weight,
    out_bias,
    second_gain,
    second_bias,
    up_weight,
    up_bias,
    down_weight,
    down_bias,
    prefix_cot,
    later_cot,
):
    pre_part = prefix_in.shape[1]
    later_part = later_in.shape[1]
    part = pre_part + later_part
    parts = lax.axis_size("pre")
    place = lax.axis_index("pre")
    seq_count = lax.axis_size("seq")
    seq_place = lax.axis_index("seq")
    own_d = D // seq_count
    cols = D // parts

    vectors_in = [
        first_gain,
        first_bias,
        query_bias,
        value_bias,
        out_bias,
        second_gain,
        second_bias,
        down_bias,
    ] + [up_bias[k * own_d : (k + 1) * own_d] for k in range(4)]
    flat = jnp.zeros((16 * own_d,), F32)
    for i, vector in enumerate(vectors_in):
        flat = flat + jnp.pad(vector.astype(F32), (i * own_d, (15 - i) * own_d))
    small = flat.reshape(16, own_d)

    doc_id, live = token_tables(doc_lengths, doc_exit, token_skip)
    live_here = lax.dynamic_slice_in_dim(live[0], place * later_part, later_part, 0)
    active = jnp.concatenate([jnp.ones((pre_part,), F32), live_here.astype(F32)])[:, None]
    codes_q = jnp.concatenate([jnp.full((PRE,), -1, jnp.int32), doc_id[0]])[:, None]
    codes_k = jnp.concatenate(
        [jnp.full((PRE,), -1, jnp.int32), jnp.where(live[0], doc_id[0], -2)]
    )[None, :]

    (w_qkv, w_out, w_up, w_down, h1, df, h2, qkv, mixed, stats, attn, acted, slope, down_grad, vectors) = forward_pass(
        seq_count,
        pre_part,
        later_part,
        small,
        qkv_weight,
        out_weight,
        up_weight,
        down_weight,
        prefix_in[0],
        later_in[0],
        prefix_cot[0],
        later_cot[0],
        active,
        codes_q,
        codes_k,
    )

    rows_in = (prefix_in[0], later_in[0], prefix_cot[0], later_cot[0], active)
    (near_down, chain_down, early_up, up_grad, dattn, middle_grad, prefix_out, later_out, feed_sums, up_sums) = feed_back(
        seq_count,
        pre_part,
        later_part,
        w_down,
        w_up,
        acted,
        df,
        h2,
        slope,
        attn,
        down_grad,
        *rows_in,
        vectors,
    )
    (fin_down, fin_up, fin_qkv, fin_out, *_, prefix_grad, later_grad, sums) = attend_back(
        seq_count,
        pre_part,
        later_part,
        w_qkv,
        w_out,
        h1,
        qkv,
        stats,
        mixed,
        dattn,
        middle_grad,
        up_grad,
        down_grad,
        near_down,
        chain_down,
        early_up,
        *rows_in,
        vectors,
        feed_sums,
        up_sums,
        codes_q,
        codes_k,
    )

    down_full, up_full, qkv_full, out_full = assemble(
        place.reshape(1).astype(jnp.int32), fin_down, fin_up, fin_qkv, fin_out
    )
    mine = lax.dynamic_slice_in_dim(sums, seq_place * own_d, own_d, 1)
    residual_rms = jnp.sqrt(jnp.sum(sums[2:5], axis=1) / (sums[15, 0] * D))
    return (
        prefix_out[None],
        later_out[None],
        prefix_grad[None],
        later_grad[None],
        mine[0],
        mine[1],
        qkv_full,
        mine[9],
        mine[10],
        out_full,
        mine[5],
        mine[6],
        mine[7],
        up_full,
        mine[11:15].reshape(-1),
        down_full,
        mine[8],
        residual_rms,
    )


def solution(mesh):
    placed = (
        P("seq", "pre", None),
        P("seq", "pre", None),
        P("seq", None),
        P("seq", None),
        P("seq", None),
        P("seq"),
        P("seq"),
        P("seq", None),
        P("seq"),
        P("seq"),
        P("seq", None),
        P("seq"),
        P("seq"),
        P("seq"),
        P("seq", None),
        P("seq"),
        P("seq", None),
        P("seq"),
        P("seq", "pre", None),
        P("seq", "pre", None),
    )
    return jax.shard_map(
        on_device,
        mesh=mesh,
        in_specs=placed,
        out_specs=(
            P("seq", "pre", None),
            P("seq", "pre", None),
            P("seq", "pre", None),
            P("seq", "pre", None),
            P("seq"),
            P("seq"),
            P("seq", None),
            P("seq"),
            P("seq"),
            P("seq", None),
            P("seq"),
            P("seq"),
            P("seq"),
            P("seq", None),
            P("seq"),
            P("seq", None),
            P("seq"),
            P(),
        ),
        check_vma=False,
    )
```
